32 devices in a mesh: gx: 2 (over x), gy: 4 (over y, core), ch: 4 (over z).
Axes of the slice: x: 2, y: 2, z: 4, core: 2. Of those that a mesh axis runs over, the one named last changes fastest.
Arguments:
- inputs: bfloat16 [8, 16, 32, 256], P('gx', 'gy', None, 'ch'), may hold values from -6 to 6
- weight: bfloat16 [3, 3, 3, 256, 256], P(None, None, None, 'ch'), may hold values from -0.109375 to 0.109375
- bias: bfloat16 [256], P('ch'), may hold values from -3 to 3
- cotangent: bfloat16 [8, 16, 32, 256], P('gx', 'gy', None, 'ch'), may hold values from -6 to 6
Outputs:
- activation: bfloat16 [8, 16, 32, 256], P('gx', 'gy', None, 'ch')
- input_grad: bfloat16 [8, 16, 32, 256], P('gx', 'gy', None, 'ch')
- weight_grad: float32 [3, 3, 3, 256, 256], P(None, None, None, 'ch')
- bias_grad: float32 [256], P('ch')
The draws below stay inside these ranges and needn't reach their ends.
All inputs are finite; a program needn't handle non-finite values.
Results may differ from the reference program's by a relative error of at most 0.0075.
Values may be sent and summed in bfloat16 or wider, within the bound.
No kernel may reach another device: no remote copies, remote signals or barrier semaphores. Data moves between devices by JAX's collectives and lax.ppermute only.
A program may use at most 64 MiB of HBM per device.

```python
import math
import jax
import jax.numpy as jnp
from jax import lax

CHANNELS = 256
DEPTH = 32
EXTENT_X = 8
EXTENT_Y = 16


def strengthened(array, rng, source, target, parts, factor):
    def block_of(axis_at):
        return (jnp.arange(array.shape[axis_at]) // (array.shape[axis_at] // parts)).reshape((-1,) + (1,) * (array.ndim - 1 - axis_at))

    one_side = jax.random.permutation(rng, parts)[block_of(target)]
    second = (block_of(target) + parts // 2) % parts
    return jnp.where((block_of(source) == one_side) | (block_of(source) == second), factor * array, array)


def block_levels(key, shape, cuts, smallest, high):
    def one(dim, blocks):
        heights = jax.random.uniform(jax.random.fold_in(jax.random.fold_in(key, 6), dim), (blocks,), jnp.float32, smallest / len(cuts), high / len(cuts))
        return jnp.repeat(jnp.exp(heights), shape[dim] // blocks).reshape((-1,) + (1,) * (len(shape) - dim - 1))

    loudness = one(*cuts[0])
    for cut in cuts[1:]:
        loudness = loudness * one(*cut)
    return loudness


def bell_draw(stream_key, extent, scale, bound, split=(), kind=jnp.bfloat16):
    result = scale * jax.random.normal(stream_key, extent, jnp.float32)
    if split:
        result = result * block_levels(stream_key, extent, split, -0.22, 0.18)
    return jnp.clip(result, -bound, bound).astype(kind)


def bell_draw_with(stream_key, extent, spread, reach, shards, heavy, held_as=jnp.bfloat16):
    result = spread * jax.random.normal(stream_key, extent, jnp.float32)
    if shards:
        result = result * block_levels(stream_key, extent, shards, -0.22, 0.18)
    return jnp.clip(strengthened(result, jax.random.fold_in(stream_key, 3), *heavy), -reach, reach).astype(held_as)


def setup_inputs(seed: int = 0) -> dict:
    key_list = jax.random.split(jax.random.key(seed), 5)
    inputs = bell_draw(key_list[0], (EXTENT_X, EXTENT_Y, DEPTH, CHANNELS), 1.0, 6.0, ((0, 2), (1, 4), (3, 4)))
    weight = bell_draw_with(key_list[1], (3, 3, 3, CHANNELS, CHANNELS), (27 * CHANNELS) ** -0.5, 0.109375, ((3, 4),), (3, 4, 4, 2.0))
    bias = bell_draw(key_list[2], (CHANNELS,), 0.5, 3.0, ((0, 4),))
    cotangent = bell_draw(key_list[3], (EXTENT_X, EXTENT_Y, DEPTH, CHANNELS), 1.0, 6.0, ((0, 2), (1, 4), (3, 4)))
    return {"inputs": inputs, "weight": weight, "bias": bias, "cotangent": cotangent}


def window(volume, first, second, third, span_x, span_y, span_z):
    piece = volume[first:first + span_x, second:second + span_y, third:third + span_z]
    return piece.reshape(span_x * span_y * span_z, volume.shape[3])

def reference(inputs, weight, bias, cotangent):
    span_x, span_y, span_z, channels = inputs.shape
    volume_cells = span_x * span_y * span_z
    edges = ((1, 1), (1, 1), (1, 1), (0, 0))
    padded = jnp.pad(inputs, edges)
    offsets = [(a, b, c) for a in range(3) for b in range(3) for c in range(3)]
    summed = jnp.zeros((volume_cells, channels), jnp.float32)
    for a, b, c in offsets:
        summed = summed + jnp.dot(window(padded, a, b, c, span_x, span_y, span_z), weight[a, b, c], preferred_element_type=jnp.float32)
    summed = summed + bias.astype(jnp.float32)
    activation = jax.nn.silu(summed).astype(jnp.bfloat16)
    sigmoid_pre = jax.nn.sigmoid(summed)
    slope = (cotangent.reshape(volume_cells, channels).astype(jnp.float32) * sigmoid_pre * (1.0 + summed * (1.0 - sigmoid_pre))).astype(jnp.bfloat16)
    slope_pad = jnp.pad(slope.reshape(span_x, span_y, span_z, channels), edges)
    back_sum = jnp.zeros((volume_cells, channels), jnp.float32)
    grads = []
    for a, b, c in offsets:
        back_sum = back_sum + jnp.dot(window(slope_pad, 2 - a, 2 - b, 2 - c, span_x, span_y, span_z), weight[a, b, c].T, preferred_element_type=jnp.float32)
        grads.append(jnp.dot(window(padded, a, b, c, span_x, span_y, span_z).T, slope, preferred_element_type=jnp.float32))
    factor = 1.0 / math.sqrt(volume_cells)
    weight_grad = jnp.stack(grads).reshape(3, 3, 3, channels, channels) * factor
    bias_grad = lax.optimization_barrier(jnp.sum(slope.astype(jnp.float32), axis=0)) * factor
    return (activation.reshape(inputs.shape), back_sum.astype(jnp.bfloat16).reshape(inputs.shape), weight_grad, bias_grad)
```

```python
import functools
import math

import jax
import jax.numpy as jnp
from jax import lax
from jax.experimental import pallas as pl
from jax.experimental.pallas import tpu as pltpu
from jax.sharding import PartitionSpec as P

VMEM = pl.BlockSpec(memory_space=pltpu.VMEM)
SMEM = pl.BlockSpec(memory_space=pltpu.SMEM)
PARAMS = pltpu.CompilerParams(vmem_limit_bytes=48 * 1024 * 1024)
F32 = jnp.float32
BF16 = jnp.bfloat16


def with_halo(x, sides, width):
    for axis, dim in sides:
        devices, length = (lax.axis_size(axis), x.shape[dim])
        up = [(i, (i + 1) % devices) for i in range(devices - 1)]
        down = [(j, i) for i, j in up]
        last = lax.slice_in_dim(x, length - width, length, axis=dim)
        initial = lax.slice_in_dim(x, 0, width, axis=dim)
        before = lax.ppermute(last, axis, up)
        after = lax.ppermute(initial, axis, down)
        x = jnp.concatenate([before, x, after], axis=dim)
    return x


def body_reduced(inputs, weight, bias, cotangent):
    span_x, span_y, span_z, local_ch = inputs.shape
    widest = weight.shape[4]
    local_cells = span_x * span_y * span_z
    offsets = [(a, b, c) for a in range(3) for b in range(3) for c in range(3)]
    depth_pad = ((0, 0), (0, 0), (1, 1), (0, 0))
    rimmed = with_halo(inputs, (("gx", 0), ("gy", 1)), 1)
    padded = jnp.pad(rimmed, depth_pad)
    blocks = []
    for a, b, c in offsets:
        blocks.append(
            padded[a : a + span_x, b : b + span_y, c : c + span_z].reshape(local_cells, local_ch)
        )
    patches = jnp.concatenate(blocks, axis=1)
    flat_weight = weight.reshape(27 * local_ch, widest)
    summed = lax.psum_scatter(
        lax.dot_general(flat_weight, patches, (((0,), (1,)), ((), ())), preferred_element_type=F32),
        "ch",
        scatter_dimension=0,
        tiled=True,
    ).T
    summed = summed + bias.astype(F32)[None, :]
    activation = jax.nn.silu(summed).astype(BF16).reshape(span_x, span_y, span_z, local_ch)
    sigmoid_pre = jax.nn.sigmoid(summed)
    slope = (
        cotangent.reshape(local_cells, local_ch).astype(F32)
        * sigmoid_pre
        * (1.0 + summed * (1.0 - sigmoid_pre))
    ).astype(BF16)
    local_bias = jnp.sum(slope.astype(F32), axis=0)
    slope_grid = slope.reshape(span_x, span_y, span_z, local_ch)
    weight_turned = jnp.transpose(weight.reshape(27, local_ch, widest), (0, 2, 1))
    slope_rimmed = with_halo(slope_grid, (("gx", 0), ("gy", 1)), 1)
    piece = lax.all_gather(slope_rimmed, "ch", axis=3, tiled=True)
    extended = jnp.pad(piece, depth_pad)
    running = jnp.zeros((local_cells, local_ch), F32)
    for index, (a, b, c) in enumerate(offsets):
        a, b, c = (2 - a, 2 - b, 2 - c)
        cut = extended[a : a + span_x, b : b + span_y, c : c + span_z].reshape(local_cells, widest)
        running = running + jnp.dot(cut, weight_turned[index], preferred_element_type=F32)
    interior = piece[1 : 1 + span_x, 1 : 1 + span_y].reshape(local_cells, widest)
    product = lax.dot_general(
        patches, interior, (((0,), (0,)), ((), ())), preferred_element_type=F32
    )
    total_cells = local_cells * lax.axis_size("gx") * lax.axis_size("gy")
    factor = 1.0 / math.sqrt(total_cells)
    kernel_total, bias_total = lax.psum((product * factor, local_bias * factor), ("gx", "gy"))
    input_grad = running.astype(BF16).reshape(span_x, span_y, span_z, local_ch)
    return (activation, input_grad, kernel_total.reshape(3, 3, 3, local_ch, widest), bias_total)


def shifted(v, by):
    depth = v.shape[1]
    row = lax.broadcasted_iota(jnp.int32, v.shape, 1)
    if by == 1:
        return jnp.where(row == 0, 0.0, pltpu.roll(v, 1, 1))
    return jnp.where(row == depth - 1, 0.0, pltpu.roll(v, depth - 1, 1))


def forward_kernel(parts_x, parts_y, spans, place, cells, weight, terms, volume):
    span_x, span_y, span_z = spans
    local = span_x * span_y * span_z
    half = local // 2
    lanes = weight.shape[1] // 3
    half_x = span_x // 2
    rows_x, rows_y = parts_x * span_x, parts_y * span_y
    width = volume.shape[3]
    zero_x = jnp.zeros((1, rows_y + 2, span_z, width), BF16)
    zero_y = jnp.zeros((rows_x + 2, 1, span_z, width), BF16)
    volume[0:1] = zero_x
    volume[rows_x + 1 : rows_x + 2] = zero_x
    volume[:, 0:1] = zero_y
    volume[:, rows_y + 1 : rows_y + 2] = zero_y
    for g in range(parts_x * parts_y):
        x0, y0 = 1 + (g // parts_y) * span_x, 1 + (g % parts_y) * span_y
        v = cells[g].astype(F32).reshape(half // span_z, span_z, 2 * lanes)
        low, high = shifted(v, 1), shifted(v, -1)
        for h in range(2):
            cut = slice(h * lanes, (h + 1) * lanes)
            joined = jnp.concatenate([low[..., cut], v[..., cut], high[..., cut]], axis=2)
            volume[x0 + h * half_x : x0 + (h + 1) * half_x, y0 : y0 + span_y] = joined.astype(
                BF16
            ).reshape(half_x, span_y, span_z, width)
    at_x, at_y = place[0] * span_x, place[1] * span_y
    sums = []
    for h in range(2):
        total = None
        for a in range(3):
            for b in range(3):
                cut = volume[pl.ds(at_x + a + h * half_x, half_x), pl.ds(at_y + b, span_y)]
                term = jnp.dot(
                    cut.reshape(half, width), weight[a * 3 + b], preferred_element_type=F32
                )
                total = term if total is None else total + term
        sums.append(total)
    for d in range(weight.shape[2] // lanes):
        cut = slice(d * lanes, (d + 1) * lanes)
        terms[d] = jnp.concatenate([sums[0][:, cut], sums[1][:, cut]], axis=1).astype(BF16)


def slope_kernel(terms, bias, cotangent, activation, slope):
    half, lanes = cotangent.shape[0] // 2, cotangent.shape[1]
    summed = terms[0].astype(F32)
    for d in range(1, terms.shape[0]):
        summed = summed + terms[d].astype(F32)
    summed = summed + bias[...].astype(F32)
    sigmoid = jax.nn.sigmoid(summed)
    active = (summed * sigmoid).astype(BF16)
    activation[:half] = active[:, :lanes]
    activation[half:] = active[:, lanes:]
    upstream = jnp.concatenate([cotangent[:half], cotangent[half:]], axis=1).astype(F32)
    slope[...] = (upstream * sigmoid * (1.0 + summed * (1.0 - sigmoid))).astype(BF16)


def backward_kernel(
    parts_x, parts_y, spans, factor, place, slopes, weight, volume, input_grad, kernel_grad, bias_grad,
    rimmed, turned,
):
    span_x, span_y, span_z = spans
    local = span_x * span_y * span_z
    half = local // 2
    lanes = weight.shape[1] // 3
    channels = weight.shape[2]
    half_x = span_x // 2
    rows_x, rows_y = parts_x * span_x, parts_y * span_y
    shards = channels // lanes
    zero_x = jnp.zeros((1, rows_y + 2, span_z, channels), BF16)
    zero_y = jnp.zeros((rows_x + 2, 1, span_z, channels), BF16)
    rimmed[0:1] = zero_x
    rimmed[rows_x + 1 : rows_x + 2] = zero_x
    rimmed[:, 0:1] = zero_y
    rimmed[:, rows_y + 1 : rows_y + 2] = zero_y
    column = jnp.zeros((1, channels), F32)
    for g in range(parts_x * parts_y):
        x0, y0 = 1 + (g // parts_y) * span_x, 1 + (g % parts_y) * span_y
        for h in range(2):
            cut = slice(h * lanes, (h + 1) * lanes)
            joined = jnp.concatenate([slopes[g, j][:, cut] for j in range(shards)], axis=1)
            rimmed[x0 + h * half_x : x0 + (h + 1) * half_x, y0 : y0 + span_y] = joined.reshape(
                half_x, span_y, span_z, channels
            )
            column = column + jnp.sum(joined.astype(F32), axis=0, keepdims=True)
            turned[:, g * local + h * half : g * local + (h + 1) * half] = joined.T
    bias_grad[...] = column * factor

    at_x, at_y = place[0] * span_x, place[1] * span_y
    for h in range(2):
        total = None
        for a in range(3):
            for b in range(3):
                cut = rimmed[pl.ds(at_x + 2 - a + h * half_x, half_x), pl.ds(at_y + 2 - b, span_y)]
                term = lax.dot_general(
                    cut.reshape(half, channels),
                    weight[a * 3 + b],
                    (((1,), (1,)), ((), ())),
                    preferred_element_type=F32,
                )
                total = term if total is None else total + term
        total = total.reshape(half // span_z, span_z, 3 * lanes)
        result = (
            shifted(total[..., :lanes], -1)
            + total[..., lanes : 2 * lanes]
            + shifted(total[..., 2 * lanes :], 1)
        )
        input_grad[h * half : (h + 1) * half] = result.reshape(half, lanes).astype(BF16)

    for a in range(3):
        for b in range(3):
            total = None
            for g in range(parts_x * parts_y):
                x0, y0 = a + (g // parts_y) * span_x, b + (g % parts_y) * span_y
                cut = volume[x0 : x0 + span_x, y0 : y0 + span_y].reshape(local, 3 * lanes)
                term = jnp.dot(
                    turned[:, g * local : (g + 1) * local], cut, preferred_element_type=F32
                )
                total = term if total is None else total + term
            kernel_grad[a * 3 + b] = (total * factor).T


def packed(x):
    half = x.shape[0] // 2
    return jnp.concatenate([x[:half], x[half:]], axis=1)


def body_gathered(inputs, weight, bias, cotangent):
    spans = inputs.shape[:3]
    span_x, span_y, span_z = spans
    local_ch, channels = weight.shape[3:]
    local = span_x * span_y * span_z
    parts_x, parts_y = lax.axis_size("gx"), lax.axis_size("gy")
    shards = lax.axis_size("ch")
    factor = 1.0 / math.sqrt(local * parts_x * parts_y)
    place = jnp.stack([lax.axis_index("gx"), lax.axis_index("gy")]).astype(jnp.int32)
    taps = weight.reshape(9, 3 * local_ch, channels)
    volume_shape = (parts_x * span_x + 2, parts_y * span_y + 2, span_z)

    cells = lax.all_gather(packed(inputs.reshape(local, local_ch)), ("gx", "gy"))
    terms, volume = pl.pallas_call(
        functools.partial(forward_kernel, parts_x, parts_y, spans),
        out_shape=(
            jax.ShapeDtypeStruct((shards, local // 2, 2 * local_ch), BF16),
            jax.ShapeDtypeStruct(volume_shape + (3 * local_ch,), BF16),
        ),
        in_specs=[SMEM, VMEM, VMEM],
        out_specs=(VMEM, VMEM),
        compiler_params=PARAMS,
        name="forward",
    )(place, cells, taps)
    terms = lax.all_to_all(terms, "ch", 0, 0)
    activation, slope = pl.pallas_call(
        slope_kernel,
        out_shape=(
            jax.ShapeDtypeStruct((local, local_ch), BF16),
            jax.ShapeDtypeStruct((local // 2, 2 * local_ch), BF16),
        ),
        in_specs=[VMEM] * 3,
        out_specs=(VMEM, VMEM),
        compiler_params=PARAMS,
        name="slope",
    )(terms, jnp.concatenate([bias, bias]).reshape(1, -1), cotangent.reshape(local, local_ch))
    slopes = lax.all_gather(lax.all_gather(slope, "ch"), ("gx", "gy"))
    input_grad, kernel_grad, bias_grad = pl.pallas_call(
        functools.partial(backward_kernel, parts_x, parts_y, spans, factor),
        out_shape=(
            jax.ShapeDtypeStruct((local, local_ch), BF16),
            jax.ShapeDtypeStruct((9, 3 * local_ch, channels), F32),
            jax.ShapeDtypeStruct((1, channels), F32),
        ),
        in_specs=[SMEM, VMEM, VMEM, VMEM],
        out_specs=(VMEM, VMEM, VMEM),
        scratch_shapes=[
            pltpu.VMEM(volume_shape + (channels,), BF16),
            pltpu.VMEM((channels, local * parts_x * parts_y), BF16),
        ],
        compiler_params=PARAMS,
        name="backward",
    )(place, slopes, taps, volume)
    bias_grad = lax.dynamic_slice(
        bias_grad.reshape(channels), (lax.axis_index("ch") * local_ch,), (local_ch,)
    )
    return (
        activation.reshape(inputs.shape),
        input_grad.reshape(inputs.shape),
        kernel_grad.reshape(weight.shape),
        bias_grad,
    )


def solution(mesh):
    few = mesh.shape["gx"] * mesh.shape["gy"] <= 8
    return jax.shard_map(
        body_gathered if few else body_reduced,
        mesh=mesh,
        in_specs=(
            P("gx", "gy", None, "ch"),
            P(None, None, None, "ch", None),
            P("ch"),
            P("gx", "gy", None, "ch"),
        ),
        out_specs=(
            P("gx", "gy", None, "ch"),
            P("gx", "gy", None, "ch"),
            P(None, None, None, "ch", None),
            P("ch"),
        ),
        check_vma=False,
    )
```

```python
import functools
import math

import jax
import jax.numpy as jnp
from jax import lax
from jax.experimental import pallas as pl
from jax.experimental.pallas import tpu as pltpu
from jax.sharding import PartitionSpec as P

VMEM = pl.BlockSpec(memory_space=pltpu.VMEM)
SMEM = pl.BlockSpec(memory_space=pltpu.SMEM)
PARAMS = pltpu.CompilerParams(vmem_limit_bytes=24 * 1024 * 1024)
F32 = jnp.float32
BF16 = jnp.bfloat16


def with_halo(x, sides, width):
    for axis, dim in sides:
        devices, length = (lax.axis_size(axis), x.shape[dim])
        up = [(i, (i + 1) % devices) for i in range(devices - 1)]
        down = [(j, i) for i, j in up]
        last = lax.slice_in_dim(x, length - width, length, axis=dim)
        initial = lax.slice_in_dim(x, 0, width, axis=dim)
        before = lax.ppermute(last, axis, up)
        after = lax.ppermute(initial, axis, down)
        x = jnp.concatenate([before, x, after], axis=dim)
    return x


def body_reduced(inputs, weight, bias, cotangent):
    span_x, span_y, span_z, local_ch = inputs.shape
    widest = weight.shape[4]
    local_cells = span_x * span_y * span_z
    offsets = [(a, b, c) for a in range(3) for b in range(3) for c in range(3)]
    depth_pad = ((0, 0), (0, 0), (1, 1), (0, 0))
    rimmed = with_halo(inputs, (("gx", 0), ("gy", 1)), 1)
    padded = jnp.pad(rimmed, depth_pad)
    blocks = []
    for a, b, c in offsets:
        blocks.append(
            padded[a : a + span_x, b : b + span_y, c : c + span_z].reshape(local_cells, local_ch)
        )
    patches = jnp.concatenate(blocks, axis=1)
    flat_weight = weight.reshape(27 * local_ch, widest)
    summed = lax.psum_scatter(
        lax.dot_general(flat_weight, patches, (((0,), (1,)), ((), ())), preferred_element_type=F32),
        "ch",
        scatter_dimension=0,
        tiled=True,
    ).T
    summed = summed + bias.astype(F32)[None, :]
    activation = jax.nn.silu(summed).astype(BF16).reshape(span_x, span_y, span_z, local_ch)
    sigmoid_pre = jax.nn.sigmoid(summed)
    slope = (
        cotangent.reshape(local_cells, local_ch).astype(F32)
        * sigmoid_pre
        * (1.0 + summed * (1.0 - sigmoid_pre))
    ).astype(BF16)
    local_bias = jnp.sum(slope.astype(F32), axis=0)
    slope_grid = slope.reshape(span_x, span_y, span_z, local_ch)
    weight_turned = jnp.transpose(weight.reshape(27, local_ch, widest), (0, 2, 1))
    slope_rimmed = with_halo(slope_grid, (("gx", 0), ("gy", 1)), 1)
    piece = lax.all_gather(slope_rimmed, "ch", axis=3, tiled=True)
    extended = jnp.pad(piece, depth_pad)
    running = jnp.zeros((local_cells, local_ch), F32)
    for index, (a, b, c) in enumerate(offsets):
        a, b, c = (2 - a, 2 - b, 2 - c)
        cut = extended[a : a + span_x, b : b + span_y, c : c + span_z].reshape(local_cells, widest)
        running = running + jnp.dot(cut, weight_turned[index], preferred_element_type=F32)
    interior = piece[1 : 1 + span_x, 1 : 1 + span_y].reshape(local_cells, widest)
    product = lax.dot_general(
        patches, interior, (((0,), (0,)), ((), ())), preferred_element_type=F32
    )
    total_cells = local_cells * lax.axis_size("gx") * lax.axis_size("gy")
    factor = 1.0 / math.sqrt(total_cells)
    kernel_total, bias_total = lax.psum((product * factor, local_bias * factor), ("gx", "gy"))
    input_grad = running.astype(BF16).reshape(span_x, span_y, span_z, local_ch)
    return (activation, input_grad, kernel_total.reshape(3, 3, 3, local_ch, widest), bias_total)


def shifted(v, by):
    depth = v.shape[1]
    row = lax.broadcasted_iota(jnp.int32, v.shape, 1)
    if by == 1:
        return jnp.where(row == 0, 0.0, pltpu.roll(v, 1, 1))
    return jnp.where(row == depth - 1, 0.0, pltpu.roll(v, depth - 1, 1))


def forward_kernel(parts_x, parts_y, spans, place, cells, weight, own, *rest):
    *others, volume, blocks = rest
    span_x, span_y, span_z = spans
    local = span_x * span_y * span_z
    half = local // 2
    lanes = weight.shape[1] // 3
    half_x = span_x // 2
    rows_x, rows_y = parts_x * span_x, parts_y * span_y
    width = volume.shape[3]
    zero_x = jnp.zeros((1, rows_y + 2, span_z, width), BF16)
    zero_y = jnp.zeros((rows_x + 2, 1, span_z, width), BF16)
    volume[0:1] = zero_x
    volume[rows_x + 1 : rows_x + 2] = zero_x
    volume[:, 0:1] = zero_y
    volume[:, rows_y + 1 : rows_y + 2] = zero_y
    for g in range(parts_x * parts_y):
        x0, y0 = 1 + (g // parts_y) * span_x, 1 + (g % parts_y) * span_y
        v = cells[g].astype(F32).reshape(half // span_z, span_z, 2 * lanes)
        low, high = shifted(v, 1), shifted(v, -1)
        for h in range(2):
            cut = slice(h * lanes, (h + 1) * lanes)
            joined = jnp.concatenate([low[..., cut], v[..., cut], high[..., cut]], axis=2)
            volume[x0 + h * half_x : x0 + (h + 1) * half_x, y0 : y0 + span_y] = joined.astype(
                BF16
            ).reshape(half_x, span_y, span_z, width)
    at_x, at_y = place[0] * span_x, place[1] * span_y
    sums = []
    for h in range(2):
        total = None
        for a in range(3):
            for b in range(3):
                cut = volume[pl.ds(at_x + a + h * half_x, half_x), pl.ds(at_y + b, span_y)]
                term = jnp.dot(
                    cut.reshape(half, width), weight[a * 3 + b], preferred_element_type=F32
                )
                total = term if total is None else total + term
        sums.append(total)
    for d in range(weight.shape[2] // lanes):
        cut = slice(d * lanes, (d + 1) * lanes)
        blocks[d] = jnp.concatenate([sums[0][:, cut], sums[1][:, cut]], axis=1)
    own[...] = blocks[place[2]]
    for k, other in enumerate(others):
        other[...] = blocks[place[2] ^ (k + 1)].astype(BF16)


def slope_kernel(own, *rest):
    *others, bias, cotangent, activation, slope = rest
    half, lanes = cotangent.shape[0] // 2, cotangent.shape[1]
    summed = own[...]
    for other in others:
        summed = summed + other[...].astype(F32)
    summed = summed + bias[...].astype(F32)
    sigmoid = jax.nn.sigmoid(summed)
    active = (summed * sigmoid).astype(BF16)
    activation[:half] = active[:, :lanes]
    activation[half:] = active[:, lanes:]
    upstream = jnp.concatenate([cotangent[:half], cotangent[half:]], axis=1).astype(F32)
    slope[...] = (upstream * sigmoid * (1.0 + summed * (1.0 - sigmoid))).astype(BF16)


def backward_kernel(
    parts_x, parts_y, spans, factor, place, weight, volume, *rest
):
    *slopes, input_grad, kernel_grad, bias_grad, rimmed, turned = rest
    span_x, span_y, span_z = spans
    local = span_x * span_y * span_z
    half = local // 2
    lanes = weight.shape[1] // 3
    channels = weight.shape[2]
    half_x = span_x // 2
    rows_x, rows_y = parts_x * span_x, parts_y * span_y
    shards = channels // lanes
    zero_x = jnp.zeros((1, rows_y + 2, span_z, channels), BF16)
    zero_y = jnp.zeros((rows_x + 2, 1, span_z, channels), BF16)
    rimmed[0:1] = zero_x
    rimmed[rows_x + 1 : rows_x + 2] = zero_x
    rimmed[:, 0:1] = zero_y
    rimmed[:, rows_y + 1 : rows_y + 2] = zero_y
    column = jnp.zeros((1, channels), F32)
    corners = []
    for m, pieces in enumerate(slopes):
        place_x, place_y = place[0] ^ (m // parts_y), place[1] ^ (m % parts_y)
        x0, y0 = place_x * span_x, place_y * span_y
        corners.append((x0, y0))
        ordered = [pieces[place[2] ^ j] for j in range(shards)]
        for h in range(2):
            cut = slice(h * lanes, (h + 1) * lanes)
            joined = jnp.concatenate([piece[:, cut] for piece in ordered], axis=1)
            rimmed[pl.ds(x0 + 1 + h * half_x, half_x), pl.ds(y0 + 1, span_y)] = joined.reshape(
                half_x, span_y, span_z, channels
            )
            column = column + jnp.sum(joined.astype(F32), axis=0, keepdims=True)
            turned[:, m * local + h * half : m * local + (h + 1) * half] = joined.T
    bias_grad[...] = column * factor

    at_x, at_y = place[0] * span_x, place[1] * span_y
    for h in range(2):
        total = None
        for a in range(3):
            for b in range(3):
                cut = rimmed[pl.ds(at_x + 2 - a + h * half_x, half_x), pl.ds(at_y + 2 - b, span_y)]
                term = lax.dot_general(
                    cut.reshape(half, channels),
                    weight[a * 3 + b],
                    (((1,), (1,)), ((), ())),
                    preferred_element_type=F32,
                )
                total = term if total is None else total + term
        total = total.reshape(half // span_z, span_z, 3 * lanes)
        result = (
            shifted(total[..., :lanes], -1)
            + total[..., lanes : 2 * lanes]
            + shifted(total[..., 2 * lanes :], 1)
        )
        input_grad[h * half : (h + 1) * half] = result.reshape(half, lanes).astype(BF16)

    for a in range(3):
        for b in range(3):
            total = None
            for m, (x0, y0) in enumerate(corners):
                cut = volume[pl.ds(x0 + a, span_x), pl.ds(y0 + b, span_y)]
                term = jnp.dot(
                    turned[:, m * local : (m + 1) * local],
                    cut.reshape(local, 3 * lanes),
                    preferred_element_type=F32,
                )
                total = term if total is None else total + term
            kernel_grad[a * 3 + b] = (total * factor).T


def exchange(x, axes, mask):
    return lax.ppermute(x, axes, [(i, i ^ mask) for i in range(lax.axis_size(axes))])


def packed(x):
    half = x.shape[0] // 2
    return jnp.concatenate([x[:half], x[half:]], axis=1)


def body_gathered(inputs, weight, bias, cotangent):
    spans = inputs.shape[:3]
    span_x, span_y, span_z = spans
    local_ch, channels = weight.shape[3:]
    local = span_x * span_y * span_z
    parts_x, parts_y = lax.axis_size("gx"), lax.axis_size("gy")
    shards = lax.axis_size("ch")
    factor = 1.0 / math.sqrt(local * parts_x * parts_y)
    place = jnp.stack([lax.axis_index(axis) for axis in ("gx", "gy", "ch")]).astype(jnp.int32)
    taps = weight.reshape(9, 3 * local_ch, channels)
    volume_shape = (parts_x * span_x + 2, parts_y * span_y + 2, span_z)

    cells = lax.all_gather(packed(inputs.reshape(local, local_ch)), ("gx", "gy"))
    packing = (local // 2, 2 * local_ch)
    own, *others, volume = pl.pallas_call(
        functools.partial(forward_kernel, parts_x, parts_y, spans),
        out_shape=(
            jax.ShapeDtypeStruct(packing, F32),
            *[jax.ShapeDtypeStruct(packing, BF16)] * (shards - 1),
            jax.ShapeDtypeStruct(volume_shape + (3 * local_ch,), BF16),
        ),
        in_specs=[SMEM, VMEM, VMEM],
        out_specs=(VMEM,) * (shards + 1),
        scratch_shapes=[pltpu.VMEM((shards,) + packing, F32)],
        compiler_params=PARAMS,
        name="forward",
    )(place, cells, taps)
    others = [exchange(x, "ch", k + 1) for k, x in enumerate(others)]
    activation, slope = pl.pallas_call(
        slope_kernel,
        out_shape=(
            jax.ShapeDtypeStruct((local, local_ch), BF16),
            jax.ShapeDtypeStruct(packing, BF16),
        ),
        in_specs=[VMEM] * (shards + 2),
        out_specs=(VMEM, VMEM),
        compiler_params=PARAMS,
        name="slope",
    )(own, *others, jnp.concatenate([bias, bias]).reshape(1, -1), cotangent.reshape(local, local_ch))
    column = jnp.stack([slope] + [exchange(slope, "ch", k) for k in range(1, shards)])
    slopes = {0: column}
    volume_axes = ("gx", "gy")
    for m in range(2, parts_x * parts_y, 2):
        slopes[m] = exchange(column, volume_axes, m)
    for m in range(0, parts_x * parts_y, 2):
        slopes[m + 1] = exchange(slopes[m], volume_axes, 1)
    slopes = [slopes[m] for m in range(parts_x * parts_y)]
    input_grad, kernel_grad, bias_grad = pl.pallas_call(
        functools.partial(backward_kernel, parts_x, parts_y, spans, factor),
        out_shape=(
            jax.ShapeDtypeStruct((local, local_ch), BF16),
            jax.ShapeDtypeStruct((9, 3 * local_ch, channels), F32),
            jax.ShapeDtypeStruct((1, channels), F32),
        ),
        in_specs=[SMEM] + [VMEM] * (2 + len(slopes)),
        out_specs=(VMEM, VMEM, VMEM),
        scratch_shapes=[
            pltpu.VMEM(volume_shape + (channels,), BF16),
            pltpu.VMEM((channels, local * parts_x * parts_y), BF16),
        ],
        compiler_params=PARAMS,
        name="backward",
    )(place, taps, volume, *slopes)
    bias_grad = lax.dynamic_slice(
        bias_grad.reshape(channels), (lax.axis_index("ch") * local_ch,), (local_ch,)
    )
    return (
        activation.reshape(inputs.shape),
        input_grad.reshape(inputs.shape),
        kernel_grad.reshape(weight.shape),
        bias_grad,
    )


def solution(mesh):
    few = mesh.shape["gx"] * mesh.shape["gy"] <= 8
    return jax.shard_map(
        body_gathered if few else body_reduced,
        mesh=mesh,
        in_specs=(
            P("gx", "gy", None, "ch"),
            P(None, None, None, "ch", None),
            P("ch"),
            P("gx", "gy", None, "ch"),
        ),
        out_specs=(
            P("gx", "gy", None, "ch"),
            P("gx", "gy", None, "ch"),
            P(None, None, None, "ch", None),
            P("ch"),
        ),
        check_vma=False,
    )
```

```python
import functools
import math

import jax
import jax.numpy as jnp
from jax import lax
from jax.experimental import pallas as pl
from jax.experimental.pallas import tpu as pltpu
from jax.sharding import PartitionSpec as P

VMEM = pl.BlockSpec(memory_space=pltpu.VMEM)
SMEM = pl.BlockSpec(memory_space=pltpu.SMEM)
PARAMS = pltpu.CompilerParams(vmem_limit_bytes=24 * 1024 * 1024)
F32 = jnp.float32
BF16 = jnp.bfloat16


def with_halo(x, sides, width):
    for axis, dim in sides:
        devices, length = (lax.axis_size(axis), x.shape[dim])
        up = [(i, (i + 1) % devices) for i in range(devices - 1)]
        down = [(j, i) for i, j in up]
        last = lax.slice_in_dim(x, length - width, length, axis=dim)
        initial = lax.slice_in_dim(x, 0, width, axis=dim)
        before = lax.ppermute(last, axis, up)
        after = lax.ppermute(initial, axis, down)
        x = jnp.concatenate([before, x, after], axis=dim)
    return x


def body_reduced(inputs, weight, bias, cotangent):
    span_x, span_y, span_z, local_ch = inputs.shape
    widest = weight.shape[4]
    local_cells = span_x * span_y * span_z
    offsets = [(a, b, c) for a in range(3) for b in range(3) for c in range(3)]
    depth_pad = ((0, 0), (0, 0), (1, 1), (0, 0))
    rimmed = with_halo(inputs, (("gx", 0), ("gy", 1)), 1)
    padded = jnp.pad(rimmed, depth_pad)
    blocks = []
    for a, b, c in offsets:
        blocks.append(
            padded[a : a + span_x, b : b + span_y, c : c + span_z].reshape(local_cells, local_ch)
        )
    patches = jnp.concatenate(blocks, axis=1)
    flat_weight = weight.reshape(27 * local_ch, widest)
    summed = lax.psum_scatter(
        lax.dot_general(flat_weight, patches, (((0,), (1,)), ((), ())), preferred_element_type=F32),
        "ch",
        scatter_dimension=0,
        tiled=True,
    ).T
    summed = summed + bias.astype(F32)[None, :]
    activation = jax.nn.silu(summed).astype(BF16).reshape(span_x, span_y, span_z, local_ch)
    sigmoid_pre = jax.nn.sigmoid(summed)
    slope = (
        cotangent.reshape(local_cells, local_ch).astype(F32)
        * sigmoid_pre
        * (1.0 + summed * (1.0 - sigmoid_pre))
    ).astype(BF16)
    local_bias = jnp.sum(slope.astype(F32), axis=0)
    slope_grid = slope.reshape(span_x, span_y, span_z, local_ch)
    weight_turned = jnp.transpose(weight.reshape(27, local_ch, widest), (0, 2, 1))
    slope_rimmed = with_halo(slope_grid, (("gx", 0), ("gy", 1)), 1)
    piece = lax.all_gather(slope_rimmed, "ch", axis=3, tiled=True)
    extended = jnp.pad(piece, depth_pad)
    running = jnp.zeros((local_cells, local_ch), F32)
    for index, (a, b, c) in enumerate(offsets):
        a, b, c = (2 - a, 2 - b, 2 - c)
        cut = extended[a : a + span_x, b : b + span_y, c : c + span_z].reshape(local_cells, widest)
        running = running + jnp.dot(cut, weight_turned[index], preferred_element_type=F32)
    interior = piece[1 : 1 + span_x, 1 : 1 + span_y].reshape(local_cells, widest)
    product = lax.dot_general(
        patches, interior, (((0,), (0,)), ((), ())), preferred_element_type=F32
    )
    total_cells = local_cells * lax.axis_size("gx") * lax.axis_size("gy")
    factor = 1.0 / math.sqrt(total_cells)
    kernel_total, bias_total = lax.psum((product * factor, local_bias * factor), ("gx", "gy"))
    input_grad = running.astype(BF16).reshape(span_x, span_y, span_z, local_ch)
    return (activation, input_grad, kernel_total.reshape(3, 3, 3, local_ch, widest), bias_total)


def shifted(v, by):
    depth = v.shape[1]
    row = lax.broadcasted_iota(jnp.int32, v.shape, 1)
    if by == 1:
        return jnp.where(row == 0, 0.0, pltpu.roll(v, 1, 1))
    return jnp.where(row == depth - 1, 0.0, pltpu.roll(v, depth - 1, 1))


def rim_sides(place, span_x, span_y):
    first = place[1] % 2 == 0
    even_at = jnp.where(first, span_y + 1, 0)
    odd_at = jnp.where(first, 0, span_y + 1)
    even_row = jnp.where(first, span_y - 1, 0)
    odd_row = jnp.where(first, 0, span_y - 1)
    x_at = jnp.where(place[0] == 0, span_x + 1, 0)
    x_row = jnp.where(place[0] == 0, span_x - 1, 0)
    return even_at, odd_at, even_row, odd_row, x_at, x_row


def prepare_kernel(place, inputs, packed, even, odd, across, even_corner, odd_corner):
    span_x, span_y, _, _ = inputs.shape
    half = span_x // 2
    _, _, even_row, odd_row, _, x_row = rim_sides(place, span_x, span_y)
    packed[...] = jnp.concatenate([inputs[:half], inputs[half:]], axis=3)
    even[...] = inputs[:, even_row]
    odd[...] = inputs[:, odd_row]
    across[...] = inputs[x_row]
    even_corner[...] = inputs[x_row, even_row]
    odd_corner[...] = inputs[x_row, odd_row]


def forward_kernel(
    place, weight, inputs, even, odd, across, even_corner, odd_corner, own, *rest
):
    *others, window, blocks = rest
    span_x, span_y, span_z, lanes = inputs.shape
    half_x = span_x // 2
    half = half_x * span_y * span_z
    even_at, odd_at, _, _, x_at, _ = rim_sides(place, span_x, span_y)

    def spread(v):
        flat = v.astype(F32).reshape(-1, span_z, lanes)
        joined = jnp.concatenate([shifted(flat, 1), flat, shifted(flat, -1)], axis=2)
        return joined.astype(BF16).reshape(v.shape[:-1] + (3 * lanes,))

    nothing = jnp.zeros((span_y + 2, span_z, 3 * lanes), BF16)
    window[0] = nothing
    window[span_x + 1] = nothing
    window[1 : span_x + 1, 1 : span_y + 1] = spread(inputs[...])
    window[1 : span_x + 1, even_at] = spread(even[...])
    window[1 : span_x + 1, odd_at] = spread(odd[...])
    window[x_at, 1 : span_y + 1] = spread(across[...])
    window[x_at, even_at] = spread(even_corner[...])
    window[x_at, odd_at] = spread(odd_corner[...])
    sums = []
    for h in range(2):
        total = None
        for a in range(3):
            for b in range(3):
                cut = window[a + h * half_x : a + (h + 1) * half_x, b : b + span_y]
                term = jnp.dot(
                    cut.reshape(half, 3 * lanes), weight[a * 3 + b], preferred_element_type=F32
                )
                total = term if total is None else total + term
        sums.append(total)
    for d in range(weight.shape[2] // lanes):
        cut = slice(d * lanes, (d + 1) * lanes)
        blocks[d] = jnp.concatenate([sums[0][:, cut], sums[1][:, cut]], axis=1)
    own[...] = blocks[place[2]]
    for k, other in enumerate(others):
        other[...] = blocks[place[2] ^ (k + 1)].astype(BF16)


def slope_kernel(own, *rest):
    *others, bias, cotangent, activation, slope = rest
    half, lanes = cotangent.shape[0] // 2, cotangent.shape[1]
    summed = own[...]
    for other in others:
        summed = summed + other[...].astype(F32)
    offset = bias[...].astype(F32)
    summed = summed + jnp.concatenate([offset, offset], axis=1)
    sigmoid = jax.nn.sigmoid(summed)
    active = (summed * sigmoid).astype(BF16)
    activation[:half] = active[:, :lanes]
    activation[half:] = active[:, lanes:]
    upstream = jnp.concatenate([cotangent[:half], cotangent[half:]], axis=1).astype(F32)
    slope[...] = (upstream * sigmoid * (1.0 + summed * (1.0 - sigmoid))).astype(BF16)


def ordered_halves(place, pieces):
    shards, _, _, _, lanes = pieces.shape
    lanes = lanes // 2
    ordered = [pieces[place[2] ^ j] for j in range(shards)]
    return [
        jnp.concatenate([piece[..., h * lanes : (h + 1) * lanes] for piece in ordered], axis=-1)
        for h in range(2)
    ]


def corner_of(place, m, parts_y, span_x, span_y):
    return (place[0] ^ (m // parts_y)) * span_x, (place[1] ^ (m % parts_y)) * span_y


def add_terms(place, parts_y, members, slopes, volume, turned, old, store):
    corners = []
    for n, (m, pieces) in enumerate(zip(members, slopes)):
        shards, half_x, span_y, span_z, lanes = pieces.shape
        span_x, channels = 2 * half_x, shards * lanes // 2
        half = half_x * span_y * span_z
        local = 2 * half
        corners.append(corner_of(place, m, parts_y, span_x, span_y))
        for h, part in enumerate(ordered_halves(place, pieces)):
            turned[:, n * local + h * half : n * local + (h + 1) * half] = part.reshape(
                half, channels
            ).T
    for a in range(3):
        for b in range(3):
            total = None if old is None else old[a * 3 + b]
            for n, (x0, y0) in enumerate(corners):
                cut = volume[pl.ds(x0 + a, span_x), pl.ds(y0 + b, span_y)]
                term = jnp.dot(
                    turned[:, n * local : (n + 1) * local],
                    cut.reshape(local, -1),
                    preferred_element_type=F32,
                )
                total = term if total is None else total + term
            store(a * 3 + b, total)


def first_kernel(parts_x, parts_y, members, place, *rest):
    count, used = parts_x * parts_y, len(members)
    cells, slopes, (volume, sums, turned) = rest[:count], rest[count : count + used], rest[count + used :]
    half_x, span_y, span_z, lanes = cells[0].shape
    span_x, lanes = 2 * half_x, lanes // 2
    rows_x, rows_y = parts_x * span_x, parts_y * span_y
    width = 3 * lanes
    zero_x = jnp.zeros((1, rows_y + 2, span_z, width), BF16)
    zero_y = jnp.zeros((rows_x + 2, 1, span_z, width), BF16)
    volume[0:1] = zero_x
    volume[rows_x + 1 : rows_x + 2] = zero_x
    volume[:, 0:1] = zero_y
    volume[:, rows_y + 1 : rows_y + 2] = zero_y
    for m in range(count):
        x0, y0 = corner_of(place, m, parts_y, span_x, span_y)
        v = cells[m][...].astype(F32).reshape(half_x * span_y, span_z, 2 * lanes)
        low, high = shifted(v, 1), shifted(v, -1)
        for h in range(2):
            cut = slice(h * lanes, (h + 1) * lanes)
            joined = jnp.concatenate([low[..., cut], v[..., cut], high[..., cut]], axis=2)
            volume[pl.ds(x0 + 1 + h * half_x, half_x), pl.ds(y0 + 1, span_y)] = joined.astype(
                BF16
            ).reshape(half_x, span_y, span_z, width)

    def store(tap, total):
        sums[tap] = total

    add_terms(place, parts_y, members, slopes, volume, turned, None, store)


def middle_kernel(parts_y, members, place, volume, old, *rest):
    *slopes, sums, turned = rest

    def store(tap, total):
        sums[tap] = total

    add_terms(place, parts_y, members, slopes, volume, turned, old, store)


def last_kernel(parts_x, parts_y, members, factor, place, weight, volume, old, *rest):
    *slopes, input_grad, kernel_grad, bias_grad, window, turned = rest
    shards, half_x, span_y, span_z, lanes = slopes[0].shape
    span_x, lanes = 2 * half_x, lanes // 2
    channels = shards * lanes
    half = half_x * span_y * span_z

    def store(tap, total):
        kernel_grad[tap] = (total * factor).T

    add_terms(
        place, parts_y, members, [slopes[m] for m in members], volume, turned, old, store
    )

    column = jnp.zeros((1, 2 * lanes), F32)
    for pieces in slopes:
        mine = pieces[0].astype(F32).reshape(half, 2 * lanes)
        column = column + jnp.sum(mine, axis=0, keepdims=True)
    bias_grad[...] = (column[:, :lanes] + column[:, lanes:]) * factor

    even_at, odd_at, even_row, odd_row, x_at, x_row = rim_sides(place, span_x, span_y)
    has_odd = (place[1] != 0) & (place[1] != parts_y - 1)
    window[...] = jnp.zeros(window.shape, BF16)
    low, high = ordered_halves(place, slopes[0])
    window[1 : half_x + 1, 1 : span_y + 1] = low
    window[half_x + 1 : span_x + 1, 1 : span_y + 1] = high

    def rows_of(m, row):
        ordered = [slopes[m][place[2] ^ j, :, row] for j in range(shards)]
        return [
            jnp.concatenate([piece[..., h * lanes : (h + 1) * lanes] for piece in ordered], axis=-1)
            for h in range(2)
        ]

    def facing(halves):
        low, high = halves
        return jnp.where(place[0] == 0, low[0], high[half_x - 1])

    for h, rows in enumerate(rows_of(1, even_row_of(even_row, span_y))):
        window[1 + h * half_x : 1 + (h + 1) * half_x, even_at] = rows
    window[x_at, 1 : span_y + 1] = facing(ordered_halves(place, slopes[parts_y]))
    window[x_at, even_at] = facing(rows_of(parts_y + 1, even_row_of(even_row, span_y)))

    @pl.when(has_odd)
    def _():
        for h, rows in enumerate(rows_of(3, even_row_of(odd_row, span_y))):
            window[1 + h * half_x : 1 + (h + 1) * half_x, odd_at] = rows
        window[x_at, odd_at] = facing(rows_of(parts_y + 3, even_row_of(odd_row, span_y)))

    for h in range(2):
        total = None
        for a in range(3):
            for b in range(3):
                cut = window[
                    2 - a + h * half_x : 2 - a + (h + 1) * half_x, 2 - b : 2 - b + span_y
                ]
                term = lax.dot_general(
                    cut.reshape(half, channels),
                    weight[a * 3 + b],
                    (((1,), (1,)), ((), ())),
                    preferred_element_type=F32,
                )
                total = term if total is None else total + term
        total = total.reshape(half // span_z, span_z, 3 * lanes)
        result = (
            shifted(total[..., :lanes], -1)
            + total[..., lanes : 2 * lanes]
            + shifted(total[..., 2 * lanes :], 1)
        )
        input_grad[h * half : (h + 1) * half] = result.reshape(half, lanes).astype(BF16)


def even_row_of(row, span_y):
    return span_y - 1 - row


def exchange(x, axes, mask, odd_parts=0):
    pairs = []
    for i in range(lax.axis_size(axes)):
        j = i ^ mask
        if odd_parts:
            y = i % odd_parts
            other = y + 1 if y % 2 else y - 1
            if not 0 <= other < odd_parts:
                continue
            j += other - y
        pairs.append((i, j))
    return lax.ppermute(x, axes, pairs)


def body_gathered(inputs, weight, bias, cotangent):
    spans = inputs.shape[:3]
    span_x, span_y, span_z = spans
    local_ch, channels = weight.shape[3:]
    local = span_x * span_y * span_z
    parts_x, parts_y = lax.axis_size("gx"), lax.axis_size("gy")
    count = parts_x * parts_y
    shards = lax.axis_size("ch")
    axes = ("gx", "gy")
    factor = 1.0 / math.sqrt(local * count)
    place = jnp.stack([lax.axis_index(axis) for axis in ("gx", "gy", "ch")]).astype(jnp.int32)
    taps = weight.reshape(9, 3 * local_ch, channels)
    packing = (span_x // 2, span_y, span_z, 2 * local_ch)
    flat = (local // 2, 2 * local_ch)

    def call(kernel, name, outs, args, scratch=(), flops=0):
        return pl.pallas_call(
            kernel,
            out_shape=[jax.ShapeDtypeStruct(shape, kind) for shape, kind in outs],
            in_specs=[SMEM if x is place else VMEM for x in args],
            out_specs=[VMEM] * len(outs),
            scratch_shapes=[pltpu.VMEM(shape, kind) for shape, kind in scratch],
            compiler_params=PARAMS,
            cost_estimate=pl.CostEstimate(flops=flops, bytes_accessed=1 << 20, transcendentals=0),
            name=name,
        )(*args)

    row_y = (span_x, span_z, local_ch)
    row_x = (span_y, span_z, local_ch)
    packed, even, odd, across, even_corner, odd_corner = call(
        prepare_kernel,
        "prepare",
        [(packing, BF16), (row_y, BF16), (row_y, BF16), (row_x, BF16)] + [(row_x[1:], BF16)] * 2,
        [place, inputs],
    )
    even = exchange(even, axes, 1)
    odd = exchange(odd, axes, 0, parts_y)
    across = exchange(across, axes, parts_y)
    even_corner = exchange(even_corner, axes, parts_y + 1)
    odd_corner = exchange(odd_corner, axes, parts_y, parts_y)
    own, *others = call(
        forward_kernel,
        "forward",
        [(flat, F32)] + [(flat, BF16)] * (shards - 1),
        [place, taps, inputs, even, odd, across, even_corner, odd_corner],
        [((span_x + 2, span_y + 2, span_z, 3 * local_ch), BF16), ((shards,) + flat, F32)],
        2 * local * 27 * local_ch * channels,
    )
    others = [exchange(x, "ch", k + 1) for k, x in enumerate(others)]
    cells = {0: packed}
    others[0], early = lax.optimization_barrier((others[0], packed))
    for m in range(1, count // 2 + 1):
        cells[m] = exchange(early, axes, m)
    activation, slope = call(
        slope_kernel,
        "slope",
        [((local, local_ch), BF16), (flat, BF16)],
        [own, *others, bias.reshape(1, local_ch), cotangent.reshape(local, local_ch)],
    )
    pieces = [exchange(slope, "ch", k) for k in range(1, shards)]
    pieces[0], late = lax.optimization_barrier((pieces[0], packed))
    for m in range(count // 2 + 1, count):
        cells[m] = exchange(late, axes, m)
    column = jnp.stack([slope] + pieces).reshape((shards,) + packing)
    slopes = {0: column}
    for m in range(2, count, 2):
        slopes[m] = exchange(column, axes, m)
    for m in range(0, count, 2):
        slopes[m + 1] = exchange(slopes[m], axes, 1)
    volume_shape = (parts_x * span_x + 2, parts_y * span_y + 2, span_z, 3 * local_ch)
    sums_shape = (9, channels, 3 * local_ch)
    per_member = 2 * local * 27 * local_ch * channels
    groups = ((0, 1), (2, 4), (3, 5, 6, 7))
    volume, sums = call(
        functools.partial(first_kernel, parts_x, parts_y, groups[0]),
        "first",
        [(volume_shape, BF16), (sums_shape, F32)],
        [place] + [cells[m] for m in range(count)] + [slopes[m] for m in groups[0]],
        [((channels, len(groups[0]) * local), BF16)],
        per_member * len(groups[0]),
    )
    for members in groups[1:-1]:
        (sums,) = call(
            functools.partial(middle_kernel, parts_y, members),
            "middle",
            [(sums_shape, F32)],
            [place, volume, sums] + [slopes[m] for m in members],
            [((channels, len(members) * local), BF16)],
            per_member * len(members),
        )
    input_grad, kernel_grad, bias_grad = call(
        functools.partial(last_kernel, parts_x, parts_y, groups[-1], factor),
        "last",
        [((local, local_ch), BF16), ((9, 3 * local_ch, channels), F32), ((1, local_ch), F32)],
        [place, taps, volume, sums] + [slopes[m] for m in range(count)],
        [
            ((span_x + 2, span_y + 2, span_z, channels), BF16),
            ((channels, len(groups[-1]) * local), BF16),
        ],
        per_member * (len(groups[-1]) + 1),
    )
    return (
        activation.reshape(inputs.shape),
        input_grad.reshape(inputs.shape),
        kernel_grad.reshape(weight.shape),
        bias_grad.reshape(local_ch),
    )


def solution(mesh):
    few = (mesh.shape["gx"], mesh.shape["gy"]) == (2, 4)
    return jax.shard_map(
        body_gathered if few else body_reduced,
        mesh=mesh,
        in_specs=(
            P("gx", "gy", None, "ch"),
            P(None, None, None, "ch", None),
            P("ch"),
            P("gx", "gy", None, "ch"),
        ),
        out_specs=(
            P("gx", "gy", None, "ch"),
            P("gx", "gy", None, "ch"),
            P(None, None, None, "ch", None),
            P("ch"),
        ),
        check_vma=False,
    )
```

```python
import functools
import math

import jax
import jax.numpy as jnp
from jax import lax
from jax.experimental import pallas as pl
from jax.experimental.pallas import tpu as pltpu
from jax.sharding import PartitionSpec as P

VMEM = pl.BlockSpec(memory_space=pltpu.VMEM)
SMEM = pl.BlockSpec(memory_space=pltpu.SMEM)
PARAMS = pltpu.CompilerParams(vmem_limit_bytes=24 * 1024 * 1024)
F32 = jnp.float32
BF16 = jnp.bfloat16


def with_halo(x, sides, width):
    for axis, dim in sides:
        devices, length = (lax.axis_size(axis), x.shape[dim])
        up = [(i, (i + 1) % devices) for i in range(devices - 1)]
        down = [(j, i) for i, j in up]
        last = lax.slice_in_dim(x, length - width, length, axis=dim)
        initial = lax.slice_in_dim(x, 0, width, axis=dim)
        before = lax.ppermute(last, axis, up)
        after = lax.ppermute(initial, axis, down)
        x = jnp.concatenate([before, x, after], axis=dim)
    return x


def body_reduced(inputs, weight, bias, cotangent):
    span_x, span_y, span_z, local_ch = inputs.shape
    widest = weight.shape[4]
    local_cells = span_x * span_y * span_z
    offsets = [(a, b, c) for a in range(3) for b in range(3) for c in range(3)]
    depth_pad = ((0, 0), (0, 0), (1, 1), (0, 0))
    rimmed = with_halo(inputs, (("gx", 0), ("gy", 1)), 1)
    padded = jnp.pad(rimmed, depth_pad)
    blocks = []
    for a, b, c in offsets:
        blocks.append(
            padded[a : a + span_x, b : b + span_y, c : c + span_z].reshape(local_cells, local_ch)
        )
    patches = jnp.concatenate(blocks, axis=1)
    flat_weight = weight.reshape(27 * local_ch, widest)
    summed = lax.psum_scatter(
        lax.dot_general(flat_weight, patches, (((0,), (1,)), ((), ())), preferred_element_type=F32),
        "ch",
        scatter_dimension=0,
        tiled=True,
    ).T
    summed = summed + bias.astype(F32)[None, :]
    activation = jax.nn.silu(summed).astype(BF16).reshape(span_x, span_y, span_z, local_ch)
    sigmoid_pre = jax.nn.sigmoid(summed)
    slope = (
        cotangent.reshape(local_cells, local_ch).astype(F32)
        * sigmoid_pre
        * (1.0 + summed * (1.0 - sigmoid_pre))
    ).astype(BF16)
    local_bias = jnp.sum(slope.astype(F32), axis=0)
    slope_grid = slope.reshape(span_x, span_y, span_z, local_ch)
    weight_turned = jnp.transpose(weight.reshape(27, local_ch, widest), (0, 2, 1))
    slope_rimmed = with_halo(slope_grid, (("gx", 0), ("gy", 1)), 1)
    piece = lax.all_gather(slope_rimmed, "ch", axis=3, tiled=True)
    extended = jnp.pad(piece, depth_pad)
    running = jnp.zeros((local_cells, local_ch), F32)
    for index, (a, b, c) in enumerate(offsets):
        a, b, c = (2 - a, 2 - b, 2 - c)
        cut = extended[a : a + span_x, b : b + span_y, c : c + span_z].reshape(local_cells, widest)
        running = running + jnp.dot(cut, weight_turned[index], preferred_element_type=F32)
    interior = piece[1 : 1 + span_x, 1 : 1 + span_y].reshape(local_cells, widest)
    product = lax.dot_general(
        patches, interior, (((0,), (0,)), ((), ())), preferred_element_type=F32
    )
    total_cells = local_cells * lax.axis_size("gx") * lax.axis_size("gy")
    factor = 1.0 / math.sqrt(total_cells)
    kernel_total, bias_total = lax.psum((product * factor, local_bias * factor), ("gx", "gy"))
    input_grad = running.astype(BF16).reshape(span_x, span_y, span_z, local_ch)
    return (activation, input_grad, kernel_total.reshape(3, 3, 3, local_ch, widest), bias_total)


def shifted(v, by):
    depth = v.shape[1]
    row = lax.broadcasted_iota(jnp.int32, v.shape, 1)
    if by == 1:
        return jnp.where(row == 0, 0.0, pltpu.roll(v, 1, 1))
    return jnp.where(row == depth - 1, 0.0, pltpu.roll(v, depth - 1, 1))


def rim_sides(place, span_x, span_y):
    first = place[1] % 2 == 0
    even_at = jnp.where(first, span_y + 1, 0)
    odd_at = jnp.where(first, 0, span_y + 1)
    even_row = jnp.where(first, span_y - 1, 0)
    odd_row = jnp.where(first, 0, span_y - 1)
    x_at = jnp.where(place[0] == 0, span_x + 1, 0)
    x_row = jnp.where(place[0] == 0, span_x - 1, 0)
    return even_at, odd_at, even_row, odd_row, x_at, x_row


def prepare_kernel(place, inputs, even, odd, even_corner, odd_corner, held):
    span_x, span_y, _, _ = inputs.shape
    _, _, even_row, odd_row, _, x_row = rim_sides(place, span_x, span_y)
    even[...] = inputs[:, even_row]
    odd[...] = inputs[:, odd_row]
    even_corner[...] = inputs[x_row, even_row]
    odd_corner[...] = inputs[x_row, odd_row]
    held[...] = inputs[...]


def stage_kernel(after, *rest):
    count = (len(rest) - 1) // 2
    sources, targets, arrived = rest[:count], rest[count : 2 * count], rest[-1]
    copies = []
    for source, target in zip(sources, targets):
        parts = source.shape[0] if source.shape[0] == 9 else 1
        for n in range(parts):
            here = pl.ds(n, 1) if parts > 1 else slice(None)
            copies.append(
                pltpu.make_async_copy(source.at[here], target.at[here], arrived.at[len(copies)])
            )
    for copy in copies:
        copy.start()
    for copy in copies:
        copy.wait()


def forward_kernel(
    place, weight, inputs, even, odd, beside, even_corner, odd_corner, own, *rest
):
    *others, pair, window, blocks = rest
    span_x, span_y, span_z, lanes = inputs.shape
    half_x = span_x // 2
    half = half_x * span_y * span_z
    even_at, odd_at, _, _, x_at, x_row = rim_sides(place, span_x, span_y)

    def spread(v):
        flat = v.astype(F32).reshape(-1, span_z, lanes)
        joined = jnp.concatenate([shifted(flat, 1), flat, shifted(flat, -1)], axis=2)
        return joined.astype(BF16).reshape(v.shape[:-1] + (3 * lanes,))

    nothing = jnp.zeros((span_y + 2, span_z, 3 * lanes), BF16)
    window[0] = nothing
    window[span_x + 1] = nothing
    window[1 : span_x + 1, 1 : span_y + 1] = spread(inputs[...])
    window[1 : span_x + 1, even_at] = spread(even[...])
    window[1 : span_x + 1, odd_at] = spread(odd[...])
    window[x_at, 1 : span_y + 1] = spread(beside[facing_row(x_row, span_x)])
    window[x_at, even_at] = spread(even_corner[...])
    window[x_at, odd_at] = spread(odd_corner[...])
    sums = []
    for h in range(2):
        total = None
        for a in range(3):
            for b in range(3):
                cut = window[a + h * half_x : a + (h + 1) * half_x, b : b + span_y]
                term = jnp.dot(
                    cut.reshape(half, 3 * lanes), weight[a * 3 + b], preferred_element_type=F32
                )
                total = term if total is None else total + term
        sums.append(total)
    for d in range(weight.shape[2] // lanes):
        cut = slice(d * lanes, (d + 1) * lanes)
        blocks[d] = jnp.concatenate([sums[0][:, cut], sums[1][:, cut]], axis=1)
    own[...] = blocks[place[2]]
    for k, other in enumerate(others):
        other[...] = blocks[place[2] ^ (k + 1)].astype(BF16)
    for n, whole in enumerate((inputs, beside)):
        pair[n] = jnp.concatenate([whole[:half_x], whole[half_x:]], axis=3)


def slope_kernel(own, *rest):
    *others, bias, cotangent, activation, slope = rest
    half, lanes = cotangent.shape[0] // 2, cotangent.shape[1]
    summed = own[...]
    for other in others:
        summed = summed + other[...].astype(F32)
    offset = bias[...].astype(F32)
    summed = summed + jnp.concatenate([offset, offset], axis=1)
    sigmoid = jax.nn.sigmoid(summed)
    active = (summed * sigmoid).astype(BF16)
    activation[:half] = active[:, :lanes]
    activation[half:] = active[:, lanes:]
    upstream = jnp.concatenate([cotangent[:half], cotangent[half:]], axis=1).astype(F32)
    slope[...] = (upstream * sigmoid * (1.0 + summed * (1.0 - sigmoid))).astype(BF16)


def ordered_halves(place, pieces):
    shards, _, _, _, lanes = pieces.shape
    lanes = lanes // 2
    ordered = [pieces[place[2] ^ j] for j in range(shards)]
    return [
        jnp.concatenate([piece[..., h * lanes : (h + 1) * lanes] for piece in ordered], axis=-1)
        for h in range(2)
    ]


def corner_of(place, m, parts_y, span_x, span_y):
    return (place[0] ^ (m // parts_y)) * span_x, (place[1] ^ (m % parts_y)) * span_y


def add_terms(place, parts_y, members, slopes, volume, turned, old, store):
    corners = []
    for n, (m, pieces) in enumerate(zip(members, slopes)):
        shards, half_x, span_y, span_z, lanes = pieces.shape
        span_x, channels = 2 * half_x, shards * lanes // 2
        half = half_x * span_y * span_z
        local = 2 * half
        corners.append(corner_of(place, m, parts_y, span_x, span_y))
        for h, part in enumerate(ordered_halves(place, pieces)):
            turned[:, n * local + h * half : n * local + (h + 1) * half] = part.reshape(
                half, channels
            ).T
    for a in range(3):
        for b in range(3):
            total = None if old is None else old[a * 3 + b]
            for n, (x0, y0) in enumerate(corners):
                cut = volume[pl.ds(x0 + a, span_x), pl.ds(y0 + b, span_y)]
                term = jnp.dot(
                    turned[:, n * local : (n + 1) * local],
                    cut.reshape(local, -1),
                    preferred_element_type=F32,
                )
                total = term if total is None else total + term
            store(a * 3 + b, total)


def first_kernel(parts_x, parts_y, members, place, pair, pair_y, quad, *rest):
    *slopes, volume, sums, turned = rest
    cells = [(0, pair, 0), (parts_y, pair, 1), (2, pair_y, 0), (parts_y + 2, pair_y, 1)]
    cells += [(m ^ 1, quad, n) for n, (m, _, _) in enumerate(cells)]
    _, half_x, span_y, span_z, lanes = pair.shape
    span_x, lanes = 2 * half_x, lanes // 2
    rows_x, rows_y = parts_x * span_x, parts_y * span_y
    width = 3 * lanes
    zero_x = jnp.zeros((1, rows_y + 2, span_z, width), BF16)
    zero_y = jnp.zeros((rows_x + 2, 1, span_z, width), BF16)
    volume[0:1] = zero_x
    volume[rows_x + 1 : rows_x + 2] = zero_x
    volume[:, 0:1] = zero_y
    volume[:, rows_y + 1 : rows_y + 2] = zero_y
    for m, array, n in cells:
        x0, y0 = corner_of(place, m, parts_y, span_x, span_y)
        v = array[n].astype(F32).reshape(half_x * span_y, span_z, 2 * lanes)
        low, high = shifted(v, 1), shifted(v, -1)
        for h in range(2):
            cut = slice(h * lanes, (h + 1) * lanes)
            joined = jnp.concatenate([low[..., cut], v[..., cut], high[..., cut]], axis=2)
            volume[pl.ds(x0 + 1 + h * half_x, half_x), pl.ds(y0 + 1, span_y)] = joined.astype(
                BF16
            ).reshape(half_x, span_y, span_z, width)

    def store(tap, total):
        sums[tap] = total

    add_terms(place, parts_y, members, slopes, volume, turned, None, store)


def middle_kernel(parts_y, members, place, volume, old, *rest):
    *slopes, sums, turned = rest

    def store(tap, total):
        sums[tap] = total

    add_terms(place, parts_y, members, slopes, volume, turned, old, store)


def last_kernel(parts_x, parts_y, members, factor, place, weight, volume, old, *rest):
    *slopes, input_grad, kernel_grad, bias_grad, window, turned = rest
    shards, half_x, span_y, span_z, lanes = slopes[0].shape
    span_x, lanes = 2 * half_x, lanes // 2
    channels = shards * lanes
    half = half_x * span_y * span_z

    def store(tap, total):
        kernel_grad[tap] = (total * factor).T

    add_terms(
        place, parts_y, members, [slopes[m] for m in members], volume, turned, old, store
    )

    column = jnp.zeros((1, 2 * lanes), F32)
    for pieces in slopes:
        mine = pieces[0].astype(F32).reshape(half, 2 * lanes)
        column = column + jnp.sum(mine, axis=0, keepdims=True)
    bias_grad[...] = (column[:, :lanes] + column[:, lanes:]) * factor

    even_at, odd_at, even_row, odd_row, x_at, x_row = rim_sides(place, span_x, span_y)
    has_odd = (place[1] != 0) & (place[1] != parts_y - 1)
    window[...] = jnp.zeros(window.shape, BF16)
    low, high = ordered_halves(place, slopes[0])
    window[1 : half_x + 1, 1 : span_y + 1] = low
    window[half_x + 1 : span_x + 1, 1 : span_y + 1] = high

    def rows_of(m, row):
        ordered = [slopes[m][place[2] ^ j, :, row] for j in range(shards)]
        return [
            jnp.concatenate([piece[..., h * lanes : (h + 1) * lanes] for piece in ordered], axis=-1)
            for h in range(2)
        ]

    def facing(halves):
        low, high = halves
        return jnp.where(place[0] == 0, low[0], high[half_x - 1])

    for h, rows in enumerate(rows_of(1, facing_row(even_row, span_y))):
        window[1 + h * half_x : 1 + (h + 1) * half_x, even_at] = rows
    window[x_at, 1 : span_y + 1] = facing(ordered_halves(place, slopes[parts_y]))
    window[x_at, even_at] = facing(rows_of(parts_y + 1, facing_row(even_row, span_y)))

    @pl.when(has_odd)
    def _():
        for h, rows in enumerate(rows_of(3, facing_row(odd_row, span_y))):
            window[1 + h * half_x : 1 + (h + 1) * half_x, odd_at] = rows
        window[x_at, odd_at] = facing(rows_of(parts_y + 3, facing_row(odd_row, span_y)))

    for h in range(2):
        total = None
        for a in range(3):
            for b in range(3):
                cut = window[
                    2 - a + h * half_x : 2 - a + (h + 1) * half_x, 2 - b : 2 - b + span_y
                ]
                term = lax.dot_general(
                    cut.reshape(half, channels),
                    weight[a * 3 + b],
                    (((1,), (1,)), ((), ())),
                    preferred_element_type=F32,
                )
                total = term if total is None else total + term
        total = total.reshape(half // span_z, span_z, 3 * lanes)
        result = (
            shifted(total[..., :lanes], -1)
            + total[..., lanes : 2 * lanes]
            + shifted(total[..., 2 * lanes :], 1)
        )
        input_grad[h * half : (h + 1) * half] = result.reshape(half, lanes).astype(BF16)


def facing_row(row, span_y):
    return span_y - 1 - row


def exchange(x, axes, mask, odd_parts=0):
    pairs = []
    for i in range(lax.axis_size(axes)):
        j = i ^ mask
        if odd_parts:
            y = i % odd_parts
            other = y + 1 if y % 2 else y - 1
            if not 0 <= other < odd_parts:
                continue
            j += other - y
        pairs.append((i, j))
    return lax.ppermute(x, axes, pairs)


def body_gathered(inputs, weight, bias, cotangent):
    spans = inputs.shape[:3]
    span_x, span_y, span_z = spans
    local_ch, channels = weight.shape[3:]
    local = span_x * span_y * span_z
    parts_x, parts_y = lax.axis_size("gx"), lax.axis_size("gy")
    count = parts_x * parts_y
    shards = lax.axis_size("ch")
    axes = ("gx", "gy")
    factor = 1.0 / math.sqrt(local * count)
    place = jnp.stack([lax.axis_index(axis) for axis in ("gx", "gy", "ch")]).astype(jnp.int32)
    taps = weight.reshape(9, 3 * local_ch, channels)
    packing = (span_x // 2, span_y, span_z, 2 * local_ch)
    flat = (local // 2, 2 * local_ch)

    def call(kernel, name, outs, args, scratch=(), flops=0):
        return pl.pallas_call(
            kernel,
            out_shape=[jax.ShapeDtypeStruct(shape, kind) for shape, kind in outs],
            in_specs=[SMEM if x is place else VMEM for x in args],
            out_specs=[VMEM] * len(outs),
            scratch_shapes=[pltpu.VMEM(shape, kind) for shape, kind in scratch],
            compiler_params=PARAMS,
            cost_estimate=pl.CostEstimate(flops=flops, bytes_accessed=1 << 20, transcendentals=0),
            name=name,
        )(*args)

    row = (span_x, span_z, local_ch)
    beside = exchange(inputs, axes, parts_y)
    even, odd, even_corner, odd_corner, held = call(
        prepare_kernel,
        "prepare",
        [(row, BF16)] * 2 + [(row[1:], BF16)] * 2 + [(inputs.shape, BF16)],
        [place, inputs],
    )
    staged = (taps, cotangent.reshape(local, local_ch), bias.reshape(1, local_ch))
    taps, cotangent, bias = pl.pallas_call(
        stage_kernel,
        out_shape=[jax.ShapeDtypeStruct(x.shape, x.dtype) for x in staged],
        in_specs=[VMEM] + [pl.BlockSpec(memory_space=pltpu.HBM)] * len(staged),
        out_specs=[VMEM] * len(staged),
        scratch_shapes=[pltpu.SemaphoreType.DMA((11,))],
        compiler_params=PARAMS,
        cost_estimate=pl.CostEstimate(flops=0, bytes_accessed=1 << 21, transcendentals=0),
        name="stage",
    )(even_corner, *staged)
    even = exchange(even, axes, 1)
    odd = exchange(odd, axes, 0, parts_y)
    even_corner = exchange(even_corner, axes, parts_y + 1)
    odd_corner = exchange(odd_corner, axes, parts_y, parts_y)
    own, *others, pair = call(
        forward_kernel,
        "forward",
        [(flat, F32)] + [(flat, BF16)] * (shards - 1) + [((2,) + packing, BF16)],
        [place, taps, held, even, odd, beside, even_corner, odd_corner],
        [((span_x + 2, span_y + 2, span_z, 3 * local_ch), BF16), ((shards,) + flat, F32)],
        2 * local * 27 * local_ch * channels,
    )
    others = [exchange(x, "ch", k + 1) for k, x in enumerate(others)]
    pair_y = exchange(pair, axes, 2)
    activation, slope = call(
        slope_kernel,
        "slope",
        [((local, local_ch), BF16), (flat, BF16)],
        [own, *others, bias, cotangent],
    )
    pieces = [exchange(slope, "ch", k) for k in range(1, shards)]
    column = jnp.stack([slope] + pieces).reshape((shards,) + packing)
    column, four = lax.optimization_barrier((column, jnp.concatenate([pair, pair_y])))
    slopes = {m: exchange(column, axes, m) if m else column for m in (0, 2, 4, 6, 1)}
    quad = exchange(four, axes, 1)
    volume_shape = (parts_x * span_x + 2, parts_y * span_y + 2, span_z, 3 * local_ch)
    sums_shape = (9, channels, 3 * local_ch)
    per_member = 2 * local * 27 * local_ch * channels
    groups = ((0, 1), (2, 4, 6), (3, 5, 7))
    volume, sums = call(
        functools.partial(first_kernel, parts_x, parts_y, groups[0]),
        "first",
        [(volume_shape, BF16), (sums_shape, F32)],
        [place, pair, pair_y, quad] + [slopes[m] for m in groups[0]],
        [((channels, len(groups[0]) * local), BF16)],
        per_member * len(groups[0]),
    )
    far = (2, 4, 6)
    *held, sums = lax.optimization_barrier([slopes[m] for m in far] + [sums])
    for m, x in zip(far, held):
        slopes[m], slopes[m + 1] = x, exchange(x, axes, 1)
    for members in groups[1:-1]:
        (sums,) = call(
            functools.partial(middle_kernel, parts_y, members),
            "middle",
            [(sums_shape, F32)],
            [place, volume, sums] + [slopes[m] for m in members],
            [((channels, len(members) * local), BF16)],
            per_member * len(members),
        )
    input_grad, kernel_grad, bias_grad = call(
        functools.partial(last_kernel, parts_x, parts_y, groups[-1], factor),
        "last",
        [((local, local_ch), BF16), ((9, 3 * local_ch, channels), F32), ((1, local_ch), F32)],
        [place, taps, volume, sums] + [slopes[m] for m in range(count)],
        [
            ((span_x + 2, span_y + 2, span_z, channels), BF16),
            ((channels, len(groups[-1]) * local), BF16),
        ],
        per_member * (len(groups[-1]) + 1),
    )
    return (
        activation.reshape(inputs.shape),
        input_grad.reshape(inputs.shape),
        kernel_grad.reshape(weight.shape),
        bias_grad.reshape(local_ch),
    )


def solution(mesh):
    few = (mesh.shape["gx"], mesh.shape["gy"]) == (2, 4)
    return jax.shard_map(
        body_gathered if few else body_reduced,
        mesh=mesh,
        in_specs=(
            P("gx", "gy", None, "ch"),
            P(None, None, None, "ch", None),
            P("ch"),
            P("gx", "gy", None, "ch"),
        ),
        out_specs=(
            P("gx", "gy", None, "ch"),
            P("gx", "gy", None, "ch"),
            P(None, None, None, "ch", None),
            P("ch"),
        ),
        check_vma=False,
    )
```

```python
import functools
import math

import jax
import jax.numpy as jnp
from jax import lax
from jax.experimental import pallas as pl
from jax.experimental.pallas import tpu as pltpu
from jax.sharding import PartitionSpec as P

VMEM = pl.BlockSpec(memory_space=pltpu.VMEM)
SMEM = pl.BlockSpec(memory_space=pltpu.SMEM)
PARAMS = pltpu.CompilerParams(vmem_limit_bytes=24 * 1024 * 1024)
F32 = jnp.float32
BF16 = jnp.bfloat16


def with_halo(x, sides, width):
    for axis, dim in sides:
        devices, length = (lax.axis_size(axis), x.shape[dim])
        up = [(i, (i + 1) % devices) for i in range(devices - 1)]
        down = [(j, i) for i, j in up]
        last = lax.slice_in_dim(x, length - width, length, axis=dim)
        initial = lax.slice_in_dim(x, 0, width, axis=dim)
        before = lax.ppermute(last, axis, up)
        after = lax.ppermute(initial, axis, down)
        x = jnp.concatenate([before, x, after], axis=dim)
    return x


def body_reduced(inputs, weight, bias, cotangent):
    span_x, span_y, span_z, local_ch = inputs.shape
    widest = weight.shape[4]
    local_cells = span_x * span_y * span_z
    offsets = [(a, b, c) for a in range(3) for b in range(3) for c in range(3)]
    depth_pad = ((0, 0), (0, 0), (1, 1), (0, 0))
    rimmed = with_halo(inputs, (("gx", 0), ("gy", 1)), 1)
    padded = jnp.pad(rimmed, depth_pad)
    blocks = []
    for a, b, c in offsets:
        blocks.append(
            padded[a : a + span_x, b : b + span_y, c : c + span_z].reshape(local_cells, local_ch)
        )
    patches = jnp.concatenate(blocks, axis=1)
    flat_weight = weight.reshape(27 * local_ch, widest)
    summed = lax.psum_scatter(
        lax.dot_general(flat_weight, patches, (((0,), (1,)), ((), ())), preferred_element_type=F32),
        "ch",
        scatter_dimension=0,
        tiled=True,
    ).T
    summed = summed + bias.astype(F32)[None, :]
    activation = jax.nn.silu(summed).astype(BF16).reshape(span_x, span_y, span_z, local_ch)
    sigmoid_pre = jax.nn.sigmoid(summed)
    slope = (
        cotangent.reshape(local_cells, local_ch).astype(F32)
        * sigmoid_pre
        * (1.0 + summed * (1.0 - sigmoid_pre))
    ).astype(BF16)
    local_bias = jnp.sum(slope.astype(F32), axis=0)
    slope_grid = slope.reshape(span_x, span_y, span_z, local_ch)
    weight_turned = jnp.transpose(weight.reshape(27, local_ch, widest), (0, 2, 1))
    slope_rimmed = with_halo(slope_grid, (("gx", 0), ("gy", 1)), 1)
    piece = lax.all_gather(slope_rimmed, "ch", axis=3, tiled=True)
    extended = jnp.pad(piece, depth_pad)
    running = jnp.zeros((local_cells, local_ch), F32)
    for index, (a, b, c) in enumerate(offsets):
        a, b, c = (2 - a, 2 - b, 2 - c)
        cut = extended[a : a + span_x, b : b + span_y, c : c + span_z].reshape(local_cells, widest)
        running = running + jnp.dot(cut, weight_turned[index], preferred_element_type=F32)
    interior = piece[1 : 1 + span_x, 1 : 1 + span_y].reshape(local_cells, widest)
    product = lax.dot_general(
        patches, interior, (((0,), (0,)), ((), ())), preferred_element_type=F32
    )
    total_cells = local_cells * lax.axis_size("gx") * lax.axis_size("gy")
    factor = 1.0 / math.sqrt(total_cells)
    kernel_total, bias_total = lax.psum((product * factor, local_bias * factor), ("gx", "gy"))
    input_grad = running.astype(BF16).reshape(span_x, span_y, span_z, local_ch)
    return (activation, input_grad, kernel_total.reshape(3, 3, 3, local_ch, widest), bias_total)


def shifted(v, by):
    depth = v.shape[1]
    row = lax.broadcasted_iota(jnp.int32, v.shape, 1)
    if by == 1:
        return jnp.where(row == 0, 0.0, pltpu.roll(v, 1, 1))
    return jnp.where(row == depth - 1, 0.0, pltpu.roll(v, depth - 1, 1))


def rim_sides(place, span_x, span_y):
    first = place[1] % 2 == 0
    even_at = jnp.where(first, span_y + 1, 0)
    odd_at = jnp.where(first, 0, span_y + 1)
    even_row = jnp.where(first, span_y - 1, 0)
    odd_row = jnp.where(first, 0, span_y - 1)
    x_at = jnp.where(place[0] == 0, span_x + 1, 0)
    x_row = jnp.where(place[0] == 0, span_x - 1, 0)
    return even_at, odd_at, even_row, odd_row, x_at, x_row


def prepare_kernel(place, *rest):
    count = (len(rest) - 6) // 2
    sources, targets = rest[:count], rest[count : 2 * count]
    packed, even, odd, even_corner, odd_corner, arrived = rest[2 * count :]
    copies = []
    for source, target in zip(sources, targets):
        parts = source.shape[0] if len(source.shape) == 3 else 1
        for n in range(parts):
            here = pl.ds(n, 1) if parts > 1 else slice(None)
            copies.append(
                pltpu.make_async_copy(source.at[here], target.at[here], arrived.at[len(copies)])
            )
    for copy in copies:
        copy.start()
    copies[0].wait()
    inputs = targets[0]
    span_x, span_y, _, _ = inputs.shape
    half = span_x // 2
    _, _, even_row, odd_row, _, x_row = rim_sides(place, span_x, span_y)
    even[...] = inputs[:, even_row]
    odd[...] = inputs[:, odd_row]
    even_corner[...] = inputs[x_row, even_row]
    odd_corner[...] = inputs[x_row, odd_row]
    packed[...] = jnp.concatenate([inputs[:half], inputs[half:]], axis=3)
    for copy in copies[1:]:
        copy.wait()


def forward_kernel(
    place, weight, inputs, packed, even, odd, beside, even_corner, odd_corner, own, *rest
):
    *others, pair, window, blocks = rest
    span_x, span_y, span_z, lanes = inputs.shape
    half_x = span_x // 2
    half = half_x * span_y * span_z
    even_at, odd_at, _, _, x_at, _ = rim_sides(place, span_x, span_y)

    def spread(v):
        flat = v.astype(F32).reshape(-1, span_z, lanes)
        joined = jnp.concatenate([shifted(flat, 1), flat, shifted(flat, -1)], axis=2)
        return joined.astype(BF16).reshape(v.shape[:-1] + (3 * lanes,))

    nothing = jnp.zeros((span_y + 2, span_z, 3 * lanes), BF16)
    window[0] = nothing
    window[span_x + 1] = nothing
    window[1 : span_x + 1, 1 : span_y + 1] = spread(inputs[...])
    window[1 : span_x + 1, even_at] = spread(even[...])
    window[1 : span_x + 1, odd_at] = spread(odd[...])
    across = jnp.where(place[0] == 0, beside[0][..., :lanes], beside[half_x - 1][..., lanes:])
    window[x_at, 1 : span_y + 1] = spread(across)
    window[x_at, even_at] = spread(even_corner[...])
    window[x_at, odd_at] = spread(odd_corner[...])
    sums = []
    for h in range(2):
        total = None
        for a in range(3):
            for b in range(3):
                cut = window[a + h * half_x : a + (h + 1) * half_x, b : b + span_y]
                term = jnp.dot(
                    cut.reshape(half, 3 * lanes), weight[a * 3 + b], preferred_element_type=F32
                )
                total = term if total is None else total + term
        sums.append(total)
    for d in range(weight.shape[2] // lanes):
        cut = slice(d * lanes, (d + 1) * lanes)
        blocks[d] = jnp.concatenate([sums[0][:, cut], sums[1][:, cut]], axis=1)
    own[...] = blocks[place[2]]
    for k, other in enumerate(others):
        other[...] = blocks[place[2] ^ (k + 1)].astype(BF16)
    pair[0] = packed[...]
    pair[1] = beside[...]


def slope_kernel(own, *rest):
    *others, bias, cotangent, activation, slope = rest
    half, lanes = cotangent.shape[0] // 2, cotangent.shape[1]
    summed = own[...]
    for other in others:
        summed = summed + other[...].astype(F32)
    offset = bias[...].astype(F32)
    summed = summed + jnp.concatenate([offset, offset], axis=1)
    sigmoid = jax.nn.sigmoid(summed)
    active = (summed * sigmoid).astype(BF16)
    activation[:half] = active[:, :lanes]
    activation[half:] = active[:, lanes:]
    upstream = jnp.concatenate([cotangent[:half], cotangent[half:]], axis=1).astype(F32)
    slope[...] = (upstream * sigmoid * (1.0 + summed * (1.0 - sigmoid))).astype(BF16)


def ordered_halves(place, pieces):
    shards, _, _, _, lanes = pieces.shape
    lanes = lanes // 2
    ordered = [pieces[place[2] ^ j] for j in range(shards)]
    return [
        jnp.concatenate([piece[..., h * lanes : (h + 1) * lanes] for piece in ordered], axis=-1)
        for h in range(2)
    ]


def corner_of(place, m, parts_y, span_x, span_y):
    return (place[0] ^ (m // parts_y)) * span_x, (place[1] ^ (m % parts_y)) * span_y


def add_terms(place, parts_y, members, slopes, volume, turned, old, store):
    corners = []
    for n, (m, pieces) in enumerate(zip(members, slopes)):
        shards, half_x, span_y, span_z, lanes = pieces.shape
        span_x, channels = 2 * half_x, shards * lanes // 2
        half = half_x * span_y * span_z
        local = 2 * half
        corners.append(corner_of(place, m, parts_y, span_x, span_y))
        for h, part in enumerate(ordered_halves(place, pieces)):
            turned[:, n * local + h * half : n * local + (h + 1) * half] = part.reshape(
                half, channels
            ).T
    for a in range(3):
        for b in range(3):
            total = None if old is None else old[a * 3 + b]
            for n, (x0, y0) in enumerate(corners):
                cut = volume[pl.ds(x0 + a, span_x), pl.ds(y0 + b, span_y)]
                term = jnp.dot(
                    turned[:, n * local : (n + 1) * local],
                    cut.reshape(local, -1),
                    preferred_element_type=F32,
                )
                total = term if total is None else total + term
            store(a * 3 + b, total)


def first_kernel(parts_x, parts_y, members, place, pair, pair_y, quad, *rest):
    *slopes, volume, sums, turned = rest
    cells = [(0, pair, 0), (parts_y, pair, 1), (2, pair_y, 0), (parts_y + 2, pair_y, 1)]
    cells += [(m ^ 1, quad, n) for n, (m, _, _) in enumerate(cells)]
    _, half_x, span_y, span_z, lanes = pair.shape
    span_x, lanes = 2 * half_x, lanes // 2
    rows_x, rows_y = parts_x * span_x, parts_y * span_y
    width = 3 * lanes
    zero_x = jnp.zeros((1, rows_y + 2, span_z, width), BF16)
    zero_y = jnp.zeros((rows_x + 2, 1, span_z, width), BF16)
    volume[0:1] = zero_x
    volume[rows_x + 1 : rows_x + 2] = zero_x
    volume[:, 0:1] = zero_y
    volume[:, rows_y + 1 : rows_y + 2] = zero_y
    for m, array, n in cells:
        x0, y0 = corner_of(place, m, parts_y, span_x, span_y)
        v = array[n].astype(F32).reshape(half_x * span_y, span_z, 2 * lanes)
        low, high = shifted(v, 1), shifted(v, -1)
        for h in range(2):
            cut = slice(h * lanes, (h + 1) * lanes)
            joined = jnp.concatenate([low[..., cut], v[..., cut], high[..., cut]], axis=2)
            volume[pl.ds(x0 + 1 + h * half_x, half_x), pl.ds(y0 + 1, span_y)] = joined.astype(
                BF16
            ).reshape(half_x, span_y, span_z, width)

    def store(tap, total):
        sums[tap] = total

    add_terms(place, parts_y, members, slopes, volume, turned, None, store)


def middle_kernel(parts_y, members, place, volume, old, *rest):
    *slopes, sums, turned = rest

    def store(tap, total):
        sums[tap] = total

    add_terms(place, parts_y, members, slopes, volume, turned, old, store)


def last_kernel(parts_x, parts_y, members, factor, place, weight, volume, old, *rest):
    *slopes, input_grad, kernel_grad, bias_grad, window, turned = rest
    shards, half_x, span_y, span_z, lanes = slopes[0].shape
    span_x, lanes = 2 * half_x, lanes // 2
    channels = shards * lanes
    half = half_x * span_y * span_z

    def store(tap, total):
        kernel_grad[tap] = (total * factor).T

    add_terms(
        place, parts_y, members, [slopes[m] for m in members], volume, turned, old, store
    )

    column = jnp.zeros((1, 2 * lanes), F32)
    for pieces in slopes:
        mine = pieces[0].astype(F32).reshape(half, 2 * lanes)
        column = column + jnp.sum(mine, axis=0, keepdims=True)
    bias_grad[...] = (column[:, :lanes] + column[:, lanes:]) * factor

    even_at, odd_at, even_row, odd_row, x_at, x_row = rim_sides(place, span_x, span_y)
    has_odd = (place[1] != 0) & (place[1] != parts_y - 1)
    window[...] = jnp.zeros(window.shape, BF16)
    low, high = ordered_halves(place, slopes[0])
    window[1 : half_x + 1, 1 : span_y + 1] = low
    window[half_x + 1 : span_x + 1, 1 : span_y + 1] = high

    def rows_of(m, row):
        ordered = [slopes[m][place[2] ^ j, :, row] for j in range(shards)]
        return [
            jnp.concatenate([piece[..., h * lanes : (h + 1) * lanes] for piece in ordered], axis=-1)
            for h in range(2)
        ]

    def facing(halves):
        low, high = halves
        return jnp.where(place[0] == 0, low[0], high[half_x - 1])

    for h, rows in enumerate(rows_of(1, facing_row(even_row, span_y))):
        window[1 + h * half_x : 1 + (h + 1) * half_x, even_at] = rows
    window[x_at, 1 : span_y + 1] = facing(ordered_halves(place, slopes[parts_y]))
    window[x_at, even_at] = facing(rows_of(parts_y + 1, facing_row(even_row, span_y)))

    @pl.when(has_odd)
    def _():
        for h, rows in enumerate(rows_of(3, facing_row(odd_row, span_y))):
            window[1 + h * half_x : 1 + (h + 1) * half_x, odd_at] = rows
        window[x_at, odd_at] = facing(rows_of(parts_y + 3, facing_row(odd_row, span_y)))

    for h in range(2):
        total = None
        for a in range(3):
            for b in range(3):
                cut = window[
                    2 - a + h * half_x : 2 - a + (h + 1) * half_x, 2 - b : 2 - b + span_y
                ]
                term = lax.dot_general(
                    cut.reshape(half, channels),
                    weight[a * 3 + b],
                    (((1,), (1,)), ((), ())),
                    preferred_element_type=F32,
                )
                total = term if total is None else total + term
        total = total.reshape(half // span_z, span_z, 3 * lanes)
        result = (
            shifted(total[..., :lanes], -1)
            + total[..., lanes : 2 * lanes]
            + shifted(total[..., 2 * lanes :], 1)
        )
        input_grad[h * half : (h + 1) * half] = result.reshape(half, lanes).astype(BF16)


def facing_row(row, span_y):
    return span_y - 1 - row


def exchange(x, axes, mask, odd_parts=0):
    pairs = []
    for i in range(lax.axis_size(axes)):
        j = i ^ mask
        if odd_parts:
            y = i % odd_parts
            other = y + 1 if y % 2 else y - 1
            if not 0 <= other < odd_parts:
                continue
            j += other - y
        pairs.append((i, j))
    return lax.ppermute(x, axes, pairs)


def body_gathered(inputs, weight, bias, cotangent):
    spans = inputs.shape[:3]
    span_x, span_y, span_z = spans
    local_ch, channels = weight.shape[3:]
    local = span_x * span_y * span_z
    parts_x, parts_y = lax.axis_size("gx"), lax.axis_size("gy")
    count = parts_x * parts_y
    shards = lax.axis_size("ch")
    axes = ("gx", "gy")
    factor = 1.0 / math.sqrt(local * count)
    place = jnp.stack([lax.axis_index(axis) for axis in ("gx", "gy", "ch")]).astype(jnp.int32)
    taps = weight.reshape(9, 3 * local_ch, channels)
    packing = (span_x // 2, span_y, span_z, 2 * local_ch)
    flat = (local // 2, 2 * local_ch)

    def call(kernel, name, outs, args, scratch=(), flops=0):
        return pl.pallas_call(
            kernel,
            out_shape=[jax.ShapeDtypeStruct(shape, kind) for shape, kind in outs],
            in_specs=[SMEM if x is place else VMEM for x in args],
            out_specs=[VMEM] * len(outs),
            scratch_shapes=[pltpu.VMEM(shape, kind) for shape, kind in scratch],
            compiler_params=PARAMS,
            cost_estimate=pl.CostEstimate(flops=0, bytes_accessed=1024, transcendentals=0),
            name=name,
        )(*args)

    row = (span_x, span_z, local_ch)
    sources = (inputs, taps, cotangent.reshape(local, local_ch), bias.reshape(1, local_ch))
    outs = [(x.shape, x.dtype) for x in sources]
    outs += [(packing, BF16)] + [(row, BF16)] * 2 + [(row[1:], BF16)] * 2
    held, taps, cotangent, bias, packed, even, odd, even_corner, odd_corner = pl.pallas_call(
        prepare_kernel,
        out_shape=[jax.ShapeDtypeStruct(shape, kind) for shape, kind in outs],
        in_specs=[SMEM] + [pl.BlockSpec(memory_space=pltpu.HBM)] * len(sources),
        out_specs=[VMEM] * len(outs),
        scratch_shapes=[pltpu.SemaphoreType.DMA((len(sources) + 8,))],
        compiler_params=PARAMS,
        name="prepare",
    )(place, *[pltpu.with_memory_space_constraint(x, pltpu.HBM) for x in sources])
    beside = exchange(packed, axes, parts_y)
    even = exchange(even, axes, 1)
    odd = exchange(odd, axes, 0, parts_y)
    even_corner = exchange(even_corner, axes, parts_y + 1)
    odd_corner = exchange(odd_corner, axes, parts_y, parts_y)
    own, *others, pair = call(
        forward_kernel,
        "forward",
        [(flat, F32)] + [(flat, BF16)] * (shards - 1) + [((2,) + packing, BF16)],
        [place, taps, held, packed, even, odd, beside, even_corner, odd_corner],
        [((span_x + 2, span_y + 2, span_z, 3 * local_ch), BF16), ((shards,) + flat, F32)],
        2 * local * 27 * local_ch * channels,
    )
    others = [exchange(x, "ch", k + 1) for k, x in enumerate(others)]
    pair_y = exchange(pair, axes, 2)
    activation, slope = call(
        slope_kernel,
        "slope",
        [((local, local_ch), BF16), (flat, BF16)],
        [own, *others, bias, cotangent],
    )
    pieces = [exchange(slope, "ch", k) for k in range(1, shards)]
    column = jnp.stack([slope] + pieces).reshape((shards,) + packing)
    four, _ = lax.optimization_barrier((jnp.concatenate([pair, pair_y]), column))
    slopes = {m: exchange(column, axes, m) if m else column for m in (0, 2, 4, 6, 1)}
    quad = exchange(four, axes, 1)
    volume_shape = (parts_x * span_x + 2, parts_y * span_y + 2, span_z, 3 * local_ch)
    sums_shape = (9, channels, 3 * local_ch)
    per_member = 2 * local * 27 * local_ch * channels
    volume, sums = call(
        functools.partial(first_kernel, parts_x, parts_y, (0, 1)),
        "first",
        [(volume_shape, BF16), (sums_shape, F32)],
        [place, pair, pair_y, quad, slopes[0], slopes[1]],
        [((channels, 2 * local), BF16)],
        per_member * 2,
    )

    def siblings(members, sums):
        *held, sums = lax.optimization_barrier([slopes[m] for m in members] + [sums])
        for m, x in zip(members, held):
            slopes[m], slopes[m + 1] = x, exchange(x, axes, 1)
        return sums

    def middle(members, sums):
        return call(
            functools.partial(middle_kernel, parts_y, members),
            "middle",
            [(sums_shape, F32)],
            [place, volume, sums] + [slopes[m] for m in members],
            [((channels, len(members) * local), BF16)],
            per_member * len(members),
        )[0]

    sums = siblings((2, 4, 6), sums)
    sums = middle((2, 4, 6), sums)
    members = (3, 5, 7)
    input_grad, kernel_grad, bias_grad = call(
        functools.partial(last_kernel, parts_x, parts_y, members, factor),
        "last",
        [((local, local_ch), BF16), ((9, 3 * local_ch, channels), F32), ((1, local_ch), F32)],
        [place, taps, volume, sums] + [slopes[m] for m in range(count)],
        [
            ((span_x + 2, span_y + 2, span_z, channels), BF16),
            ((channels, len(members) * local), BF16),
        ],
        per_member * (len(members) + 1),
    )
    return (
        activation.reshape(inputs.shape),
        input_grad.reshape(inputs.shape),
        kernel_grad.reshape(weight.shape),
        bias_grad.reshape(local_ch),
    )


def solution(mesh):
    few = (mesh.shape["gx"], mesh.shape["gy"]) == (2, 4)
    return jax.shard_map(
        body_gathered if few else body_reduced,
        mesh=mesh,
        in_specs=(
            P("gx", "gy", None, "ch"),
            P(None, None, None, "ch", None),
            P("ch"),
            P("gx", "gy", None, "ch"),
        ),
        out_specs=(
            P("gx", "gy", None, "ch"),
            P("gx", "gy", None, "ch"),
            P(None, None, None, "ch", None),
            P("ch"),
        ),
        check_vma=False,
    )
```

```python
import functools
import math

import jax
import jax.numpy as jnp
from jax import lax
from jax.experimental import pallas as pl
from jax.experimental.pallas import tpu as pltpu
from jax.sharding import PartitionSpec as P

VMEM = pl.BlockSpec(memory_space=pltpu.VMEM)
SMEM = pl.BlockSpec(memory_space=pltpu.SMEM)
PARAMS = pltpu.CompilerParams(vmem_limit_bytes=24 * 1024 * 1024)
F32 = jnp.float32
BF16 = jnp.bfloat16


def with_halo(x, sides, width):
    for axis, dim in sides:
        devices, length = (lax.axis_size(axis), x.shape[dim])
        up = [(i, (i + 1) % devices) for i in range(devices - 1)]
        down = [(j, i) for i, j in up]
        last = lax.slice_in_dim(x, length - width, length, axis=dim)
        initial = lax.slice_in_dim(x, 0, width, axis=dim)
        before = lax.ppermute(last, axis, up)
        after = lax.ppermute(initial, axis, down)
        x = jnp.concatenate([before, x, after], axis=dim)
    return x


def body_reduced(inputs, weight, bias, cotangent):
    span_x, span_y, span_z, local_ch = inputs.shape
    widest = weight.shape[4]
    local_cells = span_x * span_y * span_z
    offsets = [(a, b, c) for a in range(3) for b in range(3) for c in range(3)]
    depth_pad = ((0, 0), (0, 0), (1, 1), (0, 0))
    rimmed = with_halo(inputs, (("gx", 0), ("gy", 1)), 1)
    padded = jnp.pad(rimmed, depth_pad)
    blocks = []
    for a, b, c in offsets:
        blocks.append(
            padded[a : a + span_x, b : b + span_y, c : c + span_z].reshape(local_cells, local_ch)
        )
    patches = jnp.concatenate(blocks, axis=1)
    flat_weight = weight.reshape(27 * local_ch, widest)
    summed = lax.psum_scatter(
        lax.dot_general(flat_weight, patches, (((0,), (1,)), ((), ())), preferred_element_type=F32),
        "ch",
        scatter_dimension=0,
        tiled=True,
    ).T
    summed = summed + bias.astype(F32)[None, :]
    activation = jax.nn.silu(summed).astype(BF16).reshape(span_x, span_y, span_z, local_ch)
    sigmoid_pre = jax.nn.sigmoid(summed)
    slope = (
        cotangent.reshape(local_cells, local_ch).astype(F32)
        * sigmoid_pre
        * (1.0 + summed * (1.0 - sigmoid_pre))
    ).astype(BF16)
    local_bias = jnp.sum(slope.astype(F32), axis=0)
    slope_grid = slope.reshape(span_x, span_y, span_z, local_ch)
    weight_turned = jnp.transpose(weight.reshape(27, local_ch, widest), (0, 2, 1))
    slope_rimmed = with_halo(slope_grid, (("gx", 0), ("gy", 1)), 1)
    piece = lax.all_gather(slope_rimmed, "ch", axis=3, tiled=True)
    extended = jnp.pad(piece, depth_pad)
    running = jnp.zeros((local_cells, local_ch), F32)
    for index, (a, b, c) in enumerate(offsets):
        a, b, c = (2 - a, 2 - b, 2 - c)
        cut = extended[a : a + span_x, b : b + span_y, c : c + span_z].reshape(local_cells, widest)
        running = running + jnp.dot(cut, weight_turned[index], preferred_element_type=F32)
    interior = piece[1 : 1 + span_x, 1 : 1 + span_y].reshape(local_cells, widest)
    product = lax.dot_general(
        patches, interior, (((0,), (0,)), ((), ())), preferred_element_type=F32
    )
    total_cells = local_cells * lax.axis_size("gx") * lax.axis_size("gy")
    factor = 1.0 / math.sqrt(total_cells)
    kernel_total, bias_total = lax.psum((product * factor, local_bias * factor), ("gx", "gy"))
    input_grad = running.astype(BF16).reshape(span_x, span_y, span_z, local_ch)
    return (activation, input_grad, kernel_total.reshape(3, 3, 3, local_ch, widest), bias_total)


def shifted(v, by):
    depth = v.shape[1]
    row = lax.broadcasted_iota(jnp.int32, v.shape, 1)
    if by == 1:
        return jnp.where(row == 0, 0.0, pltpu.roll(v, 1, 1))
    return jnp.where(row == depth - 1, 0.0, pltpu.roll(v, depth - 1, 1))


def rim_sides(place, span_x, span_y):
    first = place[1] % 2 == 0
    even_at = jnp.where(first, span_y + 1, 0)
    odd_at = jnp.where(first, 0, span_y + 1)
    even_row = jnp.where(first, span_y - 1, 0)
    odd_row = jnp.where(first, 0, span_y - 1)
    x_at = jnp.where(place[0] == 0, span_x + 1, 0)
    x_row = jnp.where(place[0] == 0, span_x - 1, 0)
    return even_at, odd_at, even_row, odd_row, x_at, x_row


def prepare_kernel(place, *rest):
    count = (len(rest) - 6) // 2
    sources, targets = rest[:count], rest[count : 2 * count]
    packed, even, odd, even_corner, odd_corner, arrived = rest[2 * count :]
    copies = []
    for source, target in zip(sources, targets):
        parts = source.shape[0] if len(source.shape) == 3 else 1
        for n in range(parts):
            here = pl.ds(n, 1) if parts > 1 else slice(None)
            copies.append(
                pltpu.make_async_copy(source.at[here], target.at[here], arrived.at[len(copies)])
            )
    for copy in copies:
        copy.start()
    copies[0].wait()
    inputs = targets[0]
    span_x, span_y, _, _ = inputs.shape
    half = span_x // 2
    _, _, even_row, odd_row, _, x_row = rim_sides(place, span_x, span_y)
    even[...] = inputs[:, even_row]
    odd[...] = inputs[:, odd_row]
    even_corner[...] = inputs[x_row, even_row]
    odd_corner[...] = inputs[x_row, odd_row]
    packed[...] = jnp.concatenate([inputs[:half], inputs[half:]], axis=3)
    for copy in copies[1:]:
        copy.wait()


def forward_kernel(
    parts_y, place, weight, inputs, packed, even, odd, beside, even_corner, odd_corner, own, *rest
):
    *others, pair, window, blocks = rest
    span_x, span_y, span_z, lanes = inputs.shape
    half_x = span_x // 2
    half = half_x * span_y * span_z
    even_at, odd_at, _, _, x_at, _ = rim_sides(place, span_x, span_y)

    def spread(v):
        flat = v.astype(F32).reshape(-1, span_z, lanes)
        joined = jnp.concatenate([shifted(flat, 1), flat, shifted(flat, -1)], axis=2)
        return joined.astype(BF16).reshape(v.shape[:-1] + (3 * lanes,))

    nothing = jnp.zeros((span_y + 2, span_z, 3 * lanes), BF16)
    window[0] = nothing
    window[span_x + 1] = nothing
    window[1 : span_x + 1, 1 : span_y + 1] = spread(inputs[...])
    window[1 : span_x + 1, even_at] = spread(even[...])
    has_odd = (place[1] != 0) & (place[1] != parts_y - 1)
    window[1 : span_x + 1, odd_at] = jnp.where(has_odd, spread(odd[...]), jnp.zeros((), BF16))
    across = jnp.where(place[0] == 0, beside[0][..., :lanes], beside[half_x - 1][..., lanes:])
    window[x_at, 1 : span_y + 1] = spread(across)
    window[x_at, even_at] = spread(even_corner[...])
    window[x_at, odd_at] = jnp.where(has_odd, spread(odd_corner[...]), jnp.zeros((), BF16))
    sums = []
    for h in range(2):
        total = None
        for a in range(3):
            for b in range(3):
                cut = window[a + h * half_x : a + (h + 1) * half_x, b : b + span_y]
                term = jnp.dot(
                    cut.reshape(half, 3 * lanes), weight[a * 3 + b], preferred_element_type=F32
                )
                total = term if total is None else total + term
        sums.append(total)
    for d in range(weight.shape[2] // lanes):
        cut = slice(d * lanes, (d + 1) * lanes)
        blocks[d] = jnp.concatenate([sums[0][:, cut], sums[1][:, cut]], axis=1)
    own[...] = blocks[place[2]]
    for k, other in enumerate(others):
        other[...] = blocks[place[2] ^ (k + 1)].astype(BF16)
    pair[0] = packed[...]
    pair[1] = beside[...]


def slope_kernel(own, *rest):
    *others, bias, cotangent, activation, slope = rest
    half, lanes = cotangent.shape[0] // 2, cotangent.shape[1]
    summed = own[...]
    for other in others:
        summed = summed + other[...].astype(F32)
    offset = bias[...].astype(F32)
    summed = summed + jnp.concatenate([offset, offset], axis=1)
    sigmoid = jax.nn.sigmoid(summed)
    active = (summed * sigmoid).astype(BF16)
    activation[:half] = active[:, :lanes]
    activation[half:] = active[:, lanes:]
    upstream = jnp.concatenate([cotangent[:half], cotangent[half:]], axis=1).astype(F32)
    slope[...] = (upstream * sigmoid * (1.0 + summed * (1.0 - sigmoid))).astype(BF16)


def ordered_halves(place, pieces):
    shards, _, _, _, lanes = pieces.shape
    lanes = lanes // 2
    ordered = [pieces[place[2] ^ j] for j in range(shards)]
    return [
        jnp.concatenate([piece[..., h * lanes : (h + 1) * lanes] for piece in ordered], axis=-1)
        for h in range(2)
    ]


def corner_of(place, m, parts_y, span_x, span_y):
    return (place[0] ^ (m // parts_y)) * span_x, (place[1] ^ (m % parts_y)) * span_y


def add_terms(place, parts_y, members, slopes, volume, turned, old, store):
    corners = []
    for n, (m, pieces) in enumerate(zip(members, slopes)):
        shards, half_x, span_y, span_z, lanes = pieces.shape
        span_x, channels = 2 * half_x, shards * lanes // 2
        half = half_x * span_y * span_z
        local = 2 * half
        corners.append(corner_of(place, m, parts_y, span_x, span_y))
        for h, part in enumerate(ordered_halves(place, pieces)):
            turned[:, n * local + h * half : n * local + (h + 1) * half] = part.reshape(
                half, channels
            ).T
    for a in range(3):
        for b in range(3):
            total = None if old is None else old[a * 3 + b]
            for n, (x0, y0) in enumerate(corners):
                cut = volume[pl.ds(x0 + a, span_x), pl.ds(y0 + b, span_y)]
                term = jnp.dot(
                    turned[:, n * local : (n + 1) * local],
                    cut.reshape(local, -1),
                    preferred_element_type=F32,
                )
                total = term if total is None else total + term
            store(a * 3 + b, total)


def first_kernel(parts_x, parts_y, members, place, pair, pair_y, quad, *rest):
    *slopes, volume, sums, turned = rest
    cells = [(0, pair, 0), (parts_y, pair, 1), (2, pair_y, 0), (parts_y + 2, pair_y, 1)]
    cells += [(m ^ 1, quad, n) for n, (m, _, _) in enumerate(cells)]
    _, half_x, span_y, span_z, lanes = pair.shape
    span_x, lanes = 2 * half_x, lanes // 2
    rows_x, rows_y = parts_x * span_x, parts_y * span_y
    width = 3 * lanes
    zero_x = jnp.zeros((1, rows_y + 2, span_z, width), BF16)
    zero_y = jnp.zeros((rows_x + 2, 1, span_z, width), BF16)
    volume[0:1] = zero_x
    volume[rows_x + 1 : rows_x + 2] = zero_x
    volume[:, 0:1] = zero_y
    volume[:, rows_y + 1 : rows_y + 2] = zero_y
    for m, array, n in cells:
        x0, y0 = corner_of(place, m, parts_y, span_x, span_y)
        v = array[n].astype(F32).reshape(half_x * span_y, span_z, 2 * lanes)
        low, high = shifted(v, 1), shifted(v, -1)
        for h in range(2):
            cut = slice(h * lanes, (h + 1) * lanes)
            joined = jnp.concatenate([low[..., cut], v[..., cut], high[..., cut]], axis=2)
            volume[pl.ds(x0 + 1 + h * half_x, half_x), pl.ds(y0 + 1, span_y)] = joined.astype(
                BF16
            ).reshape(half_x, span_y, span_z, width)

    def store(tap, total):
        sums[tap] = total

    add_terms(place, parts_y, members, slopes, volume, turned, None, store)


def middle_kernel(parts_y, members, place, volume, old, *rest):
    *slopes, sums, turned = rest

    def store(tap, total):
        sums[tap] = total

    add_terms(place, parts_y, members, slopes, volume, turned, old, store)


def last_kernel(parts_x, parts_y, members, factor, place, weight, volume, old, *rest):
    *slopes, input_grad, kernel_grad, bias_grad, window, turned = rest
    shards, half_x, span_y, span_z, lanes = slopes[0].shape
    span_x, lanes = 2 * half_x, lanes // 2
    channels = shards * lanes
    half = half_x * span_y * span_z

    def store(tap, total):
        kernel_grad[tap] = (total * factor).T

    add_terms(
        place, parts_y, members, [slopes[m] for m in members], volume, turned, old, store
    )

    column = jnp.zeros((1, 2 * lanes), F32)
    for pieces in slopes:
        mine = pieces[0].astype(F32).reshape(half, 2 * lanes)
        column = column + jnp.sum(mine, axis=0, keepdims=True)
    bias_grad[...] = (column[:, :lanes] + column[:, lanes:]) * factor

    even_at, odd_at, even_row, odd_row, x_at, x_row = rim_sides(place, span_x, span_y)
    has_odd = (place[1] != 0) & (place[1] != parts_y - 1)
    window[...] = jnp.zeros(window.shape, BF16)
    low, high = ordered_halves(place, slopes[0])
    window[1 : half_x + 1, 1 : span_y + 1] = low
    window[half_x + 1 : span_x + 1, 1 : span_y + 1] = high

    def rows_of(m, row):
        ordered = [slopes[m][place[2] ^ j, :, row] for j in range(shards)]
        return [
            jnp.concatenate([piece[..., h * lanes : (h + 1) * lanes] for piece in ordered], axis=-1)
            for h in range(2)
        ]

    def facing(halves):
        low, high = halves
        return jnp.where(place[0] == 0, low[0], high[half_x - 1])

    for h, rows in enumerate(rows_of(1, facing_row(even_row, span_y))):
        window[1 + h * half_x : 1 + (h + 1) * half_x, even_at] = rows
    window[x_at, 1 : span_y + 1] = facing(ordered_halves(place, slopes[parts_y]))
    window[x_at, even_at] = facing(rows_of(parts_y + 1, facing_row(even_row, span_y)))

    @pl.when(has_odd)
    def _():
        for h, rows in enumerate(rows_of(3, facing_row(odd_row, span_y))):
            window[1 + h * half_x : 1 + (h + 1) * half_x, odd_at] = rows
        window[x_at, odd_at] = facing(rows_of(parts_y + 3, facing_row(odd_row, span_y)))

    for h in range(2):
        total = None
        for a in range(3):
            for b in range(3):
                cut = window[
                    2 - a + h * half_x : 2 - a + (h + 1) * half_x, 2 - b : 2 - b + span_y
                ]
                term = lax.dot_general(
                    cut.reshape(half, channels),
                    weight[a * 3 + b],
                    (((1,), (1,)), ((), ())),
                    preferred_element_type=F32,
                )
                total = term if total is None else total + term
        total = total.reshape(half // span_z, span_z, 3 * lanes)
        result = (
            shifted(total[..., :lanes], -1)
            + total[..., lanes : 2 * lanes]
            + shifted(total[..., 2 * lanes :], 1)
        )
        input_grad[h * half : (h + 1) * half] = result.reshape(half, lanes).astype(BF16)


def facing_row(row, span_y):
    return span_y - 1 - row


def exchange(x, axes, mask):
    return lax.ppermute(x, axes, [(i, i ^ mask) for i in range(lax.axis_size(axes))])


def body_gathered(inputs, weight, bias, cotangent):
    spans = inputs.shape[:3]
    span_x, span_y, span_z = spans
    local_ch, channels = weight.shape[3:]
    local = span_x * span_y * span_z
    parts_x, parts_y = lax.axis_size("gx"), lax.axis_size("gy")
    count = parts_x * parts_y
    shards = lax.axis_size("ch")
    axes = ("gx", "gy")
    factor = 1.0 / math.sqrt(local * count)
    place = jnp.stack([lax.axis_index(axis) for axis in ("gx", "gy", "ch")]).astype(jnp.int32)
    taps = weight.reshape(9, 3 * local_ch, channels)
    packing = (span_x // 2, span_y, span_z, 2 * local_ch)
    flat = (local // 2, 2 * local_ch)

    def call(kernel, name, outs, args, scratch=(), flops=0):
        return pl.pallas_call(
            kernel,
            out_shape=[jax.ShapeDtypeStruct(shape, kind) for shape, kind in outs],
            in_specs=[SMEM if x is place else VMEM for x in args],
            out_specs=[VMEM] * len(outs),
            scratch_shapes=[pltpu.VMEM(shape, kind) for shape, kind in scratch],
            compiler_params=PARAMS,
            cost_estimate=pl.CostEstimate(flops=0, bytes_accessed=1024, transcendentals=0),
            name=name,
        )(*args)

    row = (span_x, span_z, local_ch)
    sources = (inputs, taps, cotangent.reshape(local, local_ch), bias.reshape(1, local_ch))
    outs = [(x.shape, x.dtype) for x in sources]
    outs += [(packing, BF16)] + [(row, BF16)] * 2 + [(row[1:], BF16)] * 2
    held, taps, cotangent, bias, packed, even, odd, even_corner, odd_corner = pl.pallas_call(
        prepare_kernel,
        out_shape=[jax.ShapeDtypeStruct(shape, kind) for shape, kind in outs],
        in_specs=[SMEM] + [pl.BlockSpec(memory_space=pltpu.HBM)] * len(sources),
        out_specs=[VMEM] * len(outs),
        scratch_shapes=[pltpu.SemaphoreType.DMA((len(sources) + 8,))],
        compiler_params=PARAMS,
        name="prepare",
    )(place, *[pltpu.with_memory_space_constraint(x, pltpu.HBM) for x in sources])
    beside = exchange(packed, axes, parts_y)
    even = exchange(even, axes, 1)
    odd = exchange(odd, axes, 3)
    even_corner = exchange(even_corner, axes, parts_y + 1)
    odd_corner = exchange(odd_corner, axes, parts_y + 3)
    own, *others, pair = call(
        functools.partial(forward_kernel, parts_y),
        "forward",
        [(flat, F32)] + [(flat, BF16)] * (shards - 1) + [((2,) + packing, BF16)],
        [place, taps, held, packed, even, odd, beside, even_corner, odd_corner],
        [((span_x + 2, span_y + 2, span_z, 3 * local_ch), BF16), ((shards,) + flat, F32)],
        2 * local * 27 * local_ch * channels,
    )
    others = [exchange(x, "ch", k + 1) for k, x in enumerate(others)]
    own, pair_y = lax.optimization_barrier((own, exchange(pair, axes, 2)))
    activation, slope = call(
        slope_kernel,
        "slope",
        [((local, local_ch), BF16), (flat, BF16)],
        [own, *others, bias, cotangent],
    )
    pieces = [exchange(slope, "ch", k) for k in range(1, shards)]
    column = jnp.stack([slope] + pieces).reshape((shards,) + packing)
    four, _ = lax.optimization_barrier((jnp.concatenate([pair, pair_y]), slope))
    quad = exchange(four, axes, 1)
    column, quad = lax.optimization_barrier((column, quad))
    slopes = {m: exchange(column, axes, m) if m else column for m in (0, 2, 4, 6, 1)}
    volume_shape = (parts_x * span_x + 2, parts_y * span_y + 2, span_z, 3 * local_ch)
    sums_shape = (9, channels, 3 * local_ch)
    per_member = 2 * local * 27 * local_ch * channels
    volume, sums = call(
        functools.partial(first_kernel, parts_x, parts_y, (0, 1)),
        "first",
        [(volume_shape, BF16), (sums_shape, F32)],
        [place, pair, pair_y, quad, slopes[0], slopes[1]],
        [((channels, 2 * local), BF16)],
        per_member * 2,
    )

    def siblings(members, sums):
        *held, sums = lax.optimization_barrier([slopes[m] for m in members] + [sums])
        for m, x in zip(members, held):
            slopes[m], slopes[m + 1] = x, exchange(x, axes, 1)
        return sums

    def middle(members, sums):
        return call(
            functools.partial(middle_kernel, parts_y, members),
            "middle",
            [(sums_shape, F32)],
            [place, volume, sums] + [slopes[m] for m in members],
            [((channels, len(members) * local), BF16)],
            per_member * len(members),
        )[0]

    sums = siblings((2, 4, 6), sums)
    sums = middle((2, 4, 6), sums)
    members = (3, 5, 7)
    input_grad, kernel_grad, bias_grad = call(
        functools.partial(last_kernel, parts_x, parts_y, members, factor),
        "last",
        [((local, local_ch), BF16), ((9, 3 * local_ch, channels), F32), ((1, local_ch), F32)],
        [place, taps, volume, sums] + [slopes[m] for m in range(count)],
        [
            ((span_x + 2, span_y + 2, span_z, channels), BF16),
            ((channels, len(members) * local), BF16),
        ],
        per_member * (len(members) + 1),
    )
    return (
        activation.reshape(inputs.shape),
        input_grad.reshape(inputs.shape),
        kernel_grad.reshape(weight.shape),
        bias_grad.reshape(local_ch),
    )


def solution(mesh):
    few = (mesh.shape["gx"], mesh.shape["gy"]) == (2, 4)
    return jax.shard_map(
        body_gathered if few else body_reduced,
        mesh=mesh,
        in_specs=(
            P("gx", "gy", None, "ch"),
            P(None, None, None, "ch", None),
            P("ch"),
            P("gx", "gy", None, "ch"),
        ),
        out_specs=(
            P("gx", "gy", None, "ch"),
            P("gx", "gy", None, "ch"),
            P(None, None, None, "ch", None),
            P("ch"),
        ),
        check_vma=False,
    )
```

```python
import functools
import math

import jax
import jax.numpy as jnp
from jax import lax
from jax.experimental import pallas as pl
from jax.experimental.pallas import tpu as pltpu
from jax.sharding import PartitionSpec as P

VMEM = pl.BlockSpec(memory_space=pltpu.VMEM)
HBM = pl.BlockSpec(memory_space=pltpu.HBM)
SMEM = pl.BlockSpec(memory_space=pltpu.SMEM)
PARAMS = pltpu.CompilerParams(vmem_limit_bytes=24 * 1024 * 1024)
F32 = jnp.float32
BF16 = jnp.bfloat16


def with_halo(x, sides, width):
    for axis, dim in sides:
        devices, length = (lax.axis_size(axis), x.shape[dim])
        up = [(i, (i + 1) % devices) for i in range(devices - 1)]
        down = [(j, i) for i, j in up]
        last = lax.slice_in_dim(x, length - width, length, axis=dim)
        initial = lax.slice_in_dim(x, 0, width, axis=dim)
        before = lax.ppermute(last, axis, up)
        after = lax.ppermute(initial, axis, down)
        x = jnp.concatenate([before, x, after], axis=dim)
    return x


def body_reduced(inputs, weight, bias, cotangent):
    span_x, span_y, span_z, local_ch = inputs.shape
    widest = weight.shape[4]
    local_cells = span_x * span_y * span_z
    offsets = [(a, b, c) for a in range(3) for b in range(3) for c in range(3)]
    depth_pad = ((0, 0), (0, 0), (1, 1), (0, 0))
    rimmed = with_halo(inputs, (("gx", 0), ("gy", 1)), 1)
    padded = jnp.pad(rimmed, depth_pad)
    blocks = []
    for a, b, c in offsets:
        blocks.append(
            padded[a : a + span_x, b : b + span_y, c : c + span_z].reshape(local_cells, local_ch)
        )
    patches = jnp.concatenate(blocks, axis=1)
    flat_weight = weight.reshape(27 * local_ch, widest)
    summed = lax.psum_scatter(
        lax.dot_general(flat_weight, patches, (((0,), (1,)), ((), ())), preferred_element_type=F32),
        "ch",
        scatter_dimension=0,
        tiled=True,
    ).T
    summed = summed + bias.astype(F32)[None, :]
    activation = jax.nn.silu(summed).astype(BF16).reshape(span_x, span_y, span_z, local_ch)
    sigmoid_pre = jax.nn.sigmoid(summed)
    slope = (
        cotangent.reshape(local_cells, local_ch).astype(F32)
        * sigmoid_pre
        * (1.0 + summed * (1.0 - sigmoid_pre))
    ).astype(BF16)
    local_bias = jnp.sum(slope.astype(F32), axis=0)
    slope_grid = slope.reshape(span_x, span_y, span_z, local_ch)
    weight_turned = jnp.transpose(weight.reshape(27, local_ch, widest), (0, 2, 1))
    slope_rimmed = with_halo(slope_grid, (("gx", 0), ("gy", 1)), 1)
    piece = lax.all_gather(slope_rimmed, "ch", axis=3, tiled=True)
    extended = jnp.pad(piece, depth_pad)
    running = jnp.zeros((local_cells, local_ch), F32)
    for index, (a, b, c) in enumerate(offsets):
        a, b, c = (2 - a, 2 - b, 2 - c)
        cut = extended[a : a + span_x, b : b + span_y, c : c + span_z].reshape(local_cells, widest)
        running = running + jnp.dot(cut, weight_turned[index], preferred_element_type=F32)
    interior = piece[1 : 1 + span_x, 1 : 1 + span_y].reshape(local_cells, widest)
    product = lax.dot_general(
        patches, interior, (((0,), (0,)), ((), ())), preferred_element_type=F32
    )
    total_cells = local_cells * lax.axis_size("gx") * lax.axis_size("gy")
    factor = 1.0 / math.sqrt(total_cells)
    kernel_total, bias_total = lax.psum((product * factor, local_bias * factor), ("gx", "gy"))
    input_grad = running.astype(BF16).reshape(span_x, span_y, span_z, local_ch)
    return (activation, input_grad, kernel_total.reshape(3, 3, 3, local_ch, widest), bias_total)


def shifted(v, by):
    depth = v.shape[1]
    row = lax.broadcasted_iota(jnp.int32, v.shape, 1)
    if by == 1:
        return jnp.where(row == 0, 0.0, pltpu.roll(v, 1, 1))
    return jnp.where(row == depth - 1, 0.0, pltpu.roll(v, depth - 1, 1))


def rim_sides(place, span_x, span_y):
    first = place[1] % 2 == 0
    even_at = jnp.where(first, span_y + 1, 0)
    odd_at = jnp.where(first, 0, span_y + 1)
    even_row = jnp.where(first, span_y - 1, 0)
    odd_row = jnp.where(first, 0, span_y - 1)
    x_at = jnp.where(place[0] == 0, span_x + 1, 0)
    x_row = jnp.where(place[0] == 0, span_x - 1, 0)
    return even_at, odd_at, even_row, odd_row, x_at, x_row


def prepare_kernel(place, source, inputs, packed, even, odd, even_corner, odd_corner, arrived):
    copy = pltpu.make_async_copy(source, inputs, arrived)
    copy.start()
    copy.wait()
    span_x, span_y, _, _ = inputs.shape
    half = span_x // 2
    _, _, even_row, odd_row, _, x_row = rim_sides(place, span_x, span_y)
    even[...] = inputs[:, even_row]
    odd[...] = inputs[:, odd_row]
    even_corner[...] = inputs[x_row, even_row]
    odd_corner[...] = inputs[x_row, odd_row]
    packed[...] = jnp.concatenate([inputs[:half], inputs[half:]], axis=3)


def stage_kernel(after, *rest):
    count = (len(rest) - 1) // 2
    sources, targets, arrived = rest[:count], rest[count : 2 * count], rest[-1]
    copies = []
    for source, target in zip(sources, targets):
        parts = source.shape[0] if len(source.shape) == 3 else 1
        for n in range(parts):
            here = pl.ds(n, 1) if parts > 1 else slice(None)
            copies.append(
                pltpu.make_async_copy(source.at[here], target.at[here], arrived.at[len(copies)])
            )
    for copy in copies:
        copy.start()
    for copy in copies:
        copy.wait()


def forward_kernel(
    parts_y, place, weight, inputs, packed, even, odd, beside, even_corner, odd_corner, own, *rest
):
    *others, pair, window, blocks = rest
    span_x, span_y, span_z, lanes = inputs.shape
    half_x = span_x // 2
    half = half_x * span_y * span_z
    even_at, odd_at, _, _, x_at, _ = rim_sides(place, span_x, span_y)

    def spread(v):
        flat = v.astype(F32).reshape(-1, span_z, lanes)
        joined = jnp.concatenate([shifted(flat, 1), flat, shifted(flat, -1)], axis=2)
        return joined.astype(BF16).reshape(v.shape[:-1] + (3 * lanes,))

    nothing = jnp.zeros((span_y + 2, span_z, 3 * lanes), BF16)
    window[0] = nothing
    window[span_x + 1] = nothing
    window[1 : span_x + 1, 1 : span_y + 1] = spread(inputs[...])
    window[1 : span_x + 1, even_at] = spread(even[...])
    has_odd = (place[1] != 0) & (place[1] != parts_y - 1)
    window[1 : span_x + 1, odd_at] = jnp.where(has_odd, spread(odd[...]), jnp.zeros((), BF16))
    across = jnp.where(place[0] == 0, beside[0][..., :lanes], beside[half_x - 1][..., lanes:])
    window[x_at, 1 : span_y + 1] = spread(across)
    window[x_at, even_at] = spread(even_corner[...])
    window[x_at, odd_at] = jnp.where(has_odd, spread(odd_corner[...]), jnp.zeros((), BF16))
    sums = []
    for h in range(2):
        total = None
        for a in range(3):
            for b in range(3):
                cut = window[a + h * half_x : a + (h + 1) * half_x, b : b + span_y]
                term = jnp.dot(
                    cut.reshape(half, 3 * lanes), weight[a * 3 + b], preferred_element_type=F32
                )
                total = term if total is None else total + term
        sums.append(total)
    for d in range(weight.shape[2] // lanes):
        cut = slice(d * lanes, (d + 1) * lanes)
        blocks[d] = jnp.concatenate([sums[0][:, cut], sums[1][:, cut]], axis=1)
    own[...] = blocks[place[2]]
    for k, other in enumerate(others):
        other[...] = blocks[place[2] ^ (k + 1)].astype(BF16)
    pair[0] = packed[...]
    pair[1] = beside[...]


def slope_kernel(own, *rest):
    *others, bias, cotangent, activation, slope = rest
    half, lanes = cotangent.shape[0] // 2, cotangent.shape[1]
    summed = own[...]
    for other in others:
        summed = summed + other[...].astype(F32)
    offset = bias[...].astype(F32)
    summed = summed + jnp.concatenate([offset, offset], axis=1)
    sigmoid = jax.nn.sigmoid(summed)
    active = (summed * sigmoid).astype(BF16)
    activation[:half] = active[:, :lanes]
    activation[half:] = active[:, lanes:]
    upstream = jnp.concatenate([cotangent[:half], cotangent[half:]], axis=1).astype(F32)
    slope[...] = (upstream * sigmoid * (1.0 + summed * (1.0 - sigmoid))).astype(BF16)


def ordered_halves(place, pieces):
    shards, _, _, _, lanes = pieces.shape
    lanes = lanes // 2
    ordered = [pieces[place[2] ^ j] for j in range(shards)]
    return [
        jnp.concatenate([piece[..., h * lanes : (h + 1) * lanes] for piece in ordered], axis=-1)
        for h in range(2)
    ]


def add_terms(place, parts_y, members, slopes, turned, old, store):
    operands = []
    for m, pieces in zip(members, slopes):
        shards, half_x, span_y, span_z, lanes = pieces.shape
        channels, row = shards * lanes // 2, span_y * span_z
        right = jnp.concatenate(
            [part.reshape(half_x * row, channels) for part in ordered_halves(place, pieces)]
        )
        x0, y0 = (place[0] ^ (m // parts_y)) * 2 * half_x, place[1] ^ (m % parts_y)
        operands.append((x0, y0, row, right))
    for a in range(3):
        total = None if old is None else old[a]
        for x0, y0, row, right in operands:
            left = turned[y0, :, pl.ds(pl.multiple_of((x0 + a) * row, row), right.shape[0])]
            term = jnp.dot(left, right, preferred_element_type=F32)
            total = term if total is None else total + term
        store(a, total)


def first_kernel(parts_x, parts_y, place, pair, beside_y, sibling, column, turned, sums, volume):
    shards, half_x, span_y, span_z, lanes = column.shape
    cells = [(0, pair, 0), (parts_y, pair, 1), (2, beside_y, 1), (parts_y + 2, beside_y, 2)]
    cells += [(m ^ 1, sibling, shards + n) for n, (m, _, _) in enumerate(cells)]
    span_x, lanes = 2 * half_x, lanes // 2
    rows_x, rows_y = parts_x * span_x, parts_y * span_y
    width = 3 * lanes
    zero_x = jnp.zeros((1, rows_y + 2, span_z, width), BF16)
    zero_y = jnp.zeros((rows_x + 2, 1, span_z, width), BF16)
    volume[0:1] = zero_x
    volume[rows_x + 1 : rows_x + 2] = zero_x
    volume[:, 0:1] = zero_y
    volume[:, rows_y + 1 : rows_y + 2] = zero_y
    for m, array, n in cells:
        x0, y0 = (place[0] ^ (m // parts_y)) * span_x, (place[1] ^ (m % parts_y)) * span_y
        v = array[n].astype(F32).reshape(half_x * span_y, span_z, 2 * lanes)
        low, high = shifted(v, 1), shifted(v, -1)
        for h in range(2):
            cut = slice(h * lanes, (h + 1) * lanes)
            joined = jnp.concatenate([low[..., cut], v[..., cut], high[..., cut]], axis=2)
            volume[pl.ds(x0 + 1 + h * half_x, half_x), pl.ds(y0 + 1, span_y)] = joined.astype(
                BF16
            ).reshape(half_x, span_y, span_z, width)
    for y in range(parts_y):
        for b in range(3):
            cut = volume[:, y * span_y + b : (y + 1) * span_y + b]
            turned[y, b * width : (b + 1) * width] = cut.reshape(-1, width).T

    def store(a, total):
        sums[a] = total

    members = (0, 1)
    add_terms(place, parts_y, members, (column, sibling.at[:shards]), turned, None, store)


def middle_kernel(parts_y, members, place, turned, old, *rest):
    *slopes, sums = rest

    def store(a, total):
        sums[a] = total

    add_terms(place, parts_y, members, slopes, turned, old, store)


def last_kernel(parts_y, members, factor, place, weight, turned, old, *rest):
    *slopes, input_grad, kernel_grad, bias_grad, window = rest
    shards, half_x, span_y, span_z, lanes = slopes[0].shape
    span_x, lanes = 2 * half_x, lanes // 2
    channels = shards * lanes
    half = half_x * span_y * span_z

    def store(a, total):
        kernel_grad[a] = total * factor

    add_terms(place, parts_y, members, [slopes[m] for m in members], turned, old, store)

    column = jnp.zeros((1, 2 * lanes), F32)
    for pieces in slopes:
        mine = pieces[0].astype(F32).reshape(half, 2 * lanes)
        column = column + jnp.sum(mine, axis=0, keepdims=True)
    bias_grad[...] = (column[:, :lanes] + column[:, lanes:]) * factor

    even_at, odd_at, even_row, odd_row, x_at, x_row = rim_sides(place, span_x, span_y)
    has_odd = (place[1] != 0) & (place[1] != parts_y - 1)
    window[...] = jnp.zeros(window.shape, BF16)
    low, high = ordered_halves(place, slopes[0])
    window[1 : half_x + 1, 1 : span_y + 1] = low
    window[half_x + 1 : span_x + 1, 1 : span_y + 1] = high

    def rows_of(m, row):
        ordered = [slopes[m][place[2] ^ j, :, row] for j in range(shards)]
        return [
            jnp.concatenate([piece[..., h * lanes : (h + 1) * lanes] for piece in ordered], axis=-1)
            for h in range(2)
        ]

    def facing(halves):
        low, high = halves
        return jnp.where(place[0] == 0, low[0], high[half_x - 1])

    for h, rows in enumerate(rows_of(1, facing_row(even_row, span_y))):
        window[1 + h * half_x : 1 + (h + 1) * half_x, even_at] = rows
    window[x_at, 1 : span_y + 1] = facing(ordered_halves(place, slopes[parts_y]))
    window[x_at, even_at] = facing(rows_of(parts_y + 1, facing_row(even_row, span_y)))

    @pl.when(has_odd)
    def _():
        for h, rows in enumerate(rows_of(3, facing_row(odd_row, span_y))):
            window[1 + h * half_x : 1 + (h + 1) * half_x, odd_at] = rows
        window[x_at, odd_at] = facing(rows_of(parts_y + 3, facing_row(odd_row, span_y)))

    for h in range(2):
        total = None
        for a in range(3):
            for b in range(3):
                cut = window[
                    2 - a + h * half_x : 2 - a + (h + 1) * half_x, 2 - b : 2 - b + span_y
                ]
                term = lax.dot_general(
                    cut.reshape(half, channels),
                    weight[a * 3 + b],
                    (((1,), (1,)), ((), ())),
                    preferred_element_type=F32,
                )
                total = term if total is None else total + term
        total = total.reshape(half // span_z, span_z, 3 * lanes)
        result = (
            shifted(total[..., :lanes], -1)
            + total[..., lanes : 2 * lanes]
            + shifted(total[..., 2 * lanes :], 1)
        )
        input_grad[h * half : (h + 1) * half] = result.reshape(half, lanes).astype(BF16)


def facing_row(row, span_y):
    return span_y - 1 - row


def exchange(x, axes, mask):
    return lax.ppermute(x, axes, [(i, i ^ mask) for i in range(lax.axis_size(axes))])


def body_gathered(inputs, weight, bias, cotangent):
    spans = inputs.shape[:3]
    span_x, span_y, span_z = spans
    local_ch, channels = weight.shape[3:]
    local = span_x * span_y * span_z
    parts_x, parts_y = lax.axis_size("gx"), lax.axis_size("gy")
    count = parts_x * parts_y
    shards = lax.axis_size("ch")
    axes = ("gx", "gy")
    factor = 1.0 / math.sqrt(local * count)
    place = jnp.stack([lax.axis_index(axis) for axis in ("gx", "gy", "ch")]).astype(jnp.int32)
    taps = weight.reshape(9, 3 * local_ch, channels)
    packing = (span_x // 2, span_y, span_z, 2 * local_ch)
    flat = (local // 2, 2 * local_ch)

    def call(kernel, name, outs, args, scratch=()):
        return pl.pallas_call(
            kernel,
            out_shape=[jax.ShapeDtypeStruct(shape, kind) for shape, kind in outs],
            in_specs=[SMEM if x is place else VMEM for x in args],
            out_specs=[VMEM] * len(outs),
            scratch_shapes=[pltpu.VMEM(shape, kind) for shape, kind in scratch],
            compiler_params=PARAMS,
            cost_estimate=pl.CostEstimate(flops=0, bytes_accessed=1024, transcendentals=0),
            name=name,
        )(*args)

    row = (span_x, span_z, local_ch)
    held, packed, even, odd, even_corner, odd_corner = pl.pallas_call(
        prepare_kernel,
        out_shape=[jax.ShapeDtypeStruct(inputs.shape, BF16), jax.ShapeDtypeStruct(packing, BF16)]
        + [jax.ShapeDtypeStruct(row, BF16)] * 2
        + [jax.ShapeDtypeStruct(row[1:], BF16)] * 2,
        in_specs=[SMEM, HBM],
        out_specs=[VMEM] * 6,
        scratch_shapes=[pltpu.SemaphoreType.DMA],
        compiler_params=PARAMS,
        name="prepare",
    )(place, pltpu.with_memory_space_constraint(inputs, pltpu.HBM))
    sources = (taps, cotangent.reshape(local, local_ch), bias.reshape(1, local_ch))
    taps, cotangent, bias = pl.pallas_call(
        stage_kernel,
        out_shape=[jax.ShapeDtypeStruct(x.shape, x.dtype) for x in sources],
        in_specs=[VMEM] + [HBM] * len(sources),
        out_specs=[VMEM] * len(sources),
        scratch_shapes=[pltpu.SemaphoreType.DMA((len(sources) + 8,))],
        compiler_params=PARAMS,
        name="stage",
    )(even_corner, *[pltpu.with_memory_space_constraint(x, pltpu.HBM) for x in sources])
    beside = exchange(packed, axes, parts_y)
    even = exchange(even, axes, 1)
    odd = exchange(odd, axes, 3)
    even_corner = exchange(even_corner, axes, parts_y + 1)
    odd_corner = exchange(odd_corner, axes, parts_y + 3)
    own, *others, pair = call(
        functools.partial(forward_kernel, parts_y),
        "forward",
        [(flat, F32)] + [(flat, BF16)] * (shards - 1) + [((2,) + packing, BF16)],
        [place, taps, held, packed, even, odd, beside, even_corner, odd_corner],
        [((span_x + 2, span_y + 2, span_z, 3 * local_ch), BF16), ((shards,) + flat, F32)],
    )
    others = [exchange(others[k - 1], "ch", k) for k in range(shards - 1, 0, -1)]
    activation, slope = call(
        slope_kernel,
        "slope",
        [((local, local_ch), BF16), (flat, BF16)],
        [own, *others, bias, cotangent],
    )
    rest = [exchange(slope, "ch", k) for k in range(1, shards)]
    rest = jnp.stack(rest).reshape((shards - 1,) + packing)
    piece = slope.reshape((1,) + packing)
    x, y = parts_y, 2
    early = {x + y: exchange(piece, axes, x + y), x: exchange(piece, axes, x)}
    beside_y = exchange(jnp.concatenate([piece, pair]), axes, y)
    rest, *arrived = lax.optimization_barrier([rest, early[x + y], early[x], beside_y])
    early[x + y], early[x], beside_y = arrived
    early[y] = beside_y[:1]
    column = jnp.concatenate([piece, rest])
    far = (x + y, x, y)
    late = {m: exchange(rest, axes, m) for m in far}
    sibling = exchange(jnp.concatenate([column, pair, beside_y[1:]]), axes, 1)
    turned_shape = (parts_y, 9 * local_ch, (parts_x * span_x + 2) * span_y * span_z)
    sums_shape = (3, 9 * local_ch, channels)
    turned, sums = call(
        functools.partial(first_kernel, parts_x, parts_y),
        "first",
        [(turned_shape, BF16), (sums_shape, F32)],
        [place, pair, beside_y, sibling, column],
        [((parts_x * span_x + 2, parts_y * span_y + 2, span_z, 3 * local_ch), BF16)],
    )
    slopes = {0: column, 1: sibling[:shards]}
    *arrived, sums = lax.optimization_barrier([late[m] for m in far] + [sums])
    for m, array in zip(far, arrived):
        slopes[m] = jnp.concatenate([early[m], array])
        slopes[m + 1] = exchange(slopes[m], axes, 1)
    (sums,) = call(
        functools.partial(middle_kernel, parts_y, far),
        "middle",
        [(sums_shape, F32)],
        [place, turned, sums] + [slopes[m] for m in far],
    )
    members = (3, 5, 7)
    input_grad, kernel_grad, bias_grad = call(
        functools.partial(last_kernel, parts_y, members, factor),
        "last",
        [((local, local_ch), BF16), (sums_shape, F32), ((1, local_ch), F32)],
        [place, taps, turned, sums] + [slopes[m] for m in range(count)],
        [((span_x + 2, span_y + 2, span_z, channels), BF16)],
    )
    return (
        activation.reshape(inputs.shape),
        input_grad.reshape(inputs.shape),
        kernel_grad.reshape(weight.shape),
        bias_grad.reshape(local_ch),
    )


def solution(mesh):
    few = (mesh.shape["gx"], mesh.shape["gy"]) == (2, 4)
    return jax.shard_map(
        body_gathered if few else body_reduced,
        mesh=mesh,
        in_specs=(
            P("gx", "gy", None, "ch"),
            P(None, None, None, "ch", None),
            P("ch"),
            P("gx", "gy", None, "ch"),
        ),
        out_specs=(
            P("gx", "gy", None, "ch"),
            P("gx", "gy", None, "ch"),
            P(None, None, None, "ch", None),
            P("ch"),
        ),
        check_vma=False,
    )
```

```python
import functools
import math

import jax
import jax.numpy as jnp
from jax import lax
from jax.experimental import pallas as pl
from jax.experimental.pallas import tpu as pltpu
from jax.sharding import PartitionSpec as P

VMEM = pl.BlockSpec(memory_space=pltpu.VMEM)
HBM = pl.BlockSpec(memory_space=pltpu.HBM)
SMEM = pl.BlockSpec(memory_space=pltpu.SMEM)
PARAMS = pltpu.CompilerParams(vmem_limit_bytes=24 * 1024 * 1024)
F32 = jnp.float32
BF16 = jnp.bfloat16


def with_halo(x, sides, width):
    for axis, dim in sides:
        devices, length = (lax.axis_size(axis), x.shape[dim])
        up = [(i, (i + 1) % devices) for i in range(devices - 1)]
        down = [(j, i) for i, j in up]
        last = lax.slice_in_dim(x, length - width, length, axis=dim)
        initial = lax.slice_in_dim(x, 0, width, axis=dim)
        before = lax.ppermute(last, axis, up)
        after = lax.ppermute(initial, axis, down)
        x = jnp.concatenate([before, x, after], axis=dim)
    return x


def body_reduced(inputs, weight, bias, cotangent):
    span_x, span_y, span_z, local_ch = inputs.shape
    widest = weight.shape[4]
    local_cells = span_x * span_y * span_z
    offsets = [(a, b, c) for a in range(3) for b in range(3) for c in range(3)]
    depth_pad = ((0, 0), (0, 0), (1, 1), (0, 0))
    rimmed = with_halo(inputs, (("gx", 0), ("gy", 1)), 1)
    padded = jnp.pad(rimmed, depth_pad)
    blocks = []
    for a, b, c in offsets:
        blocks.append(
            padded[a : a + span_x, b : b + span_y, c : c + span_z].reshape(local_cells, local_ch)
        )
    patches = jnp.concatenate(blocks, axis=1)
    flat_weight = weight.reshape(27 * local_ch, widest)
    summed = lax.psum_scatter(
        lax.dot_general(flat_weight, patches, (((0,), (1,)), ((), ())), preferred_element_type=F32),
        "ch",
        scatter_dimension=0,
        tiled=True,
    ).T
    summed = summed + bias.astype(F32)[None, :]
    activation = jax.nn.silu(summed).astype(BF16).reshape(span_x, span_y, span_z, local_ch)
    sigmoid_pre = jax.nn.sigmoid(summed)
    slope = (
        cotangent.reshape(local_cells, local_ch).astype(F32)
        * sigmoid_pre
        * (1.0 + summed * (1.0 - sigmoid_pre))
    ).astype(BF16)
    local_bias = jnp.sum(slope.astype(F32), axis=0)
    slope_grid = slope.reshape(span_x, span_y, span_z, local_ch)
    weight_turned = jnp.transpose(weight.reshape(27, local_ch, widest), (0, 2, 1))
    slope_rimmed = with_halo(slope_grid, (("gx", 0), ("gy", 1)), 1)
    piece = lax.all_gather(slope_rimmed, "ch", axis=3, tiled=True)
    extended = jnp.pad(piece, depth_pad)
    running = jnp.zeros((local_cells, local_ch), F32)
    for index, (a, b, c) in enumerate(offsets):
        a, b, c = (2 - a, 2 - b, 2 - c)
        cut = extended[a : a + span_x, b : b + span_y, c : c + span_z].reshape(local_cells, widest)
        running = running + jnp.dot(cut, weight_turned[index], preferred_element_type=F32)
    interior = piece[1 : 1 + span_x, 1 : 1 + span_y].reshape(local_cells, widest)
    product = lax.dot_general(
        patches, interior, (((0,), (0,)), ((), ())), preferred_element_type=F32
    )
    total_cells = local_cells * lax.axis_size("gx") * lax.axis_size("gy")
    factor = 1.0 / math.sqrt(total_cells)
    kernel_total, bias_total = lax.psum((product * factor, local_bias * factor), ("gx", "gy"))
    input_grad = running.astype(BF16).reshape(span_x, span_y, span_z, local_ch)
    return (activation, input_grad, kernel_total.reshape(3, 3, 3, local_ch, widest), bias_total)


def shifted(v, by):
    depth = v.shape[1]
    row = lax.broadcasted_iota(jnp.int32, v.shape, 1)
    if by == 1:
        return jnp.where(row == 0, 0.0, pltpu.roll(v, 1, 1))
    return jnp.where(row == depth - 1, 0.0, pltpu.roll(v, depth - 1, 1))


def rim_sides(place, span_x, span_y):
    first = place[1] % 2 == 0
    even_at = jnp.where(first, span_y + 1, 0)
    odd_at = jnp.where(first, 0, span_y + 1)
    even_row = jnp.where(first, span_y - 1, 0)
    odd_row = jnp.where(first, 0, span_y - 1)
    x_at = jnp.where(place[0] == 0, span_x + 1, 0)
    x_row = jnp.where(place[0] == 0, span_x - 1, 0)
    return even_at, odd_at, even_row, odd_row, x_at, x_row


def prepare_kernel(place, source, inputs, packed, even, odd, even_corner, odd_corner, arrived):
    copy = pltpu.make_async_copy(source, inputs, arrived)
    copy.start()
    copy.wait()
    span_x, span_y, _, _ = inputs.shape
    half = span_x // 2
    _, _, even_row, odd_row, _, x_row = rim_sides(place, span_x, span_y)
    even[...] = inputs[:, even_row]
    odd[...] = inputs[:, odd_row]
    even_corner[...] = inputs[x_row, even_row]
    odd_corner[...] = inputs[x_row, odd_row]
    packed[...] = jnp.concatenate([inputs[:half], inputs[half:]], axis=3)


def stage_kernel(after, *rest):
    count = (len(rest) - 1) // 2
    sources, targets, arrived = rest[:count], rest[count : 2 * count], rest[-1]
    copies = []
    for source, target in zip(sources, targets):
        parts = source.shape[0] if len(source.shape) == 3 else 1
        for n in range(parts):
            here = pl.ds(n, 1) if parts > 1 else slice(None)
            copies.append(
                pltpu.make_async_copy(source.at[here], target.at[here], arrived.at[len(copies)])
            )
    for copy in copies:
        copy.start()
    for copy in copies:
        copy.wait()


def forward_kernel(
    parts_y, place, weight, inputs, packed, even, odd, beside, even_corner, odd_corner, own, *rest
):
    *others, pair, window, blocks = rest
    span_x, span_y, span_z, lanes = inputs.shape
    half_x = span_x // 2
    half = half_x * span_y * span_z
    even_at, odd_at, _, _, x_at, _ = rim_sides(place, span_x, span_y)

    def spread(v):
        flat = v.astype(F32).reshape(-1, span_z, lanes)
        joined = jnp.concatenate([shifted(flat, 1), flat, shifted(flat, -1)], axis=2)
        return joined.astype(BF16).reshape(v.shape[:-1] + (3 * lanes,))

    nothing = jnp.zeros((span_y + 2, span_z, 3 * lanes), BF16)
    window[0] = nothing
    window[span_x + 1] = nothing
    window[1 : span_x + 1, 1 : span_y + 1] = spread(inputs[...])
    window[1 : span_x + 1, even_at] = spread(even[...])
    has_odd = (place[1] != 0) & (place[1] != parts_y - 1)
    window[1 : span_x + 1, odd_at] = jnp.where(has_odd, spread(odd[...]), jnp.zeros((), BF16))
    across = jnp.where(place[0] == 0, beside[0][..., :lanes], beside[half_x - 1][..., lanes:])
    window[x_at, 1 : span_y + 1] = spread(across)
    window[x_at, even_at] = spread(even_corner[...])
    window[x_at, odd_at] = jnp.where(has_odd, spread(odd_corner[...]), jnp.zeros((), BF16))
    sums = []
    for h in range(2):
        total = None
        for a in range(3):
            for b in range(3):
                cut = window[a + h * half_x : a + (h + 1) * half_x, b : b + span_y]
                term = jnp.dot(
                    cut.reshape(half, 3 * lanes), weight[a * 3 + b], preferred_element_type=F32
                )
                total = term if total is None else total + term
        sums.append(total)
    for d in range(weight.shape[2] // lanes):
        cut = slice(d * lanes, (d + 1) * lanes)
        blocks[d] = jnp.concatenate([sums[0][:, cut], sums[1][:, cut]], axis=1)
    own[...] = blocks[place[2]]
    for k, other in enumerate(others):
        other[...] = blocks[place[2] ^ (k + 1)].astype(BF16)
    pair[0] = packed[...]
    pair[1] = beside[...]


def slope_kernel(own, *rest):
    *others, bias, cotangent, activation, slope = rest
    half, lanes = cotangent.shape[0] // 2, cotangent.shape[1]
    summed = own[...]
    for other in others:
        summed = summed + other[...].astype(F32)
    offset = bias[...].astype(F32)
    summed = summed + jnp.concatenate([offset, offset], axis=1)
    sigmoid = jax.nn.sigmoid(summed)
    active = (summed * sigmoid).astype(BF16)
    activation[:half] = active[:, :lanes]
    activation[half:] = active[:, lanes:]
    upstream = jnp.concatenate([cotangent[:half], cotangent[half:]], axis=1).astype(F32)
    slope[...] = (upstream * sigmoid * (1.0 + summed * (1.0 - sigmoid))).astype(BF16)


def ordered_halves(place, pieces):
    shards, _, _, _, lanes = pieces.shape
    lanes = lanes // 2
    ordered = [pieces[place[2] ^ j] for j in range(shards)]
    return [
        jnp.concatenate([piece[..., h * lanes : (h + 1) * lanes] for piece in ordered], axis=-1)
        for h in range(2)
    ]


def add_terms(place, parts_y, members, slopes, turned, old, store):
    operands = []
    for m, pieces in zip(members, slopes):
        shards, half_x, span_y, span_z, lanes = pieces.shape
        channels, row = shards * lanes // 2, span_y * span_z
        right = jnp.concatenate(
            [part.reshape(half_x * row, channels) for part in ordered_halves(place, pieces)]
        )
        x0, y0 = (place[0] ^ (m // parts_y)) * 2 * half_x, place[1] ^ (m % parts_y)
        operands.append((x0, y0, row, right))
    for a in range(3):
        total = None if old is None else old[a]
        for x0, y0, row, right in operands:
            left = turned[y0, :, pl.ds(pl.multiple_of((x0 + a) * row, row), right.shape[0])]
            term = jnp.dot(left, right, preferred_element_type=F32)
            total = term if total is None else total + term
        store(a, total)


def first_kernel(
    parts_x, parts_y, place, weight, pair, beside_y, sibling, column, turned, sums, weight_turned, volume
):
    shards, half_x, span_y, span_z, lanes = column.shape
    cells = [(0, pair, 0), (parts_y, pair, 1), (2, beside_y, 1), (parts_y + 2, beside_y, 2)]
    cells += [(m ^ 1, sibling, shards + n) for n, (m, _, _) in enumerate(cells)]
    span_x, lanes = 2 * half_x, lanes // 2
    rows_x, rows_y = parts_x * span_x, parts_y * span_y
    width = 3 * lanes
    zero_x = jnp.zeros((1, rows_y + 2, span_z, width), BF16)
    zero_y = jnp.zeros((rows_x + 2, 1, span_z, width), BF16)
    volume[0:1] = zero_x
    volume[rows_x + 1 : rows_x + 2] = zero_x
    volume[:, 0:1] = zero_y
    volume[:, rows_y + 1 : rows_y + 2] = zero_y
    for m, array, n in cells:
        x0, y0 = (place[0] ^ (m // parts_y)) * span_x, (place[1] ^ (m % parts_y)) * span_y
        v = array[n].astype(F32).reshape(half_x * span_y, span_z, 2 * lanes)
        low, high = shifted(v, 1), shifted(v, -1)
        for h in range(2):
            cut = slice(h * lanes, (h + 1) * lanes)
            joined = jnp.concatenate([low[..., cut], v[..., cut], high[..., cut]], axis=2)
            volume[pl.ds(x0 + 1 + h * half_x, half_x), pl.ds(y0 + 1, span_y)] = joined.astype(
                BF16
            ).reshape(half_x, span_y, span_z, width)
    for y in range(parts_y):
        for b in range(3):
            cut = volume[:, y * span_y + b : (y + 1) * span_y + b]
            turned[y, b * width : (b + 1) * width] = cut.reshape(-1, width).T

    def store(a, total):
        sums[a] = total

    for tap in range(weight.shape[0]):
        weight_turned[tap] = weight[tap].T
    members = (0, 1)
    add_terms(place, parts_y, members, (column, sibling.at[:shards]), turned, None, store)


def middle_kernel(parts_y, members, place, turned, old, *rest):
    *slopes, sums = rest

    def store(a, total):
        sums[a] = total

    add_terms(place, parts_y, members, slopes, turned, old, store)


def last_kernel(parts_y, members, factor, place, weight, turned, old, *rest):
    *slopes, input_grad, kernel_grad, bias_grad, window, sums, sent = rest
    shards, half_x, span_y, span_z, lanes = slopes[0].shape
    span_x, lanes = 2 * half_x, lanes // 2
    channels = shards * lanes
    half = half_x * span_y * span_z

    copies = [pltpu.make_async_copy(sums.at[a], kernel_grad.at[a], sent.at[a]) for a in range(3)]

    def store(a, total):
        sums[a] = total * factor
        copies[a].start()

    add_terms(place, parts_y, members, [slopes[m] for m in members], turned, old, store)

    column = jnp.zeros((1, 2 * lanes), F32)
    for pieces in slopes:
        mine = pieces[0].astype(F32).reshape(half, 2 * lanes)
        column = column + jnp.sum(mine, axis=0, keepdims=True)
    bias_grad[...] = (column[:, :lanes] + column[:, lanes:]) * factor

    even_at, odd_at, even_row, odd_row, x_at, x_row = rim_sides(place, span_x, span_y)
    has_odd = (place[1] != 0) & (place[1] != parts_y - 1)
    window[...] = jnp.zeros(window.shape, BF16)
    low, high = ordered_halves(place, slopes[0])
    window[1 : half_x + 1, 1 : span_y + 1] = low
    window[half_x + 1 : span_x + 1, 1 : span_y + 1] = high

    def rows_of(m, row):
        ordered = [slopes[m][place[2] ^ j, :, row] for j in range(shards)]
        return [
            jnp.concatenate([piece[..., h * lanes : (h + 1) * lanes] for piece in ordered], axis=-1)
            for h in range(2)
        ]

    def facing(halves):
        low, high = halves
        return jnp.where(place[0] == 0, low[0], high[half_x - 1])

    for h, rows in enumerate(rows_of(1, facing_row(even_row, span_y))):
        window[1 + h * half_x : 1 + (h + 1) * half_x, even_at] = rows
    window[x_at, 1 : span_y + 1] = facing(ordered_halves(place, slopes[parts_y]))
    window[x_at, even_at] = facing(rows_of(parts_y + 1, facing_row(even_row, span_y)))

    @pl.when(has_odd)
    def _():
        for h, rows in enumerate(rows_of(3, facing_row(odd_row, span_y))):
            window[1 + h * half_x : 1 + (h + 1) * half_x, odd_at] = rows
        window[x_at, odd_at] = facing(rows_of(parts_y + 3, facing_row(odd_row, span_y)))

    for h in range(2):
        total = None
        for a in range(3):
            for b in range(3):
                cut = window[
                    2 - a + h * half_x : 2 - a + (h + 1) * half_x, 2 - b : 2 - b + span_y
                ]
                term = jnp.dot(
                    cut.reshape(half, channels), weight[a * 3 + b], preferred_element_type=F32
                )
                total = term if total is None else total + term
        total = total.reshape(half // span_z, span_z, 3 * lanes)
        result = (
            shifted(total[..., :lanes], -1)
            + total[..., lanes : 2 * lanes]
            + shifted(total[..., 2 * lanes :], 1)
        )
        input_grad[h * half : (h + 1) * half] = result.reshape(half, lanes).astype(BF16)
    for copy in copies:
        copy.wait()


def facing_row(row, span_y):
    return span_y - 1 - row


def exchange(x, axes, mask):
    return lax.ppermute(x, axes, [(i, i ^ mask) for i in range(lax.axis_size(axes))])


def body_gathered(inputs, weight, bias, cotangent):
    spans = inputs.shape[:3]
    span_x, span_y, span_z = spans
    local_ch, channels = weight.shape[3:]
    local = span_x * span_y * span_z
    parts_x, parts_y = lax.axis_size("gx"), lax.axis_size("gy")
    count = parts_x * parts_y
    shards = lax.axis_size("ch")
    axes = ("gx", "gy")
    factor = 1.0 / math.sqrt(local * count)
    place = jnp.stack([lax.axis_index(axis) for axis in ("gx", "gy", "ch")]).astype(jnp.int32)
    taps = weight.reshape(9, 3 * local_ch, channels)
    packing = (span_x // 2, span_y, span_z, 2 * local_ch)
    flat = (local // 2, 2 * local_ch)

    def call(kernel, name, outs, args, scratch=()):
        return pl.pallas_call(
            kernel,
            out_shape=[jax.ShapeDtypeStruct(shape, kind) for shape, kind in outs],
            in_specs=[SMEM if x is place else VMEM for x in args],
            out_specs=[VMEM] * len(outs),
            scratch_shapes=[pltpu.VMEM(shape, kind) for shape, kind in scratch],
            compiler_params=PARAMS,
            cost_estimate=pl.CostEstimate(flops=0, bytes_accessed=1024, transcendentals=0),
            name=name,
        )(*args)

    row = (span_x, span_z, local_ch)
    held, packed, even, odd, even_corner, odd_corner = pl.pallas_call(
        prepare_kernel,
        out_shape=[jax.ShapeDtypeStruct(inputs.shape, BF16), jax.ShapeDtypeStruct(packing, BF16)]
        + [jax.ShapeDtypeStruct(row, BF16)] * 2
        + [jax.ShapeDtypeStruct(row[1:], BF16)] * 2,
        in_specs=[SMEM, HBM],
        out_specs=[VMEM] * 6,
        scratch_shapes=[pltpu.SemaphoreType.DMA],
        compiler_params=PARAMS,
        name="prepare",
    )(place, pltpu.with_memory_space_constraint(inputs, pltpu.HBM))
    sources = (taps, cotangent.reshape(local, local_ch), bias.reshape(1, local_ch))
    taps, cotangent, bias = pl.pallas_call(
        stage_kernel,
        out_shape=[jax.ShapeDtypeStruct(x.shape, x.dtype) for x in sources],
        in_specs=[VMEM] + [HBM] * len(sources),
        out_specs=[VMEM] * len(sources),
        scratch_shapes=[pltpu.SemaphoreType.DMA((len(sources) + 8,))],
        compiler_params=PARAMS,
        name="stage",
    )(even_corner, *[pltpu.with_memory_space_constraint(x, pltpu.HBM) for x in sources])
    beside = exchange(packed, axes, parts_y)
    even = exchange(even, axes, 1)
    odd = exchange(odd, axes, 3)
    even_corner = exchange(even_corner, axes, parts_y + 1)
    odd_corner = exchange(odd_corner, axes, parts_y + 3)
    own, *others, pair = call(
        functools.partial(forward_kernel, parts_y),
        "forward",
        [(flat, F32)] + [(flat, BF16)] * (shards - 1) + [((2,) + packing, BF16)],
        [place, taps, held, packed, even, odd, beside, even_corner, odd_corner],
        [((span_x + 2, span_y + 2, span_z, 3 * local_ch), BF16), ((shards,) + flat, F32)],
    )
    others = [exchange(others[k - 1], "ch", k) for k in range(shards - 1, 0, -1)]
    activation, slope = call(
        slope_kernel,
        "slope",
        [((local, local_ch), BF16), (flat, BF16)],
        [own, *others, bias, cotangent],
    )
    rest = [exchange(slope, "ch", k) for k in range(1, shards)]
    rest = jnp.stack(rest).reshape((shards - 1,) + packing)
    piece = slope.reshape((1,) + packing)
    x, y = parts_y, 2
    beside_x = exchange(piece, axes, x)
    beside_y = exchange(jnp.concatenate([piece, pair]), axes, y)
    beside_y, beside_x, rest = lax.optimization_barrier((beside_y, beside_x, rest))
    column = jnp.concatenate([piece, rest])
    late_y, late_x = exchange(rest, axes, y), exchange(rest, axes, x)
    diagonal = exchange(column, axes, x + y)
    sibling = exchange(jnp.concatenate([column, pair, beside_y[1:]]), axes, 1)
    turned_shape = (parts_y, 9 * local_ch, (parts_x * span_x + 2) * span_y * span_z)
    sums_shape = (3, 9 * local_ch, channels)
    turned, sums, taps = call(
        functools.partial(first_kernel, parts_x, parts_y),
        "first",
        [(turned_shape, BF16), (sums_shape, F32), ((9, channels, 3 * local_ch), BF16)],
        [place, taps, pair, beside_y, sibling, column],
        [((parts_x * span_x + 2, parts_y * span_y + 2, span_z, 3 * local_ch), BF16)],
    )
    slopes = {0: column, 1: sibling[:shards]}
    late_y, late_x, diagonal, sums = lax.optimization_barrier((late_y, late_x, diagonal, sums))
    slopes[y] = jnp.concatenate([beside_y[:1], late_y])
    slopes[x] = jnp.concatenate([beside_x, late_x])
    slopes[x + y] = diagonal
    far = (y, x, x + y)
    for m in far:
        slopes[m + 1] = exchange(slopes[m], axes, 1)
    (sums,) = call(
        functools.partial(middle_kernel, parts_y, far),
        "middle",
        [(sums_shape, F32)],
        [place, turned, sums] + [slopes[m] for m in far],
    )
    members = (3, 5, 7)
    args = [place, taps, turned, sums] + [slopes[m] for m in range(count)]
    input_grad, kernel_grad, bias_grad = pl.pallas_call(
        functools.partial(last_kernel, parts_y, members, factor),
        out_shape=[
            jax.ShapeDtypeStruct((local, local_ch), BF16),
            jax.ShapeDtypeStruct(sums_shape, F32),
            jax.ShapeDtypeStruct((1, local_ch), F32),
        ],
        in_specs=[SMEM] + [VMEM] * (len(args) - 1),
        out_specs=[VMEM, HBM, VMEM],
        scratch_shapes=[
            pltpu.VMEM((span_x + 2, span_y + 2, span_z, channels), BF16),
            pltpu.VMEM(sums_shape, F32),
            pltpu.SemaphoreType.DMA((3,)),
        ],
        compiler_params=PARAMS,
        name="last",
    )(*args)
    return (
        activation.reshape(inputs.shape),
        input_grad.reshape(inputs.shape),
        kernel_grad.reshape(weight.shape),
        bias_grad.reshape(local_ch),
    )


def solution(mesh):
    few = (mesh.shape["gx"], mesh.shape["gy"]) == (2, 4)
    return jax.shard_map(
        body_gathered if few else body_reduced,
        mesh=mesh,
        in_specs=(
            P("gx", "gy", None, "ch"),
            P(None, None, None, "ch", None),
            P("ch"),
            P("gx", "gy", None, "ch"),
        ),
        out_specs=(
            P("gx", "gy", None, "ch"),
            P("gx", "gy", None, "ch"),
            P(None, None, None, "ch", None),
            P("ch"),
        ),
        check_vma=False,
    )
```

```python
import functools
import math

import jax
import jax.numpy as jnp
from jax import lax
from jax.experimental import pallas as pl
from jax.experimental.pallas import tpu as pltpu
from jax.sharding import PartitionSpec as P

VMEM = pl.BlockSpec(memory_space=pltpu.VMEM)
HBM = pl.BlockSpec(memory_space=pltpu.HBM)
SMEM = pl.BlockSpec(memory_space=pltpu.SMEM)
PARAMS = pltpu.CompilerParams(vmem_limit_bytes=24 * 1024 * 1024)
F32 = jnp.float32
BF16 = jnp.bfloat16


def with_halo(x, sides, width):
    for axis, dim in sides:
        devices, length = (lax.axis_size(axis), x.shape[dim])
        up = [(i, (i + 1) % devices) for i in range(devices - 1)]
        down = [(j, i) for i, j in up]
        last = lax.slice_in_dim(x, length - width, length, axis=dim)
        initial = lax.slice_in_dim(x, 0, width, axis=dim)
        before = lax.ppermute(last, axis, up)
        after = lax.ppermute(initial, axis, down)
        x = jnp.concatenate([before, x, after], axis=dim)
    return x


def body_reduced(inputs, weight, bias, cotangent):
    span_x, span_y, span_z, local_ch = inputs.shape
    widest = weight.shape[4]
    local_cells = span_x * span_y * span_z
    offsets = [(a, b, c) for a in range(3) for b in range(3) for c in range(3)]
    depth_pad = ((0, 0), (0, 0), (1, 1), (0, 0))
    rimmed = with_halo(inputs, (("gx", 0), ("gy", 1)), 1)
    padded = jnp.pad(rimmed, depth_pad)
    blocks = []
    for a, b, c in offsets:
        blocks.append(
            padded[a : a + span_x, b : b + span_y, c : c + span_z].reshape(local_cells, local_ch)
        )
    patches = jnp.concatenate(blocks, axis=1)
    flat_weight = weight.reshape(27 * local_ch, widest)
    summed = lax.psum_scatter(
        lax.dot_general(flat_weight, patches, (((0,), (1,)), ((), ())), preferred_element_type=F32),
        "ch",
        scatter_dimension=0,
        tiled=True,
    ).T
    summed = summed + bias.astype(F32)[None, :]
    activation = jax.nn.silu(summed).astype(BF16).reshape(span_x, span_y, span_z, local_ch)
    sigmoid_pre = jax.nn.sigmoid(summed)
    slope = (
        cotangent.reshape(local_cells, local_ch).astype(F32)
        * sigmoid_pre
        * (1.0 + summed * (1.0 - sigmoid_pre))
    ).astype(BF16)
    local_bias = jnp.sum(slope.astype(F32), axis=0)
    slope_grid = slope.reshape(span_x, span_y, span_z, local_ch)
    weight_turned = jnp.transpose(weight.reshape(27, local_ch, widest), (0, 2, 1))
    slope_rimmed = with_halo(slope_grid, (("gx", 0), ("gy", 1)), 1)
    piece = lax.all_gather(slope_rimmed, "ch", axis=3, tiled=True)
    extended = jnp.pad(piece, depth_pad)
    running = jnp.zeros((local_cells, local_ch), F32)
    for index, (a, b, c) in enumerate(offsets):
        a, b, c = (2 - a, 2 - b, 2 - c)
        cut = extended[a : a + span_x, b : b + span_y, c : c + span_z].reshape(local_cells, widest)
        running = running + jnp.dot(cut, weight_turned[index], preferred_element_type=F32)
    interior = piece[1 : 1 + span_x, 1 : 1 + span_y].reshape(local_cells, widest)
    product = lax.dot_general(
        patches, interior, (((0,), (0,)), ((), ())), preferred_element_type=F32
    )
    total_cells = local_cells * lax.axis_size("gx") * lax.axis_size("gy")
    factor = 1.0 / math.sqrt(total_cells)
    kernel_total, bias_total = lax.psum((product * factor, local_bias * factor), ("gx", "gy"))
    input_grad = running.astype(BF16).reshape(span_x, span_y, span_z, local_ch)
    return (activation, input_grad, kernel_total.reshape(3, 3, 3, local_ch, widest), bias_total)


def shifted(v, by):
    depth = v.shape[1]
    row = lax.broadcasted_iota(jnp.int32, v.shape, 1)
    if by == 1:
        return jnp.where(row == 0, 0.0, pltpu.roll(v, 1, 1))
    return jnp.where(row == depth - 1, 0.0, pltpu.roll(v, depth - 1, 1))


def rim_sides(place, span_x, span_y):
    first = place[1] % 2 == 0
    even_at = jnp.where(first, span_y + 1, 0)
    odd_at = jnp.where(first, 0, span_y + 1)
    even_row = jnp.where(first, span_y - 1, 0)
    odd_row = jnp.where(first, 0, span_y - 1)
    x_at = jnp.where(place[0] == 0, span_x + 1, 0)
    x_row = jnp.where(place[0] == 0, span_x - 1, 0)
    return even_at, odd_at, even_row, odd_row, x_at, x_row


def prepare_kernel(place, source, inputs, packed, even, odd, even_corner, odd_corner, arrived):
    copy = pltpu.make_async_copy(source, inputs, arrived)
    copy.start()
    copy.wait()
    span_x, span_y, _, _ = inputs.shape
    half = span_x // 2
    _, _, even_row, odd_row, _, x_row = rim_sides(place, span_x, span_y)
    even[...] = inputs[:, even_row]
    odd[...] = inputs[:, odd_row]
    even_corner[...] = inputs[x_row, even_row]
    odd_corner[...] = inputs[x_row, odd_row]
    packed[...] = jnp.concatenate([inputs[:half], inputs[half:]], axis=3)


def stage_kernel(after, *rest):
    count = (len(rest) - 1) // 2
    sources, targets, arrived = rest[:count], rest[count : 2 * count], rest[-1]
    copies = []
    for source, target in zip(sources, targets):
        parts = source.shape[0] if len(source.shape) == 3 else 1
        for n in range(parts):
            here = pl.ds(n, 1) if parts > 1 else slice(None)
            copies.append(
                pltpu.make_async_copy(source.at[here], target.at[here], arrived.at[len(copies)])
            )
    for copy in copies:
        copy.start()
    for copy in copies:
        copy.wait()


def forward_kernel(
    parts_y, place, weight, inputs, packed, even, odd, beside, even_corner, odd_corner, own, *rest
):
    *others, pair, window, blocks = rest
    span_x, span_y, span_z, lanes = inputs.shape
    half_x = span_x // 2
    half = half_x * span_y * span_z
    even_at, odd_at, _, _, x_at, _ = rim_sides(place, span_x, span_y)

    def spread(v):
        flat = v.astype(F32).reshape(-1, span_z, lanes)
        joined = jnp.concatenate([shifted(flat, 1), flat, shifted(flat, -1)], axis=2)
        return joined.astype(BF16).reshape(v.shape[:-1] + (3 * lanes,))

    nothing = jnp.zeros((span_y + 2, span_z, 3 * lanes), BF16)
    window[0] = nothing
    window[span_x + 1] = nothing
    window[1 : span_x + 1, 1 : span_y + 1] = spread(inputs[...])
    window[1 : span_x + 1, even_at] = spread(even[...])
    has_odd = (place[1] != 0) & (place[1] != parts_y - 1)
    window[1 : span_x + 1, odd_at] = jnp.where(has_odd, spread(odd[...]), jnp.zeros((), BF16))
    across = jnp.where(place[0] == 0, beside[0][..., :lanes], beside[half_x - 1][..., lanes:])
    window[x_at, 1 : span_y + 1] = spread(across)
    window[x_at, even_at] = spread(even_corner[...])
    window[x_at, odd_at] = jnp.where(has_odd, spread(odd_corner[...]), jnp.zeros((), BF16))
    sums = []
    for h in range(2):
        total = None
        for a in range(3):
            for b in range(3):
                cut = window[a + h * half_x : a + (h + 1) * half_x, b : b + span_y]
                term = jnp.dot(
                    cut.reshape(half, 3 * lanes), weight[a * 3 + b], preferred_element_type=F32
                )
                total = term if total is None else total + term
        sums.append(total)
    for d in range(weight.shape[2] // lanes):
        cut = slice(d * lanes, (d + 1) * lanes)
        blocks[d] = jnp.concatenate([sums[0][:, cut], sums[1][:, cut]], axis=1)
    own[...] = blocks[place[2]]
    for k, other in enumerate(others):
        other[...] = blocks[place[2] ^ (k + 1)].astype(BF16)
    pair[0] = packed[...]
    pair[1] = beside[...]


def slope_kernel(own, *rest):
    *others, bias, cotangent, activation, slope = rest
    half, lanes = cotangent.shape[0] // 2, cotangent.shape[1]
    summed = own[...]
    for other in others:
        summed = summed + other[...].astype(F32)
    offset = bias[...].astype(F32)
    summed = summed + jnp.concatenate([offset, offset], axis=1)
    sigmoid = jax.nn.sigmoid(summed)
    active = (summed * sigmoid).astype(BF16)
    activation[:half] = active[:, :lanes]
    activation[half:] = active[:, lanes:]
    upstream = jnp.concatenate([cotangent[:half], cotangent[half:]], axis=1).astype(F32)
    slope[...] = (upstream * sigmoid * (1.0 + summed * (1.0 - sigmoid))).astype(BF16)


def ordered_halves(place, pieces):
    shards, _, _, _, lanes = pieces.shape
    lanes = lanes // 2
    ordered = [pieces[place[2] ^ j] for j in range(shards)]
    return [
        jnp.concatenate([piece[..., h * lanes : (h + 1) * lanes] for piece in ordered], axis=-1)
        for h in range(2)
    ]


def add_terms(place, parts_y, members, slopes, turned, old, store):
    operands = []
    for m, pieces in zip(members, slopes):
        shards, half_x, span_y, span_z, lanes = pieces.shape
        channels, row = shards * lanes // 2, span_y * span_z
        right = jnp.concatenate(
            [part.reshape(half_x * row, channels) for part in ordered_halves(place, pieces)]
        )
        x0, y0 = (place[0] ^ (m // parts_y)) * 2 * half_x, place[1] ^ (m % parts_y)
        operands.append((x0, y0, row, right))
    for a in range(3):
        total = None if old is None else old[a]
        for x0, y0, row, right in operands:
            left = turned[y0, :, pl.ds(pl.multiple_of((x0 + a) * row, row), right.shape[0])]
            term = jnp.dot(left, right, preferred_element_type=F32)
            total = term if total is None else total + term
        store(a, total)


def first_kernel(
    parts_x, parts_y, place, weight, pair, beside_y, sibling, column, turned, sums, weight_turned, volume
):
    shards, half_x, span_y, span_z, lanes = column.shape
    cells = [(0, pair, 0), (parts_y, pair, 1), (2, beside_y, 1), (parts_y + 2, beside_y, 2)]
    cells += [(m ^ 1, sibling, shards + n) for n, (m, _, _) in enumerate(cells)]
    span_x, lanes = 2 * half_x, lanes // 2
    rows_x, rows_y = parts_x * span_x, parts_y * span_y
    width = 3 * lanes
    zero_x = jnp.zeros((1, rows_y + 2, span_z, width), BF16)
    zero_y = jnp.zeros((rows_x + 2, 1, span_z, width), BF16)
    volume[0:1] = zero_x
    volume[rows_x + 1 : rows_x + 2] = zero_x
    volume[:, 0:1] = zero_y
    volume[:, rows_y + 1 : rows_y + 2] = zero_y
    for m, array, n in cells:
        x0, y0 = (place[0] ^ (m // parts_y)) * span_x, (place[1] ^ (m % parts_y)) * span_y
        v = array[n].astype(F32).reshape(half_x * span_y, span_z, 2 * lanes)
        low, high = shifted(v, 1), shifted(v, -1)
        for h in range(2):
            cut = slice(h * lanes, (h + 1) * lanes)
            joined = jnp.concatenate([low[..., cut], v[..., cut], high[..., cut]], axis=2)
            volume[pl.ds(x0 + 1 + h * half_x, half_x), pl.ds(y0 + 1, span_y)] = joined.astype(
                BF16
            ).reshape(half_x, span_y, span_z, width)
    for y in range(parts_y):
        for b in range(3):
            cut = volume[:, y * span_y + b : (y + 1) * span_y + b]
            turned[y, b * width : (b + 1) * width] = cut.reshape(-1, width).T

    def store(a, total):
        sums[a] = total

    for tap in range(weight.shape[0]):
        weight_turned[tap] = weight[tap].T
    members = (0, 1)
    add_terms(place, parts_y, members, (column, sibling.at[:shards]), turned, None, store)


def rows_of(place, pieces, row):
    shards, lanes = column_shape(pieces)
    ordered = [pieces[place[2] ^ j, :, row] for j in range(shards)]
    return [
        jnp.concatenate([piece[..., h * lanes : (h + 1) * lanes] for piece in ordered], axis=-1)
        for h in range(2)
    ]


def column_shape(pieces):
    return pieces.shape[0], pieces.shape[-1] // 2


def second_kernel(
    parts_y, members, place, weight, turned, old, column, sibling, *rest
):
    *slopes, partial, sums, window = rest
    shards, half_x, span_y, span_z, _ = column.shape
    span_x, half = 2 * half_x, half_x * span_y * span_z
    even_at, _, even_row, _, _, _ = rim_sides(place, span_x, span_y)
    window[...] = jnp.zeros(window.shape, BF16)
    beside = rows_of(place, sibling.at[:shards], facing_row(even_row, span_y))
    for h, own in enumerate(ordered_halves(place, column)):
        window[1 + h * half_x : 1 + (h + 1) * half_x, 1 : span_y + 1] = own
        window[1 + h * half_x : 1 + (h + 1) * half_x, even_at] = beside[h]
    for h in range(2):
        total = None
        for a in range(3):
            for b in range(3):
                cut = window[
                    2 - a + h * half_x : 2 - a + (h + 1) * half_x, 2 - b : 2 - b + span_y
                ]
                term = jnp.dot(
                    cut.reshape(half, cut.shape[-1]), weight[a * 3 + b], preferred_element_type=F32
                )
                total = term if total is None else total + term
        partial[h * half_x : (h + 1) * half_x] = total.reshape((half_x,) + partial.shape[1:])
    middle_kernel(parts_y, members, place, turned, old, *slopes, sums)


def middle_kernel(parts_y, members, place, turned, old, *rest):
    *slopes, sums = rest

    def store(a, total):
        sums[a] = total

    add_terms(place, parts_y, members, slopes, turned, old, store)


def last_kernel(parts_y, members, factor, place, weight, turned, old, partial, *rest):
    *slopes, input_grad, kernel_grad, bias_grad, rim_x, rim_y, grid, sums, sent = rest
    _, half_x, span_y, span_z, _ = slopes[0].shape
    shards, lanes = column_shape(slopes[0])
    span_x, channels = 2 * half_x, shards * lanes
    copies = [pltpu.make_async_copy(sums.at[a], kernel_grad.at[a], sent.at[a]) for a in range(3)]

    def store(a, total):
        sums[a] = total * factor
        copies[a].start()

    add_terms(place, parts_y, members, [slopes[m] for m in members], turned, old, store)

    column = jnp.zeros((1, 2 * lanes), F32)
    for pieces in slopes:
        mine = pieces[0].astype(F32).reshape(-1, 2 * lanes)
        column = column + jnp.sum(mine, axis=0, keepdims=True)
    bias_grad[...] = (column[:, :lanes] + column[:, lanes:]) * factor

    even_at, odd_at, even_row, odd_row, _, x_row = rim_sides(place, span_x, span_y)
    has_odd = (place[1] != 0) & (place[1] != parts_y - 1)
    rim_x[...] = jnp.zeros(rim_x.shape, BF16)
    rim_y[...] = jnp.zeros(rim_y.shape, BF16)

    def facing(halves):
        low, high = halves
        return jnp.where(place[0] == 0, low[0], high[half_x - 1])

    rim_x[1 : span_y + 1] = facing(ordered_halves(place, slopes[parts_y]))
    rim_x[even_at] = facing(rows_of(place, slopes[parts_y + 1], facing_row(even_row, span_y)))

    @pl.when(has_odd)
    def _():
        row = facing_row(odd_row, span_y)
        rim_x[odd_at] = facing(rows_of(place, slopes[parts_y + 3], row))
        for h, rows in enumerate(rows_of(place, slopes[3], row)):
            rim_y[1 + h * half_x : 1 + (h + 1) * half_x] = rows

    grid[...] = partial[...]
    tap_x = jnp.where(place[0] == 0, 0, 2)
    total = None
    for b in range(3):
        cut = rim_x[2 - b : 2 - b + span_y].reshape(span_y * span_z, channels)
        term = jnp.dot(cut, weight[tap_x * 3 + b], preferred_element_type=F32)
        total = term if total is None else total + term
    grid[x_row] += total.reshape(span_y, span_z, 3 * lanes)
    tap_y = jnp.where(odd_row == 0, 2, 0)
    total = None
    for a in range(3):
        cut = rim_y[2 - a : 2 - a + span_x].reshape(span_x * span_z, channels)
        term = jnp.dot(cut, weight[a * 3 + tap_y], preferred_element_type=F32)
        total = term if total is None else total + term
    grid[:, odd_row] += total.reshape(span_x, span_z, 3 * lanes)
    summed = grid[...].reshape(span_x * span_y, span_z, 3 * lanes)
    result = (
        shifted(summed[..., :lanes], -1)
        + summed[..., lanes : 2 * lanes]
        + shifted(summed[..., 2 * lanes :], 1)
    )
    input_grad[...] = result.reshape(-1, lanes).astype(BF16)
    for copy in copies:
        copy.wait()


def facing_row(row, span_y):
    return span_y - 1 - row


def exchange(x, axes, mask):
    return lax.ppermute(x, axes, [(i, i ^ mask) for i in range(lax.axis_size(axes))])


def body_gathered(inputs, weight, bias, cotangent):
    spans = inputs.shape[:3]
    span_x, span_y, span_z = spans
    local_ch, channels = weight.shape[3:]
    local = span_x * span_y * span_z
    parts_x, parts_y = lax.axis_size("gx"), lax.axis_size("gy")
    count = parts_x * parts_y
    shards = lax.axis_size("ch")
    axes = ("gx", "gy")
    factor = 1.0 / math.sqrt(local * count)
    place = jnp.stack([lax.axis_index(axis) for axis in ("gx", "gy", "ch")]).astype(jnp.int32)
    taps = weight.reshape(9, 3 * local_ch, channels)
    packing = (span_x // 2, span_y, span_z, 2 * local_ch)
    flat = (local // 2, 2 * local_ch)

    def call(kernel, name, outs, args, scratch=()):
        return pl.pallas_call(
            kernel,
            out_shape=[jax.ShapeDtypeStruct(shape, kind) for shape, kind in outs],
            in_specs=[SMEM if x is place else VMEM for x in args],
            out_specs=[VMEM] * len(outs),
            scratch_shapes=[pltpu.VMEM(shape, kind) for shape, kind in scratch],
            compiler_params=PARAMS,
            cost_estimate=pl.CostEstimate(flops=0, bytes_accessed=1024, transcendentals=0),
            name=name,
        )(*args)

    row = (span_x, span_z, local_ch)
    held, packed, even, odd, even_corner, odd_corner = pl.pallas_call(
        prepare_kernel,
        out_shape=[jax.ShapeDtypeStruct(inputs.shape, BF16), jax.ShapeDtypeStruct(packing, BF16)]
        + [jax.ShapeDtypeStruct(row, BF16)] * 2
        + [jax.ShapeDtypeStruct(row[1:], BF16)] * 2,
        in_specs=[SMEM, HBM],
        out_specs=[VMEM] * 6,
        scratch_shapes=[pltpu.SemaphoreType.DMA],
        compiler_params=PARAMS,
        name="prepare",
    )(place, pltpu.with_memory_space_constraint(inputs, pltpu.HBM))
    sources = (taps, cotangent.reshape(local, local_ch), bias.reshape(1, local_ch))
    taps, cotangent, bias = pl.pallas_call(
        stage_kernel,
        out_shape=[jax.ShapeDtypeStruct(x.shape, x.dtype) for x in sources],
        in_specs=[VMEM] + [HBM] * len(sources),
        out_specs=[VMEM] * len(sources),
        scratch_shapes=[pltpu.SemaphoreType.DMA((len(sources) + 8,))],
        compiler_params=PARAMS,
        name="stage",
    )(even_corner, *[pltpu.with_memory_space_constraint(x, pltpu.HBM) for x in sources])
    beside = exchange(packed, axes, parts_y)
    even = exchange(even, axes, 1)
    odd = exchange(odd, axes, 3)
    even_corner = exchange(even_corner, axes, parts_y + 1)
    odd_corner = exchange(odd_corner, axes, parts_y + 3)
    own, *others, pair = call(
        functools.partial(forward_kernel, parts_y),
        "forward",
        [(flat, F32)] + [(flat, BF16)] * (shards - 1) + [((2,) + packing, BF16)],
        [place, taps, held, packed, even, odd, beside, even_corner, odd_corner],
        [((span_x + 2, span_y + 2, span_z, 3 * local_ch), BF16), ((shards,) + flat, F32)],
    )
    others = [exchange(others[k - 1], "ch", k) for k in range(shards - 1, 0, -1)]
    activation, slope = call(
        slope_kernel,
        "slope",
        [((local, local_ch), BF16), (flat, BF16)],
        [own, *others, bias, cotangent],
    )
    rest = [exchange(slope, "ch", k) for k in range(1, shards)]
    rest = jnp.stack(rest).reshape((shards - 1,) + packing)
    piece = slope.reshape((1,) + packing)
    x, y = parts_y, 2
    beside_x = exchange(piece, axes, x)
    beside_y = exchange(jnp.concatenate([piece, pair]), axes, y)
    beside_y, beside_x, rest = lax.optimization_barrier((beside_y, beside_x, rest))
    column = jnp.concatenate([piece, rest])
    late_y, late_x = exchange(rest, axes, y), exchange(rest, axes, x)
    sibling = exchange(jnp.concatenate([column, pair, beside_y[1:]]), axes, 1)
    turned_shape = (parts_y, 9 * local_ch, (parts_x * span_x + 2) * span_y * span_z)
    sums_shape = (3, 9 * local_ch, channels)
    turned, sums, taps = call(
        functools.partial(first_kernel, parts_x, parts_y),
        "first",
        [(turned_shape, BF16), (sums_shape, F32), ((9, channels, 3 * local_ch), BF16)],
        [place, taps, pair, beside_y, sibling, column],
        [((parts_x * span_x + 2, parts_y * span_y + 2, span_z, 3 * local_ch), BF16)],
    )
    slopes = {0: column, 1: sibling[:shards]}
    late_y, late_x, sums = lax.optimization_barrier((late_y, late_x, sums))
    slopes[y] = jnp.concatenate([beside_y[:1], late_y])
    slopes[x] = jnp.concatenate([beside_x, late_x])
    middle = shards // 2
    diagonal = [exchange(slopes[x][:middle], axes, y), exchange(slopes[y][middle:], axes, x)]
    across = [exchange(slopes[m], axes, 1) for m in (y, x)]
    grid_shape = spans + (3 * local_ch,)
    partial, sums = call(
        functools.partial(second_kernel, parts_y, (y, x)),
        "second",
        [(grid_shape, F32), (sums_shape, F32)],
        [place, taps, turned, sums, column, sibling, slopes[y], slopes[x]],
        [((span_x + 2, span_y + 2, span_z, channels), BF16)],
    )
    diagonal[0], diagonal[1], slopes[y + 1], slopes[x + 1], sums = lax.optimization_barrier(
        (*diagonal, *across, sums)
    )
    slopes[x + y] = jnp.concatenate(diagonal)
    slopes[x + y + 1] = exchange(slopes[x + y], axes, 1)
    members = (y + 1, x + 1, x + y)
    (sums,) = call(
        functools.partial(middle_kernel, parts_y, members),
        "middle",
        [(sums_shape, F32)],
        [place, turned, sums] + [slopes[m] for m in members],
    )
    members = (x + y + 1,)
    args = [place, taps, turned, sums, partial] + [slopes[m] for m in range(count)]
    input_grad, kernel_grad, bias_grad = pl.pallas_call(
        functools.partial(last_kernel, parts_y, members, factor),
        out_shape=[
            jax.ShapeDtypeStruct((local, local_ch), BF16),
            jax.ShapeDtypeStruct(sums_shape, F32),
            jax.ShapeDtypeStruct((1, local_ch), F32),
        ],
        in_specs=[SMEM] + [VMEM] * (len(args) - 1),
        out_specs=[VMEM, HBM, VMEM],
        scratch_shapes=[
            pltpu.VMEM((span_y + 2, span_z, channels), BF16),
            pltpu.VMEM((span_x + 2, span_z, channels), BF16),
            pltpu.VMEM(grid_shape, F32),
            pltpu.VMEM(sums_shape, F32),
            pltpu.SemaphoreType.DMA((3,)),
        ],
        compiler_params=PARAMS,
        name="last",
    )(*args)
    return (
        activation.reshape(inputs.shape),
        input_grad.reshape(inputs.shape),
        kernel_grad.reshape(weight.shape),
        bias_grad.reshape(local_ch),
    )


def solution(mesh):
    few = (mesh.shape["gx"], mesh.shape["gy"]) == (2, 4)
    return jax.shard_map(
        body_gathered if few else body_reduced,
        mesh=mesh,
        in_specs=(
            P("gx", "gy", None, "ch"),
            P(None, None, None, "ch", None),
            P("ch"),
            P("gx", "gy", None, "ch"),
        ),
        out_specs=(
            P("gx", "gy", None, "ch"),
            P("gx", "gy", None, "ch"),
            P(None, None, None, "ch", None),
            P("ch"),
        ),
        check_vma=False,
    )
```

```python
import functools
import math

import jax
import jax.numpy as jnp
from jax import lax
from jax.experimental import pallas as pl
from jax.experimental.pallas import tpu as pltpu
from jax.sharding import PartitionSpec as P

VMEM = pl.BlockSpec(memory_space=pltpu.VMEM)
HBM = pl.BlockSpec(memory_space=pltpu.HBM)
SMEM = pl.BlockSpec(memory_space=pltpu.SMEM)
PARAMS = pltpu.CompilerParams(vmem_limit_bytes=24 * 1024 * 1024)
F32 = jnp.float32
BF16 = jnp.bfloat16


def with_halo(x, sides, width):
    for axis, dim in sides:
        devices, length = (lax.axis_size(axis), x.shape[dim])
        up = [(i, (i + 1) % devices) for i in range(devices - 1)]
        down = [(j, i) for i, j in up]
        last = lax.slice_in_dim(x, length - width, length, axis=dim)
        initial = lax.slice_in_dim(x, 0, width, axis=dim)
        before = lax.ppermute(last, axis, up)
        after = lax.ppermute(initial, axis, down)
        x = jnp.concatenate([before, x, after], axis=dim)
    return x


def body_reduced(inputs, weight, bias, cotangent):
    span_x, span_y, span_z, local_ch = inputs.shape
    widest = weight.shape[4]
    local_cells = span_x * span_y * span_z
    offsets = [(a, b, c) for a in range(3) for b in range(3) for c in range(3)]
    depth_pad = ((0, 0), (0, 0), (1, 1), (0, 0))
    rimmed = with_halo(inputs, (("gx", 0), ("gy", 1)), 1)
    padded = jnp.pad(rimmed, depth_pad)
    blocks = []
    for a, b, c in offsets:
        blocks.append(
            padded[a : a + span_x, b : b + span_y, c : c + span_z].reshape(local_cells, local_ch)
        )
    patches = jnp.concatenate(blocks, axis=1)
    flat_weight = weight.reshape(27 * local_ch, widest)
    summed = lax.psum_scatter(
        lax.dot_general(flat_weight, patches, (((0,), (1,)), ((), ())), preferred_element_type=F32),
        "ch",
        scatter_dimension=0,
        tiled=True,
    ).T
    summed = summed + bias.astype(F32)[None, :]
    activation = jax.nn.silu(summed).astype(BF16).reshape(span_x, span_y, span_z, local_ch)
    sigmoid_pre = jax.nn.sigmoid(summed)
    slope = (
        cotangent.reshape(local_cells, local_ch).astype(F32)
        * sigmoid_pre
        * (1.0 + summed * (1.0 - sigmoid_pre))
    ).astype(BF16)
    local_bias = jnp.sum(slope.astype(F32), axis=0)
    slope_grid = slope.reshape(span_x, span_y, span_z, local_ch)
    weight_turned = jnp.transpose(weight.reshape(27, local_ch, widest), (0, 2, 1))
    slope_rimmed = with_halo(slope_grid, (("gx", 0), ("gy", 1)), 1)
    piece = lax.all_gather(slope_rimmed, "ch", axis=3, tiled=True)
    extended = jnp.pad(piece, depth_pad)
    running = jnp.zeros((local_cells, local_ch), F32)
    for index, (a, b, c) in enumerate(offsets):
        a, b, c = (2 - a, 2 - b, 2 - c)
        cut = extended[a : a + span_x, b : b + span_y, c : c + span_z].reshape(local_cells, widest)
        running = running + jnp.dot(cut, weight_turned[index], preferred_element_type=F32)
    interior = piece[1 : 1 + span_x, 1 : 1 + span_y].reshape(local_cells, widest)
    product = lax.dot_general(
        patches, interior, (((0,), (0,)), ((), ())), preferred_element_type=F32
    )
    total_cells = local_cells * lax.axis_size("gx") * lax.axis_size("gy")
    factor = 1.0 / math.sqrt(total_cells)
    kernel_total, bias_total = lax.psum((product * factor, local_bias * factor), ("gx", "gy"))
    input_grad = running.astype(BF16).reshape(span_x, span_y, span_z, local_ch)
    return (activation, input_grad, kernel_total.reshape(3, 3, 3, local_ch, widest), bias_total)


def shifted(v, by):
    depth = v.shape[1]
    row = lax.broadcasted_iota(jnp.int32, v.shape, 1)
    if by == 1:
        return jnp.where(row == 0, 0.0, pltpu.roll(v, 1, 1))
    return jnp.where(row == depth - 1, 0.0, pltpu.roll(v, depth - 1, 1))


def rim_sides(place, span_x, span_y):
    first = place[1] % 2 == 0
    even_at = jnp.where(first, span_y + 1, 0)
    odd_at = jnp.where(first, 0, span_y + 1)
    even_row = jnp.where(first, span_y - 1, 0)
    odd_row = jnp.where(first, 0, span_y - 1)
    x_at = jnp.where(place[0] == 0, span_x + 1, 0)
    x_row = jnp.where(place[0] == 0, span_x - 1, 0)
    return even_at, odd_at, even_row, odd_row, x_at, x_row


def prepare_kernel(place, source, inputs, even, odd, even_corner, odd_corner, arrived):
    span_x, span_y, _, _ = inputs.shape
    _, _, even_row, odd_row, _, x_row = rim_sides(place, span_x, span_y)
    pieces = [
        (source.at[:, even_row], even),
        (source.at[:, odd_row], odd),
        (source.at[x_row, even_row], even_corner),
        (source.at[x_row, odd_row], odd_corner),
        (source, inputs),
    ]
    copies = [
        pltpu.make_async_copy(piece, target, arrived.at[n])
        for n, (piece, target) in enumerate(pieces)
    ]
    for copy in copies:
        copy.start()
    for copy in copies:
        copy.wait()


def stage_kernel(after, *rest):
    count = (len(rest) - 1) // 2
    sources, targets, arrived = rest[:count], rest[count : 2 * count], rest[-1]
    copies = []
    for source, target in zip(sources, targets):
        parts = source.shape[0] if len(source.shape) == 3 else 1
        for n in range(parts):
            here = pl.ds(n, 1) if parts > 1 else slice(None)
            copies.append(
                pltpu.make_async_copy(source.at[here], target.at[here], arrived.at[len(copies)])
            )
    for copy in copies:
        copy.start()
    for copy in copies:
        copy.wait()


def forward_kernel(
    parts_y, place, weight, inputs, even, odd, beside, even_corner, odd_corner, own, *rest
):
    *others, pair, window, blocks = rest
    span_x, span_y, span_z, lanes = inputs.shape
    half_x = span_x // 2
    half = half_x * span_y * span_z
    even_at, odd_at, _, _, x_at, x_row = rim_sides(place, span_x, span_y)

    def spread(v):
        flat = v.astype(F32).reshape(-1, span_z, lanes)
        joined = jnp.concatenate([shifted(flat, 1), flat, shifted(flat, -1)], axis=2)
        return joined.astype(BF16).reshape(v.shape[:-1] + (3 * lanes,))

    nothing = jnp.zeros((span_y + 2, span_z, 3 * lanes), BF16)
    window[0] = nothing
    window[span_x + 1] = nothing
    window[1 : span_x + 1, 1 : span_y + 1] = spread(inputs[...])
    window[1 : span_x + 1, even_at] = spread(even[...])
    has_odd = (place[1] != 0) & (place[1] != parts_y - 1)
    window[1 : span_x + 1, odd_at] = jnp.where(has_odd, spread(odd[...]), jnp.zeros((), BF16))
    window[x_at, 1 : span_y + 1] = spread(beside[facing_row(x_row, span_x)])
    window[x_at, even_at] = spread(even_corner[...])
    window[x_at, odd_at] = jnp.where(has_odd, spread(odd_corner[...]), jnp.zeros((), BF16))
    sums = []
    for h in range(2):
        total = None
        for a in range(3):
            for b in range(3):
                cut = window[a + h * half_x : a + (h + 1) * half_x, b : b + span_y]
                term = jnp.dot(
                    cut.reshape(half, 3 * lanes), weight[a * 3 + b], preferred_element_type=F32
                )
                total = term if total is None else total + term
        sums.append(total)
    for d in range(weight.shape[2] // lanes):
        cut = slice(d * lanes, (d + 1) * lanes)
        blocks[d] = jnp.concatenate([sums[0][:, cut], sums[1][:, cut]], axis=1)
    own[...] = blocks[place[2]]
    for k, other in enumerate(others):
        other[...] = blocks[place[2] ^ (k + 1)].astype(BF16)
    for n, whole in enumerate((inputs, beside)):
        pair[n] = jnp.concatenate([whole[:half_x], whole[half_x:]], axis=3)


def slope_kernel(own, *rest):
    *others, bias, cotangent, activation, slope = rest
    half, lanes = cotangent.shape[0] // 2, cotangent.shape[1]
    summed = own[...]
    for other in others:
        summed = summed + other[...].astype(F32)
    offset = bias[...].astype(F32)
    summed = summed + jnp.concatenate([offset, offset], axis=1)
    sigmoid = jax.nn.sigmoid(summed)
    active = (summed * sigmoid).astype(BF16)
    activation[:half] = active[:, :lanes]
    activation[half:] = active[:, lanes:]
    upstream = jnp.concatenate([cotangent[:half], cotangent[half:]], axis=1).astype(F32)
    slope[...] = (upstream * sigmoid * (1.0 + summed * (1.0 - sigmoid))).astype(BF16)


def join_kernel(own, *rest):
    *pieces, others, column = rest
    column[0] = own[...]
    for k, piece in enumerate(pieces):
        others[k] = piece[...]
        column[k + 1] = piece[...]


def ordered_halves(place, pieces):
    shards, _, _, _, lanes = pieces.shape
    lanes = lanes // 2
    ordered = [pieces[place[2] ^ j] for j in range(shards)]
    return [
        jnp.concatenate([piece[..., h * lanes : (h + 1) * lanes] for piece in ordered], axis=-1)
        for h in range(2)
    ]


def add_terms(place, parts_y, members, slopes, turned, old, store):
    operands = []
    for m, pieces in zip(members, slopes):
        shards, half_x, span_y, span_z, lanes = pieces.shape
        channels, row = shards * lanes // 2, span_y * span_z
        right = jnp.concatenate(
            [part.reshape(half_x * row, channels) for part in ordered_halves(place, pieces)]
        )
        x0, y0 = (place[0] ^ (m // parts_y)) * 2 * half_x, place[1] ^ (m % parts_y)
        operands.append((x0, y0, row, right))
    for a in range(3):
        total = None if old is None else old[a]
        for x0, y0, row, right in operands:
            left = turned[y0, :, pl.ds(pl.multiple_of((x0 + a) * row, row), right.shape[0])]
            term = jnp.dot(left, right, preferred_element_type=F32)
            total = term if total is None else total + term
        store(a, total)


def first_kernel(
    parts_x, parts_y, place, weight, pair, beside_y, sibling, column, turned, sums, weight_turned, volume
):
    shards, half_x, span_y, span_z, lanes = column.shape
    cells = [(0, pair, 0), (parts_y, pair, 1), (2, beside_y, 1), (parts_y + 2, beside_y, 2)]
    cells += [(m ^ 1, sibling, shards + n) for n, (m, _, _) in enumerate(cells)]
    span_x, lanes = 2 * half_x, lanes // 2
    rows_x, rows_y = parts_x * span_x, parts_y * span_y
    width = 3 * lanes
    zero_x = jnp.zeros((1, rows_y + 2, span_z, width), BF16)
    zero_y = jnp.zeros((rows_x + 2, 1, span_z, width), BF16)
    volume[0:1] = zero_x
    volume[rows_x + 1 : rows_x + 2] = zero_x
    volume[:, 0:1] = zero_y
    volume[:, rows_y + 1 : rows_y + 2] = zero_y
    for m, array, n in cells:
        x0, y0 = (place[0] ^ (m // parts_y)) * span_x, (place[1] ^ (m % parts_y)) * span_y
        v = array[n].astype(F32).reshape(half_x * span_y, span_z, 2 * lanes)
        low, high = shifted(v, 1), shifted(v, -1)
        for h in range(2):
            cut = slice(h * lanes, (h + 1) * lanes)
            joined = jnp.concatenate([low[..., cut], v[..., cut], high[..., cut]], axis=2)
            volume[pl.ds(x0 + 1 + h * half_x, half_x), pl.ds(y0 + 1, span_y)] = joined.astype(
                BF16
            ).reshape(half_x, span_y, span_z, width)
    for y in range(parts_y):
        for b in range(3):
            cut = volume[:, y * span_y + b : (y + 1) * span_y + b]
            turned[y, b * width : (b + 1) * width] = cut.reshape(-1, width).T

    def store(a, total):
        sums[a] = total

    for tap in range(weight.shape[0]):
        weight_turned[tap] = weight[tap].T
    members = (0, 1)
    add_terms(place, parts_y, members, (column, sibling.at[:shards]), turned, None, store)


def rows_of(place, pieces, row):
    shards, lanes = column_shape(pieces)
    ordered = [pieces[place[2] ^ j, :, row] for j in range(shards)]
    return [
        jnp.concatenate([piece[..., h * lanes : (h + 1) * lanes] for piece in ordered], axis=-1)
        for h in range(2)
    ]


def column_shape(pieces):
    return pieces.shape[0], pieces.shape[-1] // 2


def second_kernel(
    parts_y, members, place, weight, turned, old, column, sibling, *rest
):
    *slopes, partial, sums, window = rest
    shards, half_x, span_y, span_z, _ = column.shape
    span_x, half = 2 * half_x, half_x * span_y * span_z
    even_at, _, even_row, _, _, _ = rim_sides(place, span_x, span_y)
    window[...] = jnp.zeros(window.shape, BF16)
    beside = rows_of(place, sibling.at[:shards], facing_row(even_row, span_y))
    for h, own in enumerate(ordered_halves(place, column)):
        window[1 + h * half_x : 1 + (h + 1) * half_x, 1 : span_y + 1] = own
        window[1 + h * half_x : 1 + (h + 1) * half_x, even_at] = beside[h]
    for h in range(2):
        total = None
        for a in range(3):
            for b in range(3):
                cut = window[
                    2 - a + h * half_x : 2 - a + (h + 1) * half_x, 2 - b : 2 - b + span_y
                ]
                term = jnp.dot(
                    cut.reshape(half, cut.shape[-1]), weight[a * 3 + b], preferred_element_type=F32
                )
                total = term if total is None else total + term
        partial[h * half_x : (h + 1) * half_x] = total.reshape((half_x,) + partial.shape[1:])
    middle_kernel(parts_y, members, place, turned, old, *slopes, sums)


def middle_kernel(parts_y, members, place, turned, old, *rest):
    *slopes, sums = rest

    def store(a, total):
        sums[a] = total

    add_terms(place, parts_y, members, slopes, turned, old, store)


def facing(place, halves):
    low, high = halves
    return jnp.where(place[0] == 0, low[0], high[-1])


def channel_sum(pieces):
    mine = pieces[0].astype(F32).reshape(-1, pieces.shape[-1])
    return jnp.sum(mine, axis=0, keepdims=True)


def rim_kernel(parts_y, members, place, weight, turned, old, partial, *rest):
    *slopes, grid, column, sums, rim_x, rim_y = rest
    shards, half_x, span_y, span_z, _ = slopes[0].shape
    span_x, channels = 2 * half_x, rim_x.shape[-1]
    even_at, odd_at, even_row, odd_row, _, x_row = rim_sides(place, span_x, span_y)
    has_odd = (place[1] != 0) & (place[1] != parts_y - 1)
    rim_x[...] = jnp.zeros(rim_x.shape, BF16)
    rim_y[...] = jnp.zeros(rim_y.shape, BF16)
    rim_x[1 : span_y + 1] = facing(place, ordered_halves(place, slopes[parts_y]))
    even = rows_of(place, slopes[parts_y + 1], facing_row(even_row, span_y))
    rim_x[even_at] = facing(place, even)

    @pl.when(has_odd)
    def _():
        odd = rows_of(place, slopes[3], facing_row(odd_row, span_y))
        for h, rows in enumerate(odd):
            rim_y[1 + h * half_x : 1 + (h + 1) * half_x] = rows

    grid[...] = partial[...]
    tap_x, tap_y = rim_taps(place, odd_row)
    total = None
    for b in range(3):
        cut = rim_x[2 - b : 2 - b + span_y].reshape(span_y * span_z, channels)
        term = jnp.dot(cut, weight[tap_x * 3 + b], preferred_element_type=F32)
        total = term if total is None else total + term
    grid[x_row] += total.reshape((span_y,) + grid.shape[2:])
    total = None
    for a in range(3):
        cut = rim_y[2 - a : 2 - a + span_x].reshape(span_x * span_z, channels)
        term = jnp.dot(cut, weight[a * 3 + tap_y], preferred_element_type=F32)
        total = term if total is None else total + term
    grid[:, odd_row] += total.reshape((span_x,) + grid.shape[2:])
    total = channel_sum(slopes[0])
    for pieces in slopes[1:]:
        total = total + channel_sum(pieces)
    column[...] = total
    middle_kernel(parts_y, members, place, turned, old, *[slopes[m] for m in members], sums)


def rim_taps(place, odd_row):
    return jnp.where(place[0] == 0, 0, 2), jnp.where(odd_row == 0, 2, 0)


def last_kernel(parts_y, member, factor, place, weight, turned, old, partial, column, pieces, *rest):
    input_grad, kernel_grad, bias_grad, grid, sums, sent = rest
    _, half_x, span_y, span_z, _ = pieces.shape
    lanes = pieces.shape[-1] // 2
    span_x = 2 * half_x
    copies = []

    def store(a, total):
        sums[a] = total * factor
        rows = 3 * lanes
        for b in range(3):
            here = pl.ds(b * rows, rows)
            copy = pltpu.make_async_copy(
                sums.at[a, here], kernel_grad.at[a, here], sent.at[a * 3 + b]
            )
            copy.start()
            copies.append(copy)

    add_terms(place, parts_y, (member,), (pieces,), turned, old, store)

    total = column[...] + channel_sum(pieces)
    bias_grad[...] = (total[:, :lanes] + total[:, lanes:]) * factor
    _, _, _, odd_row, _, x_row = rim_sides(place, span_x, span_y)
    has_odd = (place[1] != 0) & (place[1] != parts_y - 1)
    tap_x, tap_y = rim_taps(place, odd_row)
    grid[...] = partial[...]

    @pl.when(has_odd)
    def _():
        corner = facing(place, rows_of(place, pieces, facing_row(odd_row, span_y)))
        term = jnp.dot(corner, weight[tap_x * 3 + tap_y], preferred_element_type=F32)
        grid[x_row, odd_row] += term

    summed = grid[...].reshape(span_x * span_y, span_z, 3 * lanes)
    result = (
        shifted(summed[..., :lanes], -1)
        + summed[..., lanes : 2 * lanes]
        + shifted(summed[..., 2 * lanes :], 1)
    )
    input_grad[...] = result.reshape(-1, lanes).astype(BF16)
    for copy in copies:
        copy.wait()


def facing_row(row, span_y):
    return span_y - 1 - row


def exchange(x, axes, mask):
    return lax.ppermute(x, axes, [(i, i ^ mask) for i in range(lax.axis_size(axes))])


def body_gathered(inputs, weight, bias, cotangent):
    spans = inputs.shape[:3]
    span_x, span_y, span_z = spans
    local_ch, channels = weight.shape[3:]
    local = span_x * span_y * span_z
    parts_x, parts_y = lax.axis_size("gx"), lax.axis_size("gy")
    count = parts_x * parts_y
    shards = lax.axis_size("ch")
    axes = ("gx", "gy")
    factor = 1.0 / math.sqrt(local * count)
    place = jnp.stack([lax.axis_index(axis) for axis in ("gx", "gy", "ch")]).astype(jnp.int32)
    taps = weight.reshape(9, 3 * local_ch, channels)
    packing = (span_x // 2, span_y, span_z, 2 * local_ch)
    flat = (local // 2, 2 * local_ch)

    def call(kernel, name, outs, args, scratch=(), flops=0):
        return pl.pallas_call(
            kernel,
            out_shape=[jax.ShapeDtypeStruct(shape, kind) for shape, kind in outs],
            in_specs=[SMEM if x is place else VMEM for x in args],
            out_specs=[VMEM] * len(outs),
            scratch_shapes=[pltpu.VMEM(shape, kind) for shape, kind in scratch],
            compiler_params=PARAMS,
            cost_estimate=pl.CostEstimate(flops=flops, bytes_accessed=1024, transcendentals=0),
            name=name,
        )(*args)

    row = (span_x, span_z, local_ch)
    held, even, odd, even_corner, odd_corner = pl.pallas_call(
        prepare_kernel,
        out_shape=[jax.ShapeDtypeStruct(inputs.shape, BF16)]
        + [jax.ShapeDtypeStruct(row, BF16)] * 2
        + [jax.ShapeDtypeStruct(row[1:], BF16)] * 2,
        in_specs=[SMEM, HBM],
        out_specs=[VMEM] * 5,
        scratch_shapes=[pltpu.SemaphoreType.DMA((5,))],
        compiler_params=PARAMS,
        name="prepare",
    )(place, pltpu.with_memory_space_constraint(inputs, pltpu.HBM))
    sources = (taps, cotangent.reshape(local, local_ch), bias.reshape(1, local_ch))
    taps, cotangent, bias = pl.pallas_call(
        stage_kernel,
        out_shape=[jax.ShapeDtypeStruct(x.shape, x.dtype) for x in sources],
        in_specs=[VMEM] + [HBM] * len(sources),
        out_specs=[VMEM] * len(sources),
        scratch_shapes=[pltpu.SemaphoreType.DMA((len(sources) + 8,))],
        compiler_params=PARAMS,
        name="stage",
    )(even_corner, *[pltpu.with_memory_space_constraint(x, pltpu.HBM) for x in sources])
    beside = exchange(inputs, axes, parts_y)
    even = exchange(even, axes, 1)
    odd = exchange(odd, axes, 3)
    even_corner = exchange(even_corner, axes, parts_y + 1)
    odd_corner = exchange(odd_corner, axes, parts_y + 3)
    own, *others, pair = call(
        functools.partial(forward_kernel, parts_y),
        "forward",
        [(flat, F32)] + [(flat, BF16)] * (shards - 1) + [((2,) + packing, BF16)],
        [place, taps, held, even, odd, beside, even_corner, odd_corner],
        [((span_x + 2, span_y + 2, span_z, 3 * local_ch), BF16), ((shards,) + flat, F32)],
    )
    others = [exchange(others[k - 1], "ch", k) for k in range(shards - 1, 0, -1)]
    activation, slope = call(
        slope_kernel,
        "slope",
        [((local, local_ch), BF16), (flat, BF16)],
        [own, *others, bias, cotangent],
    )
    slope = slope.reshape(packing)
    rest, column = call(
        join_kernel,
        "join",
        [((shards - 1,) + packing, BF16), ((shards,) + packing, BF16)],
        [slope] + [exchange(slope, "ch", k) for k in range(1, shards)],
        flops=1 << 32,
    )
    piece = slope.reshape((1,) + packing)
    x, y = parts_y, 2
    beside_x = exchange(piece, axes, x)
    beside_y = exchange(jnp.concatenate([piece, pair]), axes, y)
    beside_y, beside_x, rest, column = lax.optimization_barrier((beside_y, beside_x, rest, column))
    late_y, late_x = exchange(rest, axes, y), exchange(rest, axes, x)
    sibling = exchange(jnp.concatenate([column, pair, beside_y[1:]]), axes, 1)
    turned_shape = (parts_y, 9 * local_ch, (parts_x * span_x + 2) * span_y * span_z)
    sums_shape = (3, 9 * local_ch, channels)
    turned, sums, taps = call(
        functools.partial(first_kernel, parts_x, parts_y),
        "first",
        [(turned_shape, BF16), (sums_shape, F32), ((9, channels, 3 * local_ch), BF16)],
        [place, taps, pair, beside_y, sibling, column],
        [((parts_x * span_x + 2, parts_y * span_y + 2, span_z, 3 * local_ch), BF16)],
    )
    slopes = {0: column, 1: sibling[:shards]}
    late_y, late_x, sums = lax.optimization_barrier((late_y, late_x, sums))
    slopes[y] = jnp.concatenate([beside_y[:1], late_y])
    slopes[x] = jnp.concatenate([beside_x, late_x])
    middle = shards // 2
    diagonal = [exchange(slopes[x][:middle], axes, y), exchange(slopes[y][middle:], axes, x)]
    across = [exchange(slopes[m], axes, 1) for m in (y, x)]
    grid_shape = spans + (3 * local_ch,)
    partial, sums = call(
        functools.partial(second_kernel, parts_y, (y, x)),
        "second",
        [(grid_shape, F32), (sums_shape, F32)],
        [place, taps, turned, sums, column, sibling, slopes[y], slopes[x]],
        [((span_x + 2, span_y + 2, span_z, channels), BF16)],
    )
    slopes[y + 1], slopes[x + 1] = across
    (sums,) = call(
        functools.partial(middle_kernel, parts_y, (y + 1, x + 1)),
        "third",
        [(sums_shape, F32)],
        [place, turned, sums, *across],
    )
    *diagonal, sums = lax.optimization_barrier((*diagonal, sums))
    slopes[x + y] = jnp.concatenate(diagonal)
    final = exchange(slopes[x + y], axes, 1)
    partial, column, sums = call(
        functools.partial(rim_kernel, parts_y, (x + y,)),
        "rim",
        [(grid_shape, F32), ((1, 2 * local_ch), F32), (sums_shape, F32)],
        [place, taps, turned, sums, partial] + [slopes[m] for m in range(count - 1)],
        [((span_y + 2, span_z, channels), BF16), ((span_x + 2, span_z, channels), BF16)],
    )
    args = [place, taps, turned, sums, partial, column, final]
    input_grad, kernel_grad, bias_grad = pl.pallas_call(
        functools.partial(last_kernel, parts_y, x + y + 1, factor),
        out_shape=[
            jax.ShapeDtypeStruct((local, local_ch), BF16),
            jax.ShapeDtypeStruct(sums_shape, F32),
            jax.ShapeDtypeStruct((1, local_ch), F32),
        ],
        in_specs=[SMEM] + [VMEM] * (len(args) - 1),
        out_specs=[VMEM, HBM, VMEM],
        scratch_shapes=[
            pltpu.VMEM(grid_shape, F32),
            pltpu.VMEM(sums_shape, F32),
            pltpu.SemaphoreType.DMA((9,)),
        ],
        compiler_params=PARAMS,
        name="last",
    )(*args)
    return (
        activation.reshape(inputs.shape),
        input_grad.reshape(inputs.shape),
        kernel_grad.reshape(weight.shape),
        bias_grad.reshape(local_ch),
    )


def solution(mesh):
    few = (mesh.shape["gx"], mesh.shape["gy"]) == (2, 4)
    return jax.shard_map(
        body_gathered if few else body_reduced,
        mesh=mesh,
        in_specs=(
            P("gx", "gy", None, "ch"),
            P(None, None, None, "ch", None),
            P("ch"),
            P("gx", "gy", None, "ch"),
        ),
        out_specs=(
            P("gx", "gy", None, "ch"),
            P("gx", "gy", None, "ch"),
            P(None, None, None, "ch", None),
            P("ch"),
        ),
        check_vma=False,
    )
```

```python
import functools
import math

import jax
import jax.numpy as jnp
from jax import lax
from jax.experimental import pallas as pl
from jax.experimental.pallas import tpu as pltpu
from jax.sharding import PartitionSpec as P

VMEM = pl.BlockSpec(memory_space=pltpu.VMEM)
HBM = pl.BlockSpec(memory_space=pltpu.HBM)
SMEM = pl.BlockSpec(memory_space=pltpu.SMEM)
PARAMS = pltpu.CompilerParams(vmem_limit_bytes=24 * 1024 * 1024)
F32 = jnp.float32
BF16 = jnp.bfloat16


def with_halo(x, sides, width):
    for axis, dim in sides:
        devices, length = (lax.axis_size(axis), x.shape[dim])
        up = [(i, (i + 1) % devices) for i in range(devices - 1)]
        down = [(j, i) for i, j in up]
        last = lax.slice_in_dim(x, length - width, length, axis=dim)
        initial = lax.slice_in_dim(x, 0, width, axis=dim)
        before = lax.ppermute(last, axis, up)
        after = lax.ppermute(initial, axis, down)
        x = jnp.concatenate([before, x, after], axis=dim)
    return x


def body_reduced(inputs, weight, bias, cotangent):
    span_x, span_y, span_z, local_ch = inputs.shape
    widest = weight.shape[4]
    local_cells = span_x * span_y * span_z
    offsets = [(a, b, c) for a in range(3) for b in range(3) for c in range(3)]
    depth_pad = ((0, 0), (0, 0), (1, 1), (0, 0))
    rimmed = with_halo(inputs, (("gx", 0), ("gy", 1)), 1)
    padded = jnp.pad(rimmed, depth_pad)
    blocks = []
    for a, b, c in offsets:
        blocks.append(
            padded[a : a + span_x, b : b + span_y, c : c + span_z].reshape(local_cells, local_ch)
        )
    patches = jnp.concatenate(blocks, axis=1)
    flat_weight = weight.reshape(27 * local_ch, widest)
    summed = lax.psum_scatter(
        lax.dot_general(flat_weight, patches, (((0,), (1,)), ((), ())), preferred_element_type=F32),
        "ch",
        scatter_dimension=0,
        tiled=True,
    ).T
    summed = summed + bias.astype(F32)[None, :]
    activation = jax.nn.silu(summed).astype(BF16).reshape(span_x, span_y, span_z, local_ch)
    sigmoid_pre = jax.nn.sigmoid(summed)
    slope = (
        cotangent.reshape(local_cells, local_ch).astype(F32)
        * sigmoid_pre
        * (1.0 + summed * (1.0 - sigmoid_pre))
    ).astype(BF16)
    local_bias = jnp.sum(slope.astype(F32), axis=0)
    slope_grid = slope.reshape(span_x, span_y, span_z, local_ch)
    weight_turned = jnp.transpose(weight.reshape(27, local_ch, widest), (0, 2, 1))
    slope_rimmed = with_halo(slope_grid, (("gx", 0), ("gy", 1)), 1)
    piece = lax.all_gather(slope_rimmed, "ch", axis=3, tiled=True)
    extended = jnp.pad(piece, depth_pad)
    running = jnp.zeros((local_cells, local_ch), F32)
    for index, (a, b, c) in enumerate(offsets):
        a, b, c = (2 - a, 2 - b, 2 - c)
        cut = extended[a : a + span_x, b : b + span_y, c : c + span_z].reshape(local_cells, widest)
        running = running + jnp.dot(cut, weight_turned[index], preferred_element_type=F32)
    interior = piece[1 : 1 + span_x, 1 : 1 + span_y].reshape(local_cells, widest)
    product = lax.dot_general(
        patches, interior, (((0,), (0,)), ((), ())), preferred_element_type=F32
    )
    total_cells = local_cells * lax.axis_size("gx") * lax.axis_size("gy")
    factor = 1.0 / math.sqrt(total_cells)
    kernel_total, bias_total = lax.psum((product * factor, local_bias * factor), ("gx", "gy"))
    input_grad = running.astype(BF16).reshape(span_x, span_y, span_z, local_ch)
    return (activation, input_grad, kernel_total.reshape(3, 3, 3, local_ch, widest), bias_total)


def shifted(v, by):
    depth = v.shape[1]
    row = lax.broadcasted_iota(jnp.int32, v.shape, 1)
    if by == 1:
        return jnp.where(row == 0, 0.0, pltpu.roll(v, 1, 1))
    return jnp.where(row == depth - 1, 0.0, pltpu.roll(v, depth - 1, 1))


def rim_sides(place, span_x, span_y):
    first = place[1] % 2 == 0
    even_at = jnp.where(first, span_y + 1, 0)
    odd_at = jnp.where(first, 0, span_y + 1)
    even_row = jnp.where(first, span_y - 1, 0)
    odd_row = jnp.where(first, 0, span_y - 1)
    x_at = jnp.where(place[0] == 0, span_x + 1, 0)
    x_row = jnp.where(place[0] == 0, span_x - 1, 0)
    return even_at, odd_at, even_row, odd_row, x_at, x_row


def prepare_kernel(place, source, inputs, packed, even, odd, even_corner, odd_corner, arrived):
    copy = pltpu.make_async_copy(source, inputs, arrived)
    copy.start()
    copy.wait()
    span_x, span_y, _, _ = inputs.shape
    half = span_x // 2
    _, _, even_row, odd_row, _, x_row = rim_sides(place, span_x, span_y)
    even[...] = inputs[:, even_row]
    odd[...] = inputs[:, odd_row]
    even_corner[...] = inputs[x_row, even_row]
    odd_corner[...] = inputs[x_row, odd_row]
    packed[...] = jnp.concatenate([inputs[:half], inputs[half:]], axis=3)


def stage_kernel(after, *rest):
    count = (len(rest) - 1) // 2
    sources, targets, arrived = rest[:count], rest[count : 2 * count], rest[-1]
    copies = []
    for source, target in zip(sources, targets):
        parts = source.shape[0] if len(source.shape) == 3 else 1
        for n in range(parts):
            here = pl.ds(n, 1) if parts > 1 else slice(None)
            copies.append(
                pltpu.make_async_copy(source.at[here], target.at[here], arrived.at[len(copies)])
            )
    for copy in copies:
        copy.start()
    for copy in copies:
        copy.wait()


def forward_kernel(
    parts_y, place, weight, inputs, packed, even, odd, beside, even_corner, odd_corner, own, *rest
):
    *others, pair, window, blocks = rest
    span_x, span_y, span_z, lanes = inputs.shape
    half_x = span_x // 2
    half = half_x * span_y * span_z
    even_at, odd_at, _, _, x_at, _ = rim_sides(place, span_x, span_y)

    def spread(v):
        flat = v.astype(F32).reshape(-1, span_z, lanes)
        joined = jnp.concatenate([shifted(flat, 1), flat, shifted(flat, -1)], axis=2)
        return joined.astype(BF16).reshape(v.shape[:-1] + (3 * lanes,))

    nothing = jnp.zeros((span_y + 2, span_z, 3 * lanes), BF16)
    window[0] = nothing
    window[span_x + 1] = nothing
    window[1 : span_x + 1, 1 : span_y + 1] = spread(inputs[...])
    window[1 : span_x + 1, even_at] = spread(even[...])
    has_odd = (place[1] != 0) & (place[1] != parts_y - 1)
    window[1 : span_x + 1, odd_at] = jnp.where(has_odd, spread(odd[...]), jnp.zeros((), BF16))
    across = jnp.where(place[0] == 0, beside[0][..., :lanes], beside[half_x - 1][..., lanes:])
    window[x_at, 1 : span_y + 1] = spread(across)
    window[x_at, even_at] = spread(even_corner[...])
    window[x_at, odd_at] = jnp.where(has_odd, spread(odd_corner[...]), jnp.zeros((), BF16))
    sums = []
    for h in range(2):
        total = None
        for a in range(3):
            for b in range(3):
                cut = window[a + h * half_x : a + (h + 1) * half_x, b : b + span_y]
                term = jnp.dot(
                    cut.reshape(half, 3 * lanes), weight[a * 3 + b], preferred_element_type=F32
                )
                total = term if total is None else total + term
        sums.append(total)
    for d in range(weight.shape[2] // lanes):
        cut = slice(d * lanes, (d + 1) * lanes)
        blocks[d] = jnp.concatenate([sums[0][:, cut], sums[1][:, cut]], axis=1)
    own[...] = blocks[place[2]]
    for k, other in enumerate(others):
        other[...] = blocks[place[2] ^ (k + 1)].astype(BF16)
    pair[0] = packed[...]
    pair[1] = beside[...]


def slope_kernel(own, *rest):
    *others, bias, cotangent, activation, slope = rest
    half, lanes = cotangent.shape[0] // 2, cotangent.shape[1]
    summed = own[...]
    for other in others:
        summed = summed + other[...].astype(F32)
    offset = bias[...].astype(F32)
    summed = summed + jnp.concatenate([offset, offset], axis=1)
    sigmoid = jax.nn.sigmoid(summed)
    active = (summed * sigmoid).astype(BF16)
    activation[:half] = active[:, :lanes]
    activation[half:] = active[:, lanes:]
    upstream = jnp.concatenate([cotangent[:half], cotangent[half:]], axis=1).astype(F32)
    slope[...] = (upstream * sigmoid * (1.0 + summed * (1.0 - sigmoid))).astype(BF16)


def ordered_halves(place, pieces):
    shards, _, _, _, lanes = pieces.shape
    lanes = lanes // 2
    ordered = [pieces[place[2] ^ j] for j in range(shards)]
    return [
        jnp.concatenate([piece[..., h * lanes : (h + 1) * lanes] for piece in ordered], axis=-1)
        for h in range(2)
    ]


def add_terms(place, parts_y, members, slopes, turned, old, store):
    operands = []
    for m, pieces in zip(members, slopes):
        shards, half_x, span_y, span_z, lanes = pieces.shape
        channels, row = shards * lanes // 2, span_y * span_z
        right = jnp.concatenate(
            [part.reshape(half_x * row, channels) for part in ordered_halves(place, pieces)]
        )
        x0, y0 = (place[0] ^ (m // parts_y)) * 2 * half_x, place[1] ^ (m % parts_y)
        operands.append((x0, y0, row, right))
    for a in range(3):
        total = None if old is None else old[a]
        for x0, y0, row, right in operands:
            left = turned[y0, :, pl.ds(pl.multiple_of((x0 + a) * row, row), right.shape[0])]
            term = jnp.dot(left, right, preferred_element_type=F32)
            total = term if total is None else total + term
        store(a, total)


def first_kernel(
    parts_x, parts_y, place, weight, pair, beside_y, sibling, column, turned, sums, weight_turned, volume
):
    shards, half_x, span_y, span_z, lanes = column.shape
    cells = [(0, pair, 0), (parts_y, pair, 1), (2, beside_y, 1), (parts_y + 2, beside_y, 2)]
    cells += [(m ^ 1, sibling, shards + n) for n, (m, _, _) in enumerate(cells)]
    span_x, lanes = 2 * half_x, lanes // 2
    rows_x, rows_y = parts_x * span_x, parts_y * span_y
    width = 3 * lanes
    zero_x = jnp.zeros((1, rows_y + 2, span_z, width), BF16)
    zero_y = jnp.zeros((rows_x + 2, 1, span_z, width), BF16)
    volume[0:1] = zero_x
    volume[rows_x + 1 : rows_x + 2] = zero_x
    volume[:, 0:1] = zero_y
    volume[:, rows_y + 1 : rows_y + 2] = zero_y
    for m, array, n in cells:
        x0, y0 = (place[0] ^ (m // parts_y)) * span_x, (place[1] ^ (m % parts_y)) * span_y
        v = array[n].astype(F32).reshape(half_x * span_y, span_z, 2 * lanes)
        low, high = shifted(v, 1), shifted(v, -1)
        for h in range(2):
            cut = slice(h * lanes, (h + 1) * lanes)
            joined = jnp.concatenate([low[..., cut], v[..., cut], high[..., cut]], axis=2)
            volume[pl.ds(x0 + 1 + h * half_x, half_x), pl.ds(y0 + 1, span_y)] = joined.astype(
                BF16
            ).reshape(half_x, span_y, span_z, width)
    for y in range(parts_y):
        for b in range(3):
            cut = volume[:, y * span_y + b : (y + 1) * span_y + b]
            turned[y, b * width : (b + 1) * width] = cut.reshape(-1, width).T

    def store(a, total):
        sums[a] = total

    for tap in range(weight.shape[0]):
        weight_turned[tap] = weight[tap].T
    members = (0, 1)
    add_terms(place, parts_y, members, (column, sibling.at[:shards]), turned, None, store)


def rows_of(place, pieces, row):
    shards, lanes = column_shape(pieces)
    ordered = [pieces[place[2] ^ j, :, row] for j in range(shards)]
    return [
        jnp.concatenate([piece[..., h * lanes : (h + 1) * lanes] for piece in ordered], axis=-1)
        for h in range(2)
    ]


def column_shape(pieces):
    return pieces.shape[0], pieces.shape[-1] // 2


def second_kernel(
    parts_y, members, place, weight, turned, old, column, sibling, *rest
):
    *slopes, partial, sums, window = rest
    shards, half_x, span_y, span_z, _ = column.shape
    span_x, half = 2 * half_x, half_x * span_y * span_z
    even_at, _, even_row, _, _, _ = rim_sides(place, span_x, span_y)
    window[...] = jnp.zeros(window.shape, BF16)
    beside = rows_of(place, sibling.at[:shards], facing_row(even_row, span_y))
    for h, own in enumerate(ordered_halves(place, column)):
        window[1 + h * half_x : 1 + (h + 1) * half_x, 1 : span_y + 1] = own
        window[1 + h * half_x : 1 + (h + 1) * half_x, even_at] = beside[h]
    for h in range(2):
        total = None
        for a in range(3):
            for b in range(3):
                cut = window[
                    2 - a + h * half_x : 2 - a + (h + 1) * half_x, 2 - b : 2 - b + span_y
                ]
                term = jnp.dot(
                    cut.reshape(half, cut.shape[-1]), weight[a * 3 + b], preferred_element_type=F32
                )
                total = term if total is None else total + term
        partial[h * half_x : (h + 1) * half_x] = total.reshape((half_x,) + partial.shape[1:])
    middle_kernel(parts_y, members, place, turned, old, *slopes, sums)


def middle_kernel(parts_y, members, place, turned, old, *rest):
    *slopes, sums = rest

    def store(a, total):
        sums[a] = total

    add_terms(place, parts_y, members, slopes, turned, old, store)


def facing(place, halves):
    low, high = halves
    return jnp.where(place[0] == 0, low[0], high[-1])


def channel_sum(pieces):
    mine = pieces[0].astype(F32).reshape(-1, pieces.shape[-1])
    return jnp.sum(mine, axis=0, keepdims=True)


def rim_kernel(parts_y, members, place, weight, turned, old, partial, *rest):
    *slopes, grid, column, sums, rim_x, rim_y = rest
    shards, half_x, span_y, span_z, _ = slopes[0].shape
    span_x, channels = 2 * half_x, rim_x.shape[-1]
    even_at, odd_at, even_row, odd_row, _, x_row = rim_sides(place, span_x, span_y)
    has_odd = (place[1] != 0) & (place[1] != parts_y - 1)
    rim_x[...] = jnp.zeros(rim_x.shape, BF16)
    rim_y[...] = jnp.zeros(rim_y.shape, BF16)
    rim_x[1 : span_y + 1] = facing(place, ordered_halves(place, slopes[parts_y]))
    even = rows_of(place, slopes[parts_y + 1], facing_row(even_row, span_y))
    rim_x[even_at] = facing(place, even)

    @pl.when(has_odd)
    def _():
        odd = rows_of(place, slopes[3], facing_row(odd_row, span_y))
        for h, rows in enumerate(odd):
            rim_y[1 + h * half_x : 1 + (h + 1) * half_x] = rows

    grid[...] = partial[...]
    tap_x, tap_y = rim_taps(place, odd_row)
    total = None
    for b in range(3):
        cut = rim_x[2 - b : 2 - b + span_y].reshape(span_y * span_z, channels)
        term = jnp.dot(cut, weight[tap_x * 3 + b], preferred_element_type=F32)
        total = term if total is None else total + term
    grid[x_row] += total.reshape((span_y,) + grid.shape[2:])
    total = None
    for a in range(3):
        cut = rim_y[2 - a : 2 - a + span_x].reshape(span_x * span_z, channels)
        term = jnp.dot(cut, weight[a * 3 + tap_y], preferred_element_type=F32)
        total = term if total is None else total + term
    grid[:, odd_row] += total.reshape((span_x,) + grid.shape[2:])
    total = channel_sum(slopes[0])
    for pieces in slopes[1:]:
        total = total + channel_sum(pieces)
    column[...] = total
    middle_kernel(parts_y, members, place, turned, old, *[slopes[m] for m in members], sums)


def rim_taps(place, odd_row):
    return jnp.where(place[0] == 0, 0, 2), jnp.where(odd_row == 0, 2, 0)


def last_kernel(parts_y, member, factor, place, weight, turned, old, partial, column, pieces, *rest):
    input_grad, kernel_grad, bias_grad, grid, sums, sent = rest
    _, half_x, span_y, span_z, _ = pieces.shape
    lanes = pieces.shape[-1] // 2
    span_x = 2 * half_x
    copies = []

    def store(a, total):
        sums[a] = total * factor
        rows = 3 * lanes
        for b in range(3):
            here = pl.ds(b * rows, rows)
            copy = pltpu.make_async_copy(
                sums.at[a, here], kernel_grad.at[a, here], sent.at[a * 3 + b]
            )
            copy.start(priority=b % 2)
            copies.append(copy)

    add_terms(place, parts_y, (member,), (pieces,), turned, old, store)

    total = column[...] + channel_sum(pieces)
    bias_grad[...] = (total[:, :lanes] + total[:, lanes:]) * factor
    _, _, _, odd_row, _, x_row = rim_sides(place, span_x, span_y)
    has_odd = (place[1] != 0) & (place[1] != parts_y - 1)
    tap_x, tap_y = rim_taps(place, odd_row)
    grid[...] = partial[...]

    @pl.when(has_odd)
    def _():
        corner = facing(place, rows_of(place, pieces, facing_row(odd_row, span_y)))
        term = jnp.dot(corner, weight[tap_x * 3 + tap_y], preferred_element_type=F32)
        grid[x_row, odd_row] += term

    summed = grid[...].reshape(span_x * span_y, span_z, 3 * lanes)
    result = (
        shifted(summed[..., :lanes], -1)
        + summed[..., lanes : 2 * lanes]
        + shifted(summed[..., 2 * lanes :], 1)
    )
    input_grad[...] = result.reshape(-1, lanes).astype(BF16)
    for copy in copies:
        copy.wait()


def facing_row(row, span_y):
    return span_y - 1 - row


def exchange(x, axes, mask):
    return lax.ppermute(x, axes, [(i, i ^ mask) for i in range(lax.axis_size(axes))])


def body_gathered(inputs, weight, bias, cotangent):
    spans = inputs.shape[:3]
    span_x, span_y, span_z = spans
    local_ch, channels = weight.shape[3:]
    local = span_x * span_y * span_z
    parts_x, parts_y = lax.axis_size("gx"), lax.axis_size("gy")
    count = parts_x * parts_y
    shards = lax.axis_size("ch")
    axes = ("gx", "gy")
    factor = 1.0 / math.sqrt(local * count)
    place = jnp.stack([lax.axis_index(axis) for axis in ("gx", "gy", "ch")]).astype(jnp.int32)
    taps = weight.reshape(9, 3 * local_ch, channels)
    packing = (span_x // 2, span_y, span_z, 2 * local_ch)
    flat = (local // 2, 2 * local_ch)

    def call(kernel, name, outs, args, scratch=()):
        return pl.pallas_call(
            kernel,
            out_shape=[jax.ShapeDtypeStruct(shape, kind) for shape, kind in outs],
            in_specs=[SMEM if x is place else VMEM for x in args],
            out_specs=[VMEM] * len(outs),
            scratch_shapes=[pltpu.VMEM(shape, kind) for shape, kind in scratch],
            compiler_params=PARAMS,
            cost_estimate=pl.CostEstimate(flops=0, bytes_accessed=1024, transcendentals=0),
            name=name,
        )(*args)

    row = (span_x, span_z, local_ch)
    held, packed, even, odd, even_corner, odd_corner = pl.pallas_call(
        prepare_kernel,
        out_shape=[jax.ShapeDtypeStruct(inputs.shape, BF16), jax.ShapeDtypeStruct(packing, BF16)]
        + [jax.ShapeDtypeStruct(row, BF16)] * 2
        + [jax.ShapeDtypeStruct(row[1:], BF16)] * 2,
        in_specs=[SMEM, HBM],
        out_specs=[VMEM] * 6,
        scratch_shapes=[pltpu.SemaphoreType.DMA],
        compiler_params=PARAMS,
        name="prepare",
    )(place, pltpu.with_memory_space_constraint(inputs, pltpu.HBM))
    sources = (taps, cotangent.reshape(local, local_ch), bias.reshape(1, local_ch))
    taps, cotangent, bias = pl.pallas_call(
        stage_kernel,
        out_shape=[jax.ShapeDtypeStruct(x.shape, x.dtype) for x in sources],
        in_specs=[VMEM] + [HBM] * len(sources),
        out_specs=[VMEM] * len(sources),
        scratch_shapes=[pltpu.SemaphoreType.DMA((len(sources) + 8,))],
        compiler_params=PARAMS,
        name="stage",
    )(even_corner, *[pltpu.with_memory_space_constraint(x, pltpu.HBM) for x in sources])
    beside = exchange(packed, axes, parts_y)
    even = exchange(even, axes, 1)
    odd = exchange(odd, axes, 3)
    even_corner = exchange(even_corner, axes, parts_y + 1)
    odd_corner = exchange(odd_corner, axes, parts_y + 3)
    own, *others, pair = call(
        functools.partial(forward_kernel, parts_y),
        "forward",
        [(flat, F32)] + [(flat, BF16)] * (shards - 1) + [((2,) + packing, BF16)],
        [place, taps, held, packed, even, odd, beside, even_corner, odd_corner],
        [((span_x + 2, span_y + 2, span_z, 3 * local_ch), BF16), ((shards,) + flat, F32)],
    )
    others = [exchange(others[k - 1], "ch", k) for k in range(shards - 1, 0, -1)]
    activation, slope = call(
        slope_kernel,
        "slope",
        [((local, local_ch), BF16), (flat, BF16)],
        [own, *others, bias, cotangent],
    )
    rest = [exchange(slope, "ch", k) for k in range(1, shards)]
    rest = jnp.stack(rest).reshape((shards - 1,) + packing)
    piece = slope.reshape((1,) + packing)
    x, y = parts_y, 2
    beside_x = exchange(piece, axes, x)
    beside_y = exchange(jnp.concatenate([piece, pair]), axes, y)
    beside_y, beside_x, rest = lax.optimization_barrier((beside_y, beside_x, rest))
    column = jnp.concatenate([piece, rest])
    late_y, late_x = exchange(rest, axes, y), exchange(rest, axes, x)
    sibling = exchange(jnp.concatenate([column, pair, beside_y[1:]]), axes, 1)
    turned_shape = (parts_y, 9 * local_ch, (parts_x * span_x + 2) * span_y * span_z)
    sums_shape = (3, 9 * local_ch, channels)
    turned, sums, taps = call(
        functools.partial(first_kernel, parts_x, parts_y),
        "first",
        [(turned_shape, BF16), (sums_shape, F32), ((9, channels, 3 * local_ch), BF16)],
        [place, taps, pair, beside_y, sibling, column],
        [((parts_x * span_x + 2, parts_y * span_y + 2, span_z, 3 * local_ch), BF16)],
    )
    slopes = {0: column, 1: sibling[:shards]}
    late_y, late_x, sums = lax.optimization_barrier((late_y, late_x, sums))
    slopes[y] = jnp.concatenate([beside_y[:1], late_y])
    slopes[x] = jnp.concatenate([beside_x, late_x])
    middle = shards // 2
    diagonal = [exchange(slopes[x][:middle], axes, y), exchange(slopes[y][middle:], axes, x)]
    across = [exchange(slopes[m], axes, 1) for m in (y, x)]
    grid_shape = spans + (3 * local_ch,)
    partial, sums = call(
        functools.partial(second_kernel, parts_y, (y, x)),
        "second",
        [(grid_shape, F32), (sums_shape, F32)],
        [place, taps, turned, sums, column, sibling, slopes[y], slopes[x]],
        [((span_x + 2, span_y + 2, span_z, channels), BF16)],
    )
    slopes[y + 1], slopes[x + 1] = across
    (sums,) = call(
        functools.partial(middle_kernel, parts_y, (y + 1, x + 1)),
        "third",
        [(sums_shape, F32)],
        [place, turned, sums, *across],
    )
    *diagonal, sums = lax.optimization_barrier((*diagonal, sums))
    slopes[x + y] = jnp.concatenate(diagonal)
    final = exchange(slopes[x + y], axes, 1)
    partial, column, sums = call(
        functools.partial(rim_kernel, parts_y, (x + y,)),
        "rim",
        [(grid_shape, F32), ((1, 2 * local_ch), F32), (sums_shape, F32)],
        [place, taps, turned, sums, partial] + [slopes[m] for m in range(count - 1)],
        [((span_y + 2, span_z, channels), BF16), ((span_x + 2, span_z, channels), BF16)],
    )
    args = [place, taps, turned, sums, partial, column, final]
    input_grad, kernel_grad, bias_grad = pl.pallas_call(
        functools.partial(last_kernel, parts_y, x + y + 1, factor),
        out_shape=[
            jax.ShapeDtypeStruct((local, local_ch), BF16),
            jax.ShapeDtypeStruct(sums_shape, F32),
            jax.ShapeDtypeStruct((1, local_ch), F32),
        ],
        in_specs=[SMEM] + [VMEM] * (len(args) - 1),
        out_specs=[VMEM, HBM, VMEM],
        scratch_shapes=[
            pltpu.VMEM(grid_shape, F32),
            pltpu.VMEM(sums_shape, F32),
            pltpu.SemaphoreType.DMA((9,)),
        ],
        compiler_params=PARAMS,
        name="last",
    )(*args)
    return (
        activation.reshape(inputs.shape),
        input_grad.reshape(inputs.shape),
        kernel_grad.reshape(weight.shape),
        bias_grad.reshape(local_ch),
    )


def solution(mesh):
    few = (mesh.shape["gx"], mesh.shape["gy"]) == (2, 4)
    return jax.shard_map(
        body_gathered if few else body_reduced,
        mesh=mesh,
        in_specs=(
            P("gx", "gy", None, "ch"),
            P(None, None, None, "ch", None),
            P("ch"),
            P("gx", "gy", None, "ch"),
        ),
        out_specs=(
            P("gx", "gy", None, "ch"),
            P("gx", "gy", None, "ch"),
            P(None, None, None, "ch", None),
            P("ch"),
        ),
        check_vma=False,
    )
```

```python
import functools
import math

import jax
import jax.numpy as jnp
from jax import lax
from jax.experimental import pallas as pl
from jax.experimental.pallas import tpu as pltpu
from jax.sharding import PartitionSpec as P

VMEM = pl.BlockSpec(memory_space=pltpu.VMEM)
HBM = pl.BlockSpec(memory_space=pltpu.HBM)
SMEM = pl.BlockSpec(memory_space=pltpu.SMEM)
PARAMS = pltpu.CompilerParams(vmem_limit_bytes=24 * 1024 * 1024)
F32 = jnp.float32
BF16 = jnp.bfloat16


def with_halo(x, sides, width):
    for axis, dim in sides:
        devices, length = (lax.axis_size(axis), x.shape[dim])
        up = [(i, (i + 1) % devices) for i in range(devices - 1)]
        down = [(j, i) for i, j in up]
        last = lax.slice_in_dim(x, length - width, length, axis=dim)
        initial = lax.slice_in_dim(x, 0, width, axis=dim)
        before = lax.ppermute(last, axis, up)
        after = lax.ppermute(initial, axis, down)
        x = jnp.concatenate([before, x, after], axis=dim)
    return x


def body_reduced(inputs, weight, bias, cotangent):
    span_x, span_y, span_z, local_ch = inputs.shape
    widest = weight.shape[4]
    local_cells = span_x * span_y * span_z
    offsets = [(a, b, c) for a in range(3) for b in range(3) for c in range(3)]
    depth_pad = ((0, 0), (0, 0), (1, 1), (0, 0))
    rimmed = with_halo(inputs, (("gx", 0), ("gy", 1)), 1)
    padded = jnp.pad(rimmed, depth_pad)
    blocks = []
    for a, b, c in offsets:
        blocks.append(
            padded[a : a + span_x, b : b + span_y, c : c + span_z].reshape(local_cells, local_ch)
        )
    patches = jnp.concatenate(blocks, axis=1)
    flat_weight = weight.reshape(27 * local_ch, widest)
    summed = lax.psum_scatter(
        lax.dot_general(flat_weight, patches, (((0,), (1,)), ((), ())), preferred_element_type=F32),
        "ch",
        scatter_dimension=0,
        tiled=True,
    ).T
    summed = summed + bias.astype(F32)[None, :]
    activation = jax.nn.silu(summed).astype(BF16).reshape(span_x, span_y, span_z, local_ch)
    sigmoid_pre = jax.nn.sigmoid(summed)
    slope = (
        cotangent.reshape(local_cells, local_ch).astype(F32)
        * sigmoid_pre
        * (1.0 + summed * (1.0 - sigmoid_pre))
    ).astype(BF16)
    local_bias = jnp.sum(slope.astype(F32), axis=0)
    slope_grid = slope.reshape(span_x, span_y, span_z, local_ch)
    weight_turned = jnp.transpose(weight.reshape(27, local_ch, widest), (0, 2, 1))
    slope_rimmed = with_halo(slope_grid, (("gx", 0), ("gy", 1)), 1)
    piece = lax.all_gather(slope_rimmed, "ch", axis=3, tiled=True)
    extended = jnp.pad(piece, depth_pad)
    running = jnp.zeros((local_cells, local_ch), F32)
    for index, (a, b, c) in enumerate(offsets):
        a, b, c = (2 - a, 2 - b, 2 - c)
        cut = extended[a : a + span_x, b : b + span_y, c : c + span_z].reshape(local_cells, widest)
        running = running + jnp.dot(cut, weight_turned[index], preferred_element_type=F32)
    interior = piece[1 : 1 + span_x, 1 : 1 + span_y].reshape(local_cells, widest)
    product = lax.dot_general(
        patches, interior, (((0,), (0,)), ((), ())), preferred_element_type=F32
    )
    total_cells = local_cells * lax.axis_size("gx") * lax.axis_size("gy")
    factor = 1.0 / math.sqrt(total_cells)
    kernel_total, bias_total = lax.psum((product * factor, local_bias * factor), ("gx", "gy"))
    input_grad = running.astype(BF16).reshape(span_x, span_y, span_z, local_ch)
    return (activation, input_grad, kernel_total.reshape(3, 3, 3, local_ch, widest), bias_total)


def shifted(v, by):
    depth = v.shape[1]
    row = lax.broadcasted_iota(jnp.int32, v.shape, 1)
    if by == 1:
        return jnp.where(row == 0, 0.0, pltpu.roll(v, 1, 1))
    return jnp.where(row == depth - 1, 0.0, pltpu.roll(v, depth - 1, 1))


def rim_sides(place, span_x, span_y):
    first = place[1] % 2 == 0
    even_at = jnp.where(first, span_y + 1, 0)
    odd_at = jnp.where(first, 0, span_y + 1)
    even_row = jnp.where(first, span_y - 1, 0)
    odd_row = jnp.where(first, 0, span_y - 1)
    x_at = jnp.where(place[0] == 0, span_x + 1, 0)
    x_row = jnp.where(place[0] == 0, span_x - 1, 0)
    return even_at, odd_at, even_row, odd_row, x_at, x_row


def prepare_kernel(place, source, inputs, packed, even, odd, even_corner, odd_corner, arrived):
    copy = pltpu.make_async_copy(source, inputs, arrived)
    copy.start()
    copy.wait()
    span_x, span_y, _, _ = inputs.shape
    half = span_x // 2
    _, _, even_row, odd_row, _, x_row = rim_sides(place, span_x, span_y)
    even[...] = inputs[:, even_row]
    odd[...] = inputs[:, odd_row]
    even_corner[...] = inputs[x_row, even_row]
    odd_corner[...] = inputs[x_row, odd_row]
    packed[...] = jnp.concatenate([inputs[:half], inputs[half:]], axis=3)


def stage_kernel(after, *rest):
    count = (len(rest) - 1) // 2
    sources, targets, arrived = rest[:count], rest[count : 2 * count], rest[-1]
    copies = []
    for source, target in zip(sources, targets):
        parts = source.shape[0] if len(source.shape) == 3 else 1
        for n in range(parts):
            here = pl.ds(n, 1) if parts > 1 else slice(None)
            copies.append(
                pltpu.make_async_copy(source.at[here], target.at[here], arrived.at[len(copies)])
            )
    for copy in copies:
        copy.start()
    for copy in copies:
        copy.wait()


def forward_kernel(
    parts_y, place, weight, inputs, packed, even, odd, beside, even_corner, odd_corner, own, *rest
):
    *others, pair, window, blocks = rest
    span_x, span_y, span_z, lanes = inputs.shape
    half_x = span_x // 2
    half = half_x * span_y * span_z
    even_at, odd_at, _, _, x_at, _ = rim_sides(place, span_x, span_y)

    def spread(v):
        flat = v.astype(F32).reshape(-1, span_z, lanes)
        joined = jnp.concatenate([shifted(flat, 1), flat, shifted(flat, -1)], axis=2)
        return joined.astype(BF16).reshape(v.shape[:-1] + (3 * lanes,))

    nothing = jnp.zeros((span_y + 2, span_z, 3 * lanes), BF16)
    window[0] = nothing
    window[span_x + 1] = nothing
    window[1 : span_x + 1, 1 : span_y + 1] = spread(inputs[...])
    window[1 : span_x + 1, even_at] = spread(even[...])
    has_odd = (place[1] != 0) & (place[1] != parts_y - 1)
    window[1 : span_x + 1, odd_at] = jnp.where(has_odd, spread(odd[...]), jnp.zeros((), BF16))
    across = jnp.where(place[0] == 0, beside[0][..., :lanes], beside[half_x - 1][..., lanes:])
    window[x_at, 1 : span_y + 1] = spread(across)
    window[x_at, even_at] = spread(even_corner[...])
    window[x_at, odd_at] = jnp.where(has_odd, spread(odd_corner[...]), jnp.zeros((), BF16))
    sums = []
    for h in range(2):
        total = None
        for a in range(3):
            for b in range(3):
                cut = window[a + h * half_x : a + (h + 1) * half_x, b : b + span_y]
                term = jnp.dot(
                    cut.reshape(half, 3 * lanes), weight[a * 3 + b], preferred_element_type=F32
                )
                total = term if total is None else total + term
        sums.append(total)
    for d in range(weight.shape[2] // lanes):
        cut = slice(d * lanes, (d + 1) * lanes)
        blocks[d] = jnp.concatenate([sums[0][:, cut], sums[1][:, cut]], axis=1)
    own[...] = blocks[place[2]]
    for k, other in enumerate(others):
        other[...] = blocks[place[2] ^ (k + 1)].astype(BF16)
    pair[0] = packed[...]
    pair[1] = beside[...]


def slope_kernel(own, *rest):
    *others, bias, cotangent, active, slope = rest
    half = cotangent.shape[0] // 2
    summed = own[...]
    for other in others:
        summed = summed + other[...].astype(F32)
    offset = bias[...].astype(F32)
    summed = summed + jnp.concatenate([offset, offset], axis=1)
    sigmoid = jax.nn.sigmoid(summed)
    active[...] = (summed * sigmoid).astype(BF16)
    upstream = jnp.concatenate([cotangent[:half], cotangent[half:]], axis=1).astype(F32)
    slope[...] = (upstream * sigmoid * (1.0 + summed * (1.0 - sigmoid))).astype(BF16)


def ordered_halves(place, pieces):
    shards, _, _, _, lanes = pieces.shape
    lanes = lanes // 2
    ordered = [pieces[place[2] ^ j] for j in range(shards)]
    return [
        jnp.concatenate([piece[..., h * lanes : (h + 1) * lanes] for piece in ordered], axis=-1)
        for h in range(2)
    ]


def add_terms(place, parts_y, members, slopes, turned, old, store):
    operands = []
    for m, pieces in zip(members, slopes):
        shards, half_x, span_y, span_z, lanes = pieces.shape
        channels, row = shards * lanes // 2, span_y * span_z
        right = jnp.concatenate(
            [part.reshape(half_x * row, channels) for part in ordered_halves(place, pieces)]
        )
        x0, y0 = (place[0] ^ (m // parts_y)) * 2 * half_x, place[1] ^ (m % parts_y)
        operands.append((x0, y0, row, right))
    for a in range(3):
        total = None if old is None else old[a]
        for x0, y0, row, right in operands:
            left = turned[y0, :, pl.ds(pl.multiple_of((x0 + a) * row, row), right.shape[0])]
            term = jnp.dot(left, right, preferred_element_type=F32)
            total = term if total is None else total + term
        store(a, total)


def first_kernel(parts_x, parts_y, place, weight, active, pair, beside_y, sibling, column, *rest):
    activation, turned, sums, weight_turned, volume, unpacked, sent = rest
    half, lanes = active.shape[0], active.shape[1] // 2
    unpacked[:half] = active[:, :lanes]
    unpacked[half:] = active[:, lanes:]
    copy = pltpu.make_async_copy(unpacked, activation, sent)
    copy.start()
    shards, half_x, span_y, span_z, lanes = column.shape
    cells = [(0, pair, 0), (parts_y, pair, 1), (2, beside_y, 1), (parts_y + 2, beside_y, 2)]
    cells += [(m ^ 1, sibling, shards + n) for n, (m, _, _) in enumerate(cells)]
    span_x, lanes = 2 * half_x, lanes // 2
    rows_x, rows_y = parts_x * span_x, parts_y * span_y
    width = 3 * lanes
    zero_x = jnp.zeros((1, rows_y + 2, span_z, width), BF16)
    zero_y = jnp.zeros((rows_x + 2, 1, span_z, width), BF16)
    volume[0:1] = zero_x
    volume[rows_x + 1 : rows_x + 2] = zero_x
    volume[:, 0:1] = zero_y
    volume[:, rows_y + 1 : rows_y + 2] = zero_y
    for m, array, n in cells:
        x0, y0 = (place[0] ^ (m // parts_y)) * span_x, (place[1] ^ (m % parts_y)) * span_y
        v = array[n].astype(F32).reshape(half_x * span_y, span_z, 2 * lanes)
        low, high = shifted(v, 1), shifted(v, -1)
        for h in range(2):
            cut = slice(h * lanes, (h + 1) * lanes)
            joined = jnp.concatenate([low[..., cut], v[..., cut], high[..., cut]], axis=2)
            volume[pl.ds(x0 + 1 + h * half_x, half_x), pl.ds(y0 + 1, span_y)] = joined.astype(
                BF16
            ).reshape(half_x, span_y, span_z, width)
    for y in range(parts_y):
        for b in range(3):
            cut = volume[:, y * span_y + b : (y + 1) * span_y + b]
            turned[y, b * width : (b + 1) * width] = cut.reshape(-1, width).T

    def store(a, total):
        sums[a] = total

    for tap in range(weight.shape[0]):
        weight_turned[tap] = weight[tap].T
    members = (0, 1)
    add_terms(place, parts_y, members, (column, sibling.at[:shards]), turned, None, store)
    copy.wait()


def rows_of(place, pieces, row):
    shards, lanes = column_shape(pieces)
    ordered = [pieces[place[2] ^ j, :, row] for j in range(shards)]
    return [
        jnp.concatenate([piece[..., h * lanes : (h + 1) * lanes] for piece in ordered], axis=-1)
        for h in range(2)
    ]


def column_shape(pieces):
    return pieces.shape[0], pieces.shape[-1] // 2


def second_kernel(
    parts_y, members, place, weight, turned, old, column, sibling, *rest
):
    *slopes, partial, sums, window = rest
    shards, half_x, span_y, span_z, _ = column.shape
    span_x, half = 2 * half_x, half_x * span_y * span_z
    even_at, _, even_row, _, _, _ = rim_sides(place, span_x, span_y)
    window[...] = jnp.zeros(window.shape, BF16)
    beside = rows_of(place, sibling.at[:shards], facing_row(even_row, span_y))
    for h, own in enumerate(ordered_halves(place, column)):
        window[1 + h * half_x : 1 + (h + 1) * half_x, 1 : span_y + 1] = own
        window[1 + h * half_x : 1 + (h + 1) * half_x, even_at] = beside[h]
    for h in range(2):
        total = None
        for a in range(3):
            for b in range(3):
                cut = window[
                    2 - a + h * half_x : 2 - a + (h + 1) * half_x, 2 - b : 2 - b + span_y
                ]
                term = jnp.dot(
                    cut.reshape(half, cut.shape[-1]), weight[a * 3 + b], preferred_element_type=F32
                )
                total = term if total is None else total + term
        partial[h * half_x : (h + 1) * half_x] = total.reshape((half_x,) + partial.shape[1:])
    middle_kernel(parts_y, members, place, turned, old, *slopes, sums)


def middle_kernel(parts_y, members, place, turned, old, *rest):
    *slopes, sums = rest

    def store(a, total):
        sums[a] = total

    add_terms(place, parts_y, members, slopes, turned, old, store)


def facing(place, halves):
    low, high = halves
    return jnp.where(place[0] == 0, low[0], high[-1])


def channel_sum(pieces):
    mine = pieces[0].astype(F32).reshape(-1, pieces.shape[-1])
    return jnp.sum(mine, axis=0, keepdims=True)


def rim_kernel(parts_y, members, place, weight, turned, old, partial, *rest):
    *slopes, grid, column, sums, rim_x, rim_y = rest
    shards, half_x, span_y, span_z, _ = slopes[0].shape
    span_x, channels = 2 * half_x, rim_x.shape[-1]
    even_at, odd_at, even_row, odd_row, _, x_row = rim_sides(place, span_x, span_y)
    has_odd = (place[1] != 0) & (place[1] != parts_y - 1)
    rim_x[...] = jnp.zeros(rim_x.shape, BF16)
    rim_y[...] = jnp.zeros(rim_y.shape, BF16)
    rim_x[1 : span_y + 1] = facing(place, ordered_halves(place, slopes[parts_y]))
    even = rows_of(place, slopes[parts_y + 1], facing_row(even_row, span_y))
    rim_x[even_at] = facing(place, even)

    @pl.when(has_odd)
    def _():
        odd = rows_of(place, slopes[3], facing_row(odd_row, span_y))
        for h, rows in enumerate(odd):
            rim_y[1 + h * half_x : 1 + (h + 1) * half_x] = rows

    grid[...] = partial[...]
    tap_x, tap_y = rim_taps(place, odd_row)
    total = None
    for b in range(3):
        cut = rim_x[2 - b : 2 - b + span_y].reshape(span_y * span_z, channels)
        term = jnp.dot(cut, weight[tap_x * 3 + b], preferred_element_type=F32)
        total = term if total is None else total + term
    grid[x_row] += total.reshape((span_y,) + grid.shape[2:])
    total = None
    for a in range(3):
        cut = rim_y[2 - a : 2 - a + span_x].reshape(span_x * span_z, channels)
        term = jnp.dot(cut, weight[a * 3 + tap_y], preferred_element_type=F32)
        total = term if total is None else total + term
    grid[:, odd_row] += total.reshape((span_x,) + grid.shape[2:])
    total = channel_sum(slopes[0])
    for pieces in slopes[1:]:
        total = total + channel_sum(pieces)
    column[...] = total
    middle_kernel(parts_y, members, place, turned, old, *[slopes[m] for m in members], sums)


def rim_taps(place, odd_row):
    return jnp.where(place[0] == 0, 0, 2), jnp.where(odd_row == 0, 2, 0)


def last_kernel(parts_y, member, factor, place, weight, turned, old, partial, column, pieces, *rest):
    input_grad, kernel_grad, bias_grad, grid, sums, cells, bias, sent = rest
    _, half_x, span_y, span_z, _ = pieces.shape
    lanes = pieces.shape[-1] // 2
    span_x = 2 * half_x
    copies = []

    def send(source, target):
        copies.append(pltpu.make_async_copy(source, target, sent.at[len(copies)]))
        copies[-1].start()

    def store(a, total):
        sums[a] = total * factor
        send(sums.at[a], kernel_grad.at[a])

    add_terms(place, parts_y, (member,), (pieces,), turned, old, store)

    _, _, _, odd_row, _, x_row = rim_sides(place, span_x, span_y)
    has_odd = (place[1] != 0) & (place[1] != parts_y - 1)
    tap_x, tap_y = rim_taps(place, odd_row)
    grid[...] = partial[...]

    @pl.when(has_odd)
    def _():
        corner = facing(place, rows_of(place, pieces, facing_row(odd_row, span_y)))
        term = jnp.dot(corner, weight[tap_x * 3 + tap_y], preferred_element_type=F32)
        grid[x_row, odd_row] += term

    summed = grid[...].reshape(span_x * span_y, span_z, 3 * lanes)
    result = (
        shifted(summed[..., :lanes], -1)
        + summed[..., lanes : 2 * lanes]
        + shifted(summed[..., 2 * lanes :], 1)
    )
    cells[...] = result.reshape(-1, lanes).astype(BF16)
    send(cells, input_grad)
    total = column[...] + channel_sum(pieces)
    bias[...] = (total[:, :lanes] + total[:, lanes:]) * factor
    send(bias, bias_grad)
    for copy in copies:
        copy.wait()


def facing_row(row, span_y):
    return span_y - 1 - row


def exchange(x, axes, mask):
    return lax.ppermute(x, axes, [(i, i ^ mask) for i in range(lax.axis_size(axes))])


def body_gathered(inputs, weight, bias, cotangent):
    spans = inputs.shape[:3]
    span_x, span_y, span_z = spans
    local_ch, channels = weight.shape[3:]
    local = span_x * span_y * span_z
    parts_x, parts_y = lax.axis_size("gx"), lax.axis_size("gy")
    count = parts_x * parts_y
    shards = lax.axis_size("ch")
    axes = ("gx", "gy")
    factor = 1.0 / math.sqrt(local * count)
    place = jnp.stack([lax.axis_index(axis) for axis in ("gx", "gy", "ch")]).astype(jnp.int32)
    taps = weight.reshape(9, 3 * local_ch, channels)
    packing = (span_x // 2, span_y, span_z, 2 * local_ch)
    flat = (local // 2, 2 * local_ch)

    def call(kernel, name, outs, args, scratch=()):
        return pl.pallas_call(
            kernel,
            out_shape=[jax.ShapeDtypeStruct(shape, kind) for shape, kind in outs],
            in_specs=[SMEM if x is place else VMEM for x in args],
            out_specs=[VMEM] * len(outs),
            scratch_shapes=[pltpu.VMEM(shape, kind) for shape, kind in scratch],
            compiler_params=PARAMS,
            cost_estimate=pl.CostEstimate(flops=0, bytes_accessed=1024, transcendentals=0),
            name=name,
        )(*args)

    row = (span_x, span_z, local_ch)
    held, packed, even, odd, even_corner, odd_corner = pl.pallas_call(
        prepare_kernel,
        out_shape=[jax.ShapeDtypeStruct(inputs.shape, BF16), jax.ShapeDtypeStruct(packing, BF16)]
        + [jax.ShapeDtypeStruct(row, BF16)] * 2
        + [jax.ShapeDtypeStruct(row[1:], BF16)] * 2,
        in_specs=[SMEM, HBM],
        out_specs=[VMEM] * 6,
        scratch_shapes=[pltpu.SemaphoreType.DMA],
        compiler_params=PARAMS,
        name="prepare",
    )(place, pltpu.with_memory_space_constraint(inputs, pltpu.HBM))
    sources = (taps, cotangent.reshape(local, local_ch), bias.reshape(1, local_ch))
    taps, cotangent, bias = pl.pallas_call(
        stage_kernel,
        out_shape=[jax.ShapeDtypeStruct(x.shape, x.dtype) for x in sources],
        in_specs=[VMEM] + [HBM] * len(sources),
        out_specs=[VMEM] * len(sources),
        scratch_shapes=[pltpu.SemaphoreType.DMA((len(sources) + 8,))],
        compiler_params=PARAMS,
        name="stage",
    )(even_corner, *[pltpu.with_memory_space_constraint(x, pltpu.HBM) for x in sources])
    beside = exchange(packed, axes, parts_y)
    even = exchange(even, axes, 1)
    odd = exchange(odd, axes, 3)
    even_corner = exchange(even_corner, axes, parts_y + 1)
    odd_corner = exchange(odd_corner, axes, parts_y + 3)
    own, *others, pair = call(
        functools.partial(forward_kernel, parts_y),
        "forward",
        [(flat, F32)] + [(flat, BF16)] * (shards - 1) + [((2,) + packing, BF16)],
        [place, taps, held, packed, even, odd, beside, even_corner, odd_corner],
        [((span_x + 2, span_y + 2, span_z, 3 * local_ch), BF16), ((shards,) + flat, F32)],
    )
    others = [exchange(others[k - 1], "ch", k) for k in range(shards - 1, 0, -1)]
    active, slope = call(
        slope_kernel,
        "slope",
        [(flat, BF16), (flat, BF16)],
        [own, *others, bias, cotangent],
    )
    rest = [exchange(slope, "ch", k) for k in range(1, shards)]
    rest = jnp.stack(rest).reshape((shards - 1,) + packing)
    piece = slope.reshape((1,) + packing)
    x, y = parts_y, 2
    beside_x = exchange(piece, axes, x)
    beside_y = exchange(jnp.concatenate([piece, pair]), axes, y)
    beside_y, beside_x, rest = lax.optimization_barrier((beside_y, beside_x, rest))
    column = jnp.concatenate([piece, rest])
    late_y, late_x = exchange(rest, axes, y), exchange(rest, axes, x)
    sibling = exchange(jnp.concatenate([column, pair, beside_y[1:]]), axes, 1)
    turned_shape = (parts_y, 9 * local_ch, (parts_x * span_x + 2) * span_y * span_z)
    sums_shape = (3, 9 * local_ch, channels)
    first_outs = [((local, local_ch), BF16), (turned_shape, BF16), (sums_shape, F32)]
    first_outs += [((9, channels, 3 * local_ch), BF16)]
    args = [place, taps, active, pair, beside_y, sibling, column]
    activation, turned, sums, taps = pl.pallas_call(
        functools.partial(first_kernel, parts_x, parts_y),
        out_shape=[jax.ShapeDtypeStruct(shape, kind) for shape, kind in first_outs],
        in_specs=[SMEM] + [VMEM] * (len(args) - 1),
        out_specs=[HBM] + [VMEM] * 3,
        scratch_shapes=[
            pltpu.VMEM((parts_x * span_x + 2, parts_y * span_y + 2, span_z, 3 * local_ch), BF16),
            pltpu.VMEM((local, local_ch), BF16),
            pltpu.SemaphoreType.DMA,
        ],
        compiler_params=PARAMS,
        cost_estimate=pl.CostEstimate(flops=0, bytes_accessed=1024, transcendentals=0),
        name="first",
    )(*args)
    slopes = {0: column, 1: sibling[:shards]}
    late_y, late_x, sums = lax.optimization_barrier((late_y, late_x, sums))
    slopes[y] = jnp.concatenate([beside_y[:1], late_y])
    slopes[x] = jnp.concatenate([beside_x, late_x])
    middle = shards // 2
    diagonal = [exchange(slopes[x][:middle], axes, y), exchange(slopes[y][middle:], axes, x)]
    across = [exchange(slopes[m], axes, 1) for m in (y, x)]
    grid_shape = spans + (3 * local_ch,)
    partial, sums = call(
        functools.partial(second_kernel, parts_y, (y, x)),
        "second",
        [(grid_shape, F32), (sums_shape, F32)],
        [place, taps, turned, sums, column, sibling, slopes[y], slopes[x]],
        [((span_x + 2, span_y + 2, span_z, channels), BF16)],
    )
    slopes[y + 1], slopes[x + 1] = across
    (sums,) = call(
        functools.partial(middle_kernel, parts_y, (y + 1, x + 1)),
        "third",
        [(sums_shape, F32)],
        [place, turned, sums, *across],
    )
    *diagonal, sums = lax.optimization_barrier((*diagonal, sums))
    slopes[x + y] = jnp.concatenate(diagonal)
    final = exchange(slopes[x + y], axes, 1)
    partial, column, sums = call(
        functools.partial(rim_kernel, parts_y, (x + y,)),
        "rim",
        [(grid_shape, F32), ((1, 2 * local_ch), F32), (sums_shape, F32)],
        [place, taps, turned, sums, partial] + [slopes[m] for m in range(count - 1)],
        [((span_y + 2, span_z, channels), BF16), ((span_x + 2, span_z, channels), BF16)],
    )
    args = [place, taps, turned, sums, partial, column, final]
    input_grad, kernel_grad, bias_grad = pl.pallas_call(
        functools.partial(last_kernel, parts_y, x + y + 1, factor),
        out_shape=[
            jax.ShapeDtypeStruct((local, local_ch), BF16),
            jax.ShapeDtypeStruct(sums_shape, F32),
            jax.ShapeDtypeStruct((1, local_ch), F32),
        ],
        in_specs=[SMEM] + [VMEM] * (len(args) - 1),
        out_specs=[HBM] * 3,
        scratch_shapes=[
            pltpu.VMEM(grid_shape, F32),
            pltpu.VMEM(sums_shape, F32),
            pltpu.VMEM((local, local_ch), BF16),
            pltpu.VMEM((1, local_ch), F32),
            pltpu.SemaphoreType.DMA((5,)),
        ],
        compiler_params=PARAMS,
        name="last",
    )(*args)
    return (
        activation.reshape(inputs.shape),
        input_grad.reshape(inputs.shape),
        kernel_grad.reshape(weight.shape),
        bias_grad.reshape(local_ch),
    )


def solution(mesh):
    few = (mesh.shape["gx"], mesh.shape["gy"]) == (2, 4)
    return jax.shard_map(
        body_gathered if few else body_reduced,
        mesh=mesh,
        in_specs=(
            P("gx", "gy", None, "ch"),
            P(None, None, None, "ch", None),
            P("ch"),
            P("gx", "gy", None, "ch"),
        ),
        out_specs=(
            P("gx", "gy", None, "ch"),
            P("gx", "gy", None, "ch"),
            P(None, None, None, "ch", None),
            P("ch"),
        ),
        check_vma=False,
    )
```

```python
import functools
import math

import jax
import jax.numpy as jnp
from jax import lax
from jax.experimental import pallas as pl
from jax.experimental.pallas import tpu as pltpu
from jax.sharding import PartitionSpec as P

VMEM = pl.BlockSpec(memory_space=pltpu.VMEM)
HBM = pl.BlockSpec(memory_space=pltpu.HBM)
SMEM = pl.BlockSpec(memory_space=pltpu.SMEM)
PARAMS = pltpu.CompilerParams(vmem_limit_bytes=24 * 1024 * 1024)
F32 = jnp.float32
BF16 = jnp.bfloat16


def with_halo(x, sides, width):
    for axis, dim in sides:
        devices, length = (lax.axis_size(axis), x.shape[dim])
        up = [(i, (i + 1) % devices) for i in range(devices - 1)]
        down = [(j, i) for i, j in up]
        last = lax.slice_in_dim(x, length - width, length, axis=dim)
        initial = lax.slice_in_dim(x, 0, width, axis=dim)
        before = lax.ppermute(last, axis, up)
        after = lax.ppermute(initial, axis, down)
        x = jnp.concatenate([before, x, after], axis=dim)
    return x


def body_reduced(inputs, weight, bias, cotangent):
    span_x, span_y, span_z, local_ch = inputs.shape
    widest = weight.shape[4]
    local_cells = span_x * span_y * span_z
    offsets = [(a, b, c) for a in range(3) for b in range(3) for c in range(3)]
    depth_pad = ((0, 0), (0, 0), (1, 1), (0, 0))
    rimmed = with_halo(inputs, (("gx", 0), ("gy", 1)), 1)
    padded = jnp.pad(rimmed, depth_pad)
    blocks = []
    for a, b, c in offsets:
        blocks.append(
            padded[a : a + span_x, b : b + span_y, c : c + span_z].reshape(local_cells, local_ch)
        )
    patches = jnp.concatenate(blocks, axis=1)
    flat_weight = weight.reshape(27 * local_ch, widest)
    summed = lax.psum_scatter(
        lax.dot_general(flat_weight, patches, (((0,), (1,)), ((), ())), preferred_element_type=F32),
        "ch",
        scatter_dimension=0,
        tiled=True,
    ).T
    summed = summed + bias.astype(F32)[None, :]
    activation = jax.nn.silu(summed).astype(BF16).reshape(span_x, span_y, span_z, local_ch)
    sigmoid_pre = jax.nn.sigmoid(summed)
    slope = (
        cotangent.reshape(local_cells, local_ch).astype(F32)
        * sigmoid_pre
        * (1.0 + summed * (1.0 - sigmoid_pre))
    ).astype(BF16)
    local_bias = jnp.sum(slope.astype(F32), axis=0)
    slope_grid = slope.reshape(span_x, span_y, span_z, local_ch)
    weight_turned = jnp.transpose(weight.reshape(27, local_ch, widest), (0, 2, 1))
    slope_rimmed = with_halo(slope_grid, (("gx", 0), ("gy", 1)), 1)
    piece = lax.all_gather(slope_rimmed, "ch", axis=3, tiled=True)
    extended = jnp.pad(piece, depth_pad)
    running = jnp.zeros((local_cells, local_ch), F32)
    for index, (a, b, c) in enumerate(offsets):
        a, b, c = (2 - a, 2 - b, 2 - c)
        cut = extended[a : a + span_x, b : b + span_y, c : c + span_z].reshape(local_cells, widest)
        running = running + jnp.dot(cut, weight_turned[index], preferred_element_type=F32)
    interior = piece[1 : 1 + span_x, 1 : 1 + span_y].reshape(local_cells, widest)
    product = lax.dot_general(
        patches, interior, (((0,), (0,)), ((), ())), preferred_element_type=F32
    )
    total_cells = local_cells * lax.axis_size("gx") * lax.axis_size("gy")
    factor = 1.0 / math.sqrt(total_cells)
    kernel_total, bias_total = lax.psum((product * factor, local_bias * factor), ("gx", "gy"))
    input_grad = running.astype(BF16).reshape(span_x, span_y, span_z, local_ch)
    return (activation, input_grad, kernel_total.reshape(3, 3, 3, local_ch, widest), bias_total)


def shifted(v, by):
    depth = v.shape[1]
    row = lax.broadcasted_iota(jnp.int32, v.shape, 1)
    if by == 1:
        return jnp.where(row == 0, 0.0, pltpu.roll(v, 1, 1))
    return jnp.where(row == depth - 1, 0.0, pltpu.roll(v, depth - 1, 1))


def rim_sides(place, span_x, span_y):
    first = place[1] % 2 == 0
    even_at = jnp.where(first, span_y + 1, 0)
    odd_at = jnp.where(first, 0, span_y + 1)
    even_row = jnp.where(first, span_y - 1, 0)
    odd_row = jnp.where(first, 0, span_y - 1)
    x_at = jnp.where(place[0] == 0, span_x + 1, 0)
    x_row = jnp.where(place[0] == 0, span_x - 1, 0)
    return even_at, odd_at, even_row, odd_row, x_at, x_row


def prepare_kernel(
    place, source, weight_source, inputs, weight, packed, even, odd, even_corner, odd_corner, arrived
):
    copies = [pltpu.make_async_copy(source, inputs, arrived.at[0])]
    for n in range(weight.shape[0]):
        copies.append(
            pltpu.make_async_copy(weight_source.at[n], weight.at[n], arrived.at[n + 1])
        )
    for copy in copies:
        copy.start()
    copies[0].wait()
    span_x, span_y, _, _ = inputs.shape
    half = span_x // 2
    _, _, even_row, odd_row, _, x_row = rim_sides(place, span_x, span_y)
    even[...] = inputs[:, even_row]
    odd[...] = inputs[:, odd_row]
    even_corner[...] = inputs[x_row, even_row]
    odd_corner[...] = inputs[x_row, odd_row]
    packed[...] = jnp.concatenate([inputs[:half], inputs[half:]], axis=3)
    for copy in copies[1:]:
        copy.wait()


def stage_kernel(after, weight, cotangent_source, bias_source, cotangent, bias, weight_turned, arrived):
    copies = [
        pltpu.make_async_copy(cotangent_source, cotangent, arrived.at[0]),
        pltpu.make_async_copy(bias_source, bias, arrived.at[1]),
    ]
    for copy in copies:
        copy.start()
    for tap in range(weight.shape[0]):
        weight_turned[tap] = weight[tap].T
    for copy in copies:
        copy.wait()


def forward_kernel(
    parts_y, place, weight, inputs, packed, even, odd, beside, even_corner, odd_corner, own, *rest
):
    *others, pair, window, blocks = rest
    span_x, span_y, span_z, lanes = inputs.shape
    half_x = span_x // 2
    half = half_x * span_y * span_z
    even_at, odd_at, _, _, x_at, _ = rim_sides(place, span_x, span_y)

    def spread(v):
        flat = v.astype(F32).reshape(-1, span_z, lanes)
        joined = jnp.concatenate([shifted(flat, 1), flat, shifted(flat, -1)], axis=2)
        return joined.astype(BF16).reshape(v.shape[:-1] + (3 * lanes,))

    nothing = jnp.zeros((span_y + 2, span_z, 3 * lanes), BF16)
    window[0] = nothing
    window[span_x + 1] = nothing
    window[1 : span_x + 1, 1 : span_y + 1] = spread(inputs[...])
    window[1 : span_x + 1, even_at] = spread(even[...])
    has_odd = (place[1] != 0) & (place[1] != parts_y - 1)
    window[1 : span_x + 1, odd_at] = jnp.where(has_odd, spread(odd[...]), jnp.zeros((), BF16))
    across = jnp.where(place[0] == 0, beside[0][..., :lanes], beside[half_x - 1][..., lanes:])
    window[x_at, 1 : span_y + 1] = spread(across)
    window[x_at, even_at] = spread(even_corner[...])
    window[x_at, odd_at] = jnp.where(has_odd, spread(odd_corner[...]), jnp.zeros((), BF16))
    sums = []
    for h in range(2):
        total = None
        for a in range(3):
            for b in range(3):
                cut = window[a + h * half_x : a + (h + 1) * half_x, b : b + span_y]
                term = jnp.dot(
                    cut.reshape(half, 3 * lanes), weight[a * 3 + b], preferred_element_type=F32
                )
                total = term if total is None else total + term
        sums.append(total)
    for d in range(weight.shape[2] // lanes):
        cut = slice(d * lanes, (d + 1) * lanes)
        blocks[d] = jnp.concatenate([sums[0][:, cut], sums[1][:, cut]], axis=1)
    own[...] = blocks[place[2]]
    for k, other in enumerate(others):
        other[...] = blocks[place[2] ^ (k + 1)].astype(BF16)
    pair[0] = packed[...]
    pair[1] = beside[...]


def slope_kernel(own, *rest):
    *others, bias, cotangent, active, slope = rest
    half = cotangent.shape[0] // 2
    summed = own[...]
    for other in others:
        summed = summed + other[...].astype(F32)
    offset = bias[...].astype(F32)
    summed = summed + jnp.concatenate([offset, offset], axis=1)
    sigmoid = jax.nn.sigmoid(summed)
    active[...] = (summed * sigmoid).astype(BF16)
    upstream = jnp.concatenate([cotangent[:half], cotangent[half:]], axis=1).astype(F32)
    slope[...] = (upstream * sigmoid * (1.0 + summed * (1.0 - sigmoid))).astype(BF16)


def ordered_halves(place, pieces):
    shards, _, _, _, lanes = pieces.shape
    lanes = lanes // 2
    ordered = [pieces[place[2] ^ j] for j in range(shards)]
    return [
        jnp.concatenate([piece[..., h * lanes : (h + 1) * lanes] for piece in ordered], axis=-1)
        for h in range(2)
    ]


def add_terms(place, parts_y, members, slopes, turned, old, store):
    operands = []
    for m, pieces in zip(members, slopes):
        shards, half_x, span_y, span_z, lanes = pieces.shape
        channels, row = shards * lanes // 2, span_y * span_z
        right = jnp.concatenate(
            [part.reshape(half_x * row, channels) for part in ordered_halves(place, pieces)]
        )
        x0, y0 = (place[0] ^ (m // parts_y)) * 2 * half_x, place[1] ^ (m % parts_y)
        operands.append((x0, y0, row, right))
    for a in range(3):
        total = None if old is None else old[a]
        for x0, y0, row, right in operands:
            left = turned[y0, :, pl.ds(pl.multiple_of((x0 + a) * row, row), right.shape[0])]
            term = jnp.dot(left, right, preferred_element_type=F32)
            total = term if total is None else total + term
        store(a, total)


def first_kernel(parts_x, parts_y, place, active, pair, beside_y, sibling, column, *rest):
    activation, turned, sums, volume, unpacked, sent = rest
    half, lanes = active.shape[0], active.shape[1] // 2
    unpacked[:half] = active[:, :lanes]
    unpacked[half:] = active[:, lanes:]
    copy = pltpu.make_async_copy(unpacked, activation, sent)
    copy.start()
    shards, half_x, span_y, span_z, lanes = column.shape
    cells = [(0, pair, 0), (parts_y, pair, 1), (2, beside_y, 1), (parts_y + 2, beside_y, 2)]
    cells += [(m ^ 1, sibling, shards + n) for n, (m, _, _) in enumerate(cells)]
    span_x, lanes = 2 * half_x, lanes // 2
    rows_x, rows_y = parts_x * span_x, parts_y * span_y
    width = 3 * lanes
    zero_x = jnp.zeros((1, rows_y + 2, span_z, width), BF16)
    zero_y = jnp.zeros((rows_x + 2, 1, span_z, width), BF16)
    volume[0:1] = zero_x
    volume[rows_x + 1 : rows_x + 2] = zero_x
    volume[:, 0:1] = zero_y
    volume[:, rows_y + 1 : rows_y + 2] = zero_y
    for m, array, n in cells:
        x0, y0 = (place[0] ^ (m // parts_y)) * span_x, (place[1] ^ (m % parts_y)) * span_y
        v = array[n].astype(F32).reshape(half_x * span_y, span_z, 2 * lanes)
        low, high = shifted(v, 1), shifted(v, -1)
        for h in range(2):
            cut = slice(h * lanes, (h + 1) * lanes)
            joined = jnp.concatenate([low[..., cut], v[..., cut], high[..., cut]], axis=2)
            volume[pl.ds(x0 + 1 + h * half_x, half_x), pl.ds(y0 + 1, span_y)] = joined.astype(
                BF16
            ).reshape(half_x, span_y, span_z, width)
    for y in range(parts_y):
        for b in range(3):
            cut = volume[:, y * span_y + b : (y + 1) * span_y + b]
            turned[y, b * width : (b + 1) * width] = cut.reshape(-1, width).T

    def store(a, total):
        sums[a] = total

    members = (0, 1)
    add_terms(place, parts_y, members, (column, sibling.at[:shards]), turned, None, store)
    copy.wait()


def rows_of(place, pieces, row):
    shards, lanes = column_shape(pieces)
    ordered = [pieces[place[2] ^ j, :, row] for j in range(shards)]
    return [
        jnp.concatenate([piece[..., h * lanes : (h + 1) * lanes] for piece in ordered], axis=-1)
        for h in range(2)
    ]


def column_shape(pieces):
    return pieces.shape[0], pieces.shape[-1] // 2


def second_kernel(
    parts_y, members, place, weight, turned, old, column, sibling, *rest
):
    *slopes, partial, sums, window = rest
    shards, half_x, span_y, span_z, _ = column.shape
    span_x, half = 2 * half_x, half_x * span_y * span_z
    even_at, _, even_row, _, _, _ = rim_sides(place, span_x, span_y)
    window[...] = jnp.zeros(window.shape, BF16)
    beside = rows_of(place, sibling.at[:shards], facing_row(even_row, span_y))
    for h, own in enumerate(ordered_halves(place, column)):
        window[1 + h * half_x : 1 + (h + 1) * half_x, 1 : span_y + 1] = own
        window[1 + h * half_x : 1 + (h + 1) * half_x, even_at] = beside[h]
    for h in range(2):
        total = None
        for a in range(3):
            for b in range(3):
                cut = window[
                    2 - a + h * half_x : 2 - a + (h + 1) * half_x, 2 - b : 2 - b + span_y
                ]
                term = jnp.dot(
                    cut.reshape(half, cut.shape[-1]), weight[a * 3 + b], preferred_element_type=F32
                )
                total = term if total is None else total + term
        partial[h * half_x : (h + 1) * half_x] = total.reshape((half_x,) + partial.shape[1:])
    middle_kernel(parts_y, members, place, turned, old, *slopes, sums)


def middle_kernel(parts_y, members, place, turned, old, *rest):
    *slopes, sums = rest

    def store(a, total):
        sums[a] = total

    add_terms(place, parts_y, members, slopes, turned, old, store)


def facing(place, halves):
    low, high = halves
    return jnp.where(place[0] == 0, low[0], high[-1])


def channel_sum(pieces):
    mine = pieces[0].astype(F32).reshape(-1, pieces.shape[-1])
    return jnp.sum(mine, axis=0, keepdims=True)


def rim_kernel(parts_y, members, place, weight, turned, old, partial, *rest):
    *slopes, grid, column, sums, rim_x, rim_y = rest
    shards, half_x, span_y, span_z, _ = slopes[0].shape
    span_x, channels = 2 * half_x, rim_x.shape[-1]
    even_at, odd_at, even_row, odd_row, _, x_row = rim_sides(place, span_x, span_y)
    has_odd = (place[1] != 0) & (place[1] != parts_y - 1)
    rim_x[...] = jnp.zeros(rim_x.shape, BF16)
    rim_y[...] = jnp.zeros(rim_y.shape, BF16)
    rim_x[1 : span_y + 1] = facing(place, ordered_halves(place, slopes[parts_y]))
    even = rows_of(place, slopes[parts_y + 1], facing_row(even_row, span_y))
    rim_x[even_at] = facing(place, even)

    @pl.when(has_odd)
    def _():
        odd = rows_of(place, slopes[3], facing_row(odd_row, span_y))
        for h, rows in enumerate(odd):
            rim_y[1 + h * half_x : 1 + (h + 1) * half_x] = rows

    grid[...] = partial[...]
    tap_x, tap_y = rim_taps(place, odd_row)
    total = None
    for b in range(3):
        cut = rim_x[2 - b : 2 - b + span_y].reshape(span_y * span_z, channels)
        term = jnp.dot(cut, weight[tap_x * 3 + b], preferred_element_type=F32)
        total = term if total is None else total + term
    grid[x_row] += total.reshape((span_y,) + grid.shape[2:])
    total = None
    for a in range(3):
        cut = rim_y[2 - a : 2 - a + span_x].reshape(span_x * span_z, channels)
        term = jnp.dot(cut, weight[a * 3 + tap_y], preferred_element_type=F32)
        total = term if total is None else total + term
    grid[:, odd_row] += total.reshape((span_x,) + grid.shape[2:])
    total = channel_sum(slopes[0])
    for pieces in slopes[1:]:
        total = total + channel_sum(pieces)
    column[...] = total
    middle_kernel(parts_y, members, place, turned, old, *[slopes[m] for m in members], sums)


def rim_taps(place, odd_row):
    return jnp.where(place[0] == 0, 0, 2), jnp.where(odd_row == 0, 2, 0)


def last_kernel(parts_y, member, factor, place, weight, turned, old, partial, column, pieces, *rest):
    input_grad, kernel_grad, bias_grad, grid, sums, cells, bias, sent = rest
    _, half_x, span_y, span_z, _ = pieces.shape
    lanes = pieces.shape[-1] // 2
    span_x = 2 * half_x
    copies = []

    def send(source, target):
        copies.append(pltpu.make_async_copy(source, target, sent.at[len(copies)]))
        copies[-1].start()

    def finish_cells():
        _, _, _, odd_row, _, x_row = rim_sides(place, span_x, span_y)
        has_odd = (place[1] != 0) & (place[1] != parts_y - 1)
        tap_x, tap_y = rim_taps(place, odd_row)
        grid[...] = partial[...]

        @pl.when(has_odd)
        def _():
            corner = facing(place, rows_of(place, pieces, facing_row(odd_row, span_y)))
            term = jnp.dot(corner, weight[tap_x * 3 + tap_y], preferred_element_type=F32)
            grid[x_row, odd_row] += term

        summed = grid[...].reshape(span_x * span_y, span_z, 3 * lanes)
        result = (
            shifted(summed[..., :lanes], -1)
            + summed[..., lanes : 2 * lanes]
            + shifted(summed[..., 2 * lanes :], 1)
        )
        cells[...] = result.reshape(-1, lanes).astype(BF16)
        send(cells, input_grad)
        total = column[...] + channel_sum(pieces)
        bias[...] = (total[:, :lanes] + total[:, lanes:]) * factor
        send(bias, bias_grad)

    def store(a, total):
        sums[a] = total * factor
        for b in range(3):
            here = pl.ds(b * 3 * lanes, 3 * lanes)
            send(sums.at[a, here], kernel_grad.at[a, here])
        if a == 0:
            finish_cells()

    add_terms(place, parts_y, (member,), (pieces,), turned, old, store)
    for copy in copies:
        copy.wait()


def facing_row(row, span_y):
    return span_y - 1 - row


def exchange(x, axes, mask):
    return lax.ppermute(x, axes, [(i, i ^ mask) for i in range(lax.axis_size(axes))])


def body_gathered(inputs, weight, bias, cotangent):
    spans = inputs.shape[:3]
    span_x, span_y, span_z = spans
    local_ch, channels = weight.shape[3:]
    local = span_x * span_y * span_z
    parts_x, parts_y = lax.axis_size("gx"), lax.axis_size("gy")
    count = parts_x * parts_y
    shards = lax.axis_size("ch")
    axes = ("gx", "gy")
    factor = 1.0 / math.sqrt(local * count)
    place = jnp.stack([lax.axis_index(axis) for axis in ("gx", "gy", "ch")]).astype(jnp.int32)
    taps = weight.reshape(9, 3 * local_ch, channels)
    packing = (span_x // 2, span_y, span_z, 2 * local_ch)
    flat = (local // 2, 2 * local_ch)

    def call(kernel, name, outs, args, scratch=()):
        return pl.pallas_call(
            kernel,
            out_shape=[jax.ShapeDtypeStruct(shape, kind) for shape, kind in outs],
            in_specs=[SMEM if x is place else VMEM for x in args],
            out_specs=[VMEM] * len(outs),
            scratch_shapes=[pltpu.VMEM(shape, kind) for shape, kind in scratch],
            compiler_params=PARAMS,
            cost_estimate=pl.CostEstimate(flops=0, bytes_accessed=1024, transcendentals=0),
            name=name,
        )(*args)

    row = (span_x, span_z, local_ch)
    sources = [pltpu.with_memory_space_constraint(array, pltpu.HBM) for array in (inputs, taps)]
    shapes = [inputs.shape, taps.shape, packing, row, row, row[1:], row[1:]]
    held, taps, packed, even, odd, even_corner, odd_corner = pl.pallas_call(
        prepare_kernel,
        out_shape=[jax.ShapeDtypeStruct(shape, BF16) for shape in shapes],
        in_specs=[SMEM, HBM, HBM],
        out_specs=[VMEM] * len(shapes),
        scratch_shapes=[pltpu.SemaphoreType.DMA((1 + taps.shape[0],))],
        compiler_params=PARAMS,
        name="prepare",
    )(place, *sources)
    beside = exchange(packed, axes, parts_y)
    even = exchange(even, axes, 1)
    odd = exchange(odd, axes, 3)
    even_corner = exchange(even_corner, axes, parts_y + 1)
    odd_corner = exchange(odd_corner, axes, parts_y + 3)
    own, *others, pair = call(
        functools.partial(forward_kernel, parts_y),
        "forward",
        [(flat, F32)] + [(flat, BF16)] * (shards - 1) + [((2,) + packing, BF16)],
        [place, taps, held, packed, even, odd, beside, even_corner, odd_corner],
        [((span_x + 2, span_y + 2, span_z, 3 * local_ch), BF16), ((shards,) + flat, F32)],
    )
    sources = (cotangent.reshape(local, local_ch), bias.reshape(1, local_ch))
    turned_weight_shape = (9, channels, 3 * local_ch)
    cotangent, bias, taps_turned = pl.pallas_call(
        stage_kernel,
        out_shape=[
            *[jax.ShapeDtypeStruct(array.shape, BF16) for array in sources],
            jax.ShapeDtypeStruct(turned_weight_shape, BF16),
        ],
        in_specs=[VMEM, VMEM, HBM, HBM],
        out_specs=[VMEM] * 3,
        scratch_shapes=[pltpu.SemaphoreType.DMA((2,))],
        compiler_params=PARAMS,
        cost_estimate=pl.CostEstimate(flops=0, bytes_accessed=1024, transcendentals=0),
        name="stage",
    )(own, taps, *[pltpu.with_memory_space_constraint(array, pltpu.HBM) for array in sources])
    others = [exchange(others[k - 1], "ch", k) for k in range(shards - 1, 0, -1)]
    active, slope = call(
        slope_kernel,
        "slope",
        [(flat, BF16), (flat, BF16)],
        [own, *others, bias, cotangent],
    )
    rest = [exchange(slope, "ch", k) for k in range(1, shards)]
    rest = jnp.stack(rest).reshape((shards - 1,) + packing)
    piece = slope.reshape((1,) + packing)
    x, y = parts_y, 2
    beside_x = exchange(piece, axes, x)
    beside_y = exchange(jnp.concatenate([piece, pair]), axes, y)
    beside_y, beside_x, rest = lax.optimization_barrier((beside_y, beside_x, rest))
    column = jnp.concatenate([piece, rest])
    late_y, late_x = exchange(rest, axes, y), exchange(rest, axes, x)
    sibling = exchange(jnp.concatenate([column, pair, beside_y[1:]]), axes, 1)
    turned_shape = (parts_y, 9 * local_ch, (parts_x * span_x + 2) * span_y * span_z)
    sums_shape = (3, 9 * local_ch, channels)
    first_outs = [((local, local_ch), BF16), (turned_shape, BF16), (sums_shape, F32)]
    args = [place, active, pair, beside_y, sibling, column]
    activation, turned, sums = pl.pallas_call(
        functools.partial(first_kernel, parts_x, parts_y),
        out_shape=[jax.ShapeDtypeStruct(shape, kind) for shape, kind in first_outs],
        in_specs=[SMEM] + [VMEM] * (len(args) - 1),
        out_specs=[HBM] + [VMEM] * 2,
        scratch_shapes=[
            pltpu.VMEM((parts_x * span_x + 2, parts_y * span_y + 2, span_z, 3 * local_ch), BF16),
            pltpu.VMEM((local, local_ch), BF16),
            pltpu.SemaphoreType.DMA,
        ],
        compiler_params=PARAMS,
        cost_estimate=pl.CostEstimate(flops=0, bytes_accessed=1024, transcendentals=0),
        name="first",
    )(*args)
    slopes = {0: column, 1: sibling[:shards]}
    late_y, late_x, sums = lax.optimization_barrier((late_y, late_x, sums))
    slopes[y] = jnp.concatenate([beside_y[:1], late_y])
    slopes[x] = jnp.concatenate([beside_x, late_x])
    middle = shards // 2
    diagonal = [exchange(slopes[x][:middle], axes, y), exchange(slopes[y][middle:], axes, x)]
    across = [exchange(slopes[m], axes, 1) for m in (y, x)]
    grid_shape = spans + (3 * local_ch,)
    partial, sums = call(
        functools.partial(second_kernel, parts_y, (y, x)),
        "second",
        [(grid_shape, F32), (sums_shape, F32)],
        [place, taps_turned, turned, sums, column, sibling, slopes[y], slopes[x]],
        [((span_x + 2, span_y + 2, span_z, channels), BF16)],
    )
    slopes[y + 1], slopes[x + 1] = across
    (sums,) = call(
        functools.partial(middle_kernel, parts_y, (y + 1, x + 1)),
        "third",
        [(sums_shape, F32)],
        [place, turned, sums, *across],
    )
    *diagonal, sums = lax.optimization_barrier((*diagonal, sums))
    slopes[x + y] = jnp.concatenate(diagonal)
    final = exchange(slopes[x + y], axes, 1)
    partial, column, sums = call(
        functools.partial(rim_kernel, parts_y, (x + y,)),
        "rim",
        [(grid_shape, F32), ((1, 2 * local_ch), F32), (sums_shape, F32)],
        [place, taps_turned, turned, sums, partial] + [slopes[m] for m in range(count - 1)],
        [((span_y + 2, span_z, channels), BF16), ((span_x + 2, span_z, channels), BF16)],
    )
    args = [place, taps_turned, turned, sums, partial, column, final]
    input_grad, kernel_grad, bias_grad = pl.pallas_call(
        functools.partial(last_kernel, parts_y, x + y + 1, factor),
        out_shape=[
            jax.ShapeDtypeStruct((local, local_ch), BF16),
            jax.ShapeDtypeStruct(sums_shape, F32),
            jax.ShapeDtypeStruct((1, local_ch), F32),
        ],
        in_specs=[SMEM] + [VMEM] * (len(args) - 1),
        out_specs=[HBM] * 3,
        scratch_shapes=[
            pltpu.VMEM(grid_shape, F32),
            pltpu.VMEM(sums_shape, F32),
            pltpu.VMEM((local, local_ch), BF16),
            pltpu.VMEM((1, local_ch), F32),
            pltpu.SemaphoreType.DMA((11,)),
        ],
        compiler_params=PARAMS,
        name="last",
    )(*args)
    return (
        activation.reshape(inputs.shape),
        input_grad.reshape(inputs.shape),
        kernel_grad.reshape(weight.shape),
        bias_grad.reshape(local_ch),
    )


def solution(mesh):
    few = (mesh.shape["gx"], mesh.shape["gy"]) == (2, 4)
    return jax.shard_map(
        body_gathered if few else body_reduced,
        mesh=mesh,
        in_specs=(
            P("gx", "gy", None, "ch"),
            P(None, None, None, "ch", None),
            P("ch"),
            P("gx", "gy", None, "ch"),
        ),
        out_specs=(
            P("gx", "gy", None, "ch"),
            P("gx", "gy", None, "ch"),
            P(None, None, None, "ch", None),
            P("ch"),
        ),
        check_vma=False,
    )
```

```python
import functools
import math

import jax
import jax.numpy as jnp
from jax import lax
from jax.experimental import pallas as pl
from jax.experimental.pallas import tpu as pltpu
from jax.sharding import PartitionSpec as P

VMEM = pl.BlockSpec(memory_space=pltpu.VMEM)
HBM = pl.BlockSpec(memory_space=pltpu.HBM)
SMEM = pl.BlockSpec(memory_space=pltpu.SMEM)
PARAMS = pltpu.CompilerParams(vmem_limit_bytes=24 * 1024 * 1024)
F32 = jnp.float32
BF16 = jnp.bfloat16


def with_halo(x, sides, width):
    for axis, dim in sides:
        devices, length = (lax.axis_size(axis), x.shape[dim])
        up = [(i, (i + 1) % devices) for i in range(devices - 1)]
        down = [(j, i) for i, j in up]
        last = lax.slice_in_dim(x, length - width, length, axis=dim)
        initial = lax.slice_in_dim(x, 0, width, axis=dim)
        before = lax.ppermute(last, axis, up)
        after = lax.ppermute(initial, axis, down)
        x = jnp.concatenate([before, x, after], axis=dim)
    return x


def body_reduced(inputs, weight, bias, cotangent):
    span_x, span_y, span_z, local_ch = inputs.shape
    widest = weight.shape[4]
    local_cells = span_x * span_y * span_z
    offsets = [(a, b, c) for a in range(3) for b in range(3) for c in range(3)]
    depth_pad = ((0, 0), (0, 0), (1, 1), (0, 0))
    rimmed = with_halo(inputs, (("gx", 0), ("gy", 1)), 1)
    padded = jnp.pad(rimmed, depth_pad)
    blocks = []
    for a, b, c in offsets:
        blocks.append(
            padded[a : a + span_x, b : b + span_y, c : c + span_z].reshape(local_cells, local_ch)
        )
    patches = jnp.concatenate(blocks, axis=1)
    flat_weight = weight.reshape(27 * local_ch, widest)
    summed = lax.psum_scatter(
        lax.dot_general(flat_weight, patches, (((0,), (1,)), ((), ())), preferred_element_type=F32),
        "ch",
        scatter_dimension=0,
        tiled=True,
    ).T
    summed = summed + bias.astype(F32)[None, :]
    activation = jax.nn.silu(summed).astype(BF16).reshape(span_x, span_y, span_z, local_ch)
    sigmoid_pre = jax.nn.sigmoid(summed)
    slope = (
        cotangent.reshape(local_cells, local_ch).astype(F32)
        * sigmoid_pre
        * (1.0 + summed * (1.0 - sigmoid_pre))
    ).astype(BF16)
    local_bias = jnp.sum(slope.astype(F32), axis=0)
    slope_grid = slope.reshape(span_x, span_y, span_z, local_ch)
    weight_turned = jnp.transpose(weight.reshape(27, local_ch, widest), (0, 2, 1))
    slope_rimmed = with_halo(slope_grid, (("gx", 0), ("gy", 1)), 1)
    piece = lax.all_gather(slope_rimmed, "ch", axis=3, tiled=True)
    extended = jnp.pad(piece, depth_pad)
    running = jnp.zeros((local_cells, local_ch), F32)
    for index, (a, b, c) in enumerate(offsets):
        a, b, c = (2 - a, 2 - b, 2 - c)
        cut = extended[a : a + span_x, b : b + span_y, c : c + span_z].reshape(local_cells, widest)
        running = running + jnp.dot(cut, weight_turned[index], preferred_element_type=F32)
    interior = piece[1 : 1 + span_x, 1 : 1 + span_y].reshape(local_cells, widest)
    product = lax.dot_general(
        patches, interior, (((0,), (0,)), ((), ())), preferred_element_type=F32
    )
    total_cells = local_cells * lax.axis_size("gx") * lax.axis_size("gy")
    factor = 1.0 / math.sqrt(total_cells)
    kernel_total, bias_total = lax.psum((product * factor, local_bias * factor), ("gx", "gy"))
    input_grad = running.astype(BF16).reshape(span_x, span_y, span_z, local_ch)
    return (activation, input_grad, kernel_total.reshape(3, 3, 3, local_ch, widest), bias_total)


def shifted(v, by):
    depth = v.shape[1]
    row = lax.broadcasted_iota(jnp.int32, v.shape, 1)
    if by == 1:
        return jnp.where(row == 0, 0.0, pltpu.roll(v, 1, 1))
    return jnp.where(row == depth - 1, 0.0, pltpu.roll(v, depth - 1, 1))


def rim_sides(place, span_x, span_y):
    first = place[1] % 2 == 0
    even_at = jnp.where(first, span_y + 1, 0)
    odd_at = jnp.where(first, 0, span_y + 1)
    even_row = jnp.where(first, span_y - 1, 0)
    odd_row = jnp.where(first, 0, span_y - 1)
    x_at = jnp.where(place[0] == 0, span_x + 1, 0)
    x_row = jnp.where(place[0] == 0, span_x - 1, 0)
    return even_at, odd_at, even_row, odd_row, x_at, x_row


def prepare_kernel(place, source, inputs, packed, even, odd, even_corner, odd_corner, arrived):
    copy = pltpu.make_async_copy(source, inputs, arrived)
    copy.start()
    copy.wait()
    span_x, span_y, _, _ = inputs.shape
    half = span_x // 2
    _, _, even_row, odd_row, _, x_row = rim_sides(place, span_x, span_y)
    even[...] = inputs[:, even_row]
    odd[...] = inputs[:, odd_row]
    even_corner[...] = inputs[x_row, even_row]
    odd_corner[...] = inputs[x_row, odd_row]
    packed[...] = jnp.concatenate([inputs[:half], inputs[half:]], axis=3)


def stage_kernel(after, *rest):
    count = (len(rest) - 1) // 2
    sources, targets, arrived = rest[:count], rest[count : 2 * count], rest[-1]
    copies = []
    for source, target in zip(sources, targets):
        parts = source.shape[0] if len(source.shape) == 3 else 1
        for n in range(parts):
            here = pl.ds(n, 1) if parts > 1 else slice(None)
            copies.append(
                pltpu.make_async_copy(source.at[here], target.at[here], arrived.at[len(copies)])
            )
    for copy in copies:
        copy.start()
    for copy in copies:
        copy.wait()


def forward_kernel(
    parts_y, place, weight, inputs, packed, even, odd, beside, even_corner, odd_corner, own, *rest
):
    *others, pair, window, blocks = rest
    span_x, span_y, span_z, lanes = inputs.shape
    half_x = span_x // 2
    half = half_x * span_y * span_z
    even_at, odd_at, _, _, x_at, _ = rim_sides(place, span_x, span_y)

    def spread(v):
        flat = v.astype(F32).reshape(-1, span_z, lanes)
        joined = jnp.concatenate([shifted(flat, 1), flat, shifted(flat, -1)], axis=2)
        return joined.astype(BF16).reshape(v.shape[:-1] + (3 * lanes,))

    nothing = jnp.zeros((span_y + 2, span_z, 3 * lanes), BF16)
    window[0] = nothing
    window[span_x + 1] = nothing
    window[1 : span_x + 1, 1 : span_y + 1] = spread(inputs[...])
    window[1 : span_x + 1, even_at] = spread(even[...])
    has_odd = (place[1] != 0) & (place[1] != parts_y - 1)
    window[1 : span_x + 1, odd_at] = jnp.where(has_odd, spread(odd[...]), jnp.zeros((), BF16))
    across = jnp.where(place[0] == 0, beside[0][..., :lanes], beside[half_x - 1][..., lanes:])
    window[x_at, 1 : span_y + 1] = spread(across)
    window[x_at, even_at] = spread(even_corner[...])
    window[x_at, odd_at] = jnp.where(has_odd, spread(odd_corner[...]), jnp.zeros((), BF16))
    sums = []
    for h in range(2):
        total = None
        for a in range(3):
            for b in range(3):
                cut = window[a + h * half_x : a + (h + 1) * half_x, b : b + span_y]
                term = jnp.dot(
                    cut.reshape(half, 3 * lanes), weight[a * 3 + b], preferred_element_type=F32
                )
                total = term if total is None else total + term
        sums.append(total)
    for d in range(weight.shape[2] // lanes):
        cut = slice(d * lanes, (d + 1) * lanes)
        blocks[d] = jnp.concatenate([sums[0][:, cut], sums[1][:, cut]], axis=1)
    own[...] = blocks[place[2]]
    for k, other in enumerate(others):
        other[...] = blocks[place[2] ^ (k + 1)].astype(BF16)
    pair[0] = packed[...]
    pair[1] = beside[...]


def slope_kernel(own, *rest):
    *others, bias, cotangent, active, slope = rest
    half = cotangent.shape[0] // 2
    summed = own[...]
    for other in others:
        summed = summed + other[...].astype(F32)
    offset = bias[...].astype(F32)
    summed = summed + jnp.concatenate([offset, offset], axis=1)
    sigmoid = jax.nn.sigmoid(summed)
    active[...] = (summed * sigmoid).astype(BF16)
    upstream = jnp.concatenate([cotangent[:half], cotangent[half:]], axis=1).astype(F32)
    slope[...] = (upstream * sigmoid * (1.0 + summed * (1.0 - sigmoid))).astype(BF16)


def slot_of(partner):
    return partner ^ (partner >> 1)


def ordered_halves(place, pieces):
    shards, _, _, _, lanes = pieces.shape
    lanes = lanes // 2
    ordered = [pieces[slot_of(place[2] ^ j)] for j in range(shards)]
    return [
        jnp.concatenate([piece[..., h * lanes : (h + 1) * lanes] for piece in ordered], axis=-1)
        for h in range(2)
    ]


def add_terms(place, parts_y, members, slopes, turned, old, store):
    operands = []
    for m, pieces in zip(members, slopes):
        shards, half_x, span_y, span_z, lanes = pieces.shape
        channels, row = shards * lanes // 2, span_y * span_z
        right = jnp.concatenate(
            [part.reshape(half_x * row, channels) for part in ordered_halves(place, pieces)]
        )
        x0, y0 = (place[0] ^ (m // parts_y)) * 2 * half_x, place[1] ^ (m % parts_y)
        operands.append((x0, y0, row, right))
    for a in range(3):
        total = None if old is None else old[a]
        for x0, y0, row, right in operands:
            left = turned[y0, :, pl.ds(pl.multiple_of((x0 + a) * row, row), right.shape[0])]
            term = jnp.dot(left, right, preferred_element_type=F32)
            total = term if total is None else total + term
        store(a, total)


def first_kernel(parts_x, parts_y, place, weight, active, pair, beside_y, sibling, column, *rest):
    activation, turned, sums, weight_turned, volume, unpacked, sent = rest
    half, lanes = active.shape[0], active.shape[1] // 2
    unpacked[:half] = active[:, :lanes]
    unpacked[half:] = active[:, lanes:]
    copy = pltpu.make_async_copy(unpacked, activation, sent)
    copy.start()
    shards, half_x, span_y, span_z, lanes = column.shape
    cells = [(0, pair, 0), (parts_y, pair, 1), (2, beside_y, 1), (parts_y + 2, beside_y, 2)]
    cells += [(m ^ 1, sibling, shards + n) for n, (m, _, _) in enumerate(cells)]
    span_x, lanes = 2 * half_x, lanes // 2
    rows_x, rows_y = parts_x * span_x, parts_y * span_y
    width = 3 * lanes
    zero_x = jnp.zeros((1, rows_y + 2, span_z, width), BF16)
    zero_y = jnp.zeros((rows_x + 2, 1, span_z, width), BF16)
    volume[0:1] = zero_x
    volume[rows_x + 1 : rows_x + 2] = zero_x
    volume[:, 0:1] = zero_y
    volume[:, rows_y + 1 : rows_y + 2] = zero_y
    for m, array, n in cells:
        x0, y0 = (place[0] ^ (m // parts_y)) * span_x, (place[1] ^ (m % parts_y)) * span_y
        v = array[n].astype(F32).reshape(half_x * span_y, span_z, 2 * lanes)
        low, high = shifted(v, 1), shifted(v, -1)
        for h in range(2):
            cut = slice(h * lanes, (h + 1) * lanes)
            joined = jnp.concatenate([low[..., cut], v[..., cut], high[..., cut]], axis=2)
            volume[pl.ds(x0 + 1 + h * half_x, half_x), pl.ds(y0 + 1, span_y)] = joined.astype(
                BF16
            ).reshape(half_x, span_y, span_z, width)
    for y in range(parts_y):
        for b in range(3):
            cut = volume[:, y * span_y + b : (y + 1) * span_y + b]
            turned[y, b * width : (b + 1) * width] = cut.reshape(-1, width).T

    def store(a, total):
        sums[a] = total

    for tap in range(weight.shape[0]):
        weight_turned[tap] = weight[tap].T
    members = (0, 1)
    add_terms(place, parts_y, members, (column, sibling.at[:shards]), turned, None, store)
    copy.wait()


def rows_of(place, pieces, row):
    shards, lanes = column_shape(pieces)
    ordered = [pieces[slot_of(place[2] ^ j), :, row] for j in range(shards)]
    return [
        jnp.concatenate([piece[..., h * lanes : (h + 1) * lanes] for piece in ordered], axis=-1)
        for h in range(2)
    ]


def column_shape(pieces):
    return pieces.shape[0], pieces.shape[-1] // 2


def second_kernel(
    parts_y, members, place, weight, turned, old, column, sibling, *rest
):
    *slopes, partial, sums, window = rest
    shards, half_x, span_y, span_z, _ = column.shape
    span_x, half = 2 * half_x, half_x * span_y * span_z
    even_at, _, even_row, _, _, _ = rim_sides(place, span_x, span_y)
    window[...] = jnp.zeros(window.shape, BF16)
    beside = rows_of(place, sibling.at[:shards], facing_row(even_row, span_y))
    for h, own in enumerate(ordered_halves(place, column)):
        window[1 + h * half_x : 1 + (h + 1) * half_x, 1 : span_y + 1] = own
        window[1 + h * half_x : 1 + (h + 1) * half_x, even_at] = beside[h]
    for h in range(2):
        total = None
        for a in range(3):
            for b in range(3):
                cut = window[
                    2 - a + h * half_x : 2 - a + (h + 1) * half_x, 2 - b : 2 - b + span_y
                ]
                term = jnp.dot(
                    cut.reshape(half, cut.shape[-1]), weight[a * 3 + b], preferred_element_type=F32
                )
                total = term if total is None else total + term
        partial[h * half_x : (h + 1) * half_x] = total.reshape((half_x,) + partial.shape[1:])
    middle_kernel(parts_y, members, place, turned, old, *slopes, sums)


def middle_kernel(parts_y, members, place, turned, old, *rest):
    *slopes, sums = rest

    def store(a, total):
        sums[a] = total

    add_terms(place, parts_y, members, slopes, turned, old, store)


def facing(place, halves):
    low, high = halves
    return jnp.where(place[0] == 0, low[0], high[-1])


def channel_sum(pieces):
    mine = pieces[0].astype(F32).reshape(-1, pieces.shape[-1])
    return jnp.sum(mine, axis=0, keepdims=True)


def rim_kernel(parts_y, members, place, weight, turned, old, partial, *rest):
    *slopes, grid, column, sums, rim_x, rim_y = rest
    shards, half_x, span_y, span_z, _ = slopes[0].shape
    span_x, channels = 2 * half_x, rim_x.shape[-1]
    even_at, odd_at, even_row, odd_row, _, x_row = rim_sides(place, span_x, span_y)
    has_odd = (place[1] != 0) & (place[1] != parts_y - 1)
    rim_x[...] = jnp.zeros(rim_x.shape, BF16)
    rim_y[...] = jnp.zeros(rim_y.shape, BF16)
    rim_x[1 : span_y + 1] = facing(place, ordered_halves(place, slopes[parts_y]))
    even = rows_of(place, slopes[parts_y + 1], facing_row(even_row, span_y))
    rim_x[even_at] = facing(place, even)

    @pl.when(has_odd)
    def _():
        odd = rows_of(place, slopes[3], facing_row(odd_row, span_y))
        for h, rows in enumerate(odd):
            rim_y[1 + h * half_x : 1 + (h + 1) * half_x] = rows

    grid[...] = partial[...]
    tap_x, tap_y = rim_taps(place, odd_row)
    total = None
    for b in range(3):
        cut = rim_x[2 - b : 2 - b + span_y].reshape(span_y * span_z, channels)
        term = jnp.dot(cut, weight[tap_x * 3 + b], preferred_element_type=F32)
        total = term if total is None else total + term
    grid[x_row] += total.reshape((span_y,) + grid.shape[2:])
    total = None
    for a in range(3):
        cut = rim_y[2 - a : 2 - a + span_x].reshape(span_x * span_z, channels)
        term = jnp.dot(cut, weight[a * 3 + tap_y], preferred_element_type=F32)
        total = term if total is None else total + term
    grid[:, odd_row] += total.reshape((span_x,) + grid.shape[2:])
    total = channel_sum(slopes[0])
    for pieces in slopes[1:]:
        total = total + channel_sum(pieces)
    column[...] = total
    middle_kernel(parts_y, members, place, turned, old, *[slopes[m] for m in members], sums)


def rim_taps(place, odd_row):
    return jnp.where(place[0] == 0, 0, 2), jnp.where(odd_row == 0, 2, 0)


def last_kernel(parts_y, member, factor, place, weight, turned, old, partial, column, pieces, *rest):
    input_grad, kernel_grad, bias_grad, grid, sums, cells, bias, sent = rest
    _, half_x, span_y, span_z, _ = pieces.shape
    lanes = pieces.shape[-1] // 2
    span_x = 2 * half_x
    copies = []

    def send(source, target):
        copies.append(pltpu.make_async_copy(source, target, sent.at[len(copies)]))
        copies[-1].start()

    def store(a, total):
        sums[a] = total * factor
        send(sums.at[a], kernel_grad.at[a])

    add_terms(place, parts_y, (member,), (pieces,), turned, old, store)

    _, _, _, odd_row, _, x_row = rim_sides(place, span_x, span_y)
    has_odd = (place[1] != 0) & (place[1] != parts_y - 1)
    tap_x, tap_y = rim_taps(place, odd_row)
    grid[...] = partial[...]

    @pl.when(has_odd)
    def _():
        corner = facing(place, rows_of(place, pieces, facing_row(odd_row, span_y)))
        term = jnp.dot(corner, weight[tap_x * 3 + tap_y], preferred_element_type=F32)
        grid[x_row, odd_row] += term

    summed = grid[...].reshape(span_x * span_y, span_z, 3 * lanes)
    result = (
        shifted(summed[..., :lanes], -1)
        + summed[..., lanes : 2 * lanes]
        + shifted(summed[..., 2 * lanes :], 1)
    )
    cells[...] = result.reshape(-1, lanes).astype(BF16)
    send(cells, input_grad)
    total = column[...] + channel_sum(pieces)
    bias[...] = (total[:, :lanes] + total[:, lanes:]) * factor
    send(bias, bias_grad)
    for copy in copies:
        copy.wait()


def facing_row(row, span_y):
    return span_y - 1 - row


def exchange(x, axes, mask):
    return lax.ppermute(x, axes, [(i, i ^ mask) for i in range(lax.axis_size(axes))])


def body_gathered(inputs, weight, bias, cotangent):
    spans = inputs.shape[:3]
    span_x, span_y, span_z = spans
    local_ch, channels = weight.shape[3:]
    local = span_x * span_y * span_z
    parts_x, parts_y = lax.axis_size("gx"), lax.axis_size("gy")
    count = parts_x * parts_y
    shards = lax.axis_size("ch")
    axes = ("gx", "gy")
    factor = 1.0 / math.sqrt(local * count)
    place = jnp.stack([lax.axis_index(axis) for axis in ("gx", "gy", "ch")]).astype(jnp.int32)
    taps = weight.reshape(9, 3 * local_ch, channels)
    packing = (span_x // 2, span_y, span_z, 2 * local_ch)
    flat = (local // 2, 2 * local_ch)

    def call(kernel, name, outs, args, scratch=()):
        return pl.pallas_call(
            kernel,
            out_shape=[jax.ShapeDtypeStruct(shape, kind) for shape, kind in outs],
            in_specs=[SMEM if x is place else VMEM for x in args],
            out_specs=[VMEM] * len(outs),
            scratch_shapes=[pltpu.VMEM(shape, kind) for shape, kind in scratch],
            compiler_params=PARAMS,
            cost_estimate=pl.CostEstimate(flops=0, bytes_accessed=1024, transcendentals=0),
            name=name,
        )(*args)

    row = (span_x, span_z, local_ch)
    held, packed, even, odd, even_corner, odd_corner = pl.pallas_call(
        prepare_kernel,
        out_shape=[jax.ShapeDtypeStruct(inputs.shape, BF16), jax.ShapeDtypeStruct(packing, BF16)]
        + [jax.ShapeDtypeStruct(row, BF16)] * 2
        + [jax.ShapeDtypeStruct(row[1:], BF16)] * 2,
        in_specs=[SMEM, HBM],
        out_specs=[VMEM] * 6,
        scratch_shapes=[pltpu.SemaphoreType.DMA],
        compiler_params=PARAMS,
        name="prepare",
    )(place, pltpu.with_memory_space_constraint(inputs, pltpu.HBM))
    sources = (taps, cotangent.reshape(local, local_ch), bias.reshape(1, local_ch))
    taps, cotangent, bias = pl.pallas_call(
        stage_kernel,
        out_shape=[jax.ShapeDtypeStruct(x.shape, x.dtype) for x in sources],
        in_specs=[VMEM] + [HBM] * len(sources),
        out_specs=[VMEM] * len(sources),
        scratch_shapes=[pltpu.SemaphoreType.DMA((len(sources) + 8,))],
        compiler_params=PARAMS,
        name="stage",
    )(even_corner, *[pltpu.with_memory_space_constraint(x, pltpu.HBM) for x in sources])
    beside = exchange(packed, axes, parts_y)
    even = exchange(even, axes, 1)
    odd = exchange(odd, axes, 3)
    even_corner = exchange(even_corner, axes, parts_y + 1)
    odd_corner = exchange(odd_corner, axes, parts_y + 3)
    own, *others, pair = call(
        functools.partial(forward_kernel, parts_y),
        "forward",
        [(flat, F32)] + [(flat, BF16)] * (shards - 1) + [((2,) + packing, BF16)],
        [place, taps, held, packed, even, odd, beside, even_corner, odd_corner],
        [((span_x + 2, span_y + 2, span_z, 3 * local_ch), BF16), ((shards,) + flat, F32)],
    )
    order = sorted(range(1, shards), key=lambda k: (k < 2, k))
    others = [exchange(others[k - 1], "ch", k) for k in order]
    active, slope = call(
        slope_kernel,
        "slope",
        [(flat, BF16), (flat, BF16)],
        [own, *others, bias, cotangent],
    )
    rest = [exchange(slope, "ch", k) for k in sorted(range(1, shards), key=slot_of)]
    rest = jnp.stack(rest).reshape((shards - 1,) + packing)
    piece = slope.reshape((1,) + packing)
    x, y = parts_y, 2
    beside_x = exchange(piece, axes, x)
    beside_y = exchange(jnp.concatenate([piece, pair]), axes, y)
    beside_y, beside_x, rest = lax.optimization_barrier((beside_y, beside_x, rest))
    column = jnp.concatenate([piece, rest])
    late_y, late_x = exchange(rest, axes, y), exchange(rest, axes, x)
    sibling = exchange(jnp.concatenate([column, pair, beside_y[1:]]), axes, 1)
    turned_shape = (parts_y, 9 * local_ch, (parts_x * span_x + 2) * span_y * span_z)
    sums_shape = (3, 9 * local_ch, channels)
    first_outs = [((local, local_ch), BF16), (turned_shape, BF16), (sums_shape, F32)]
    first_outs += [((9, channels, 3 * local_ch), BF16)]
    args = [place, taps, active, pair, beside_y, sibling, column]
    activation, turned, sums, taps = pl.pallas_call(
        functools.partial(first_kernel, parts_x, parts_y),
        out_shape=[jax.ShapeDtypeStruct(shape, kind) for shape, kind in first_outs],
        in_specs=[SMEM] + [VMEM] * (len(args) - 1),
        out_specs=[HBM] + [VMEM] * 3,
        scratch_shapes=[
            pltpu.VMEM((parts_x * span_x + 2, parts_y * span_y + 2, span_z, 3 * local_ch), BF16),
            pltpu.VMEM((local, local_ch), BF16),
            pltpu.SemaphoreType.DMA,
        ],
        compiler_params=PARAMS,
        cost_estimate=pl.CostEstimate(flops=0, bytes_accessed=1024, transcendentals=0),
        name="first",
    )(*args)
    slopes = {0: column, 1: sibling[:shards]}
    late_y, late_x, sums = lax.optimization_barrier((late_y, late_x, sums))
    slopes[y] = jnp.concatenate([beside_y[:1], late_y])
    slopes[x] = jnp.concatenate([beside_x, late_x])
    middle = shards // 2
    diagonal = [exchange(slopes[x][:middle], axes, y), exchange(slopes[y][middle:], axes, x)]
    across = [exchange(slopes[m], axes, 1) for m in (y, x)]
    grid_shape = spans + (3 * local_ch,)
    partial, sums = call(
        functools.partial(second_kernel, parts_y, (y, x)),
        "second",
        [(grid_shape, F32), (sums_shape, F32)],
        [place, taps, turned, sums, column, sibling, slopes[y], slopes[x]],
        [((span_x + 2, span_y + 2, span_z, channels), BF16)],
    )
    slopes[y + 1], slopes[x + 1] = across
    (sums,) = call(
        functools.partial(middle_kernel, parts_y, (y + 1, x + 1)),
        "third",
        [(sums_shape, F32)],
        [place, turned, sums, *across],
    )
    *diagonal, sums = lax.optimization_barrier((*diagonal, sums))
    slopes[x + y] = jnp.concatenate(diagonal)
    final = exchange(slopes[x + y], axes, 1)
    partial, column, sums = call(
        functools.partial(rim_kernel, parts_y, (x + y,)),
        "rim",
        [(grid_shape, F32), ((1, 2 * local_ch), F32), (sums_shape, F32)],
        [place, taps, turned, sums, partial] + [slopes[m] for m in range(count - 1)],
        [((span_y + 2, span_z, channels), BF16), ((span_x + 2, span_z, channels), BF16)],
    )
    args = [place, taps, turned, sums, partial, column, final]
    input_grad, kernel_grad, bias_grad = pl.pallas_call(
        functools.partial(last_kernel, parts_y, x + y + 1, factor),
        out_shape=[
            jax.ShapeDtypeStruct((local, local_ch), BF16),
            jax.ShapeDtypeStruct(sums_shape, F32),
            jax.ShapeDtypeStruct((1, local_ch), F32),
        ],
        in_specs=[SMEM] + [VMEM] * (len(args) - 1),
        out_specs=[HBM] * 3,
        scratch_shapes=[
            pltpu.VMEM(grid_shape, F32),
            pltpu.VMEM(sums_shape, F32),
            pltpu.VMEM((local, local_ch), BF16),
            pltpu.VMEM((1, local_ch), F32),
            pltpu.SemaphoreType.DMA((5,)),
        ],
        compiler_params=PARAMS,
        name="last",
    )(*args)
    return (
        activation.reshape(inputs.shape),
        input_grad.reshape(inputs.shape),
        kernel_grad.reshape(weight.shape),
        bias_grad.reshape(local_ch),
    )


def solution(mesh):
    few = (mesh.shape["gx"], mesh.shape["gy"]) == (2, 4)
    return jax.shard_map(
        body_gathered if few else body_reduced,
        mesh=mesh,
        in_specs=(
            P("gx", "gy", None, "ch"),
            P(None, None, None, "ch", None),
            P("ch"),
            P("gx", "gy", None, "ch"),
        ),
        out_specs=(
            P("gx", "gy", None, "ch"),
            P("gx", "gy", None, "ch"),
            P(None, None, None, "ch", None),
            P("ch"),
        ),
        check_vma=False,
    )
```

```python
import functools
import math

import jax
import jax.numpy as jnp
from jax import lax
from jax.experimental import pallas as pl
from jax.experimental.pallas import tpu as pltpu
from jax.sharding import PartitionSpec as P

VMEM = pl.BlockSpec(memory_space=pltpu.VMEM)
HBM = pl.BlockSpec(memory_space=pltpu.HBM)
SMEM = pl.BlockSpec(memory_space=pltpu.SMEM)
PARAMS = pltpu.CompilerParams(vmem_limit_bytes=24 * 1024 * 1024)
F32 = jnp.float32
BF16 = jnp.bfloat16


def with_halo(x, sides, width):
    for axis, dim in sides:
        devices, length = (lax.axis_size(axis), x.shape[dim])
        up = [(i, (i + 1) % devices) for i in range(devices - 1)]
        down = [(j, i) for i, j in up]
        last = lax.slice_in_dim(x, length - width, length, axis=dim)
        initial = lax.slice_in_dim(x, 0, width, axis=dim)
        before = lax.ppermute(last, axis, up)
        after = lax.ppermute(initial, axis, down)
        x = jnp.concatenate([before, x, after], axis=dim)
    return x


def body_reduced(inputs, weight, bias, cotangent):
    span_x, span_y, span_z, local_ch = inputs.shape
    widest = weight.shape[4]
    local_cells = span_x * span_y * span_z
    offsets = [(a, b, c) for a in range(3) for b in range(3) for c in range(3)]
    depth_pad = ((0, 0), (0, 0), (1, 1), (0, 0))
    rimmed = with_halo(inputs, (("gx", 0), ("gy", 1)), 1)
    padded = jnp.pad(rimmed, depth_pad)
    blocks = []
    for a, b, c in offsets:
        blocks.append(
            padded[a : a + span_x, b : b + span_y, c : c + span_z].reshape(local_cells, local_ch)
        )
    patches = jnp.concatenate(blocks, axis=1)
    flat_weight = weight.reshape(27 * local_ch, widest)
    summed = lax.psum_scatter(
        lax.dot_general(flat_weight, patches, (((0,), (1,)), ((), ())), preferred_element_type=F32),
        "ch",
        scatter_dimension=0,
        tiled=True,
    ).T
    summed = summed + bias.astype(F32)[None, :]
    activation = jax.nn.silu(summed).astype(BF16).reshape(span_x, span_y, span_z, local_ch)
    sigmoid_pre = jax.nn.sigmoid(summed)
    slope = (
        cotangent.reshape(local_cells, local_ch).astype(F32)
        * sigmoid_pre
        * (1.0 + summed * (1.0 - sigmoid_pre))
    ).astype(BF16)
    local_bias = jnp.sum(slope.astype(F32), axis=0)
    slope_grid = slope.reshape(span_x, span_y, span_z, local_ch)
    weight_turned = jnp.transpose(weight.reshape(27, local_ch, widest), (0, 2, 1))
    slope_rimmed = with_halo(slope_grid, (("gx", 0), ("gy", 1)), 1)
    piece = lax.all_gather(slope_rimmed, "ch", axis=3, tiled=True)
    extended = jnp.pad(piece, depth_pad)
    running = jnp.zeros((local_cells, local_ch), F32)
    for index, (a, b, c) in enumerate(offsets):
        a, b, c = (2 - a, 2 - b, 2 - c)
        cut = extended[a : a + span_x, b : b + span_y, c : c + span_z].reshape(local_cells, widest)
        running = running + jnp.dot(cut, weight_turned[index], preferred_element_type=F32)
    interior = piece[1 : 1 + span_x, 1 : 1 + span_y].reshape(local_cells, widest)
    product = lax.dot_general(
        patches, interior, (((0,), (0,)), ((), ())), preferred_element_type=F32
    )
    total_cells = local_cells * lax.axis_size("gx") * lax.axis_size("gy")
    factor = 1.0 / math.sqrt(total_cells)
    kernel_total, bias_total = lax.psum((product * factor, local_bias * factor), ("gx", "gy"))
    input_grad = running.astype(BF16).reshape(span_x, span_y, span_z, local_ch)
    return (activation, input_grad, kernel_total.reshape(3, 3, 3, local_ch, widest), bias_total)


def shifted(v, by):
    depth = v.shape[1]
    row = lax.broadcasted_iota(jnp.int32, v.shape, 1)
    if by == 1:
        return jnp.where(row == 0, 0.0, pltpu.roll(v, 1, 1))
    return jnp.where(row == depth - 1, 0.0, pltpu.roll(v, depth - 1, 1))


def rim_sides(place, span_x, span_y):
    first = place[1] % 2 == 0
    even_at = jnp.where(first, span_y + 1, 0)
    odd_at = jnp.where(first, 0, span_y + 1)
    even_row = jnp.where(first, span_y - 1, 0)
    odd_row = jnp.where(first, 0, span_y - 1)
    x_at = jnp.where(place[0] == 0, span_x + 1, 0)
    x_row = jnp.where(place[0] == 0, span_x - 1, 0)
    return even_at, odd_at, even_row, odd_row, x_at, x_row


def prepare_kernel(place, source, inputs, packed, even, odd, even_corner, odd_corner, arrived):
    copy = pltpu.make_async_copy(source, inputs, arrived)
    copy.start()
    copy.wait()
    span_x, span_y, _, _ = inputs.shape
    half = span_x // 2
    _, _, even_row, odd_row, _, x_row = rim_sides(place, span_x, span_y)
    even[...] = inputs[:, even_row]
    odd[...] = inputs[:, odd_row]
    even_corner[...] = inputs[x_row, even_row]
    odd_corner[...] = inputs[x_row, odd_row]
    packed[...] = jnp.concatenate([inputs[:half], inputs[half:]], axis=3)


def stage_kernel(after, *rest):
    count = (len(rest) - 1) // 2
    sources, targets, arrived = rest[:count], rest[count : 2 * count], rest[-1]
    copies = []
    for source, target in zip(sources, targets):
        parts = source.shape[0] if len(source.shape) == 3 else 1
        for n in range(parts):
            here = pl.ds(n, 1) if parts > 1 else slice(None)
            copies.append(
                pltpu.make_async_copy(source.at[here], target.at[here], arrived.at[len(copies)])
            )
    for copy in copies:
        copy.start()
    for copy in copies:
        copy.wait()


def forward_kernel(
    parts_y, place, weight, inputs, packed, even, odd, beside, even_corner, odd_corner, own, *rest
):
    *others, pair, window, blocks = rest
    span_x, span_y, span_z, lanes = inputs.shape
    half_x = span_x // 2
    half = half_x * span_y * span_z
    even_at, odd_at, _, _, x_at, _ = rim_sides(place, span_x, span_y)

    def spread(v):
        flat = v.astype(F32).reshape(-1, span_z, lanes)
        joined = jnp.concatenate([shifted(flat, 1), flat, shifted(flat, -1)], axis=2)
        return joined.astype(BF16).reshape(v.shape[:-1] + (3 * lanes,))

    nothing = jnp.zeros((span_y + 2, span_z, 3 * lanes), BF16)
    window[0] = nothing
    window[span_x + 1] = nothing
    window[1 : span_x + 1, 1 : span_y + 1] = spread(inputs[...])
    window[1 : span_x + 1, even_at] = spread(even[...])
    has_odd = (place[1] != 0) & (place[1] != parts_y - 1)
    window[1 : span_x + 1, odd_at] = jnp.where(has_odd, spread(odd[...]), jnp.zeros((), BF16))
    across = jnp.where(place[0] == 0, beside[0][..., :lanes], beside[half_x - 1][..., lanes:])
    window[x_at, 1 : span_y + 1] = spread(across)
    window[x_at, even_at] = spread(even_corner[...])
    window[x_at, odd_at] = jnp.where(has_odd, spread(odd_corner[...]), jnp.zeros((), BF16))
    total = None
    for a in range(3):
        for b in range(3):
            cut = window[a : a + span_x, b : b + span_y].reshape(2 * half, 3 * lanes)
            term = jnp.dot(cut, weight[a * 3 + b], preferred_element_type=F32)
            total = term if total is None else total + term
    for d in range(weight.shape[2] // lanes):
        cut = slice(d * lanes, (d + 1) * lanes)
        blocks[d] = jnp.concatenate([total[:half, cut], total[half:, cut]], axis=1)
    own[...] = blocks[place[2]]
    for k, other in enumerate(others):
        other[...] = blocks[place[2] ^ (k + 1)].astype(BF16)
    pair[0] = packed[...]
    pair[1] = beside[...]


def slope_kernel(own, *rest):
    *others, bias, cotangent, active, slope = rest
    half = cotangent.shape[0] // 2
    summed = own[...]
    for other in others:
        summed = summed + other[...].astype(F32)
    offset = bias[...].astype(F32)
    summed = summed + jnp.concatenate([offset, offset], axis=1)
    sigmoid = jax.nn.sigmoid(summed)
    active[...] = (summed * sigmoid).astype(BF16)
    upstream = jnp.concatenate([cotangent[:half], cotangent[half:]], axis=1).astype(F32)
    slope[...] = (upstream * sigmoid * (1.0 + summed * (1.0 - sigmoid))).astype(BF16)


def slot_of(partner):
    return partner ^ (partner >> 1)


def ordered_halves(place, pieces):
    shards, _, _, _, lanes = pieces.shape
    lanes = lanes // 2
    ordered = [pieces[slot_of(place[2] ^ j)] for j in range(shards)]
    return [
        jnp.concatenate([piece[..., h * lanes : (h + 1) * lanes] for piece in ordered], axis=-1)
        for h in range(2)
    ]


def add_terms(place, parts_y, members, slopes, turned, old, store):
    operands = []
    for m, pieces in zip(members, slopes):
        shards, half_x, span_y, span_z, lanes = pieces.shape
        channels, row = shards * lanes // 2, span_y * span_z
        right = jnp.concatenate(
            [part.reshape(half_x * row, channels) for part in ordered_halves(place, pieces)]
        )
        x0, y0 = (place[0] ^ (m // parts_y)) * 2 * half_x, place[1] ^ (m % parts_y)
        operands.append((x0, y0, row, right))
    for a in range(3):
        total = None if old is None else old[a]
        for x0, y0, row, right in operands:
            left = turned[y0, :, pl.ds(pl.multiple_of((x0 + a) * row, row), right.shape[0])]
            term = jnp.dot(left, right, preferred_element_type=F32)
            total = term if total is None else total + term
        store(a, total)


def first_kernel(parts_x, parts_y, place, weight, active, pair, beside_y, sibling, column, *rest):
    activation, turned, sums, weight_turned, volume, unpacked, sent = rest
    half, lanes = active.shape[0], active.shape[1] // 2
    unpacked[:half] = active[:, :lanes]
    unpacked[half:] = active[:, lanes:]
    copy = pltpu.make_async_copy(unpacked, activation, sent)
    copy.start()
    shards, half_x, span_y, span_z, lanes = column.shape
    cells = [(0, pair, 0), (parts_y, pair, 1), (2, beside_y, 1), (parts_y + 2, beside_y, 2)]
    cells += [(m ^ 1, sibling, shards + n) for n, (m, _, _) in enumerate(cells)]
    span_x, lanes = 2 * half_x, lanes // 2
    rows_x, rows_y = parts_x * span_x, parts_y * span_y
    width = 3 * lanes
    zero_x = jnp.zeros((1, rows_y + 2, span_z, width), BF16)
    zero_y = jnp.zeros((rows_x + 2, 1, span_z, width), BF16)
    volume[0:1] = zero_x
    volume[rows_x + 1 : rows_x + 2] = zero_x
    volume[:, 0:1] = zero_y
    volume[:, rows_y + 1 : rows_y + 2] = zero_y
    for m, array, n in cells:
        x0, y0 = (place[0] ^ (m // parts_y)) * span_x, (place[1] ^ (m % parts_y)) * span_y
        v = array[n].astype(F32).reshape(half_x * span_y, span_z, 2 * lanes)
        low, high = shifted(v, 1), shifted(v, -1)
        for h in range(2):
            cut = slice(h * lanes, (h + 1) * lanes)
            joined = jnp.concatenate([low[..., cut], v[..., cut], high[..., cut]], axis=2)
            volume[pl.ds(x0 + 1 + h * half_x, half_x), pl.ds(y0 + 1, span_y)] = joined.astype(
                BF16
            ).reshape(half_x, span_y, span_z, width)
    for y in range(parts_y):
        for b in range(3):
            cut = volume[:, y * span_y + b : (y + 1) * span_y + b]
            turned[y, b * width : (b + 1) * width] = cut.reshape(-1, width).T

    def store(a, total):
        sums[a] = total

    for tap in range(weight.shape[0]):
        weight_turned[tap] = weight[tap].T
    members = (0, 1)
    add_terms(place, parts_y, members, (column, sibling.at[:shards]), turned, None, store)
    copy.wait()


def rows_of(place, pieces, row):
    shards, lanes = column_shape(pieces)
    ordered = [pieces[slot_of(place[2] ^ j), :, row] for j in range(shards)]
    return [
        jnp.concatenate([piece[..., h * lanes : (h + 1) * lanes] for piece in ordered], axis=-1)
        for h in range(2)
    ]


def column_shape(pieces):
    return pieces.shape[0], pieces.shape[-1] // 2


def second_kernel(
    parts_y, members, place, weight, turned, old, column, sibling, *rest
):
    *slopes, partial, sums, window = rest
    shards, half_x, span_y, span_z, _ = column.shape
    span_x, half = 2 * half_x, half_x * span_y * span_z
    even_at, _, even_row, _, _, _ = rim_sides(place, span_x, span_y)
    window[...] = jnp.zeros(window.shape, BF16)
    beside = rows_of(place, sibling.at[:shards], facing_row(even_row, span_y))
    for h, own in enumerate(ordered_halves(place, column)):
        window[1 + h * half_x : 1 + (h + 1) * half_x, 1 : span_y + 1] = own
        window[1 + h * half_x : 1 + (h + 1) * half_x, even_at] = beside[h]
    total = None
    for a in range(3):
        for b in range(3):
            cut = window[2 - a : 2 - a + span_x, 2 - b : 2 - b + span_y]
            term = jnp.dot(
                cut.reshape(2 * half, cut.shape[-1]),
                weight[a * 3 + b],
                preferred_element_type=F32,
            )
            total = term if total is None else total + term
    partial[...] = total.reshape(partial.shape)
    middle_kernel(parts_y, members, place, turned, old, *slopes, sums)


def middle_kernel(parts_y, members, place, turned, old, *rest):
    *slopes, sums = rest

    def store(a, total):
        sums[a] = total

    add_terms(place, parts_y, members, slopes, turned, old, store)


def facing(place, halves):
    low, high = halves
    return jnp.where(place[0] == 0, low[0], high[-1])


def channel_sum(pieces):
    mine = pieces[0].astype(F32).reshape(-1, pieces.shape[-1])
    return jnp.sum(mine, axis=0, keepdims=True)


def rim_kernel(parts_y, members, place, weight, turned, old, partial, *rest):
    *slopes, grid, column, sums, rim_x, rim_y = rest
    shards, half_x, span_y, span_z, _ = slopes[0].shape
    span_x, channels = 2 * half_x, rim_x.shape[-1]
    even_at, odd_at, even_row, odd_row, _, x_row = rim_sides(place, span_x, span_y)
    has_odd = (place[1] != 0) & (place[1] != parts_y - 1)
    rim_x[...] = jnp.zeros(rim_x.shape, BF16)
    rim_y[...] = jnp.zeros(rim_y.shape, BF16)
    rim_x[1 : span_y + 1] = facing(place, ordered_halves(place, slopes[parts_y]))
    even = rows_of(place, slopes[parts_y + 1], facing_row(even_row, span_y))
    rim_x[even_at] = facing(place, even)

    @pl.when(has_odd)
    def _():
        odd = rows_of(place, slopes[3], facing_row(odd_row, span_y))
        for h, rows in enumerate(odd):
            rim_y[1 + h * half_x : 1 + (h + 1) * half_x] = rows

    grid[...] = partial[...]
    tap_x, tap_y = rim_taps(place, odd_row)
    total = None
    for b in range(3):
        cut = rim_x[2 - b : 2 - b + span_y].reshape(span_y * span_z, channels)
        term = jnp.dot(cut, weight[tap_x * 3 + b], preferred_element_type=F32)
        total = term if total is None else total + term
    grid[x_row] += total.reshape((span_y,) + grid.shape[2:])
    total = None
    for a in range(3):
        cut = rim_y[2 - a : 2 - a + span_x].reshape(span_x * span_z, channels)
        term = jnp.dot(cut, weight[a * 3 + tap_y], preferred_element_type=F32)
        total = term if total is None else total + term
    grid[:, odd_row] += total.reshape((span_x,) + grid.shape[2:])
    total = channel_sum(slopes[0])
    for pieces in slopes[1:]:
        total = total + channel_sum(pieces)
    column[...] = total
    middle_kernel(parts_y, members, place, turned, old, *[slopes[m] for m in members], sums)


def rim_taps(place, odd_row):
    return jnp.where(place[0] == 0, 0, 2), jnp.where(odd_row == 0, 2, 0)


def last_kernel(parts_y, member, factor, place, weight, turned, old, partial, column, pieces, *rest):
    input_grad, kernel_grad, bias_grad, grid, sums, cells, bias, sent = rest
    _, half_x, span_y, span_z, _ = pieces.shape
    lanes = pieces.shape[-1] // 2
    span_x = 2 * half_x
    copies = []

    def send(source, target):
        copies.append(pltpu.make_async_copy(source, target, sent.at[len(copies)]))
        copies[-1].start()

    def store(a, total):
        sums[a] = total * factor
        send(sums.at[a], kernel_grad.at[a])

    add_terms(place, parts_y, (member,), (pieces,), turned, old, store)

    _, _, _, odd_row, _, x_row = rim_sides(place, span_x, span_y)
    has_odd = (place[1] != 0) & (place[1] != parts_y - 1)
    tap_x, tap_y = rim_taps(place, odd_row)
    grid[...] = partial[...]

    @pl.when(has_odd)
    def _():
        corner = facing(place, rows_of(place, pieces, facing_row(odd_row, span_y)))
        term = jnp.dot(corner, weight[tap_x * 3 + tap_y], preferred_element_type=F32)
        grid[x_row, odd_row] += term

    summed = grid[...].reshape(span_x * span_y, span_z, 3 * lanes)
    result = (
        shifted(summed[..., :lanes], -1)
        + summed[..., lanes : 2 * lanes]
        + shifted(summed[..., 2 * lanes :], 1)
    )
    cells[...] = result.reshape(-1, lanes).astype(BF16)
    send(cells, input_grad)
    total = column[...] + channel_sum(pieces)
    bias[...] = (total[:, :lanes] + total[:, lanes:]) * factor
    send(bias, bias_grad)
    for copy in copies:
        copy.wait()


def facing_row(row, span_y):
    return span_y - 1 - row


def exchange(x, axes, mask):
    return lax.ppermute(x, axes, [(i, i ^ mask) for i in range(lax.axis_size(axes))])


def body_gathered(inputs, weight, bias, cotangent):
    spans = inputs.shape[:3]
    span_x, span_y, span_z = spans
    local_ch, channels = weight.shape[3:]
    local = span_x * span_y * span_z
    parts_x, parts_y = lax.axis_size("gx"), lax.axis_size("gy")
    count = parts_x * parts_y
    shards = lax.axis_size("ch")
    axes = ("gx", "gy")
    factor = 1.0 / math.sqrt(local * count)
    place = jnp.stack([lax.axis_index(axis) for axis in ("gx", "gy", "ch")]).astype(jnp.int32)
    taps = weight.reshape(9, 3 * local_ch, channels)
    packing = (span_x // 2, span_y, span_z, 2 * local_ch)
    flat = (local // 2, 2 * local_ch)

    def call(kernel, name, outs, args, scratch=()):
        return pl.pallas_call(
            kernel,
            out_shape=[jax.ShapeDtypeStruct(shape, kind) for shape, kind in outs],
            in_specs=[SMEM if x is place else VMEM for x in args],
            out_specs=[VMEM] * len(outs),
            scratch_shapes=[pltpu.VMEM(shape, kind) for shape, kind in scratch],
            compiler_params=PARAMS,
            cost_estimate=pl.CostEstimate(flops=0, bytes_accessed=1024, transcendentals=0),
            name=name,
        )(*args)

    row = (span_x, span_z, local_ch)
    held, packed, even, odd, even_corner, odd_corner = pl.pallas_call(
        prepare_kernel,
        out_shape=[jax.ShapeDtypeStruct(inputs.shape, BF16), jax.ShapeDtypeStruct(packing, BF16)]
        + [jax.ShapeDtypeStruct(row, BF16)] * 2
        + [jax.ShapeDtypeStruct(row[1:], BF16)] * 2,
        in_specs=[SMEM, HBM],
        out_specs=[VMEM] * 6,
        scratch_shapes=[pltpu.SemaphoreType.DMA],
        compiler_params=PARAMS,
        name="prepare",
    )(place, pltpu.with_memory_space_constraint(inputs, pltpu.HBM))
    sources = (taps, cotangent.reshape(local, local_ch), bias.reshape(1, local_ch))
    taps, cotangent, bias = pl.pallas_call(
        stage_kernel,
        out_shape=[jax.ShapeDtypeStruct(x.shape, x.dtype) for x in sources],
        in_specs=[VMEM] + [HBM] * len(sources),
        out_specs=[VMEM] * len(sources),
        scratch_shapes=[pltpu.SemaphoreType.DMA((len(sources) + 8,))],
        compiler_params=PARAMS,
        name="stage",
    )(even_corner, *[pltpu.with_memory_space_constraint(x, pltpu.HBM) for x in sources])
    beside = exchange(packed, axes, parts_y)
    even = exchange(even, axes, 1)
    odd = exchange(odd, axes, 3)
    even_corner = exchange(even_corner, axes, parts_y + 1)
    odd_corner = exchange(odd_corner, axes, parts_y + 3)
    own, *others, pair = call(
        functools.partial(forward_kernel, parts_y),
        "forward",
        [(flat, F32)] + [(flat, BF16)] * (shards - 1) + [((2,) + packing, BF16)],
        [place, taps, held, packed, even, odd, beside, even_corner, odd_corner],
        [((span_x + 2, span_y + 2, span_z, 3 * local_ch), BF16), ((shards,) + flat, F32)],
    )
    order = sorted(range(1, shards), key=lambda k: (k < 2, k))
    others = [exchange(others[k - 1], "ch", k) for k in order]
    active, slope = call(
        slope_kernel,
        "slope",
        [(flat, BF16), (flat, BF16)],
        [own, *others, bias, cotangent],
    )
    rest = [exchange(slope, "ch", k) for k in sorted(range(1, shards), key=slot_of)]
    rest = jnp.stack(rest).reshape((shards - 1,) + packing)
    piece = slope.reshape((1,) + packing)
    x, y = parts_y, 2
    beside_x = exchange(piece, axes, x)
    beside_y = exchange(jnp.concatenate([piece, pair]), axes, y)
    beside_y, beside_x, rest = lax.optimization_barrier((beside_y, beside_x, rest))
    column = jnp.concatenate([piece, rest])
    late_y, late_x = exchange(rest, axes, y), exchange(rest, axes, x)
    sibling = exchange(jnp.concatenate([column, pair, beside_y[1:]]), axes, 1)
    turned_shape = (parts_y, 9 * local_ch, (parts_x * span_x + 2) * span_y * span_z)
    sums_shape = (3, 9 * local_ch, channels)
    first_outs = [((local, local_ch), BF16), (turned_shape, BF16), (sums_shape, F32)]
    first_outs += [((9, channels, 3 * local_ch), BF16)]
    args = [place, taps, active, pair, beside_y, sibling, column]
    activation, turned, sums, taps = pl.pallas_call(
        functools.partial(first_kernel, parts_x, parts_y),
        out_shape=[jax.ShapeDtypeStruct(shape, kind) for shape, kind in first_outs],
        in_specs=[SMEM] + [VMEM] * (len(args) - 1),
        out_specs=[HBM] + [VMEM] * 3,
        scratch_shapes=[
            pltpu.VMEM((parts_x * span_x + 2, parts_y * span_y + 2, span_z, 3 * local_ch), BF16),
            pltpu.VMEM((local, local_ch), BF16),
            pltpu.SemaphoreType.DMA,
        ],
        compiler_params=PARAMS,
        cost_estimate=pl.CostEstimate(flops=0, bytes_accessed=1024, transcendentals=0),
        name="first",
    )(*args)
    slopes = {0: column, 1: sibling[:shards]}
    late_y, late_x, sums = lax.optimization_barrier((late_y, late_x, sums))
    slopes[y] = jnp.concatenate([beside_y[:1], late_y])
    slopes[x] = jnp.concatenate([beside_x, late_x])
    middle = shards // 2
    diagonal = [exchange(slopes[x][:middle], axes, y), exchange(slopes[y][middle:], axes, x)]
    across = [exchange(slopes[m], axes, 1) for m in (y, x)]
    grid_shape = spans + (3 * local_ch,)
    partial, sums = call(
        functools.partial(second_kernel, parts_y, (y, x)),
        "second",
        [(grid_shape, F32), (sums_shape, F32)],
        [place, taps, turned, sums, column, sibling, slopes[y], slopes[x]],
        [((span_x + 2, span_y + 2, span_z, channels), BF16)],
    )
    slopes[y + 1], slopes[x + 1] = across
    (sums,) = call(
        functools.partial(middle_kernel, parts_y, (y + 1, x + 1)),
        "third",
        [(sums_shape, F32)],
        [place, turned, sums, *across],
    )
    *diagonal, sums = lax.optimization_barrier((*diagonal, sums))
    slopes[x + y] = jnp.concatenate(diagonal)
    final = exchange(slopes[x + y], axes, 1)
    partial, column, sums = call(
        functools.partial(rim_kernel, parts_y, (x + y,)),
        "rim",
        [(grid_shape, F32), ((1, 2 * local_ch), F32), (sums_shape, F32)],
        [place, taps, turned, sums, partial] + [slopes[m] for m in range(count - 1)],
        [((span_y + 2, span_z, channels), BF16), ((span_x + 2, span_z, channels), BF16)],
    )
    args = [place, taps, turned, sums, partial, column, final]
    input_grad, kernel_grad, bias_grad = pl.pallas_call(
        functools.partial(last_kernel, parts_y, x + y + 1, factor),
        out_shape=[
            jax.ShapeDtypeStruct((local, local_ch), BF16),
            jax.ShapeDtypeStruct(sums_shape, F32),
            jax.ShapeDtypeStruct((1, local_ch), F32),
        ],
        in_specs=[SMEM] + [VMEM] * (len(args) - 1),
        out_specs=[HBM] * 3,
        scratch_shapes=[
            pltpu.VMEM(grid_shape, F32),
            pltpu.VMEM(sums_shape, F32),
            pltpu.VMEM((local, local_ch), BF16),
            pltpu.VMEM((1, local_ch), F32),
            pltpu.SemaphoreType.DMA((5,)),
        ],
        compiler_params=PARAMS,
        name="last",
    )(*args)
    return (
        activation.reshape(inputs.shape),
        input_grad.reshape(inputs.shape),
        kernel_grad.reshape(weight.shape),
        bias_grad.reshape(local_ch),
    )


def solution(mesh):
    few = (mesh.shape["gx"], mesh.shape["gy"]) == (2, 4)
    return jax.shard_map(
        body_gathered if few else body_reduced,
        mesh=mesh,
        in_specs=(
            P("gx", "gy", None, "ch"),
            P(None, None, None, "ch", None),
            P("ch"),
            P("gx", "gy", None, "ch"),
        ),
        out_specs=(
            P("gx", "gy", None, "ch"),
            P("gx", "gy", None, "ch"),
            P(None, None, None, "ch", None),
            P("ch"),
        ),
        check_vma=False,
    )
```

```python
import functools
import math

import jax
import jax.numpy as jnp
from jax import lax
from jax.experimental import pallas as pl
from jax.experimental.pallas import tpu as pltpu
from jax.sharding import PartitionSpec as P

VMEM = pl.BlockSpec(memory_space=pltpu.VMEM)
HBM = pl.BlockSpec(memory_space=pltpu.HBM)
SMEM = pl.BlockSpec(memory_space=pltpu.SMEM)
PARAMS = pltpu.CompilerParams(vmem_limit_bytes=24 * 1024 * 1024)
F32 = jnp.float32
BF16 = jnp.bfloat16


def with_halo(x, sides, width):
    for axis, dim in sides:
        devices, length = (lax.axis_size(axis), x.shape[dim])
        up = [(i, (i + 1) % devices) for i in range(devices - 1)]
        down = [(j, i) for i, j in up]
        last = lax.slice_in_dim(x, length - width, length, axis=dim)
        initial = lax.slice_in_dim(x, 0, width, axis=dim)
        before = lax.ppermute(last, axis, up)
        after = lax.ppermute(initial, axis, down)
        x = jnp.concatenate([before, x, after], axis=dim)
    return x


def body_reduced(inputs, weight, bias, cotangent):
    span_x, span_y, span_z, local_ch = inputs.shape
    widest = weight.shape[4]
    local_cells = span_x * span_y * span_z
    offsets = [(a, b, c) for a in range(3) for b in range(3) for c in range(3)]
    depth_pad = ((0, 0), (0, 0), (1, 1), (0, 0))
    rimmed = with_halo(inputs, (("gx", 0), ("gy", 1)), 1)
    padded = jnp.pad(rimmed, depth_pad)
    blocks = []
    for a, b, c in offsets:
        blocks.append(
            padded[a : a + span_x, b : b + span_y, c : c + span_z].reshape(local_cells, local_ch)
        )
    patches = jnp.concatenate(blocks, axis=1)
    flat_weight = weight.reshape(27 * local_ch, widest)
    summed = lax.psum_scatter(
        lax.dot_general(flat_weight, patches, (((0,), (1,)), ((), ())), preferred_element_type=F32),
        "ch",
        scatter_dimension=0,
        tiled=True,
    ).T
    summed = summed + bias.astype(F32)[None, :]
    activation = jax.nn.silu(summed).astype(BF16).reshape(span_x, span_y, span_z, local_ch)
    sigmoid_pre = jax.nn.sigmoid(summed)
    slope = (
        cotangent.reshape(local_cells, local_ch).astype(F32)
        * sigmoid_pre
        * (1.0 + summed * (1.0 - sigmoid_pre))
    ).astype(BF16)
    local_bias = jnp.sum(slope.astype(F32), axis=0)
    slope_grid = slope.reshape(span_x, span_y, span_z, local_ch)
    weight_turned = jnp.transpose(weight.reshape(27, local_ch, widest), (0, 2, 1))
    slope_rimmed = with_halo(slope_grid, (("gx", 0), ("gy", 1)), 1)
    piece = lax.all_gather(slope_rimmed, "ch", axis=3, tiled=True)
    extended = jnp.pad(piece, depth_pad)
    running = jnp.zeros((local_cells, local_ch), F32)
    for index, (a, b, c) in enumerate(offsets):
        a, b, c = (2 - a, 2 - b, 2 - c)
        cut = extended[a : a + span_x, b : b + span_y, c : c + span_z].reshape(local_cells, widest)
        running = running + jnp.dot(cut, weight_turned[index], preferred_element_type=F32)
    interior = piece[1 : 1 + span_x, 1 : 1 + span_y].reshape(local_cells, widest)
    product = lax.dot_general(
        patches, interior, (((0,), (0,)), ((), ())), preferred_element_type=F32
    )
    total_cells = local_cells * lax.axis_size("gx") * lax.axis_size("gy")
    factor = 1.0 / math.sqrt(total_cells)
    kernel_total, bias_total = lax.psum((product * factor, local_bias * factor), ("gx", "gy"))
    input_grad = running.astype(BF16).reshape(span_x, span_y, span_z, local_ch)
    return (activation, input_grad, kernel_total.reshape(3, 3, 3, local_ch, widest), bias_total)


def shifted(v, by):
    depth = v.shape[1]
    row = lax.broadcasted_iota(jnp.int32, v.shape, 1)
    if by == 1:
        return jnp.where(row == 0, 0.0, pltpu.roll(v, 1, 1))
    return jnp.where(row == depth - 1, 0.0, pltpu.roll(v, depth - 1, 1))


def rim_sides(place, span_x, span_y):
    first = place[1] % 2 == 0
    even_at = jnp.where(first, span_y + 1, 0)
    odd_at = jnp.where(first, 0, span_y + 1)
    even_row = jnp.where(first, span_y - 1, 0)
    odd_row = jnp.where(first, 0, span_y - 1)
    x_at = jnp.where(place[0] == 0, span_x + 1, 0)
    x_row = jnp.where(place[0] == 0, span_x - 1, 0)
    return even_at, odd_at, even_row, odd_row, x_at, x_row


def prepare_kernel(place, source, inputs, packed, even, odd, even_corner, odd_corner, arrived):
    copy = pltpu.make_async_copy(source, inputs, arrived)
    copy.start()
    copy.wait()
    span_x, span_y, _, _ = inputs.shape
    half = span_x // 2
    _, _, even_row, odd_row, _, x_row = rim_sides(place, span_x, span_y)
    even[...] = inputs[:, even_row]
    odd[...] = inputs[:, odd_row]
    even_corner[...] = inputs[x_row, even_row]
    odd_corner[...] = inputs[x_row, odd_row]
    packed[...] = jnp.concatenate([inputs[:half], inputs[half:]], axis=3)


def stage_kernel(after, *rest):
    count = (len(rest) - 1) // 2
    sources, targets, arrived = rest[:count], rest[count : 2 * count], rest[-1]
    copies = []
    for source, target in zip(sources, targets):
        parts = source.shape[0] if len(source.shape) == 3 else 1
        for n in range(parts):
            here = pl.ds(n, 1) if parts > 1 else slice(None)
            copies.append(
                pltpu.make_async_copy(source.at[here], target.at[here], arrived.at[len(copies)])
            )
    for copy in copies:
        copy.start()
    for copy in copies:
        copy.wait()


def forward_kernel(
    parts_y, place, weight, inputs, packed, even, odd, beside, even_corner, odd_corner, own, *rest
):
    *others, pair, window, blocks = rest
    span_x, span_y, span_z, lanes = inputs.shape
    half_x = span_x // 2
    half = half_x * span_y * span_z
    even_at, odd_at, _, _, x_at, _ = rim_sides(place, span_x, span_y)

    def spread(v):
        flat = v.astype(F32).reshape(-1, span_z, lanes)
        joined = jnp.concatenate([shifted(flat, 1), flat, shifted(flat, -1)], axis=2)
        return joined.astype(BF16).reshape(v.shape[:-1] + (3 * lanes,))

    nothing = jnp.zeros((span_y + 2, span_z, 3 * lanes), BF16)
    window[0] = nothing
    window[span_x + 1] = nothing
    window[1 : span_x + 1, 1 : span_y + 1] = spread(inputs[...])
    window[1 : span_x + 1, even_at] = spread(even[...])
    has_odd = (place[1] != 0) & (place[1] != parts_y - 1)
    window[1 : span_x + 1, odd_at] = jnp.where(has_odd, spread(odd[...]), jnp.zeros((), BF16))
    across = jnp.where(place[0] == 0, beside[0][..., :lanes], beside[half_x - 1][..., lanes:])
    window[x_at, 1 : span_y + 1] = spread(across)
    window[x_at, even_at] = spread(even_corner[...])
    window[x_at, odd_at] = jnp.where(has_odd, spread(odd_corner[...]), jnp.zeros((), BF16))
    total = None
    for a in range(3):
        for b in range(3):
            cut = window[a : a + span_x, b : b + span_y].reshape(2 * half, 3 * lanes)
            term = jnp.dot(cut, weight[a * 3 + b], preferred_element_type=F32)
            total = term if total is None else total + term
    for d in range(weight.shape[2] // lanes):
        cut = slice(d * lanes, (d + 1) * lanes)
        blocks[d] = jnp.concatenate([total[:half, cut], total[half:, cut]], axis=1)
    own[...] = blocks[place[2]]
    for k, other in enumerate(others):
        other[...] = blocks[place[2] ^ (k + 1)].astype(BF16)
    pair[0] = packed[...]
    pair[1] = beside[...]


def slope_kernel(own, *rest):
    *others, bias, cotangent, active, slope = rest
    half = cotangent.shape[0] // 2
    summed = own[...]
    for other in others:
        summed = summed + other[...].astype(F32)
    offset = bias[...].astype(F32)
    summed = summed + jnp.concatenate([offset, offset], axis=1)
    sigmoid = jax.nn.sigmoid(summed)
    active[...] = (summed * sigmoid).astype(BF16)
    upstream = jnp.concatenate([cotangent[:half], cotangent[half:]], axis=1).astype(F32)
    slope[...] = (upstream * sigmoid * (1.0 + summed * (1.0 - sigmoid))).astype(BF16)


def slot_of(partner):
    return partner ^ (partner >> 1)


def ordered_halves(place, pieces):
    shards, _, _, _, lanes = pieces.shape
    lanes = lanes // 2
    ordered = [pieces[slot_of(place[2] ^ j)] for j in range(shards)]
    return [
        jnp.concatenate([piece[..., h * lanes : (h + 1) * lanes] for piece in ordered], axis=-1)
        for h in range(2)
    ]


def add_terms(place, parts_y, members, slopes, turned, old, store):
    operands = []
    for m, pieces in zip(members, slopes):
        shards, half_x, span_y, span_z, lanes = pieces.shape
        channels, row = shards * lanes // 2, span_y * span_z
        right = jnp.concatenate(
            [part.reshape(half_x * row, channels) for part in ordered_halves(place, pieces)]
        )
        x0, y0 = (place[0] ^ (m // parts_y)) * 2 * half_x, place[1] ^ (m % parts_y)
        operands.append((x0, y0, row, right))
    for a in range(3):
        total = None if old is None else old[a]
        for x0, y0, row, right in operands:
            left = turned[y0, :, pl.ds(pl.multiple_of((x0 + a) * row, row), right.shape[0])]
            term = jnp.dot(left, right, preferred_element_type=F32)
            total = term if total is None else total + term
        store(a, total)


def first_kernel(parts_x, parts_y, place, weight, active, pair, beside_y, sibling, column, *rest):
    activation, turned, sums, weight_turned, volume, unpacked, sent = rest
    half, lanes = active.shape[0], active.shape[1] // 2
    unpacked[:half] = active[:, :lanes]
    unpacked[half:] = active[:, lanes:]
    copy = pltpu.make_async_copy(unpacked, activation, sent)
    copy.start()
    shards, half_x, span_y, span_z, lanes = column.shape
    cells = [(0, pair, 0), (parts_y, pair, 1), (2, beside_y, 1), (parts_y + 2, beside_y, 2)]
    cells += [(m ^ 1, sibling, shards + n) for n, (m, _, _) in enumerate(cells)]
    span_x, lanes = 2 * half_x, lanes // 2
    rows_x, rows_y = parts_x * span_x, parts_y * span_y
    width = 3 * lanes
    zero_x = jnp.zeros((1, rows_y + 2, span_z, width), BF16)
    zero_y = jnp.zeros((rows_x + 2, 1, span_z, width), BF16)
    volume[0:1] = zero_x
    volume[rows_x + 1 : rows_x + 2] = zero_x
    volume[:, 0:1] = zero_y
    volume[:, rows_y + 1 : rows_y + 2] = zero_y
    for m, array, n in cells:
        x0, y0 = (place[0] ^ (m // parts_y)) * span_x, (place[1] ^ (m % parts_y)) * span_y
        v = array[n].astype(F32).reshape(half_x * span_y, span_z, 2 * lanes)
        low, high = shifted(v, 1), shifted(v, -1)
        for h in range(2):
            cut = slice(h * lanes, (h + 1) * lanes)
            joined = jnp.concatenate([low[..., cut], v[..., cut], high[..., cut]], axis=2)
            volume[pl.ds(x0 + 1 + h * half_x, half_x), pl.ds(y0 + 1, span_y)] = joined.astype(
                BF16
            ).reshape(half_x, span_y, span_z, width)
    for y in range(parts_y):
        for b in range(3):
            cut = volume[:, y * span_y + b : (y + 1) * span_y + b]
            turned[y, b * width : (b + 1) * width] = cut.reshape(-1, width).T

    def store(a, total):
        sums[a] = total

    for tap in range(weight.shape[0]):
        weight_turned[tap] = weight[tap].T
    members = (0, 1)
    add_terms(place, parts_y, members, (column, sibling.at[:shards]), turned, None, store)
    copy.wait()


def rows_of(place, pieces, row):
    shards, lanes = column_shape(pieces)
    ordered = [pieces[slot_of(place[2] ^ j), :, row] for j in range(shards)]
    return [
        jnp.concatenate([piece[..., h * lanes : (h + 1) * lanes] for piece in ordered], axis=-1)
        for h in range(2)
    ]


def column_shape(pieces):
    return pieces.shape[0], pieces.shape[-1] // 2


def second_kernel(
    parts_y, members, place, weight, turned, old, column, sibling, *rest
):
    *slopes, partial, sums, window = rest
    shards, half_x, span_y, span_z, _ = column.shape
    span_x, half = 2 * half_x, half_x * span_y * span_z
    even_at, _, even_row, _, _, _ = rim_sides(place, span_x, span_y)
    window[...] = jnp.zeros(window.shape, BF16)
    beside = rows_of(place, sibling.at[:shards], facing_row(even_row, span_y))
    for h, own in enumerate(ordered_halves(place, column)):
        window[1 + h * half_x : 1 + (h + 1) * half_x, 1 : span_y + 1] = own
        window[1 + h * half_x : 1 + (h + 1) * half_x, even_at] = beside[h]
    total = None
    for a in range(3):
        for b in range(3):
            cut = window[2 - a : 2 - a + span_x, 2 - b : 2 - b + span_y]
            term = jnp.dot(
                cut.reshape(2 * half, cut.shape[-1]),
                weight[a * 3 + b],
                preferred_element_type=F32,
            )
            total = term if total is None else total + term
    partial[...] = total.reshape(partial.shape)
    middle_kernel(parts_y, members, place, turned, old, *slopes, sums)


def middle_kernel(parts_y, members, place, turned, old, *rest):
    *slopes, sums = rest

    def store(a, total):
        sums[a] = total

    add_terms(place, parts_y, members, slopes, turned, old, store)


def facing(place, halves):
    low, high = halves
    return jnp.where(place[0] == 0, low[0], high[-1])


def channel_sum(pieces):
    mine = pieces[0].astype(F32).reshape(-1, pieces.shape[-1])
    return jnp.sum(mine, axis=0, keepdims=True)


def rim_kernel(parts_y, members, place, weight, turned, old, partial, *rest):
    *slopes, grid, column, sums, rim_x, rim_y = rest
    shards, half_x, span_y, span_z, _ = slopes[0].shape
    span_x, channels = 2 * half_x, rim_x.shape[-1]
    even_at, odd_at, even_row, odd_row, _, x_row = rim_sides(place, span_x, span_y)
    has_odd = (place[1] != 0) & (place[1] != parts_y - 1)
    rim_x[...] = jnp.zeros(rim_x.shape, BF16)
    rim_y[...] = jnp.zeros(rim_y.shape, BF16)
    rim_x[1 : span_y + 1] = facing(place, ordered_halves(place, slopes[parts_y]))
    even = rows_of(place, slopes[parts_y + 1], facing_row(even_row, span_y))
    rim_x[even_at] = facing(place, even)

    @pl.when(has_odd)
    def _():
        odd = rows_of(place, slopes[3], facing_row(odd_row, span_y))
        for h, rows in enumerate(odd):
            rim_y[1 + h * half_x : 1 + (h + 1) * half_x] = rows

    grid[...] = partial[...]
    tap_x, tap_y = rim_taps(place, odd_row)
    total = None
    for b in range(3):
        cut = rim_x[2 - b : 2 - b + span_y].reshape(span_y * span_z, channels)
        term = jnp.dot(cut, weight[tap_x * 3 + b], preferred_element_type=F32)
        total = term if total is None else total + term
    grid[x_row] += total.reshape((span_y,) + grid.shape[2:])
    total = None
    for a in range(3):
        cut = rim_y[2 - a : 2 - a + span_x].reshape(span_x * span_z, channels)
        term = jnp.dot(cut, weight[a * 3 + tap_y], preferred_element_type=F32)
        total = term if total is None else total + term
    grid[:, odd_row] += total.reshape((span_x,) + grid.shape[2:])
    total = channel_sum(slopes[0])
    for pieces in slopes[1:]:
        total = total + channel_sum(pieces)
    column[...] = total
    middle_kernel(parts_y, members, place, turned, old, *[slopes[m] for m in members], sums)


def rim_taps(place, odd_row):
    return jnp.where(place[0] == 0, 0, 2), jnp.where(odd_row == 0, 2, 0)


def last_kernel(
    parts_y, member, factor, place, weight, turned, old, partial, column, beside, pieces, *rest
):
    input_grad, kernel_grad, bias_grad, grid, sums, cells, bias, sent = rest
    _, half_x, span_y, span_z, _ = pieces.shape
    lanes = pieces.shape[-1] // 2
    span_x = 2 * half_x
    copies = []

    def send(source, target):
        copies.append(pltpu.make_async_copy(source, target, sent.at[len(copies)]))
        copies[-1].start()

    def store(a, total):
        sums[a] = total * factor
        send(sums.at[a], kernel_grad.at[a])

    add_terms(place, parts_y, (member,), (pieces,), turned, old, store)

    _, _, _, odd_row, _, x_row = rim_sides(place, span_x, span_y)
    has_odd = (place[1] != 0) & (place[1] != parts_y - 1)
    tap_x, tap_y = rim_taps(place, odd_row)
    grid[...] = partial[...]

    @pl.when(has_odd)
    def _():
        corner = facing(place, rows_of(place, pieces, facing_row(odd_row, span_y)))
        term = jnp.dot(corner, weight[tap_x * 3 + tap_y], preferred_element_type=F32)
        grid[x_row, odd_row] += term

    summed = grid[...].reshape(span_x * span_y, span_z, 3 * lanes)
    result = (
        shifted(summed[..., :lanes], -1)
        + summed[..., lanes : 2 * lanes]
        + shifted(summed[..., 2 * lanes :], 1)
    )
    cells[...] = result.reshape(-1, lanes).astype(BF16)
    send(cells, input_grad)
    total = column[...] + channel_sum(beside) + channel_sum(pieces)
    bias[...] = (total[:, :lanes] + total[:, lanes:]) * factor
    send(bias, bias_grad)
    for copy in copies:
        copy.wait()


def facing_row(row, span_y):
    return span_y - 1 - row


def exchange(x, axes, mask):
    return lax.ppermute(x, axes, [(i, i ^ mask) for i in range(lax.axis_size(axes))])


def body_gathered(inputs, weight, bias, cotangent):
    spans = inputs.shape[:3]
    span_x, span_y, span_z = spans
    local_ch, channels = weight.shape[3:]
    local = span_x * span_y * span_z
    parts_x, parts_y = lax.axis_size("gx"), lax.axis_size("gy")
    count = parts_x * parts_y
    shards = lax.axis_size("ch")
    axes = ("gx", "gy")
    factor = 1.0 / math.sqrt(local * count)
    place = jnp.stack([lax.axis_index(axis) for axis in ("gx", "gy", "ch")]).astype(jnp.int32)
    taps = weight.reshape(9, 3 * local_ch, channels)
    packing = (span_x // 2, span_y, span_z, 2 * local_ch)
    flat = (local // 2, 2 * local_ch)

    def call(kernel, name, outs, args, scratch=()):
        return pl.pallas_call(
            kernel,
            out_shape=[jax.ShapeDtypeStruct(shape, kind) for shape, kind in outs],
            in_specs=[SMEM if x is place else VMEM for x in args],
            out_specs=[VMEM] * len(outs),
            scratch_shapes=[pltpu.VMEM(shape, kind) for shape, kind in scratch],
            compiler_params=PARAMS,
            cost_estimate=pl.CostEstimate(flops=0, bytes_accessed=1024, transcendentals=0),
            name=name,
        )(*args)

    row = (span_x, span_z, local_ch)
    held, packed, even, odd, even_corner, odd_corner = pl.pallas_call(
        prepare_kernel,
        out_shape=[jax.ShapeDtypeStruct(inputs.shape, BF16), jax.ShapeDtypeStruct(packing, BF16)]
        + [jax.ShapeDtypeStruct(row, BF16)] * 2
        + [jax.ShapeDtypeStruct(row[1:], BF16)] * 2,
        in_specs=[SMEM, HBM],
        out_specs=[VMEM] * 6,
        scratch_shapes=[pltpu.SemaphoreType.DMA],
        compiler_params=PARAMS,
        name="prepare",
    )(place, pltpu.with_memory_space_constraint(inputs, pltpu.HBM))
    sources = (taps, cotangent.reshape(local, local_ch), bias.reshape(1, local_ch))
    taps, cotangent, bias = pl.pallas_call(
        stage_kernel,
        out_shape=[jax.ShapeDtypeStruct(x.shape, x.dtype) for x in sources],
        in_specs=[VMEM] + [HBM] * len(sources),
        out_specs=[VMEM] * len(sources),
        scratch_shapes=[pltpu.SemaphoreType.DMA((len(sources) + 8,))],
        compiler_params=PARAMS,
        name="stage",
    )(even_corner, *[pltpu.with_memory_space_constraint(x, pltpu.HBM) for x in sources])
    beside = exchange(packed, axes, parts_y)
    even = exchange(even, axes, 1)
    odd = exchange(odd, axes, 3)
    even_corner = exchange(even_corner, axes, parts_y + 1)
    odd_corner = exchange(odd_corner, axes, parts_y + 3)
    own, *others, pair = call(
        functools.partial(forward_kernel, parts_y),
        "forward",
        [(flat, F32)] + [(flat, BF16)] * (shards - 1) + [((2,) + packing, BF16)],
        [place, taps, held, packed, even, odd, beside, even_corner, odd_corner],
        [((span_x + 2, span_y + 2, span_z, 3 * local_ch), BF16), ((shards,) + flat, F32)],
    )
    order = sorted(range(1, shards), key=lambda k: (k < 2, k))
    others = [exchange(others[k - 1], "ch", k) for k in order]
    active, slope = call(
        slope_kernel,
        "slope",
        [(flat, BF16), (flat, BF16)],
        [own, *others, bias, cotangent],
    )
    rest = [exchange(slope, "ch", k) for k in sorted(range(1, shards), key=slot_of)]
    rest = jnp.stack(rest).reshape((shards - 1,) + packing)
    piece = slope.reshape((1,) + packing)
    x, y = parts_y, 2
    beside_x = exchange(piece, axes, x)
    beside_y = exchange(jnp.concatenate([piece, pair]), axes, y)
    beside_y, beside_x, rest = lax.optimization_barrier((beside_y, beside_x, rest))
    column = jnp.concatenate([piece, rest])
    late_y, late_x = exchange(rest, axes, y), exchange(rest, axes, x)
    sibling = exchange(jnp.concatenate([column, pair, beside_y[1:]]), axes, 1)
    turned_shape = (parts_y, 9 * local_ch, (parts_x * span_x + 2) * span_y * span_z)
    sums_shape = (3, 9 * local_ch, channels)
    first_outs = [((local, local_ch), BF16), (turned_shape, BF16), (sums_shape, F32)]
    first_outs += [((9, channels, 3 * local_ch), BF16)]
    args = [place, taps, active, pair, beside_y, sibling, column]
    activation, turned, sums, taps = pl.pallas_call(
        functools.partial(first_kernel, parts_x, parts_y),
        out_shape=[jax.ShapeDtypeStruct(shape, kind) for shape, kind in first_outs],
        in_specs=[SMEM] + [VMEM] * (len(args) - 1),
        out_specs=[HBM] + [VMEM] * 3,
        scratch_shapes=[
            pltpu.VMEM((parts_x * span_x + 2, parts_y * span_y + 2, span_z, 3 * local_ch), BF16),
            pltpu.VMEM((local, local_ch), BF16),
            pltpu.SemaphoreType.DMA,
        ],
        compiler_params=PARAMS,
        cost_estimate=pl.CostEstimate(flops=0, bytes_accessed=1024, transcendentals=0),
        name="first",
    )(*args)
    slopes = {0: column, 1: sibling[:shards]}
    late_y, late_x, sums = lax.optimization_barrier((late_y, late_x, sums))
    slopes[y] = jnp.concatenate([beside_y[:1], late_y])
    slopes[x] = jnp.concatenate([beside_x, late_x])
    middle = shards // 2
    diagonal = [exchange(slopes[x][:middle], axes, y), exchange(slopes[y][middle:], axes, x)]
    across = [exchange(slopes[m], axes, 1) for m in (y, x)]
    grid_shape = spans + (3 * local_ch,)
    partial, sums = call(
        functools.partial(second_kernel, parts_y, (y, x)),
        "second",
        [(grid_shape, F32), (sums_shape, F32)],
        [place, taps, turned, sums, column, sibling, slopes[y], slopes[x]],
        [((span_x + 2, span_y + 2, span_z, channels), BF16)],
    )
    slopes[y + 1], slopes[x + 1] = across
    partial, column, sums = call(
        functools.partial(rim_kernel, parts_y, (y + 1, x + 1)),
        "third",
        [(grid_shape, F32), ((1, 2 * local_ch), F32), (sums_shape, F32)],
        [place, taps, turned, sums, partial] + [slopes[m] for m in range(x + y)],
        [((span_y + 2, span_z, channels), BF16), ((span_x + 2, span_z, channels), BF16)],
    )
    *diagonal, sums = lax.optimization_barrier((*diagonal, sums))
    slopes[x + y] = jnp.concatenate(diagonal)
    final = exchange(slopes[x + y], axes, 1)
    (sums,) = call(
        functools.partial(middle_kernel, parts_y, (x + y,)),
        "fourth",
        [(sums_shape, F32)],
        [place, turned, sums, slopes[x + y]],
    )
    args = [place, taps, turned, sums, partial, column, slopes[x + y], final]
    input_grad, kernel_grad, bias_grad = pl.pallas_call(
        functools.partial(last_kernel, parts_y, x + y + 1, factor),
        out_shape=[
            jax.ShapeDtypeStruct((local, local_ch), BF16),
            jax.ShapeDtypeStruct(sums_shape, F32),
            jax.ShapeDtypeStruct((1, local_ch), F32),
        ],
        in_specs=[SMEM] + [VMEM] * (len(args) - 1),
        out_specs=[HBM] * 3,
        scratch_shapes=[
            pltpu.VMEM(grid_shape, F32),
            pltpu.VMEM(sums_shape, F32),
            pltpu.VMEM((local, local_ch), BF16),
            pltpu.VMEM((1, local_ch), F32),
            pltpu.SemaphoreType.DMA((5,)),
        ],
        compiler_params=PARAMS,
        name="last",
    )(*args)
    return (
        activation.reshape(inputs.shape),
        input_grad.reshape(inputs.shape),
        kernel_grad.reshape(weight.shape),
        bias_grad.reshape(local_ch),
    )


def solution(mesh):
    few = (mesh.shape["gx"], mesh.shape["gy"]) == (2, 4)
    return jax.shard_map(
        body_gathered if few else body_reduced,
        mesh=mesh,
        in_specs=(
            P("gx", "gy", None, "ch"),
            P(None, None, None, "ch", None),
            P("ch"),
            P("gx", "gy", None, "ch"),
        ),
        out_specs=(
            P("gx", "gy", None, "ch"),
            P("gx", "gy", None, "ch"),
            P(None, None, None, "ch", None),
            P("ch"),
        ),
        check_vma=False,
    )
```

```python
import functools
import math

import jax
import jax.numpy as jnp
from jax import lax
from jax.experimental import pallas as pl
from jax.experimental.pallas import tpu as pltpu
from jax.sharding import PartitionSpec as P

VMEM = pl.BlockSpec(memory_space=pltpu.VMEM)
HBM = pl.BlockSpec(memory_space=pltpu.HBM)
SMEM = pl.BlockSpec(memory_space=pltpu.SMEM)
PARAMS = pltpu.CompilerParams(vmem_limit_bytes=24 * 1024 * 1024)
F32 = jnp.float32
BF16 = jnp.bfloat16


def with_halo(x, sides, width):
    for axis, dim in sides:
        devices, length = (lax.axis_size(axis), x.shape[dim])
        up = [(i, (i + 1) % devices) for i in range(devices - 1)]
        down = [(j, i) for i, j in up]
        last = lax.slice_in_dim(x, length - width, length, axis=dim)
        initial = lax.slice_in_dim(x, 0, width, axis=dim)
        before = lax.ppermute(last, axis, up)
        after = lax.ppermute(initial, axis, down)
        x = jnp.concatenate([before, x, after], axis=dim)
    return x


def body_reduced(inputs, weight, bias, cotangent):
    span_x, span_y, span_z, local_ch = inputs.shape
    widest = weight.shape[4]
    local_cells = span_x * span_y * span_z
    offsets = [(a, b, c) for a in range(3) for b in range(3) for c in range(3)]
    depth_pad = ((0, 0), (0, 0), (1, 1), (0, 0))
    rimmed = with_halo(inputs, (("gx", 0), ("gy", 1)), 1)
    padded = jnp.pad(rimmed, depth_pad)
    blocks = []
    for a, b, c in offsets:
        blocks.append(
            padded[a : a + span_x, b : b + span_y, c : c + span_z].reshape(local_cells, local_ch)
        )
    patches = jnp.concatenate(blocks, axis=1)
    flat_weight = weight.reshape(27 * local_ch, widest)
    summed = lax.psum_scatter(
        lax.dot_general(flat_weight, patches, (((0,), (1,)), ((), ())), preferred_element_type=F32),
        "ch",
        scatter_dimension=0,
        tiled=True,
    ).T
    summed = summed + bias.astype(F32)[None, :]
    activation = jax.nn.silu(summed).astype(BF16).reshape(span_x, span_y, span_z, local_ch)
    sigmoid_pre = jax.nn.sigmoid(summed)
    slope = (
        cotangent.reshape(local_cells, local_ch).astype(F32)
        * sigmoid_pre
        * (1.0 + summed * (1.0 - sigmoid_pre))
    ).astype(BF16)
    local_bias = jnp.sum(slope.astype(F32), axis=0)
    slope_grid = slope.reshape(span_x, span_y, span_z, local_ch)
    weight_turned = jnp.transpose(weight.reshape(27, local_ch, widest), (0, 2, 1))
    slope_rimmed = with_halo(slope_grid, (("gx", 0), ("gy", 1)), 1)
    piece = lax.all_gather(slope_rimmed, "ch", axis=3, tiled=True)
    extended = jnp.pad(piece, depth_pad)
    running = jnp.zeros((local_cells, local_ch), F32)
    for index, (a, b, c) in enumerate(offsets):
        a, b, c = (2 - a, 2 - b, 2 - c)
        cut = extended[a : a + span_x, b : b + span_y, c : c + span_z].reshape(local_cells, widest)
        running = running + jnp.dot(cut, weight_turned[index], preferred_element_type=F32)
    interior = piece[1 : 1 + span_x, 1 : 1 + span_y].reshape(local_cells, widest)
    product = lax.dot_general(
        patches, interior, (((0,), (0,)), ((), ())), preferred_element_type=F32
    )
    total_cells = local_cells * lax.axis_size("gx") * lax.axis_size("gy")
    factor = 1.0 / math.sqrt(total_cells)
    kernel_total, bias_total = lax.psum((product * factor, local_bias * factor), ("gx", "gy"))
    input_grad = running.astype(BF16).reshape(span_x, span_y, span_z, local_ch)
    return (activation, input_grad, kernel_total.reshape(3, 3, 3, local_ch, widest), bias_total)


def shifted(v, by):
    depth = v.shape[1]
    row = lax.broadcasted_iota(jnp.int32, v.shape, 1)
    if by == 1:
        return jnp.where(row == 0, 0.0, pltpu.roll(v, 1, 1))
    return jnp.where(row == depth - 1, 0.0, pltpu.roll(v, depth - 1, 1))


def rim_sides(place, span_x, span_y):
    first = place[1] % 2 == 0
    even_at = jnp.where(first, span_y + 1, 0)
    odd_at = jnp.where(first, 0, span_y + 1)
    even_row = jnp.where(first, span_y - 1, 0)
    odd_row = jnp.where(first, 0, span_y - 1)
    x_at = jnp.where(place[0] == 0, span_x + 1, 0)
    x_row = jnp.where(place[0] == 0, span_x - 1, 0)
    return even_at, odd_at, even_row, odd_row, x_at, x_row


def prepare_kernel(place, source, inputs, packed, even, odd, even_corner, odd_corner, arrived):
    copy = pltpu.make_async_copy(source, inputs, arrived)
    copy.start()
    copy.wait()
    span_x, span_y, _, _ = inputs.shape
    half = span_x // 2
    _, _, even_row, odd_row, _, x_row = rim_sides(place, span_x, span_y)
    even[...] = inputs[:, even_row]
    odd[...] = inputs[:, odd_row]
    even_corner[...] = inputs[x_row, even_row]
    odd_corner[...] = inputs[x_row, odd_row]
    packed[...] = jnp.concatenate([inputs[:half], inputs[half:]], axis=3)


def stage_kernel(after, *rest):
    count = (len(rest) - 1) // 2
    sources, targets, arrived = rest[:count], rest[count : 2 * count], rest[-1]
    copies = []
    for source, target in zip(sources, targets):
        parts = source.shape[0] if len(source.shape) == 3 else 1
        for n in range(parts):
            here = pl.ds(n, 1) if parts > 1 else slice(None)
            copies.append(
                pltpu.make_async_copy(source.at[here], target.at[here], arrived.at[len(copies)])
            )
    for copy in copies:
        copy.start()
    for copy in copies:
        copy.wait()


def forward_kernel(
    parts_y, place, weight, inputs, packed, even, odd, beside, even_corner, odd_corner, own, *rest
):
    *others, pair, window, blocks = rest
    span_x, span_y, span_z, lanes = inputs.shape
    half_x = span_x // 2
    half = half_x * span_y * span_z
    even_at, odd_at, _, _, x_at, _ = rim_sides(place, span_x, span_y)

    def spread(v):
        flat = v.astype(F32).reshape(-1, span_z, lanes)
        joined = jnp.concatenate([shifted(flat, 1), flat, shifted(flat, -1)], axis=2)
        return joined.astype(BF16).reshape(v.shape[:-1] + (3 * lanes,))

    nothing = jnp.zeros((span_y + 2, span_z, 3 * lanes), BF16)
    window[0] = nothing
    window[span_x + 1] = nothing
    window[1 : span_x + 1, 1 : span_y + 1] = spread(inputs[...])
    window[1 : span_x + 1, even_at] = spread(even[...])
    has_odd = (place[1] != 0) & (place[1] != parts_y - 1)
    window[1 : span_x + 1, odd_at] = jnp.where(has_odd, spread(odd[...]), jnp.zeros((), BF16))
    across = jnp.where(place[0] == 0, beside[0][..., :lanes], beside[half_x - 1][..., lanes:])
    window[x_at, 1 : span_y + 1] = spread(across)
    window[x_at, even_at] = spread(even_corner[...])
    window[x_at, odd_at] = jnp.where(has_odd, spread(odd_corner[...]), jnp.zeros((), BF16))
    total = None
    for a in range(3):
        for b in range(3):
            cut = window[a : a + span_x, b : b + span_y].reshape(2 * half, 3 * lanes)
            term = jnp.dot(cut, weight[a * 3 + b], preferred_element_type=F32)
            total = term if total is None else total + term
    for d in range(weight.shape[2] // lanes):
        cut = slice(d * lanes, (d + 1) * lanes)
        blocks[d] = jnp.concatenate([total[:half, cut], total[half:, cut]], axis=1)
    own[...] = blocks[place[2]]
    for k, other in enumerate(others):
        other[...] = blocks[place[2] ^ (k + 1)].astype(BF16)
    pair[0] = packed[...]
    pair[1] = beside[...]


def slope_kernel(own, *rest):
    *others, bias, cotangent, active, slope = rest
    half = cotangent.shape[0] // 2
    summed = own[...]
    for other in others:
        summed = summed + other[...].astype(F32)
    offset = bias[...].astype(F32)
    summed = summed + jnp.concatenate([offset, offset], axis=1)
    sigmoid = jax.nn.sigmoid(summed)
    active[...] = (summed * sigmoid).astype(BF16)
    upstream = jnp.concatenate([cotangent[:half], cotangent[half:]], axis=1).astype(F32)
    slope[...] = (upstream * sigmoid * (1.0 + summed * (1.0 - sigmoid))).astype(BF16)


def slot_of(partner):
    return ((partner & 1) << 1) | ((partner ^ (partner >> 1)) & 1)


def ordered_halves(place, pieces):
    shards, _, _, _, lanes = pieces.shape
    lanes = lanes // 2
    ordered = [pieces[slot_of(place[2] ^ j)] for j in range(shards)]
    return [
        jnp.concatenate([piece[..., h * lanes : (h + 1) * lanes] for piece in ordered], axis=-1)
        for h in range(2)
    ]


def add_terms(place, parts_y, members, slopes, turned, old, store):
    operands = []
    for m, pieces in zip(members, slopes):
        shards, half_x, span_y, span_z, lanes = pieces.shape
        channels, row = shards * lanes // 2, span_y * span_z
        right = jnp.concatenate(
            [part.reshape(half_x * row, channels) for part in ordered_halves(place, pieces)]
        )
        x0, y0 = (place[0] ^ (m // parts_y)) * 2 * half_x, place[1] ^ (m % parts_y)
        operands.append((x0, y0, row, right))
    for a in range(3):
        total = None if old is None else old[a]
        for x0, y0, row, right in operands:
            left = turned[y0, :, pl.ds(pl.multiple_of((x0 + a) * row, row), right.shape[0])]
            term = jnp.dot(left, right, preferred_element_type=F32)
            total = term if total is None else total + term
        store(a, total)


def first_kernel(parts_x, parts_y, place, weight, active, pair, beside_y, sibling, column, *rest):
    activation, turned, sums, weight_turned, volume, unpacked, sent = rest
    half, lanes = active.shape[0], active.shape[1] // 2
    unpacked[:half] = active[:, :lanes]
    unpacked[half:] = active[:, lanes:]
    copy = pltpu.make_async_copy(unpacked, activation, sent)
    copy.start()
    shards, half_x, span_y, span_z, lanes = column.shape
    cells = [(0, pair, 0), (parts_y, pair, 1), (2, beside_y, 1), (parts_y + 2, beside_y, 2)]
    cells += [(m ^ 1, sibling, shards + n) for n, (m, _, _) in enumerate(cells)]
    span_x, lanes = 2 * half_x, lanes // 2
    rows_x, rows_y = parts_x * span_x, parts_y * span_y
    width = 3 * lanes
    zero_x = jnp.zeros((1, rows_y + 2, span_z, width), BF16)
    zero_y = jnp.zeros((rows_x + 2, 1, span_z, width), BF16)
    volume[0:1] = zero_x
    volume[rows_x + 1 : rows_x + 2] = zero_x
    volume[:, 0:1] = zero_y
    volume[:, rows_y + 1 : rows_y + 2] = zero_y
    for m, array, n in cells:
        x0, y0 = (place[0] ^ (m // parts_y)) * span_x, (place[1] ^ (m % parts_y)) * span_y
        v = array[n].astype(F32).reshape(half_x * span_y, span_z, 2 * lanes)
        low, high = shifted(v, 1), shifted(v, -1)
        for h in range(2):
            cut = slice(h * lanes, (h + 1) * lanes)
            joined = jnp.concatenate([low[..., cut], v[..., cut], high[..., cut]], axis=2)
            volume[pl.ds(x0 + 1 + h * half_x, half_x), pl.ds(y0 + 1, span_y)] = joined.astype(
                BF16
            ).reshape(half_x, span_y, span_z, width)
    for y in range(parts_y):
        for b in range(3):
            cut = volume[:, y * span_y + b : (y + 1) * span_y + b]
            turned[y, b * width : (b + 1) * width] = cut.reshape(-1, width).T

    def store(a, total):
        sums[a] = total

    for tap in range(weight.shape[0]):
        weight_turned[tap] = weight[tap].T
    members = (0, 1)
    add_terms(place, parts_y, members, (column, sibling.at[:shards]), turned, None, store)
    copy.wait()


def rows_of(place, pieces, row):
    shards, lanes = column_shape(pieces)
    ordered = [pieces[slot_of(place[2] ^ j), :, row] for j in range(shards)]
    return [
        jnp.concatenate([piece[..., h * lanes : (h + 1) * lanes] for piece in ordered], axis=-1)
        for h in range(2)
    ]


def column_shape(pieces):
    return pieces.shape[0], pieces.shape[-1] // 2


def second_kernel(
    parts_y, members, place, weight, turned, old, column, sibling, *rest
):
    *slopes, partial, sums, window = rest
    shards, half_x, span_y, span_z, _ = column.shape
    span_x, half = 2 * half_x, half_x * span_y * span_z
    even_at, _, even_row, _, _, _ = rim_sides(place, span_x, span_y)
    window[...] = jnp.zeros(window.shape, BF16)
    beside = rows_of(place, sibling.at[:shards], facing_row(even_row, span_y))
    for h, own in enumerate(ordered_halves(place, column)):
        window[1 + h * half_x : 1 + (h + 1) * half_x, 1 : span_y + 1] = own
        window[1 + h * half_x : 1 + (h + 1) * half_x, even_at] = beside[h]
    total = None
    for a in range(3):
        for b in range(3):
            cut = window[2 - a : 2 - a + span_x, 2 - b : 2 - b + span_y]
            term = jnp.dot(
                cut.reshape(2 * half, cut.shape[-1]),
                weight[a * 3 + b],
                preferred_element_type=F32,
            )
            total = term if total is None else total + term
    partial[...] = total.reshape(partial.shape)
    middle_kernel(parts_y, members, place, turned, old, *slopes, sums)


def middle_kernel(parts_y, members, place, turned, old, *rest):
    *slopes, sums = rest

    def store(a, total):
        sums[a] = total

    add_terms(place, parts_y, members, slopes, turned, old, store)


def facing(place, halves):
    low, high = halves
    return jnp.where(place[0] == 0, low[0], high[-1])


def channel_sum(pieces):
    mine = pieces[0].astype(F32).reshape(-1, pieces.shape[-1])
    return jnp.sum(mine, axis=0, keepdims=True)


def rim_kernel(parts_y, members, place, weight, turned, old, partial, *rest):
    *slopes, grid, column, sums, rim_x, rim_y = rest
    shards, half_x, span_y, span_z, _ = slopes[0].shape
    span_x, channels = 2 * half_x, rim_x.shape[-1]
    even_at, odd_at, even_row, odd_row, _, x_row = rim_sides(place, span_x, span_y)
    has_odd = (place[1] != 0) & (place[1] != parts_y - 1)
    rim_x[...] = jnp.zeros(rim_x.shape, BF16)
    rim_y[...] = jnp.zeros(rim_y.shape, BF16)
    rim_x[1 : span_y + 1] = facing(place, ordered_halves(place, slopes[parts_y]))
    even = rows_of(place, slopes[parts_y + 1], facing_row(even_row, span_y))
    rim_x[even_at] = facing(place, even)

    @pl.when(has_odd)
    def _():
        odd = rows_of(place, slopes[3], facing_row(odd_row, span_y))
        for h, rows in enumerate(odd):
            rim_y[1 + h * half_x : 1 + (h + 1) * half_x] = rows

    grid[...] = partial[...]
    tap_x, tap_y = rim_taps(place, odd_row)
    total = None
    for b in range(3):
        cut = rim_x[2 - b : 2 - b + span_y].reshape(span_y * span_z, channels)
        term = jnp.dot(cut, weight[tap_x * 3 + b], preferred_element_type=F32)
        total = term if total is None else total + term
    grid[x_row] += total.reshape((span_y,) + grid.shape[2:])
    total = None
    for a in range(3):
        cut = rim_y[2 - a : 2 - a + span_x].reshape(span_x * span_z, channels)
        term = jnp.dot(cut, weight[a * 3 + tap_y], preferred_element_type=F32)
        total = term if total is None else total + term
    grid[:, odd_row] += total.reshape((span_x,) + grid.shape[2:])
    total = channel_sum(slopes[0])
    for pieces in slopes[1:]:
        total = total + channel_sum(pieces)
    column[...] = total
    middle_kernel(parts_y, members, place, turned, old, *[slopes[m] for m in members], sums)


def rim_taps(place, odd_row):
    return jnp.where(place[0] == 0, 0, 2), jnp.where(odd_row == 0, 2, 0)


def last_kernel(
    parts_y, member, factor, place, weight, turned, old, partial, column, beside, pieces, *rest
):
    input_grad, kernel_grad, bias_grad, grid, sums, cells, bias, sent = rest
    _, half_x, span_y, span_z, _ = pieces.shape
    lanes = pieces.shape[-1] // 2
    span_x = 2 * half_x
    copies = []

    def send(source, target):
        copies.append(pltpu.make_async_copy(source, target, sent.at[len(copies)]))
        copies[-1].start()

    def store(a, total):
        sums[a] = total * factor
        send(sums.at[a], kernel_grad.at[a])

    add_terms(place, parts_y, (member,), (pieces,), turned, old, store)

    _, _, _, odd_row, _, x_row = rim_sides(place, span_x, span_y)
    has_odd = (place[1] != 0) & (place[1] != parts_y - 1)
    tap_x, tap_y = rim_taps(place, odd_row)
    grid[...] = partial[...]

    @pl.when(has_odd)
    def _():
        corner = facing(place, rows_of(place, pieces, facing_row(odd_row, span_y)))
        term = jnp.dot(corner, weight[tap_x * 3 + tap_y], preferred_element_type=F32)
        grid[x_row, odd_row] += term

    summed = grid[...].reshape(span_x * span_y, span_z, 3 * lanes)
    result = (
        shifted(summed[..., :lanes], -1)
        + summed[..., lanes : 2 * lanes]
        + shifted(summed[..., 2 * lanes :], 1)
    )
    cells[...] = result.reshape(-1, lanes).astype(BF16)
    send(cells, input_grad)
    total = column[...] + channel_sum(beside) + channel_sum(pieces)
    bias[...] = (total[:, :lanes] + total[:, lanes:]) * factor
    send(bias, bias_grad)
    for copy in copies:
        copy.wait()


def facing_row(row, span_y):
    return span_y - 1 - row


def exchange(x, axes, mask):
    return lax.ppermute(x, axes, [(i, i ^ mask) for i in range(lax.axis_size(axes))])


def body_gathered(inputs, weight, bias, cotangent):
    spans = inputs.shape[:3]
    span_x, span_y, span_z = spans
    local_ch, channels = weight.shape[3:]
    local = span_x * span_y * span_z
    parts_x, parts_y = lax.axis_size("gx"), lax.axis_size("gy")
    count = parts_x * parts_y
    shards = lax.axis_size("ch")
    axes = ("gx", "gy")
    factor = 1.0 / math.sqrt(local * count)
    place = jnp.stack([lax.axis_index(axis) for axis in ("gx", "gy", "ch")]).astype(jnp.int32)
    taps = weight.reshape(9, 3 * local_ch, channels)
    packing = (span_x // 2, span_y, span_z, 2 * local_ch)
    flat = (local // 2, 2 * local_ch)

    def call(kernel, name, outs, args, scratch=()):
        return pl.pallas_call(
            kernel,
            out_shape=[jax.ShapeDtypeStruct(shape, kind) for shape, kind in outs],
            in_specs=[SMEM if x is place else VMEM for x in args],
            out_specs=[VMEM] * len(outs),
            scratch_shapes=[pltpu.VMEM(shape, kind) for shape, kind in scratch],
            compiler_params=PARAMS,
            cost_estimate=pl.CostEstimate(flops=0, bytes_accessed=1024, transcendentals=0),
            name=name,
        )(*args)

    row = (span_x, span_z, local_ch)
    held, packed, even, odd, even_corner, odd_corner = pl.pallas_call(
        prepare_kernel,
        out_shape=[jax.ShapeDtypeStruct(inputs.shape, BF16), jax.ShapeDtypeStruct(packing, BF16)]
        + [jax.ShapeDtypeStruct(row, BF16)] * 2
        + [jax.ShapeDtypeStruct(row[1:], BF16)] * 2,
        in_specs=[SMEM, HBM],
        out_specs=[VMEM] * 6,
        scratch_shapes=[pltpu.SemaphoreType.DMA],
        compiler_params=PARAMS,
        name="prepare",
    )(place, pltpu.with_memory_space_constraint(inputs, pltpu.HBM))
    sources = (taps, cotangent.reshape(local, local_ch), bias.reshape(1, local_ch))
    taps, cotangent, bias = pl.pallas_call(
        stage_kernel,
        out_shape=[jax.ShapeDtypeStruct(x.shape, x.dtype) for x in sources],
        in_specs=[VMEM] + [HBM] * len(sources),
        out_specs=[VMEM] * len(sources),
        scratch_shapes=[pltpu.SemaphoreType.DMA((len(sources) + 8,))],
        compiler_params=PARAMS,
        name="stage",
    )(even_corner, *[pltpu.with_memory_space_constraint(x, pltpu.HBM) for x in sources])
    beside = exchange(packed, axes, parts_y)
    even = exchange(even, axes, 1)
    odd = exchange(odd, axes, 3)
    even_corner = exchange(even_corner, axes, parts_y + 1)
    odd_corner = exchange(odd_corner, axes, parts_y + 3)
    own, *others, pair = call(
        functools.partial(forward_kernel, parts_y),
        "forward",
        [(flat, F32)] + [(flat, BF16)] * (shards - 1) + [((2,) + packing, BF16)],
        [place, taps, held, packed, even, odd, beside, even_corner, odd_corner],
        [((span_x + 2, span_y + 2, span_z, 3 * local_ch), BF16), ((shards,) + flat, F32)],
    )
    order = sorted(range(1, shards), key=lambda k: (k < 2, k))
    others = [exchange(others[k - 1], "ch", k) for k in order]
    active, slope = call(
        slope_kernel,
        "slope",
        [(flat, BF16), (flat, BF16)],
        [own, *others, bias, cotangent],
    )
    rest = [exchange(slope, "ch", k) for k in sorted(range(1, shards), key=slot_of)]
    rest = jnp.stack(rest).reshape((shards - 1,) + packing)
    piece = slope.reshape((1,) + packing)
    x, y = parts_y, 2
    beside_x = exchange(piece, axes, x)
    beside_y = exchange(jnp.concatenate([piece, pair]), axes, y)
    beside_y, beside_x, rest = lax.optimization_barrier((beside_y, beside_x, rest))
    column = jnp.concatenate([piece, rest])
    late_y, late_x = exchange(rest, axes, y), exchange(rest, axes, x)
    sibling = exchange(jnp.concatenate([column, pair, beside_y[1:]]), axes, 1)
    turned_shape = (parts_y, 9 * local_ch, (parts_x * span_x + 2) * span_y * span_z)
    sums_shape = (3, 9 * local_ch, channels)
    first_outs = [((local, local_ch), BF16), (turned_shape, BF16), (sums_shape, F32)]
    first_outs += [((9, channels, 3 * local_ch), BF16)]
    args = [place, taps, active, pair, beside_y, sibling, column]
    activation, turned, sums, taps = pl.pallas_call(
        functools.partial(first_kernel, parts_x, parts_y),
        out_shape=[jax.ShapeDtypeStruct(shape, kind) for shape, kind in first_outs],
        in_specs=[SMEM] + [VMEM] * (len(args) - 1),
        out_specs=[HBM] + [VMEM] * 3,
        scratch_shapes=[
            pltpu.VMEM((parts_x * span_x + 2, parts_y * span_y + 2, span_z, 3 * local_ch), BF16),
            pltpu.VMEM((local, local_ch), BF16),
            pltpu.SemaphoreType.DMA,
        ],
        compiler_params=PARAMS,
        cost_estimate=pl.CostEstimate(flops=0, bytes_accessed=1024, transcendentals=0),
        name="first",
    )(*args)
    slopes = {0: column, 1: sibling[:shards]}
    late_y, late_x, sums = lax.optimization_barrier((late_y, late_x, sums))
    slopes[y] = jnp.concatenate([beside_y[:1], late_y])
    slopes[x] = jnp.concatenate([beside_x, late_x])
    middle = shards // 2
    diagonal = [exchange(slopes[x][:middle], axes, y), exchange(slopes[y][middle:], axes, x)]
    across = [exchange(slopes[m], axes, 1) for m in (y, x)]
    grid_shape = spans + (3 * local_ch,)
    partial, sums = call(
        functools.partial(second_kernel, parts_y, (y, x)),
        "second",
        [(grid_shape, F32), (sums_shape, F32)],
        [place, taps, turned, sums, column, sibling, slopes[y], slopes[x]],
        [((span_x + 2, span_y + 2, span_z, channels), BF16)],
    )
    slopes[y + 1], slopes[x + 1] = across
    partial, column, sums = call(
        functools.partial(rim_kernel, parts_y, (y + 1, x + 1)),
        "third",
        [(grid_shape, F32), ((1, 2 * local_ch), F32), (sums_shape, F32)],
        [place, taps, turned, sums, partial] + [slopes[m] for m in range(x + y)],
        [((span_y + 2, span_z, channels), BF16), ((span_x + 2, span_z, channels), BF16)],
    )
    *diagonal, sums = lax.optimization_barrier((*diagonal, sums))
    slopes[x + y] = jnp.concatenate(diagonal)
    final = exchange(slopes[x + y], axes, 1)
    (sums,) = call(
        functools.partial(middle_kernel, parts_y, (x + y,)),
        "fourth",
        [(sums_shape, F32)],
        [place, turned, sums, slopes[x + y]],
    )
    args = [place, taps, turned, sums, partial, column, slopes[x + y], final]
    input_grad, kernel_grad, bias_grad = pl.pallas_call(
        functools.partial(last_kernel, parts_y, x + y + 1, factor),
        out_shape=[
            jax.ShapeDtypeStruct((local, local_ch), BF16),
            jax.ShapeDtypeStruct(sums_shape, F32),
            jax.ShapeDtypeStruct((1, local_ch), F32),
        ],
        in_specs=[SMEM] + [VMEM] * (len(args) - 1),
        out_specs=[HBM] * 3,
        scratch_shapes=[
            pltpu.VMEM(grid_shape, F32),
            pltpu.VMEM(sums_shape, F32),
            pltpu.VMEM((local, local_ch), BF16),
            pltpu.VMEM((1, local_ch), F32),
            pltpu.SemaphoreType.DMA((5,)),
        ],
        compiler_params=PARAMS,
        name="last",
    )(*args)
    return (
        activation.reshape(inputs.shape),
        input_grad.reshape(inputs.shape),
        kernel_grad.reshape(weight.shape),
        bias_grad.reshape(local_ch),
    )


def solution(mesh):
    few = (mesh.shape["gx"], mesh.shape["gy"]) == (2, 4)
    return jax.shard_map(
        body_gathered if few else body_reduced,
        mesh=mesh,
        in_specs=(
            P("gx", "gy", None, "ch"),
            P(None, None, None, "ch", None),
            P("ch"),
            P("gx", "gy", None, "ch"),
        ),
        out_specs=(
            P("gx", "gy", None, "ch"),
            P("gx", "gy", None, "ch"),
            P(None, None, None, "ch", None),
            P("ch"),
        ),
        check_vma=False,
    )
```
